32 devices in a mesh: rows: 8 (over z, x), coil: 4 (over y, core).
Axes of the slice: x: 2, y: 2, z: 4, core: 2. Of those that a mesh axis runs over, the one named last changes fastest.
Arguments:
- kspace: float32 [128, 4096], P('coil', 'rows'), may hold values from -6 to 6
- sample_mask: int32 [128, 4096], P('coil', 'rows'), may hold values 0 or 1
- start_basis: float32 [4, 2048, 128], P('coil', 'rows'), may hold values from -6 to 6
Outputs:
- recovered: float32 [128, 4096], P('coil', 'rows')
- basis: float32 [4, 2048, 128], P('coil', 'rows')
The draws below stay inside these ranges and needn't reach their ends.
All inputs are finite; a program needn't handle non-finite values. No bound on the sum of `sample_mask` on one device may be relied on, other than what follows from the above.
Results may differ from the reference program's by a relative error of at most 0.00011.
Values sent between devices are 32-bit elements; how exact they have to be, the bound alone decides.
No kernel may reach another device: no remote copies, remote signals or barrier semaphores. Data moves between devices by JAX's collectives and lax.ppermute only.
A program may use at most 64 MiB of HBM per device.

```python
import jax
import jax.numpy as jnp
from jax import lax

KER = 64
CH = 128
RANK = 128
ITERS = 2
TILE_DEV = 512
POS = 4096
GROUPS = 4
CHG = 32
GW = 2048
N_ROWS = 8


def with_ends(drawn, key, smallest, largest):
    shape = drawn.shape
    index_at = [jax.random.randint(jax.random.fold_in(key, axis), (), 0, shape[axis]) for axis in range(len(shape))]
    drawn = drawn.at[tuple(index_at)].set(smallest)
    longest = shape.index(max(shape))
    index_at[longest] = (index_at[longest] + 1) % shape[longest]
    return drawn.at[tuple(index_at)].set(largest)


def block_scale(rng, dims, shards, low, high):
    def one(axis_at, blocks):
        heights = jax.random.uniform(jax.random.fold_in(jax.random.fold_in(rng, 6), axis_at), (blocks,), jnp.float32, low / len(shards), high / len(shards))
        return jnp.repeat(jnp.exp(heights), dims[axis_at] // blocks).reshape((-1,) + (1,) * (len(dims) - axis_at - 1))

    gain = one(*shards[0])
    for cut in shards[1:]:
        gain = gain * one(*cut)
    return gain


def bell_draw(stream_key, extent, deviation, bound, pieces=(), kind=jnp.bfloat16):
    level = block_scale(stream_key, extent, pieces, -0.22, 0.18) if pieces else 1.0
    array = jax.random.normal(stream_key, extent, jnp.float32) * deviation * level
    return jnp.minimum(jnp.maximum(array, -bound), bound).astype(kind)


def setup_inputs(seed: int = 0) -> dict:
    key_list = jax.random.split(jax.random.key(seed), 4)
    kspace = bell_draw(key_list[0], (CH, POS), 1.0, 6.0, ((0, 4), (1, 8)), jnp.float32)
    sample_mask = with_ends((jax.random.randint(key_list[1], (CH, POS), 0, 2) < 1).astype(jnp.int32), jax.random.fold_in(key_list[1], 1), 0, 1)
    start_basis = bell_draw(key_list[2], (GROUPS, GW, RANK), 1.0, 6.0, ((0, 4), (1, 8)), jnp.float32)
    return dict(kspace=kspace, sample_mask=sample_mask, start_basis=start_basis)


threshold = 0.05

def hankel_block(extended, block_index):
    window = lax.dynamic_slice_in_dim(extended, block_index * TILE_DEV, TILE_DEV + KER - 1, 0)
    shifted = jnp.stack([window[offset:offset + TILE_DEV] for offset in range(KER)], axis=1)
    shifted = shifted.reshape(TILE_DEV, KER, GROUPS, CHG).transpose(0, 2, 1, 3)
    return shifted.reshape(TILE_DEV, GROUPS * GW)

def reference(kspace, sample_mask, start_basis):
    highest = lax.Precision.HIGHEST
    kspace_rows = kspace.T
    mask_rows = sample_mask.T.astype(jnp.float32)
    sampled = kspace_rows * mask_rows
    extended = jnp.concatenate([sampled, sampled[:KER - 1]], axis=0)
    blocks = jnp.arange(N_ROWS, dtype=jnp.int32)
    basis_now = start_basis.reshape(GROUPS * GW, RANK)
    for iteration in range(ITERS):

        def image_block(block_index):
            return jnp.dot(hankel_block(extended, block_index).astype(jnp.float32), basis_now.astype(jnp.float32), precision=highest, preferred_element_type=jnp.float32)
        images = lax.map(image_block, blocks)

        def add_block(running, block_index):
            hankel_rows = hankel_block(extended, block_index)
            term = lax.dot_general(hankel_rows.astype(jnp.float32), images[block_index].astype(jnp.float32), (((0,), (0,)), ((), ())), precision=highest, preferred_element_type=jnp.float32)
            return (running + term, None)
        normal_whole, unused = lax.scan(add_block, jnp.zeros((GROUPS * GW, RANK), jnp.float32), blocks)
        gram_matrix = jnp.dot(normal_whole.T.astype(jnp.float32), normal_whole.astype(jnp.float32), precision=highest, preferred_element_type=jnp.float32)
        factor = jnp.linalg.cholesky(gram_matrix)
        basis_now = lax.linalg.triangular_solve(factor, normal_whole, left_side=False, lower=True, transpose_a=True)

    def spread_block(block_index):
        images = jnp.dot(hankel_block(extended, block_index).astype(jnp.float32), basis_now.astype(jnp.float32), precision=highest, preferred_element_type=jnp.float32)
        projected = jnp.dot(images.astype(jnp.float32), basis_now.T.astype(jnp.float32), precision=highest, preferred_element_type=jnp.float32)
        stacked = projected.reshape(TILE_DEV, GROUPS, KER, CHG).transpose(0, 2, 1, 3).reshape(TILE_DEV, KER, CH)
        spread = jnp.zeros((TILE_DEV + KER - 1, CH), jnp.float32)
        for offset in range(KER):
            spread = spread.at[offset:offset + TILE_DEV].add(stacked[:, offset])
        return spread
    spreads = lax.map(spread_block, blocks)
    main_part = spreads[:, :TILE_DEV]
    tail_parts = spreads[:, TILE_DEV:]
    previous = jnp.roll(tail_parts, 1, axis=0)
    main_part = main_part.at[:, :KER - 1].add(previous)
    estimate = main_part.reshape(POS, CH) / KER
    residual = mask_rows * (kspace_rows - estimate)
    recovered = estimate + residual - jnp.clip(residual, -threshold, threshold)
    return (recovered.T, basis_now.reshape(GROUPS, GW, RANK))
```

```python
import functools

import jax
import jax.numpy as jnp
from jax import lax
from jax.experimental import pallas as pl
from jax.experimental.pallas import tpu as pltpu
from jax.sharding import PartitionSpec as P

KER = 64
ITERS = 2
LANES = 128
SUB = 8
AXES = ("rows", "coil")


threshold = 0.05


def shifted(block, axis, distance):
    devices = range(lax.axis_size(axis))
    route = [((i - distance) % len(devices), i) for i in devices]
    return lax.ppermute(block, axis, route)


def orthonormal(normal_rows, gram_matrix):
    factor = jnp.linalg.cholesky(gram_matrix)
    return lax.linalg.triangular_solve(
        factor, normal_rows, left_side=False, lower=True, transpose_a=True
    )


def coil_total(partial_value):
    return lax.psum(partial_value, "coil")


def general_shards(kspace, sample_mask, start_basis):
    highest = lax.Precision.HIGHEST
    channels = kspace.shape[0]
    tile_rows = kspace.shape[1]
    mask_float = sample_mask.astype(jnp.float32)
    sampled = kspace * mask_float
    next_rim = shifted(sampled[:, : KER - 1], "rows", -1)
    extended = jnp.concatenate([sampled, next_rim], axis=1)
    hankel_cols = jnp.stack(
        [extended[:, offset : offset + tile_rows] for offset in range(KER)], axis=0
    )
    hankel_cols = hankel_cols.reshape(KER * channels, tile_rows)
    owned_basis = start_basis.reshape(start_basis.shape[1], start_basis.shape[2])
    whole_basis = lax.all_gather(owned_basis, "rows", axis=0, tiled=True)
    for iteration in range(ITERS):
        images = coil_total(
            lax.dot_general(
                whole_basis,
                hankel_cols,
                (((0,), (0,)), ((), ())),
                precision=highest,
                preferred_element_type=jnp.float32,
            )
        )
        local_normal = lax.dot_general(
            hankel_cols,
            images,
            (((1,), (1,)), ((), ())),
            precision=highest,
            preferred_element_type=jnp.float32,
        )
        normal_whole = lax.psum(local_normal, "rows")
        local_gram = jnp.dot(
            normal_whole.T, normal_whole, precision=highest, preferred_element_type=jnp.float32
        )
        gram_matrix = lax.psum(local_gram, "coil")
        whole_basis = orthonormal(normal_whole, gram_matrix)
    images = coil_total(
        lax.dot_general(
            whole_basis,
            hankel_cols,
            (((0,), (0,)), ((), ())),
            precision=highest,
            preferred_element_type=jnp.float32,
        )
    )
    projected = jnp.dot(whole_basis, images, precision=highest, preferred_element_type=jnp.float32)
    owned_count = whole_basis.shape[0] // lax.axis_size("rows")
    owned_basis = lax.dynamic_slice_in_dim(
        whole_basis, lax.axis_index("rows") * owned_count, owned_count, 0
    )
    stacked = projected.reshape(KER, channels, tile_rows)
    spread = jnp.zeros((channels, tile_rows + KER - 1), jnp.float32)
    for offset in range(KER):
        spread = spread.at[:, offset : offset + tile_rows].add(stacked[offset])
    carried = shifted(spread[:, tile_rows:], "rows", 1)
    estimate = spread[:, :tile_rows].at[:, : KER - 1].add(carried) / KER
    residual = mask_float * (kspace - estimate)
    recovered = estimate + residual - jnp.clip(residual, -threshold, threshold)
    return (recovered, owned_basis.reshape(1, owned_basis.shape[0], owned_basis.shape[1]))


def split(value):
    high = value.astype(jnp.bfloat16)
    low = (value - high.astype(jnp.float32)).astype(jnp.bfloat16)
    return high, low


def dot(a, b, dims=((1,), (0,))):
    return lax.dot_general(a, b, (dims, ((), ())), preferred_element_type=jnp.float32)


def dot3(a, b, dims=((1,), (0,))):
    a_high, a_low = split(a)
    b_high, b_low = split(b)
    return dot(a_high, b_high, dims) + (dot(a_high, b_low, dims) + dot(a_low, b_high, dims))


def prepare_kernel(cols, chg, per_tile, kspace_ref, mask_ref, basis_ref, sampled_ref, send_ref):
    sampled_ref[...] = kspace_ref[...] * mask_ref[...].astype(jnp.float32)
    turned = basis_ref[...].T
    devices = turned.shape[0] // cols
    for j in range(per_tile):
        part = turned[:, j * chg : (j + 1) * chg]
        row = jnp.concatenate([part[k * devices : (k + 1) * devices] for k in range(cols)], axis=1)
        send_ref[pl.ds(j, devices, stride=per_tile), :] = row


def images_of(vectors, samples_ref, wide_ref):
    rows, channels = vectors.shape
    cols = rows // KER
    high, low = split(vectors)
    at_row = lax.broadcasted_iota(jnp.int32, (rows, rows), 0)
    at_col = lax.broadcasted_iota(jnp.int32, (rows, rows), 1)
    flip = ((at_row // KER == at_col // KER) & (at_row % KER + at_col % KER == KER - 1)).astype(
        jnp.float32
    ).astype(jnp.bfloat16)
    both = dot(flip, jnp.concatenate([high, low], axis=1)).astype(jnp.bfloat16)
    high, low = both[:, :channels], both[:, channels:]
    twice = jnp.concatenate([high, high], axis=1)
    tiles = samples_ref.shape[0]
    tile = samples_ref.shape[-1]
    for t in range(tiles):
        block = samples_ref[t].reshape(2 * channels, tile)
        wide_ref[:, t * tile : (t + 1) * tile] = dot(twice, block) + dot(low, block[:channels])
    images = []
    for k in range(cols):
        total = None
        for i in reversed(range(0, KER, SUB)):
            part = wide_ref[k * KER + i : k * KER + i + SUB, :]
            total = part if total is None else pltpu.roll(total, SUB, 1) + part
        total = pltpu.roll(total, 0, 1, stride=1, stride_axis=0)
        images.append(jnp.sum(total, axis=0, keepdims=True))
    return images


def normal_of(images, samples_ref, moved_ref):
    cols = len(images)
    positions = images[0].shape[1]
    tiles = samples_ref.shape[0]
    tile = samples_ref.shape[-1]
    channels = samples_ref.shape[2] * samples_ref.shape[3]
    rows = cols * KER
    for k in range(cols):
        base = jnp.broadcast_to(images[k], (SUB, positions))
        base = pltpu.roll(base, positions - (KER - 1), 1, stride=1, stride_axis=0)
        for j in range(0, KER, 2 * SUB):
            first = base if j == 0 else pltpu.roll(base, j, 1)
            second = pltpu.roll(base, j + SUB, 1)
            high, low = split(jnp.concatenate([first, second], axis=0))
            moved_ref[k * KER + j : k * KER + j + 2 * SUB, :] = high
            moved_ref[rows + k * KER + j : rows + k * KER + j + 2 * SUB, :] = low
    total = jnp.zeros((2 * rows, 2 * channels), jnp.float32)
    for t in range(tiles):
        block = samples_ref[t].reshape(2 * channels, tile)
        total = total + dot(moved_ref[:, t * tile : (t + 1) * tile], block, ((1,), (1,)))
    return total[:rows, :channels] + (
        total[:rows, channels:] + total[rows:, :channels] + total[rows:, channels:]
    )


def store_by_rows(normal, send_ref):
    tiles, groups, per_tile, lanes = send_ref.shape
    cols = normal.shape[0] // KER
    chg = normal.shape[1] // groups
    for g in range(groups):
        joined = jnp.concatenate(
            [normal[k * KER : (k + 1) * KER, g * chg : (g + 1) * chg] for k in range(cols)], axis=1
        )
        send_ref[:, g] = joined.reshape(tiles, per_tile, lanes)


def first_kernel(
    masks, pieces_ref, late_ref, basis_ref, samples_ref, normal_ref, send_ref, wide_ref, moved_ref
):
    tiles, _, groups, chg, tile = samples_ref.shape
    me = lax.axis_index("rows") * groups + lax.axis_index("coil")
    half = pieces_ref.shape[0]
    for slot, mask in enumerate(masks):
        value = pieces_ref[slot] if slot < half else late_ref[slot - half]
        high, low = split(value)
        source = lax.bitwise_xor(me, mask)
        t, g = source // groups, source % groups
        samples_ref[t, 0, g] = high
        samples_ref[t, 1, g] = low
    cols = basis_ref.shape[-1] // chg
    rows = []
    for k in range(cols):
        rows.append(
            jnp.concatenate(
                [
                    basis_ref[:, g].reshape(KER, cols * chg)[:, k * chg : (k + 1) * chg]
                    for g in range(groups)
                ],
                axis=1,
            )
        )
    vectors = jnp.concatenate(rows, axis=0)
    normal = normal_of(images_of(vectors, samples_ref, wide_ref), samples_ref, moved_ref)
    scaled = []
    for k in range(cols):
        part = normal[k * KER : (k + 1) * KER]
        scaled.append(part * (1.0 / jnp.max(jnp.abs(part))))
    normal = jnp.concatenate(scaled, axis=0)
    normal_ref[...] = normal
    store_by_rows(normal, send_ref)


def second_kernel(samples_ref, vectors_ref, normal_ref, send_ref, wide_ref, moved_ref):
    normal = normal_of(
        images_of(vectors_ref[...], samples_ref, wide_ref), samples_ref, moved_ref
    )
    normal_ref[...] = normal
    store_by_rows(normal, send_ref)


def third_kernel(samples_ref, vectors_ref, send_ref, wide_ref):
    tiles, cols, reach = send_ref.shape
    tile = samples_ref.shape[-1]
    images = jnp.concatenate(images_of(vectors_ref[...], samples_ref, wide_ref), axis=0)
    positions = images.shape[1]
    images = pltpu.roll(images, positions - (KER - 1), 1)
    rim = reach - tile
    for t in range(tiles):
        if t == 0:
            part = jnp.concatenate([images[:, positions - rim :], images[:, :tile]], axis=1)
        else:
            part = images[:, t * tile - rim : (t + 1) * tile]
        send_ref[t] = part


def gather_turned(received_ref, cols, per_tile):
    count, lanes = received_ref.shape
    devices = count // per_tile
    chg = lanes // cols
    loaded = [received_ref[pl.ds(j, devices, stride=per_tile), :] for j in range(per_tile)]
    return jnp.concatenate(
        [
            jnp.concatenate(
                [loaded[j][:, k * chg : (k + 1) * chg] for j in range(per_tile)], axis=1
            )
            for k in range(cols)
        ],
        axis=0,
    )


def exact(a, b, dims=((1,), (0,))):
    return lax.dot_general(
        a, b, (dims, ((), ())), precision=lax.Precision.HIGHEST, preferred_element_type=jnp.float32
    )


def gram_kernel(cols, per_tile, received_ref, gram_ref):
    turned = gather_turned(received_ref, cols, per_tile)
    gram_ref[...] = exact(turned, turned, ((1,), (1,)))


def second_gram_kernel(cols, per_tile, received_ref, inverse_ref, turned_ref, gram_ref):
    turned = gather_turned(received_ref, cols, per_tile)
    turned = exact(inverse_ref[...], turned)
    turned_ref[...] = turned
    gram_ref[...] = exact(turned, turned, ((1,), (1,)))


def inverse_factor(gram):
    size = gram.shape[0]
    at_row = lax.broadcasted_iota(jnp.int32, (size, size), 0)
    at_col = lax.broadcasted_iota(jnp.int32, (size, size), 1)
    unit = (at_row == at_col).astype(jnp.float32)
    left = [gram[b : b + SUB] for b in range(0, size, SUB)]
    right = [unit[b : b + SUB] for b in range(0, size, SUB)]
    sub = lax.broadcasted_iota(jnp.int32, (SUB, size), 0)
    for j in range(size):
        b, s = j // SUB, j % SUB
        pivot = left[b][s : s + 1, j : j + 1]
        root = lax.rsqrt(pivot)
        root = root * (1.5 - 0.5 * pivot * root * root)
        upper = left[b][s : s + 1] * root
        lower = right[b][s : s + 1] * root
        for c in range(b, len(left)):
            factor = left[c][:, j : j + 1] * root
            if c == b:
                factor = jnp.where(sub > s, factor, 0.0)
            new_left = left[c] - factor * upper
            new_right = right[c] - factor * lower
            if c == b:
                new_left = jnp.where(sub == s, upper, new_left)
                new_right = jnp.where(sub == s, lower, new_right)
            left[c], right[c] = new_left, new_right
    return jnp.concatenate(right, axis=0)


def factor_kernel(gram_ref, inverse_ref):
    inverse_ref[...] = inverse_factor(gram_ref[...])


def last_kernel(
    cols,
    masks,
    images_ref,
    turned_ref,
    near_ref,
    far_ref,
    first_ref,
    gram_ref,
    kspace_ref,
    mask_ref,
    recovered_ref,
    basis_ref,
):
    inverse = inverse_factor(gram_ref[...])
    count, reach = images_ref.shape
    devices = count // cols
    at_row = lax.broadcasted_iota(jnp.int32, (count, count), 0)
    at_col = lax.broadcasted_iota(jnp.int32, (count, count), 1)
    order = ((at_row // devices == at_col % cols) & (at_row % devices == at_col // cols)).astype(
        jnp.float32
    )
    images = exact(inverse, exact(exact(first_ref[...], order), images_ref[...]))
    images_high, images_low = split(images)
    stacked = jnp.concatenate([images_high, images_low], axis=0)
    chg, tile = kspace_ref.shape
    me = lax.axis_index("rows")
    half = near_ref.shape[0]
    estimate = jnp.zeros((chg, tile), jnp.float32)
    for slot, mask in enumerate(masks):
        turned = near_ref[slot] if slot < half else far_ref[slot - half]
        vectors = exact(inverse, turned).T
        if slot == 0:
            basis_ref[...] = vectors
        high, low = split(vectors)
        projected = dot(jnp.concatenate([high, high], axis=1), stacked) + dot(low, images_high)
        per_tile = vectors.shape[0] // chg
        total = projected[:chg]
        for j in range(1, per_tile):
            total = total + pltpu.roll(projected[j * chg : (j + 1) * chg], j, 1)
        t = lax.bitwise_xor(me, mask)
        total = pltpu.roll(total, t * per_tile, 1)
        estimate = estimate + total[:, reach - tile :]
    estimate = estimate / KER
    residual = mask_ref[...].astype(jnp.float32) * (kspace_ref[...] - estimate)
    recovered_ref[...] = estimate + residual - jnp.clip(residual, -threshold, threshold)


def call(kernel, outs, *args, scratch=()):
    return pl.pallas_call(
        kernel,
        out_shape=[jax.ShapeDtypeStruct(shape, kind) for shape, kind in outs],
        in_specs=[pl.BlockSpec(memory_space=pltpu.VMEM)] * len(args),
        out_specs=[pl.BlockSpec(memory_space=pltpu.VMEM)] * len(outs),
        scratch_shapes=[pltpu.VMEM(shape, kind) for shape, kind in scratch],
        compiler_params=pltpu.CompilerParams(vmem_limit_bytes=40 * 2**20),
    )(*args)


def exchange(block, devices, mask, axes):
    return lax.ppermute(block, axes, [(i, i ^ mask) for i in range(devices)])


def gather_by_halves(block, devices, axes):
    masks = [0]
    near = block[None]
    far = None
    mask = devices // 2
    while mask:
        if far is not None:
            near = jnp.concatenate([near, far], axis=0)
        far = exchange(near, devices, mask, axes)
        masks = masks + [m ^ mask for m in masks]
        mask //= 2
    return near, far, masks


def to_all(pieces):
    return lax.all_to_all(pieces, AXES, 0, 0, tiled=True)


def total_of(gram, devices):
    size = gram.shape[0]
    parts = to_all(gram.reshape(devices, size // devices, size))
    mine = jnp.sum(parts, axis=0)
    spread = to_all(jnp.broadcast_to(mine[None], parts.shape))
    return spread.reshape(size, size)


def column_shards(kspace, sample_mask, start_basis):
    f32, bf16 = jnp.float32, jnp.bfloat16
    tiles, groups = lax.axis_size("rows"), lax.axis_size("coil")
    devices = tiles * groups
    chg, tile = kspace.shape
    channels = chg * groups
    positions = tile * tiles
    owned, rank = start_basis.shape[1:]
    per_tile = owned // chg
    cols = rank // devices
    rows = cols * KER
    lanes = cols * chg

    sampled, basis_send = call(
        functools.partial(prepare_kernel, cols, chg, per_tile),
        [((chg, tile), f32), ((devices * per_tile, lanes), f32)],
        kspace,
        sample_mask,
        start_basis.reshape(owned, rank),
    )
    basis_parts = to_all(basis_send.reshape(devices, per_tile, lanes))
    near, far, masks = gather_by_halves(sampled, devices, AXES)
    wide = ((rows, positions), f32)
    moved = ((2 * rows, positions), bf16)
    by_rows = ((tiles, groups, per_tile, lanes), f32)
    samples, normal, send = call(
        functools.partial(first_kernel, masks),
        [((tiles, 2, groups, chg, tile), bf16), ((rows, channels), f32), by_rows],
        near,
        far,
        basis_parts.reshape(tiles, groups, per_tile, lanes),
        scratch=[wide, moved],
    )
    received = to_all(send.reshape(devices, per_tile, lanes))
    (gram,) = call(
        functools.partial(gram_kernel, cols, per_tile),
        [((rank, rank), f32)],
        received.reshape(devices * per_tile, lanes),
    )
    gram = total_of(gram, devices)
    (first,) = call(factor_kernel, [((rank, rank), f32)], gram)

    normal, send = call(
        second_kernel, [((rows, channels), f32), by_rows], samples, normal, scratch=[wide, moved]
    )
    received = to_all(send.reshape(devices, per_tile, lanes))
    reach = tile + LANES
    (images,) = call(third_kernel, [((tiles, cols, reach), f32)], samples, normal, scratch=[wide])
    images = jnp.broadcast_to(images[:, None], (tiles, groups, cols, reach))
    images = to_all(images.reshape(devices, cols, reach)).reshape(rank, reach)

    turned, gram = call(
        functools.partial(second_gram_kernel, cols, per_tile),
        [((rank, owned), f32), ((rank, rank), f32)],
        received.reshape(devices * per_tile, lanes),
        first,
    )
    gram = total_of(gram, devices)
    near, far, masks = gather_by_halves(turned, tiles, "rows")
    recovered, basis = call(
        functools.partial(last_kernel, cols, masks),
        [((chg, tile), f32), ((owned, rank), f32)],
        images,
        turned,
        near,
        far,
        first,
        gram,
        kspace,
        sample_mask,
    )
    return (recovered, basis.reshape(1, owned, rank))


def divides_columns(kspace, start_basis):
    tiles, groups = lax.axis_size("rows"), lax.axis_size("coil")
    devices = tiles * groups
    chg, tile = kspace.shape
    owned, rank = start_basis.shape[1:]
    return (
        devices & (devices - 1) == 0
        and tiles > 1
        and rank % devices == 0
        and rank % LANES == 0
        and tile % LANES == 0
        and owned % (SUB * chg) == 0
        and chg * (rank // devices) == LANES
        and chg % (2 * SUB) == 0
        and (chg * groups) % LANES == 0
        and KER <= LANES
    )


def shards(kspace, sample_mask, start_basis):
    if divides_columns(kspace, start_basis):
        return column_shards(kspace, sample_mask, start_basis)
    return general_shards(kspace, sample_mask, start_basis)


def solution(mesh):
    return jax.shard_map(
        shards,
        mesh=mesh,
        in_specs=(P("coil", "rows"), P("coil", "rows"), P("coil", "rows", None)),
        out_specs=(P("coil", "rows"), P("coil", "rows", None)),
        check_vma=False,
    )
```

```python
import functools

import jax
import jax.numpy as jnp
from jax import lax
from jax.experimental import pallas as pl
from jax.experimental.pallas import tpu as pltpu
from jax.sharding import PartitionSpec as P

KER = 64
ITERS = 2
LANES = 128
SUB = 8
AXES = ("rows", "coil")


threshold = 0.05


def shifted(block, axis, distance):
    devices = range(lax.axis_size(axis))
    route = [((i - distance) % len(devices), i) for i in devices]
    return lax.ppermute(block, axis, route)


def orthonormal(normal_rows, gram_matrix):
    factor = jnp.linalg.cholesky(gram_matrix)
    return lax.linalg.triangular_solve(
        factor, normal_rows, left_side=False, lower=True, transpose_a=True
    )


def coil_total(partial_value):
    return lax.psum(partial_value, "coil")


def general_shards(kspace, sample_mask, start_basis):
    highest = lax.Precision.HIGHEST
    channels = kspace.shape[0]
    tile_rows = kspace.shape[1]
    mask_float = sample_mask.astype(jnp.float32)
    sampled = kspace * mask_float
    next_rim = shifted(sampled[:, : KER - 1], "rows", -1)
    extended = jnp.concatenate([sampled, next_rim], axis=1)
    hankel_cols = jnp.stack(
        [extended[:, offset : offset + tile_rows] for offset in range(KER)], axis=0
    )
    hankel_cols = hankel_cols.reshape(KER * channels, tile_rows)
    owned_basis = start_basis.reshape(start_basis.shape[1], start_basis.shape[2])
    whole_basis = lax.all_gather(owned_basis, "rows", axis=0, tiled=True)
    for iteration in range(ITERS):
        images = coil_total(
            lax.dot_general(
                whole_basis,
                hankel_cols,
                (((0,), (0,)), ((), ())),
                precision=highest,
                preferred_element_type=jnp.float32,
            )
        )
        local_normal = lax.dot_general(
            hankel_cols,
            images,
            (((1,), (1,)), ((), ())),
            precision=highest,
            preferred_element_type=jnp.float32,
        )
        normal_whole = lax.psum(local_normal, "rows")
        local_gram = jnp.dot(
            normal_whole.T, normal_whole, precision=highest, preferred_element_type=jnp.float32
        )
        gram_matrix = lax.psum(local_gram, "coil")
        whole_basis = orthonormal(normal_whole, gram_matrix)
    images = coil_total(
        lax.dot_general(
            whole_basis,
            hankel_cols,
            (((0,), (0,)), ((), ())),
            precision=highest,
            preferred_element_type=jnp.float32,
        )
    )
    projected = jnp.dot(whole_basis, images, precision=highest, preferred_element_type=jnp.float32)
    owned_count = whole_basis.shape[0] // lax.axis_size("rows")
    owned_basis = lax.dynamic_slice_in_dim(
        whole_basis, lax.axis_index("rows") * owned_count, owned_count, 0
    )
    stacked = projected.reshape(KER, channels, tile_rows)
    spread = jnp.zeros((channels, tile_rows + KER - 1), jnp.float32)
    for offset in range(KER):
        spread = spread.at[:, offset : offset + tile_rows].add(stacked[offset])
    carried = shifted(spread[:, tile_rows:], "rows", 1)
    estimate = spread[:, :tile_rows].at[:, : KER - 1].add(carried) / KER
    residual = mask_float * (kspace - estimate)
    recovered = estimate + residual - jnp.clip(residual, -threshold, threshold)
    return (recovered, owned_basis.reshape(1, owned_basis.shape[0], owned_basis.shape[1]))


def split(value):
    high = value.astype(jnp.bfloat16)
    low = (value - high.astype(jnp.float32)).astype(jnp.bfloat16)
    return high, low


def dot(a, b, dims=((1,), (0,))):
    return lax.dot_general(a, b, (dims, ((), ())), preferred_element_type=jnp.float32)


def dot3(a, b, dims=((1,), (0,))):
    a_high, a_low = split(a)
    b_high, b_low = split(b)
    return dot(a_high, b_high, dims) + (dot(a_high, b_low, dims) + dot(a_low, b_high, dims))


def prepare_kernel(
    cols,
    chg,
    per_tile,
    kspace_hbm,
    mask_hbm,
    basis_hbm,
    sampled_ref,
    send_ref,
    kspace_ref,
    mask_ref,
    basis_ref,
    sems,
):
    fetches = [
        pltpu.make_async_copy(source, target, sems.at[i])
        for i, (source, target) in enumerate(
            [(kspace_hbm, kspace_ref), (mask_hbm, mask_ref), (basis_hbm, basis_ref)]
        )
    ]
    for fetch in fetches:
        fetch.start()
    fetches[0].wait()
    fetches[1].wait()
    sampled_ref[...] = kspace_ref[...] * mask_ref[...].astype(jnp.float32)
    fetches[2].wait()
    turned = basis_ref[...].T
    devices = turned.shape[0] // cols
    for j in range(per_tile):
        part = turned[:, j * chg : (j + 1) * chg]
        row = jnp.concatenate([part[k * devices : (k + 1) * devices] for k in range(cols)], axis=1)
        send_ref[pl.ds(j, devices, stride=per_tile), :] = row


def images_of(vectors, samples_ref, wide_ref):
    rows, channels = vectors.shape
    cols = rows // KER
    high, low = split(vectors)
    at_row = lax.broadcasted_iota(jnp.int32, (rows, rows), 0)
    at_col = lax.broadcasted_iota(jnp.int32, (rows, rows), 1)
    flip = ((at_row // KER == at_col // KER) & (at_row % KER + at_col % KER == KER - 1)).astype(
        jnp.float32
    ).astype(jnp.bfloat16)
    both = dot(flip, jnp.concatenate([high, low], axis=1)).astype(jnp.bfloat16)
    high, low = both[:, :channels], both[:, channels:]
    twice = jnp.concatenate([high, high], axis=1)
    tiles = samples_ref.shape[0]
    tile = samples_ref.shape[-1]
    for t in range(tiles):
        block = samples_ref[t].reshape(2 * channels, tile)
        wide_ref[:, t * tile : (t + 1) * tile] = dot(twice, block) + dot(low, block[:channels])
    images = []
    for k in range(cols):
        total = None
        for i in reversed(range(0, KER, SUB)):
            part = wide_ref[k * KER + i : k * KER + i + SUB, :]
            total = part if total is None else pltpu.roll(total, SUB, 1) + part
        total = pltpu.roll(total, 0, 1, stride=1, stride_axis=0)
        images.append(jnp.sum(total, axis=0, keepdims=True))
    return images


def normal_of(images, samples_ref, moved_ref):
    cols = len(images)
    positions = images[0].shape[1]
    tiles = samples_ref.shape[0]
    tile = samples_ref.shape[-1]
    channels = samples_ref.shape[2] * samples_ref.shape[3]
    rows = cols * KER
    for k in range(cols):
        base = jnp.broadcast_to(images[k], (SUB, positions))
        base = pltpu.roll(base, positions - (KER - 1), 1, stride=1, stride_axis=0)
        for j in range(0, KER, 2 * SUB):
            first = base if j == 0 else pltpu.roll(base, j, 1)
            second = pltpu.roll(base, j + SUB, 1)
            high, low = split(jnp.concatenate([first, second], axis=0))
            moved_ref[k * KER + j : k * KER + j + 2 * SUB, :] = high
            moved_ref[rows + k * KER + j : rows + k * KER + j + 2 * SUB, :] = low
    total = jnp.zeros((2 * rows, 2 * channels), jnp.float32)
    for t in range(tiles):
        block = samples_ref[t].reshape(2 * channels, tile)
        total = total + dot(moved_ref[:, t * tile : (t + 1) * tile], block, ((1,), (1,)))
    return total[:rows, :channels] + (
        total[:rows, channels:] + total[rows:, :channels] + total[rows:, channels:]
    )


def store_by_rows(normal, send_ref, part):
    tiles, groups, _, per_tile, lanes = send_ref.shape
    cols = normal.shape[0] // KER
    chg = normal.shape[1] // groups
    for g in range(groups):
        joined = jnp.concatenate(
            [normal[k * KER : (k + 1) * KER, g * chg : (g + 1) * chg] for k in range(cols)], axis=1
        )
        send_ref[:, g, part] = joined.reshape(tiles, per_tile, lanes)


def passes_kernel(
    masks,
    top_near_ref,
    top_far_ref,
    low_near_ref,
    low_far_ref,
    basis_ref,
    samples_ref,
    normal_ref,
    send_ref,
    wide_ref,
    moved_ref,
):
    tiles, _, groups, chg, tile = samples_ref.shape
    me = lax.axis_index("rows") * groups + lax.axis_index("coil")
    start = 0
    for near_ref, far_ref, order in (
        (top_near_ref, top_far_ref, masks[0]),
        (low_near_ref, low_far_ref, masks[1]),
    ):
        half, count = near_ref.shape[:2]
        for slot, mask in enumerate(order):
            value = near_ref[slot] if slot < half else far_ref[slot - half]
            high, low = split(value)
            source = lax.bitwise_xor(me, mask)
            t, g = source // groups, source % groups
            samples_ref[t, 0, g, start : start + count] = high
            samples_ref[t, 1, g, start : start + count] = low
        start += count
    cols = basis_ref.shape[-1] // chg
    rows = []
    for k in range(cols):
        rows.append(
            jnp.concatenate(
                [
                    basis_ref[:, g].reshape(KER, cols * chg)[:, k * chg : (k + 1) * chg]
                    for g in range(groups)
                ],
                axis=1,
            )
        )
    vectors = jnp.concatenate(rows, axis=0)
    normal = normal_of(images_of(vectors, samples_ref, wide_ref), samples_ref, moved_ref)
    scaled = []
    for k in range(cols):
        part = normal[k * KER : (k + 1) * KER]
        scaled.append(part * (1.0 / jnp.max(jnp.abs(part))))
    normal = jnp.concatenate(scaled, axis=0)
    store_by_rows(normal, send_ref, 0)
    normal = normal_of(images_of(normal, samples_ref, wide_ref), samples_ref, moved_ref)
    normal_ref[...] = normal
    store_by_rows(normal, send_ref, 1)


def images_kernel(samples_ref, vectors_ref, send_ref, wide_ref):
    tiles, cols, reach = send_ref.shape
    tile = samples_ref.shape[-1]
    images = jnp.concatenate(images_of(vectors_ref[...], samples_ref, wide_ref), axis=0)
    positions = images.shape[1]
    images = pltpu.roll(images, positions - (KER - 1), 1)
    rim = reach - tile
    for t in range(tiles):
        if t == 0:
            part = jnp.concatenate([images[:, positions - rim :], images[:, :tile]], axis=1)
        else:
            part = images[:, t * tile - rim : (t + 1) * tile]
        send_ref[t] = part


def gather_turned(received_ref, cols, per_tile, part):
    count, lanes = received_ref.shape
    devices = count // (2 * per_tile)
    chg = lanes // cols
    loaded = [
        received_ref[pl.ds(part * per_tile + j, devices, stride=2 * per_tile), :]
        for j in range(per_tile)
    ]
    return jnp.concatenate(
        [
            jnp.concatenate(
                [loaded[j][:, k * chg : (k + 1) * chg] for j in range(per_tile)], axis=1
            )
            for k in range(cols)
        ],
        axis=0,
    )


def exact(a, b, dims=((1,), (0,))):
    return lax.dot_general(
        a, b, (dims, ((), ())), precision=lax.Precision.HIGHEST, preferred_element_type=jnp.float32
    )


def gram_kernel(cols, per_tile, received_ref, gram_ref, turned_ref):
    turned = gather_turned(received_ref, cols, per_tile, 0)
    gram_ref[...] = exact(turned, turned, ((1,), (1,)))
    turned_ref[...] = gather_turned(received_ref, cols, per_tile, 1)


def inverse_factor(gram):
    size = gram.shape[0]
    shape = (SUB, size)
    at_row = lax.broadcasted_iota(jnp.int32, (size, size), 0)
    at_col = lax.broadcasted_iota(jnp.int32, (size, size), 1)
    unit = (at_row == at_col).astype(jnp.float32)
    left = [gram[b : b + SUB] for b in range(0, size, SUB)]
    right = [unit[b : b + SUB] for b in range(0, size, SUB)]
    sub = lax.broadcasted_iota(jnp.int32, shape, 0)
    done = []
    for b in range(len(left)):
        spread = {
            c: [
                jnp.broadcast_to(left[c][:, b * SUB + k : b * SUB + k + 1], shape)
                for k in range(SUB)
            ]
            for c in range(b, len(left))
        }
        entry = {
            (i, k): jnp.broadcast_to(spread[b][k][i : i + 1], shape)
            for k in range(SUB)
            for i in range(k, SUB)
        }
        inverse = {}
        for k in range(SUB):
            root = lax.rsqrt(entry[k, k])
            root = root * (1.5 - (0.5 * entry[k, k]) * (root * root))
            inverse[k, k] = root
            for i in range(k + 1, SUB):
                entry[i, k] = entry[i, k] * root
            for i in range(k + 1, SUB):
                for m in range(k + 1, i + 1):
                    entry[i, m] = entry[i, m] - entry[i, k] * entry[m, k]
        for i in range(1, SUB):
            for k in range(i):
                total = entry[i, k] * inverse[k, k]
                for m in range(k + 1, i):
                    total = total + entry[i, m] * inverse[m, k]
                inverse[i, k] = -(total * inverse[i, i])

        def solved(rows):
            whole = [jnp.broadcast_to(rows[k : k + 1], shape) for k in range(SUB)]
            first = []
            for i in range(SUB):
                total = inverse[i, 0] * whole[0]
                for k in range(1, i + 1):
                    total = total + inverse[i, k] * whole[k]
                first.append(total)
            second = []
            for k in range(SUB):
                total = inverse[k, k] * first[k]
                for i in range(k + 1, SUB):
                    total = total + inverse[i, k] * first[i]
                second.append(total)
            return first, second

        lower, lower_again = solved(right[b])
        row = lower[0]
        for i in range(1, SUB):
            row = jnp.where(sub == i, lower[i], row)
        done.append(row)
        if b + 1 < len(left):
            _, upper_again = solved(left[b])
            for c in range(b + 1, len(left)):
                for k in range(SUB):
                    left[c] = left[c] - spread[c][k] * upper_again[k]
                    right[c] = right[c] - spread[c][k] * lower_again[k]
    return jnp.concatenate(done, axis=0)


def middle_kernel(gram_ref, turned_ref, inverse_ref, next_ref):
    inverse = inverse_factor(gram_ref[...])
    inverse_ref[...] = inverse
    turned = exact(inverse, turned_ref[...])
    next_ref[...] = exact(turned, turned, ((1,), (1,)))


def last_kernel(
    cols,
    masks,
    images_ref,
    near_ref,
    far_ref,
    first_ref,
    gram_ref,
    kspace_ref,
    mask_ref,
    recovered_ref,
    basis_ref,
):
    inverse = inverse_factor(gram_ref[...])
    count, reach = images_ref.shape
    devices = count // cols
    at_row = lax.broadcasted_iota(jnp.int32, (count, count), 0)
    at_col = lax.broadcasted_iota(jnp.int32, (count, count), 1)
    order = ((at_row // devices == at_col % cols) & (at_row % devices == at_col // cols)).astype(
        jnp.float32
    )
    inverse = exact(inverse, first_ref[...])
    images = exact(exact(inverse, order), images_ref[...])
    images_high, images_low = split(images)
    stacked = jnp.concatenate([images_high, images_low], axis=0)
    chg, tile = kspace_ref.shape
    me = lax.axis_index("rows")
    half = near_ref.shape[0]
    estimate = jnp.zeros((chg, tile), jnp.float32)
    for slot, mask in enumerate(masks):
        turned = near_ref[slot] if slot < half else far_ref[slot - half]
        vectors = exact(inverse, turned).T
        if slot == 0:
            basis_ref[...] = vectors
        high, low = split(vectors)
        projected = dot(jnp.concatenate([high, high], axis=1), stacked) + dot(low, images_high)
        per_tile = vectors.shape[0] // chg
        total = projected[:chg]
        for j in range(1, per_tile):
            total = total + pltpu.roll(projected[j * chg : (j + 1) * chg], j, 1)
        t = lax.bitwise_xor(me, mask)
        total = pltpu.roll(total, t * per_tile, 1)
        estimate = estimate + total[:, reach - tile :]
    estimate = estimate / KER
    residual = mask_ref[...].astype(jnp.float32) * (kspace_ref[...] - estimate)
    recovered_ref[...] = estimate + residual - jnp.clip(residual, -threshold, threshold)


def call(kernel, outs, *args, scratch=(), space=pltpu.VMEM):
    return pl.pallas_call(
        kernel,
        out_shape=[jax.ShapeDtypeStruct(shape, kind) for shape, kind in outs],
        in_specs=[pl.BlockSpec(memory_space=space)] * len(args),
        out_specs=[pl.BlockSpec(memory_space=pltpu.VMEM)] * len(outs),
        scratch_shapes=list(scratch),
        compiler_params=pltpu.CompilerParams(vmem_limit_bytes=40 * 2**20),
    )(*args)


def exchange(block, devices, mask, axes):
    return lax.ppermute(block, axes, [(i, i ^ mask) for i in range(devices)])


def joined(near, far):
    return jnp.concatenate([near, far], axis=0)


def with_masks(masks, mask):
    return masks + [m ^ mask for m in masks]


def after(value, *others):
    return lax.optimization_barrier((value,) + others)[0]


def gather_samples(sampled, tiles, groups, beside):
    devices = tiles * groups
    near, masks = sampled[None], [0]
    mask = devices // 2
    while mask > groups:
        near = joined(near, exchange(near, devices, mask, AXES))
        masks = with_masks(masks, mask)
        mask //= 2
    near = after(near, beside)
    half = near.shape[1] // 2
    parts = [near[:, :half], near[:, half:]]
    orders = [masks, masks]
    ways = [(groups, groups // 2), (groups // 2, groups)]
    for step in range(2):
        parts = [
            joined(part, exchange(part, devices, way[step], AXES)) for part, way in zip(parts, ways)
        ]
        orders = [with_masks(order, way[step]) for order, way in zip(orders, ways)]
    mask = groups // 4
    while mask > 1:
        parts = [joined(part, exchange(part, devices, mask, AXES)) for part in parts]
        orders = [with_masks(order, mask) for order in orders]
        mask //= 2
    far = [exchange(part, devices, 1, AXES) for part in parts]
    orders = [with_masks(order, 1) for order in orders]
    return parts, far, orders


def to_all(pieces, axes=AXES):
    return lax.all_to_all(pieces, axes, 0, 0, tiled=True)


def total_of(gram, tiles, groups):
    size = gram.shape[0]
    block = (size // groups, size)
    mine = jnp.sum(to_all(gram.reshape((groups,) + block), "coil"), axis=0)
    mine = jnp.sum(to_all(jnp.broadcast_to(mine[None], (tiles,) + block), "rows"), axis=0)
    whole = to_all(jnp.broadcast_to(mine[None], (groups,) + block), "coil")
    return whole.reshape(size, size)


def column_shards(kspace, sample_mask, start_basis):
    f32, bf16 = jnp.float32, jnp.bfloat16
    tiles, groups = lax.axis_size("rows"), lax.axis_size("coil")
    devices = tiles * groups
    chg, tile = kspace.shape
    channels = chg * groups
    positions = tile * tiles
    owned, rank = start_basis.shape[1:]
    per_tile = owned // chg
    cols = rank // devices
    rows = cols * KER
    lanes = cols * chg

    sampled, basis_send = call(
        functools.partial(prepare_kernel, cols, chg, per_tile),
        [((chg, tile), f32), ((devices * per_tile, lanes), f32)],
        kspace,
        sample_mask,
        start_basis.reshape(owned, rank),
        scratch=[
            pltpu.VMEM((chg, tile), f32),
            pltpu.VMEM((chg, tile), sample_mask.dtype),
            pltpu.VMEM((owned, rank), f32),
            pltpu.SemaphoreType.DMA((3,)),
        ],
        space=pl.ANY,
    )
    basis_parts = to_all(basis_send.reshape(devices, per_tile, lanes))
    near, far, masks = gather_samples(sampled, tiles, groups, basis_parts)
    wide = pltpu.VMEM((rows, positions), f32)
    moved = pltpu.VMEM((2 * rows, positions), bf16)
    samples, normal, send = call(
        functools.partial(passes_kernel, masks),
        [
            ((tiles, 2, groups, chg, tile), bf16),
            ((rows, channels), f32),
            ((tiles, groups, 2, per_tile, lanes), f32),
        ],
        near[0],
        far[0],
        near[1],
        far[1],
        basis_parts.reshape(tiles, groups, per_tile, lanes),
        scratch=[wide, moved],
    )
    received = to_all(send.reshape(devices, 2 * per_tile, lanes))
    reach = tile + LANES
    (images,) = call(images_kernel, [((tiles, cols, reach), f32)], samples, normal, scratch=[wide])
    images = jnp.broadcast_to(images[:, None], (tiles, groups, cols, reach))
    gram, turned = call(
        functools.partial(gram_kernel, cols, per_tile),
        [((rank, rank), f32), ((rank, owned), f32)],
        received.reshape(devices * 2 * per_tile, lanes),
    )
    gram = total_of(gram, tiles, groups)
    images = to_all(images.reshape(devices, cols, reach)).reshape(rank, reach)
    near, masks = turned[None], [0]
    mask = tiles // 2
    while mask > 1:
        near = joined(near, exchange(near, tiles, mask, "rows"))
        masks = with_masks(masks, mask)
        mask //= 2
    far = exchange(near, tiles, 1, "rows")
    masks = with_masks(masks, 1)
    inverse, gram = call(
        middle_kernel, [((rank, rank), f32), ((rank, rank), f32)], gram, turned
    )
    gram = total_of(gram, tiles, groups)
    recovered, basis = call(
        functools.partial(last_kernel, cols, masks),
        [((chg, tile), f32), ((owned, rank), f32)],
        images,
        near,
        far,
        inverse,
        gram,
        kspace,
        sample_mask,
    )
    return (recovered, basis.reshape(1, owned, rank))


def divides_columns(kspace, start_basis):
    tiles, groups = lax.axis_size("rows"), lax.axis_size("coil")
    devices = tiles * groups
    chg, tile = kspace.shape
    owned, rank = start_basis.shape[1:]
    return (
        devices & (devices - 1) == 0
        and tiles > 1
        and groups > 2
        and rank % devices == 0
        and rank % LANES == 0
        and tile % LANES == 0
        and owned % (SUB * chg) == 0
        and chg * (rank // devices) == LANES
        and chg % (4 * SUB) == 0
        and (chg * groups) % LANES == 0
        and KER <= LANES
    )


def shards(kspace, sample_mask, start_basis):
    if divides_columns(kspace, start_basis):
        return column_shards(kspace, sample_mask, start_basis)
    return general_shards(kspace, sample_mask, start_basis)


def solution(mesh):
    return jax.shard_map(
        shards,
        mesh=mesh,
        in_specs=(P("coil", "rows"), P("coil", "rows"), P("coil", "rows", None)),
        out_specs=(P("coil", "rows"), P("coil", "rows", None)),
        check_vma=False,
    )
```

```python
import functools

import jax
import jax.numpy as jnp
from jax import lax
from jax.experimental import pallas as pl
from jax.experimental.pallas import tpu as pltpu
from jax.sharding import PartitionSpec as P

KER = 64
ITERS = 2
LANES = 128
SUB = 8
AXES = ("rows", "coil")


threshold = 0.05


def shifted(block, axis, distance):
    devices = range(lax.axis_size(axis))
    route = [((i - distance) % len(devices), i) for i in devices]
    return lax.ppermute(block, axis, route)


def orthonormal(normal_rows, gram_matrix):
    factor = jnp.linalg.cholesky(gram_matrix)
    return lax.linalg.triangular_solve(
        factor, normal_rows, left_side=False, lower=True, transpose_a=True
    )


def coil_total(partial_value):
    return lax.psum(partial_value, "coil")


def general_shards(kspace, sample_mask, start_basis):
    highest = lax.Precision.HIGHEST
    channels = kspace.shape[0]
    tile_rows = kspace.shape[1]
    mask_float = sample_mask.astype(jnp.float32)
    sampled = kspace * mask_float
    next_rim = shifted(sampled[:, : KER - 1], "rows", -1)
    extended = jnp.concatenate([sampled, next_rim], axis=1)
    hankel_cols = jnp.stack(
        [extended[:, offset : offset + tile_rows] for offset in range(KER)], axis=0
    )
    hankel_cols = hankel_cols.reshape(KER * channels, tile_rows)
    owned_basis = start_basis.reshape(start_basis.shape[1], start_basis.shape[2])
    whole_basis = lax.all_gather(owned_basis, "rows", axis=0, tiled=True)
    for iteration in range(ITERS):
        images = coil_total(
            lax.dot_general(
                whole_basis,
                hankel_cols,
                (((0,), (0,)), ((), ())),
                precision=highest,
                preferred_element_type=jnp.float32,
            )
        )
        local_normal = lax.dot_general(
            hankel_cols,
            images,
            (((1,), (1,)), ((), ())),
            precision=highest,
            preferred_element_type=jnp.float32,
        )
        normal_whole = lax.psum(local_normal, "rows")
        local_gram = jnp.dot(
            normal_whole.T, normal_whole, precision=highest, preferred_element_type=jnp.float32
        )
        gram_matrix = lax.psum(local_gram, "coil")
        whole_basis = orthonormal(normal_whole, gram_matrix)
    images = coil_total(
        lax.dot_general(
            whole_basis,
            hankel_cols,
            (((0,), (0,)), ((), ())),
            precision=highest,
            preferred_element_type=jnp.float32,
        )
    )
    projected = jnp.dot(whole_basis, images, precision=highest, preferred_element_type=jnp.float32)
    owned_count = whole_basis.shape[0] // lax.axis_size("rows")
    owned_basis = lax.dynamic_slice_in_dim(
        whole_basis, lax.axis_index("rows") * owned_count, owned_count, 0
    )
    stacked = projected.reshape(KER, channels, tile_rows)
    spread = jnp.zeros((channels, tile_rows + KER - 1), jnp.float32)
    for offset in range(KER):
        spread = spread.at[:, offset : offset + tile_rows].add(stacked[offset])
    carried = shifted(spread[:, tile_rows:], "rows", 1)
    estimate = spread[:, :tile_rows].at[:, : KER - 1].add(carried) / KER
    residual = mask_float * (kspace - estimate)
    recovered = estimate + residual - jnp.clip(residual, -threshold, threshold)
    return (recovered, owned_basis.reshape(1, owned_basis.shape[0], owned_basis.shape[1]))


def split(value):
    high = value.astype(jnp.bfloat16)
    low = (value - high.astype(jnp.float32)).astype(jnp.bfloat16)
    return high, low


def dot(a, b, dims=((1,), (0,))):
    return lax.dot_general(a, b, (dims, ((), ())), preferred_element_type=jnp.float32)


def dot3(a, b, dims=((1,), (0,))):
    a_high, a_low = split(a)
    b_high, b_low = split(b)
    return dot(a_high, b_high, dims) + (dot(a_high, b_low, dims) + dot(a_low, b_high, dims))


def prepare_kernel(
    cols,
    chg,
    per_tile,
    kspace_hbm,
    mask_hbm,
    basis_hbm,
    sampled_ref,
    send_ref,
    kspace_ref,
    mask_ref,
    basis_ref,
    sems,
):
    fetches = [
        pltpu.make_async_copy(source, target, sems.at[i])
        for i, (source, target) in enumerate(
            [(kspace_hbm, kspace_ref), (mask_hbm, mask_ref), (basis_hbm, basis_ref)]
        )
    ]
    for fetch in fetches:
        fetch.start()
    fetches[0].wait()
    fetches[1].wait()
    sampled_ref[...] = kspace_ref[...] * mask_ref[...].astype(jnp.float32)
    fetches[2].wait()
    turned = basis_ref[...].T
    devices = turned.shape[0] // cols
    for j in range(per_tile):
        part = turned[:, j * chg : (j + 1) * chg]
        row = jnp.concatenate([part[k * devices : (k + 1) * devices] for k in range(cols)], axis=1)
        send_ref[pl.ds(j, devices, stride=per_tile), :] = row


def images_of(vectors, samples_ref, wide_ref):
    rows, channels = vectors.shape
    cols = rows // KER
    high, low = split(vectors)
    at_row = lax.broadcasted_iota(jnp.int32, (rows, rows), 0)
    at_col = lax.broadcasted_iota(jnp.int32, (rows, rows), 1)
    flip = ((at_row // KER == at_col // KER) & (at_row % KER + at_col % KER == KER - 1)).astype(
        jnp.float32
    ).astype(jnp.bfloat16)
    both = dot(flip, jnp.concatenate([high, low], axis=1)).astype(jnp.bfloat16)
    high, low = both[:, :channels], both[:, channels:]
    twice = jnp.concatenate([high, high], axis=1)
    tiles = samples_ref.shape[0]
    tile = samples_ref.shape[-1]
    for t in range(tiles):
        block = samples_ref[t].reshape(2 * channels, tile)
        wide_ref[:, t * tile : (t + 1) * tile] = dot(twice, block) + dot(low, block[:channels])
    images = []
    for k in range(cols):
        total = None
        for i in reversed(range(0, KER, SUB)):
            part = wide_ref[k * KER + i : k * KER + i + SUB, :]
            total = part if total is None else pltpu.roll(total, SUB, 1) + part
        total = pltpu.roll(total, 0, 1, stride=1, stride_axis=0)
        images.append(jnp.sum(total, axis=0, keepdims=True))
    return images


def normal_of(images, samples_ref, moved_ref):
    cols = len(images)
    positions = images[0].shape[1]
    tiles = samples_ref.shape[0]
    tile = samples_ref.shape[-1]
    channels = samples_ref.shape[2] * samples_ref.shape[3]
    rows = cols * KER
    for k in range(cols):
        base = jnp.broadcast_to(images[k], (SUB, positions))
        base = pltpu.roll(base, positions - (KER - 1), 1, stride=1, stride_axis=0)
        for j in range(0, KER, 2 * SUB):
            first = base if j == 0 else pltpu.roll(base, j, 1)
            second = pltpu.roll(base, j + SUB, 1)
            high, low = split(jnp.concatenate([first, second], axis=0))
            moved_ref[k * KER + j : k * KER + j + 2 * SUB, :] = high
            moved_ref[rows + k * KER + j : rows + k * KER + j + 2 * SUB, :] = low
    total = jnp.zeros((2 * rows, 2 * channels), jnp.float32)
    for t in range(tiles):
        block = samples_ref[t].reshape(2 * channels, tile)
        total = total + dot(moved_ref[:, t * tile : (t + 1) * tile], block, ((1,), (1,)))
    return total[:rows, :channels] + (
        total[:rows, channels:] + total[rows:, :channels] + total[rows:, channels:]
    )


def store_by_rows(normal, send_ref, part):
    tiles, groups, _, per_tile, lanes = send_ref.shape
    cols = normal.shape[0] // KER
    chg = normal.shape[1] // groups
    for g in range(groups):
        joined = jnp.concatenate(
            [normal[k * KER : (k + 1) * KER, g * chg : (g + 1) * chg] for k in range(cols)], axis=1
        )
        send_ref[:, g, part] = joined.reshape(tiles, per_tile, lanes)


def passes_kernel(
    masks,
    top_near_ref,
    top_far_ref,
    low_near_ref,
    low_far_ref,
    basis_ref,
    samples_ref,
    normal_ref,
    send_ref,
    wide_ref,
    moved_ref,
):
    tiles, _, groups, chg, tile = samples_ref.shape
    me = lax.axis_index("rows") * groups + lax.axis_index("coil")
    start = 0
    for near_ref, far_ref, order in (
        (top_near_ref, top_far_ref, masks[0]),
        (low_near_ref, low_far_ref, masks[1]),
    ):
        half, count = near_ref.shape[:2]
        for slot, mask in enumerate(order):
            value = near_ref[slot] if slot < half else far_ref[slot - half]
            high, low = split(value)
            source = lax.bitwise_xor(me, mask)
            t, g = source // groups, source % groups
            samples_ref[t, 0, g, start : start + count] = high
            samples_ref[t, 1, g, start : start + count] = low
        start += count
    cols = basis_ref.shape[-1] // chg
    rows = []
    for k in range(cols):
        rows.append(
            jnp.concatenate(
                [
                    basis_ref[:, g].reshape(KER, cols * chg)[:, k * chg : (k + 1) * chg]
                    for g in range(groups)
                ],
                axis=1,
            )
        )
    vectors = jnp.concatenate(rows, axis=0)
    normal = normal_of(images_of(vectors, samples_ref, wide_ref), samples_ref, moved_ref)
    scaled = []
    for k in range(cols):
        part = normal[k * KER : (k + 1) * KER]
        scaled.append(part * (1.0 / jnp.max(jnp.abs(part))))
    normal = jnp.concatenate(scaled, axis=0)
    store_by_rows(normal, send_ref, 0)
    normal = normal_of(images_of(normal, samples_ref, wide_ref), samples_ref, moved_ref)
    normal_ref[...] = normal
    store_by_rows(normal, send_ref, 1)


def images_kernel(samples_ref, vectors_ref, send_ref, wide_ref):
    tiles, cols, reach = send_ref.shape
    tile = samples_ref.shape[-1]
    images = jnp.concatenate(images_of(vectors_ref[...], samples_ref, wide_ref), axis=0)
    positions = images.shape[1]
    images = pltpu.roll(images, positions - (KER - 1), 1)
    rim = reach - tile
    for t in range(tiles):
        if t == 0:
            part = jnp.concatenate([images[:, positions - rim :], images[:, :tile]], axis=1)
        else:
            part = images[:, t * tile - rim : (t + 1) * tile]
        send_ref[t] = part


def gather_turned(received_ref, cols, per_tile, part):
    count, lanes = received_ref.shape
    devices = count // (2 * per_tile)
    chg = lanes // cols
    loaded = [
        received_ref[pl.ds(part * per_tile + j, devices, stride=2 * per_tile), :]
        for j in range(per_tile)
    ]
    return jnp.concatenate(
        [
            jnp.concatenate(
                [loaded[j][:, k * chg : (k + 1) * chg] for j in range(per_tile)], axis=1
            )
            for k in range(cols)
        ],
        axis=0,
    )


def exact(a, b, dims=((1,), (0,))):
    return lax.dot_general(
        a, b, (dims, ((), ())), precision=lax.Precision.HIGHEST, preferred_element_type=jnp.float32
    )


def store_halves(gram, kept_ref, given_ref):
    half = gram.shape[0] // 2
    odd = lax.axis_index("coil") % 2 == 1
    kept_ref[...] = jnp.where(odd, gram[half:], gram[:half])
    given_ref[...] = jnp.where(odd, gram[:half], gram[half:])


def load_halves(kept_ref, other_ref):
    odd = lax.axis_index("coil") % 2 == 1
    kept, other = kept_ref[...], other_ref[...]
    return jnp.concatenate([jnp.where(odd, other, kept), jnp.where(odd, kept, other)], axis=0)


def gram_kernel(cols, per_tile, received_ref, kept_ref, given_ref, rows_ref):
    turned = gather_turned(received_ref, cols, per_tile, 0)
    store_halves(exact(turned, turned, ((1,), (1,))), kept_ref, given_ref)
    rows_ref[...] = gather_turned(received_ref, cols, per_tile, 1).T


def inverse_factor(gram):
    size = gram.shape[0]
    shape = (SUB, size)
    at_row = lax.broadcasted_iota(jnp.int32, (size, size), 0)
    at_col = lax.broadcasted_iota(jnp.int32, (size, size), 1)
    unit = (at_row == at_col).astype(jnp.float32)
    left = [gram[b : b + SUB] for b in range(0, size, SUB)]
    right = [unit[b : b + SUB] for b in range(0, size, SUB)]
    sub = lax.broadcasted_iota(jnp.int32, shape, 0)
    done = []
    for b in range(len(left)):
        spread = {
            c: [
                jnp.broadcast_to(left[c][:, b * SUB + k : b * SUB + k + 1], shape)
                for k in range(SUB)
            ]
            for c in range(b, len(left))
        }
        entry = {
            (i, k): jnp.broadcast_to(spread[b][k][i : i + 1], shape)
            for k in range(SUB)
            for i in range(k, SUB)
        }
        inverse = {}
        for k in range(SUB):
            root = lax.rsqrt(entry[k, k])
            root = root * (1.5 - (0.5 * entry[k, k]) * (root * root))
            inverse[k, k] = root
            for i in range(k + 1, SUB):
                entry[i, k] = entry[i, k] * root
            for i in range(k + 1, SUB):
                for m in range(k + 1, i + 1):
                    entry[i, m] = entry[i, m] - entry[i, k] * entry[m, k]
        for i in range(1, SUB):
            for k in range(i):
                total = entry[i, k] * inverse[k, k]
                for m in range(k + 1, i):
                    total = total + entry[i, m] * inverse[m, k]
                inverse[i, k] = -(total * inverse[i, i])

        def solved(rows):
            whole = [jnp.broadcast_to(rows[k : k + 1], shape) for k in range(SUB)]
            first = []
            for i in range(SUB):
                total = inverse[i, 0] * whole[0]
                for k in range(1, i + 1):
                    total = total + inverse[i, k] * whole[k]
                first.append(total)
            second = []
            for k in range(SUB):
                total = inverse[k, k] * first[k]
                for i in range(k + 1, SUB):
                    total = total + inverse[i, k] * first[i]
                second.append(total)
            return first, second

        lower, lower_again = solved(right[b])
        row = lower[0]
        for i in range(1, SUB):
            row = jnp.where(sub == i, lower[i], row)
        done.append(row)
        if b + 1 < len(left):
            _, upper_again = solved(left[b])
            for c in range(b + 1, len(left)):
                for k in range(SUB):
                    left[c] = left[c] - spread[c][k] * upper_again[k]
                    right[c] = right[c] - spread[c][k] * lower_again[k]
    return jnp.concatenate(done, axis=0)


def middle_kernel(gram_ref, other_ref, rows_ref, inverse_ref, kept_ref, given_ref):
    inverse = inverse_factor(load_halves(gram_ref, other_ref))
    inverse_ref[...] = inverse
    rows = exact(rows_ref[...], inverse, ((1,), (1,)))
    store_halves(exact(rows, rows, ((0,), (0,))), kept_ref, given_ref)


def last_kernel(
    cols,
    masks,
    images_ref,
    near_ref,
    far_ref,
    first_ref,
    gram_ref,
    other_ref,
    kspace_ref,
    mask_ref,
    recovered_ref,
    basis_ref,
):
    inverse = inverse_factor(load_halves(gram_ref, other_ref))
    count, reach = images_ref.shape
    devices = count // cols
    at_row = lax.broadcasted_iota(jnp.int32, (count, count), 0)
    at_col = lax.broadcasted_iota(jnp.int32, (count, count), 1)
    order = ((at_row // devices == at_col % cols) & (at_row % devices == at_col // cols)).astype(
        jnp.float32
    )
    inverse = exact(inverse, first_ref[...])
    images = exact(exact(inverse, order), images_ref[...])
    images_high, images_low = split(images)
    stacked = jnp.concatenate([images_high, images_low], axis=0)
    chg, tile = kspace_ref.shape
    me = lax.axis_index("rows")
    half = near_ref.shape[0]
    estimate = jnp.zeros((chg, tile), jnp.float32)
    for slot, mask in enumerate(masks):
        rows = near_ref[slot] if slot < half else far_ref[slot - half]
        vectors = dot3(rows, inverse, ((1,), (1,)))
        if slot == 0:
            basis_ref[...] = vectors
        high, low = split(vectors)
        projected = dot(jnp.concatenate([high, high], axis=1), stacked) + dot(low, images_high)
        per_tile = vectors.shape[0] // chg
        total = projected[:chg]
        for j in range(1, per_tile):
            total = total + pltpu.roll(projected[j * chg : (j + 1) * chg], j, 1)
        t = lax.bitwise_xor(me, mask)
        total = pltpu.roll(total, t * per_tile, 1)
        estimate = estimate + total[:, reach - tile :]
    estimate = estimate / KER
    residual = mask_ref[...].astype(jnp.float32) * (kspace_ref[...] - estimate)
    recovered_ref[...] = estimate + residual - jnp.clip(residual, -threshold, threshold)


def call(kernel, outs, *args, scratch=(), space=pltpu.VMEM, limit=40):
    return pl.pallas_call(
        kernel,
        out_shape=[jax.ShapeDtypeStruct(shape, kind) for shape, kind in outs],
        in_specs=[pl.BlockSpec(memory_space=space)] * len(args),
        out_specs=[pl.BlockSpec(memory_space=pltpu.VMEM)] * len(outs),
        scratch_shapes=list(scratch),
        compiler_params=pltpu.CompilerParams(vmem_limit_bytes=limit * 2**20),
    )(*args)


def exchange(block, devices, mask, axes):
    return lax.ppermute(block, axes, [(i, i ^ mask) for i in range(devices)])


def with_masks(masks, mask):
    return masks + [m ^ mask for m in masks]


def after(value, *others):
    return lax.optimization_barrier((value,) + others)[0]


def rounds_of(low, high):
    masks = []
    while low < high:
        if 2 * low < high:
            masks.append([low, 2 * low, 3 * low])
        else:
            masks.append([low])
        low *= 4
    return masks


def gather_round(part, order, masks, devices, axes):
    part = jnp.concatenate(
        [part] + [exchange(part, devices, mask, axes) for mask in masks], axis=0
    )
    return part, order + [m ^ mask for mask in masks for m in order]


def gather_samples(sampled, tiles, groups, beside):
    devices = tiles * groups
    near, masks = sampled[None], [0]
    for partners in rounds_of(2 * groups, devices):
        near, masks = gather_round(near, masks, partners, devices, AXES)
    half = near.shape[1] // 2
    parts = [near[:, :half], near[:, half:]]
    orders = [masks, masks]
    ways = [(groups, groups // 2), (groups // 2, groups)]
    for step in range(2):
        for i in range(2):
            parts[i], orders[i] = gather_round(
                parts[i], orders[i], [ways[i][step]], devices, AXES
            )
        if step == 0:
            parts = list(lax.optimization_barrier((*parts, beside))[:2])
    for partners in rounds_of(2, groups // 2):
        for i in range(2):
            parts[i], orders[i] = gather_round(parts[i], orders[i], partners, devices, AXES)
    far = [exchange(part, devices, 1, AXES) for part in parts]
    orders = [with_masks(order, 1) for order in orders]
    return parts, far, orders


def to_all(pieces, axes=AXES):
    return lax.all_to_all(pieces, axes, 0, 0, tiled=True)


def total_of(kept, given, devices):
    total = kept + exchange(given, devices, 1, AXES)
    for partners in rounds_of(2, devices):
        terms = [exchange(total, devices, mask, AXES) for mask in partners]
        for term in terms:
            total = total + term
    return total, exchange(total, devices, 1, AXES)


def column_shards(kspace, sample_mask, start_basis):
    f32, bf16 = jnp.float32, jnp.bfloat16
    tiles, groups = lax.axis_size("rows"), lax.axis_size("coil")
    devices = tiles * groups
    chg, tile = kspace.shape
    channels = chg * groups
    positions = tile * tiles
    owned, rank = start_basis.shape[1:]
    per_tile = owned // chg
    cols = rank // devices
    rows = cols * KER
    lanes = cols * chg

    sampled, basis_send = call(
        functools.partial(prepare_kernel, cols, chg, per_tile),
        [((chg, tile), f32), ((devices * per_tile, lanes), f32)],
        kspace,
        sample_mask,
        start_basis.reshape(owned, rank),
        scratch=[
            pltpu.VMEM((chg, tile), f32),
            pltpu.VMEM((chg, tile), sample_mask.dtype),
            pltpu.VMEM((owned, rank), f32),
            pltpu.SemaphoreType.DMA((3,)),
        ],
        space=pltpu.HBM,
        limit=60,
    )
    basis_parts = to_all(basis_send.reshape(devices, per_tile, lanes))
    near, far, masks = gather_samples(sampled, tiles, groups, basis_parts)
    wide = pltpu.VMEM((rows, positions), f32)
    moved = pltpu.VMEM((2 * rows, positions), bf16)
    samples, normal, send = call(
        functools.partial(passes_kernel, masks),
        [
            ((tiles, 2, groups, chg, tile), bf16),
            ((rows, channels), f32),
            ((tiles, groups, 2, per_tile, lanes), f32),
        ],
        near[0],
        far[0],
        near[1],
        far[1],
        basis_parts.reshape(tiles, groups, per_tile, lanes),
        scratch=[wide, moved],
    )
    received = to_all(send.reshape(devices, 2 * per_tile, lanes))
    reach = tile + LANES
    (images,) = call(images_kernel, [((tiles, cols, reach), f32)], samples, normal, scratch=[wide])
    images = jnp.broadcast_to(images[:, None], (tiles, groups, cols, reach))
    received = after(received, images)
    half = ((rank // 2, rank), f32)
    kept, given, by_row = call(
        functools.partial(gram_kernel, cols, per_tile),
        [half, half, ((owned, rank), f32)],
        received.reshape(devices * 2 * per_tile, lanes),
    )
    gram = total_of(kept, given, devices)
    images = to_all(images.reshape(devices, cols, reach)).reshape(rank, reach)
    near, order = by_row[None], [0]
    for partners in rounds_of(2, tiles):
        near, order = gather_round(near, order, partners, tiles, "rows")
    by_row, images, near = lax.optimization_barrier((by_row, images, near))
    far = exchange(near, tiles, 1, "rows")
    order = with_masks(order, 1)
    inverse, kept, given = call(
        middle_kernel, [((rank, rank), f32), half, half], *gram, by_row
    )
    gram = total_of(kept, given, devices)
    recovered, basis = call(
        functools.partial(last_kernel, cols, order),
        [((chg, tile), f32), ((owned, rank), f32)],
        images,
        near,
        far,
        inverse,
        *gram,
        kspace,
        sample_mask,
    )
    return (recovered, basis.reshape(1, owned, rank))


def divides_columns(kspace, start_basis):
    tiles, groups = lax.axis_size("rows"), lax.axis_size("coil")
    devices = tiles * groups
    chg, tile = kspace.shape
    owned, rank = start_basis.shape[1:]
    return (
        devices & (devices - 1) == 0
        and tiles > 1
        and groups > 2
        and rank % (2 * SUB) == 0
        and rank % devices == 0
        and rank % LANES == 0
        and tile % LANES == 0
        and owned % (SUB * chg) == 0
        and chg * (rank // devices) == LANES
        and chg % (4 * SUB) == 0
        and (chg * groups) % LANES == 0
        and KER <= LANES
    )


def shards(kspace, sample_mask, start_basis):
    if divides_columns(kspace, start_basis):
        return column_shards(kspace, sample_mask, start_basis)
    return general_shards(kspace, sample_mask, start_basis)


def solution(mesh):
    return jax.shard_map(
        shards,
        mesh=mesh,
        in_specs=(P("coil", "rows"), P("coil", "rows"), P("coil", "rows", None)),
        out_specs=(P("coil", "rows"), P("coil", "rows", None)),
        check_vma=False,
    )
```

```python
import functools

import jax
import jax.numpy as jnp
from jax import lax
from jax.experimental import pallas as pl
from jax.experimental.pallas import tpu as pltpu
from jax.sharding import PartitionSpec as P

KER = 64
ITERS = 2
LANES = 128
SUB = 8
AXES = ("rows", "coil")


threshold = 0.05


def shifted(block, axis, distance):
    devices = range(lax.axis_size(axis))
    route = [((i - distance) % len(devices), i) for i in devices]
    return lax.ppermute(block, axis, route)


def orthonormal(normal_rows, gram_matrix):
    factor = jnp.linalg.cholesky(gram_matrix)
    return lax.linalg.triangular_solve(
        factor, normal_rows, left_side=False, lower=True, transpose_a=True
    )


def coil_total(partial_value):
    return lax.psum(partial_value, "coil")


def general_shards(kspace, sample_mask, start_basis):
    highest = lax.Precision.HIGHEST
    channels = kspace.shape[0]
    tile_rows = kspace.shape[1]
    mask_float = sample_mask.astype(jnp.float32)
    sampled = kspace * mask_float
    next_rim = shifted(sampled[:, : KER - 1], "rows", -1)
    extended = jnp.concatenate([sampled, next_rim], axis=1)
    hankel_cols = jnp.stack(
        [extended[:, offset : offset + tile_rows] for offset in range(KER)], axis=0
    )
    hankel_cols = hankel_cols.reshape(KER * channels, tile_rows)
    owned_basis = start_basis.reshape(start_basis.shape[1], start_basis.shape[2])
    whole_basis = lax.all_gather(owned_basis, "rows", axis=0, tiled=True)
    for iteration in range(ITERS):
        images = coil_total(
            lax.dot_general(
                whole_basis,
                hankel_cols,
                (((0,), (0,)), ((), ())),
                precision=highest,
                preferred_element_type=jnp.float32,
            )
        )
        local_normal = lax.dot_general(
            hankel_cols,
            images,
            (((1,), (1,)), ((), ())),
            precision=highest,
            preferred_element_type=jnp.float32,
        )
        normal_whole = lax.psum(local_normal, "rows")
        local_gram = jnp.dot(
            normal_whole.T, normal_whole, precision=highest, preferred_element_type=jnp.float32
        )
        gram_matrix = lax.psum(local_gram, "coil")
        whole_basis = orthonormal(normal_whole, gram_matrix)
    images = coil_total(
        lax.dot_general(
            whole_basis,
            hankel_cols,
            (((0,), (0,)), ((), ())),
            precision=highest,
            preferred_element_type=jnp.float32,
        )
    )
    projected = jnp.dot(whole_basis, images, precision=highest, preferred_element_type=jnp.float32)
    owned_count = whole_basis.shape[0] // lax.axis_size("rows")
    owned_basis = lax.dynamic_slice_in_dim(
        whole_basis, lax.axis_index("rows") * owned_count, owned_count, 0
    )
    stacked = projected.reshape(KER, channels, tile_rows)
    spread = jnp.zeros((channels, tile_rows + KER - 1), jnp.float32)
    for offset in range(KER):
        spread = spread.at[:, offset : offset + tile_rows].add(stacked[offset])
    carried = shifted(spread[:, tile_rows:], "rows", 1)
    estimate = spread[:, :tile_rows].at[:, : KER - 1].add(carried) / KER
    residual = mask_float * (kspace - estimate)
    recovered = estimate + residual - jnp.clip(residual, -threshold, threshold)
    return (recovered, owned_basis.reshape(1, owned_basis.shape[0], owned_basis.shape[1]))


def split(value):
    high = value.astype(jnp.bfloat16)
    low = (value - high.astype(jnp.float32)).astype(jnp.bfloat16)
    return high, low


def dot(a, b, dims=((1,), (0,))):
    return lax.dot_general(a, b, (dims, ((), ())), preferred_element_type=jnp.float32)


def dot3(a, b, dims=((1,), (0,))):
    a_high, a_low = split(a)
    b_high, b_low = split(b)
    return dot(a_high, b_high, dims) + (dot(a_high, b_low, dims) + dot(a_low, b_high, dims))


def prepare_kernel(
    cols,
    chg,
    per_tile,
    kspace_hbm,
    mask_hbm,
    basis_hbm,
    sampled_ref,
    send_ref,
    kspace_ref,
    mask_ref,
    basis_ref,
    sems,
):
    fetches = [
        pltpu.make_async_copy(source, target, sems.at[i])
        for i, (source, target) in enumerate(
            [(kspace_hbm, kspace_ref), (mask_hbm, mask_ref), (basis_hbm, basis_ref)]
        )
    ]
    for fetch in fetches:
        fetch.start()
    fetches[0].wait()
    fetches[1].wait()
    sampled_ref[...] = kspace_ref[...] * mask_ref[...].astype(jnp.float32)
    fetches[2].wait()
    turned = basis_ref[...].T
    devices = turned.shape[0] // cols
    for j in range(per_tile):
        part = turned[:, j * chg : (j + 1) * chg]
        row = jnp.concatenate([part[k * devices : (k + 1) * devices] for k in range(cols)], axis=1)
        send_ref[pl.ds(j, devices, stride=per_tile), :] = row


def images_of(vectors, samples_ref, wide_ref):
    rows, channels = vectors.shape
    cols = rows // KER
    high, low = split(vectors)
    at_row = lax.broadcasted_iota(jnp.int32, (rows, rows), 0)
    at_col = lax.broadcasted_iota(jnp.int32, (rows, rows), 1)
    flip = ((at_row // KER == at_col // KER) & (at_row % KER + at_col % KER == KER - 1)).astype(
        jnp.float32
    ).astype(jnp.bfloat16)
    both = dot(flip, jnp.concatenate([high, low], axis=1)).astype(jnp.bfloat16)
    high, low = both[:, :channels], both[:, channels:]
    twice = jnp.concatenate([high, high], axis=1)
    tiles = samples_ref.shape[0]
    tile = samples_ref.shape[-1]
    for t in range(tiles):
        block = samples_ref[t].reshape(2 * channels, tile)
        wide_ref[:, t * tile : (t + 1) * tile] = dot(twice, block) + dot(low, block[:channels])
    images = []
    for k in range(cols):
        total = None
        for i in reversed(range(0, KER, SUB)):
            part = wide_ref[k * KER + i : k * KER + i + SUB, :]
            total = part if total is None else pltpu.roll(total, SUB, 1) + part
        total = pltpu.roll(total, 0, 1, stride=1, stride_axis=0)
        images.append(jnp.sum(total, axis=0, keepdims=True))
    return images


def normal_of(images, samples_ref, moved_ref):
    cols = len(images)
    positions = images[0].shape[1]
    tiles = samples_ref.shape[0]
    tile = samples_ref.shape[-1]
    channels = samples_ref.shape[2] * samples_ref.shape[3]
    rows = cols * KER
    for k in range(cols):
        base = jnp.broadcast_to(images[k], (SUB, positions))
        base = pltpu.roll(base, positions - (KER - 1), 1, stride=1, stride_axis=0)
        for j in range(0, KER, 2 * SUB):
            first = base if j == 0 else pltpu.roll(base, j, 1)
            second = pltpu.roll(base, j + SUB, 1)
            high, low = split(jnp.concatenate([first, second], axis=0))
            moved_ref[k * KER + j : k * KER + j + 2 * SUB, :] = high
            moved_ref[rows + k * KER + j : rows + k * KER + j + 2 * SUB, :] = low
    total = jnp.zeros((2 * rows, 2 * channels), jnp.float32)
    for t in range(tiles):
        block = samples_ref[t].reshape(2 * channels, tile)
        total = total + dot(moved_ref[:, t * tile : (t + 1) * tile], block, ((1,), (1,)))
    return total[:rows, :channels] + (
        total[:rows, channels:] + total[rows:, :channels] + total[rows:, channels:]
    )


def store_by_rows(normal, send_ref, part):
    tiles, groups, _, per_tile, lanes = send_ref.shape
    cols = normal.shape[0] // KER
    chg = normal.shape[1] // groups
    for g in range(groups):
        joined = jnp.concatenate(
            [normal[k * KER : (k + 1) * KER, g * chg : (g + 1) * chg] for k in range(cols)], axis=1
        )
        send_ref[:, g, part] = joined.reshape(tiles, per_tile, lanes)


def passes_kernel(
    masks,
    top_near_ref,
    top_far_ref,
    low_near_ref,
    low_far_ref,
    basis_ref,
    samples_ref,
    normal_ref,
    send_ref,
    wide_ref,
    moved_ref,
):
    tiles, _, groups, chg, tile = samples_ref.shape
    me = lax.axis_index("rows") * groups + lax.axis_index("coil")
    start = 0
    for near_ref, far_ref, order in (
        (top_near_ref, top_far_ref, masks[0]),
        (low_near_ref, low_far_ref, masks[1]),
    ):
        half, count = near_ref.shape[:2]
        for slot, mask in enumerate(order):
            value = near_ref[slot] if slot < half else far_ref[slot - half]
            high, low = split(value)
            source = lax.bitwise_xor(me, mask)
            t, g = source // groups, source % groups
            samples_ref[t, 0, g, start : start + count] = high
            samples_ref[t, 1, g, start : start + count] = low
        start += count
    cols = basis_ref.shape[-1] // chg
    rows = []
    for k in range(cols):
        rows.append(
            jnp.concatenate(
                [
                    basis_ref[:, g].reshape(KER, cols * chg)[:, k * chg : (k + 1) * chg]
                    for g in range(groups)
                ],
                axis=1,
            )
        )
    vectors = jnp.concatenate(rows, axis=0)
    normal = normal_of(images_of(vectors, samples_ref, wide_ref), samples_ref, moved_ref)
    scaled = []
    for k in range(cols):
        part = normal[k * KER : (k + 1) * KER]
        scaled.append(part * (1.0 / jnp.max(jnp.abs(part))))
    normal = jnp.concatenate(scaled, axis=0)
    store_by_rows(normal, send_ref, 0)
    normal = normal_of(images_of(normal, samples_ref, wide_ref), samples_ref, moved_ref)
    normal_ref[...] = normal
    store_by_rows(normal, send_ref, 1)


def images_kernel(samples_ref, vectors_ref, send_ref, wide_ref):
    tiles, cols, reach = send_ref.shape
    tile = samples_ref.shape[-1]
    images = jnp.concatenate(images_of(vectors_ref[...], samples_ref, wide_ref), axis=0)
    positions = images.shape[1]
    images = pltpu.roll(images, positions - (KER - 1), 1)
    rim = reach - tile
    for t in range(tiles):
        if t == 0:
            part = jnp.concatenate([images[:, positions - rim :], images[:, :tile]], axis=1)
        else:
            part = images[:, t * tile - rim : (t + 1) * tile]
        send_ref[t] = part


def gather_turned(received_ref, cols, per_tile, part):
    count, lanes = received_ref.shape
    devices = count // (2 * per_tile)
    chg = lanes // cols
    loaded = [
        received_ref[pl.ds(part * per_tile + j, devices, stride=2 * per_tile), :]
        for j in range(per_tile)
    ]
    return jnp.concatenate(
        [
            jnp.concatenate(
                [loaded[j][:, k * chg : (k + 1) * chg] for j in range(per_tile)], axis=1
            )
            for k in range(cols)
        ],
        axis=0,
    )


def exact(a, b, dims=((1,), (0,))):
    return lax.dot_general(
        a, b, (dims, ((), ())), precision=lax.Precision.HIGHEST, preferred_element_type=jnp.float32
    )


def square(size):
    at_row = lax.broadcasted_iota(jnp.int32, (size, size), 0)
    at_col = lax.broadcasted_iota(jnp.int32, (size, size), 1)
    return at_row, at_col


def gram_kernel(cols, per_tile, received_ref, kept_ref, given_ref, rows_ref):
    turned = gather_turned(received_ref, cols, per_tile, 0)
    first = exact(turned, turned, ((1,), (1,)))
    turned = gather_turned(received_ref, cols, per_tile, 1)
    second = exact(turned, turned, ((1,), (1,)))
    rows_ref[...] = turned.T
    at_row, at_col = square(first.shape[0])
    packed = jnp.where(at_row >= at_col, first, second)
    line = jnp.sum(jnp.where(at_row == at_col, second, 0.0), axis=0, keepdims=True)
    line = jnp.broadcast_to(line, (SUB, line.shape[1]))
    half = packed.shape[0] // 2
    odd = lax.axis_index("coil") % 2 == 1
    kept_ref[:half] = jnp.where(odd, packed[half:], packed[:half])
    given_ref[:half] = jnp.where(odd, packed[:half], packed[half:])
    kept_ref[half:] = line
    given_ref[half:] = line


def load_grams(kept_ref, other_ref):
    odd = lax.axis_index("coil") % 2 == 1
    kept, other = kept_ref[...], other_ref[...]
    low, high = jnp.where(odd, other, kept), jnp.where(odd, kept, other)
    half = low.shape[0] - SUB
    packed = jnp.concatenate([low[:half], high[:half]], axis=0)
    line = low[half : half + 1]
    at_row, at_col = square(packed.shape[0])
    turned = packed.T
    first = jnp.where(at_row >= at_col, packed, turned)
    second = jnp.where(at_row > at_col, turned, packed)
    return first, jnp.where(at_row == at_col, line, second), line


def inverse_factor(gram):
    size = gram.shape[0]
    shape = (SUB, size)
    at_row = lax.broadcasted_iota(jnp.int32, (size, size), 0)
    at_col = lax.broadcasted_iota(jnp.int32, (size, size), 1)
    unit = (at_row == at_col).astype(jnp.float32)
    left = [gram[b : b + SUB] for b in range(0, size, SUB)]
    right = [unit[b : b + SUB] for b in range(0, size, SUB)]
    sub = lax.broadcasted_iota(jnp.int32, shape, 0)
    done = []
    for b in range(len(left)):
        spread = {
            c: [
                jnp.broadcast_to(left[c][:, b * SUB + k : b * SUB + k + 1], shape)
                for k in range(SUB)
            ]
            for c in range(b, len(left))
        }
        entry = {
            (i, k): jnp.broadcast_to(spread[b][k][i : i + 1], shape)
            for k in range(SUB)
            for i in range(k, SUB)
        }
        inverse = {}
        for k in range(SUB):
            root = lax.rsqrt(entry[k, k])
            root = root * (1.5 - (0.5 * entry[k, k]) * (root * root))
            inverse[k, k] = root
            for i in range(k + 1, SUB):
                entry[i, k] = entry[i, k] * root
            for i in range(k + 1, SUB):
                for m in range(k + 1, i + 1):
                    entry[i, m] = entry[i, m] - entry[i, k] * entry[m, k]
        for i in range(1, SUB):
            for k in range(i):
                total = entry[i, k] * inverse[k, k]
                for m in range(k + 1, i):
                    total = total + entry[i, m] * inverse[m, k]
                inverse[i, k] = -(total * inverse[i, i])

        def solved(rows):
            whole = [jnp.broadcast_to(rows[k : k + 1], shape) for k in range(SUB)]
            first = []
            for i in range(SUB):
                total = inverse[i, 0] * whole[0]
                for k in range(1, i + 1):
                    total = total + inverse[i, k] * whole[k]
                first.append(total)
            second = []
            for k in range(SUB):
                total = inverse[k, k] * first[k]
                for i in range(k + 1, SUB):
                    total = total + inverse[i, k] * first[i]
                second.append(total)
            return first, second

        lower, lower_again = solved(right[b])
        row = lower[0]
        for i in range(1, SUB):
            row = jnp.where(sub == i, lower[i], row)
        done.append(row)
        if b + 1 < len(left):
            _, upper_again = solved(left[b])
            for c in range(b + 1, len(left)):
                for k in range(SUB):
                    left[c] = left[c] - spread[c][k] * upper_again[k]
                    right[c] = right[c] - spread[c][k] * lower_again[k]
    return jnp.concatenate(done, axis=0)


def factors_kernel(gram_ref, other_ref, first_ref, both_ref, sound_ref):
    gram, raw, line = load_grams(gram_ref, other_ref)
    inverse = inverse_factor(gram)
    first_ref[...] = inverse
    gram = exact(exact(inverse, raw), inverse, ((1,), (1,)))
    both_ref[...] = exact(inverse_factor(gram), inverse)
    at_row, at_col = square(gram.shape[0])
    terms = jnp.sum(inverse * inverse * line, axis=1, keepdims=True)
    result = jnp.sum(jnp.where(at_row == at_col, gram, 0.0), axis=1, keepdims=True)
    worst = jnp.max(jnp.where(terms <= 64.0 * result, 0, 1))
    sound_ref[0] = 1 - worst


def rows_kernel(rows_ref, inverse_ref, gram_ref):
    rows = exact(rows_ref[...], inverse_ref[...], ((1,), (1,)))
    gram_ref[...] = exact(rows, rows, ((0,), (0,)))


def again_kernel(gram_ref, inverse_ref, both_ref):
    both_ref[...] = exact(inverse_factor(gram_ref[...]), inverse_ref[...])


def last_kernel(
    cols,
    per_tile,
    parts,
    images_ref,
    both_ref,
    kspace_ref,
    mask_ref,
    *refs,
):
    recovered_ref, basis_ref = refs[-2:]
    both = both_ref[...]
    count, reach = images_ref.shape
    devices = count // cols
    at_row, at_col = square(count)
    order = ((at_row // devices == at_col % cols) & (at_row % devices == at_col // cols)).astype(
        jnp.float32
    )
    images = exact(exact(both, order), images_ref[...])
    images_high, images_low = split(images)
    stacked = jnp.concatenate([images_high, images_low], axis=0)
    chg, tile = kspace_ref.shape
    me = lax.axis_index("rows")
    estimate = jnp.zeros((chg, tile), jnp.float32)
    for (start, masks), rows_ref in zip(parts, refs):
        blocks, owned, rank = rows_ref.shape
        vectors = dot3(rows_ref[...].reshape(blocks * owned, rank), both, ((1,), (1,)))
        if masks[0] == 0:
            basis_ref[start * chg : start * chg + owned] = vectors[:owned]
        high, low = split(vectors)
        projected = dot(jnp.concatenate([high, high], axis=1), stacked) + dot(low, images_high)
        for slot, mask in enumerate(masks):
            total = None
            for j in range(owned // chg):
                part = projected[slot * owned + j * chg : slot * owned + (j + 1) * chg]
                part = pltpu.roll(part, start + j, 1) if start + j else part
                total = part if total is None else total + part
            total = pltpu.roll(total, lax.bitwise_xor(me, mask) * per_tile, 1)
            estimate = estimate + total[:, reach - tile :]
    estimate = estimate / KER
    residual = mask_ref[...].astype(jnp.float32) * (kspace_ref[...] - estimate)
    recovered_ref[...] = estimate + residual - jnp.clip(residual, -threshold, threshold)


def call(kernel, outs, *args, scratch=(), space=pltpu.VMEM, limit=40, scalars=0, micros=1):
    return pl.pallas_call(
        kernel,
        out_shape=[jax.ShapeDtypeStruct(shape, kind) for shape, kind in outs],
        in_specs=[pl.BlockSpec(memory_space=space)] * len(args),
        out_specs=[pl.BlockSpec(memory_space=pltpu.VMEM)] * (len(outs) - scalars)
        + [pl.BlockSpec(memory_space=pltpu.SMEM)] * scalars,
        scratch_shapes=list(scratch),
        compiler_params=pltpu.CompilerParams(vmem_limit_bytes=limit * 2**20),
        cost_estimate=pl.CostEstimate(
            flops=micros * 10**9, bytes_accessed=0, transcendentals=0
        ),
    )(*args)


def exchange(block, devices, mask, axes):
    return lax.ppermute(block, axes, [(i, i ^ mask) for i in range(devices)])


def with_masks(masks, mask):
    return masks + [m ^ mask for m in masks]


def after(value, *others):
    return lax.optimization_barrier((value,) + others)[0]


def rounds_of(low, high):
    masks = []
    while low < high:
        if 2 * low < high:
            masks.append([low, 2 * low, 3 * low])
        else:
            masks.append([low])
        low *= 4
    return masks


def gather_round(part, order, masks, devices, axes):
    part = jnp.concatenate(
        [part] + [exchange(part, devices, mask, axes) for mask in masks], axis=0
    )
    return part, order + [m ^ mask for mask in masks for m in order]


def gather_samples(sampled, tiles, groups, beside):
    devices = tiles * groups
    near, masks = sampled[None], [0]
    for partners in rounds_of(2 * groups, devices):
        near, masks = gather_round(near, masks, partners, devices, AXES)
    near = after(near, beside)
    half = near.shape[1] // 2
    parts = [near[:, :half], near[:, half:]]
    orders = [masks, masks]
    ways = [(groups, groups // 2), (groups // 2, groups)]
    for step in range(2):
        for i in range(2):
            parts[i], orders[i] = gather_round(
                parts[i], orders[i], [ways[i][step]], devices, AXES
            )
    for partners in rounds_of(2, groups // 2):
        for i in range(2):
            parts[i], orders[i] = gather_round(parts[i], orders[i], partners, devices, AXES)
    far = [exchange(part, devices, 1, AXES) for part in parts]
    orders = [with_masks(order, 1) for order in orders]
    return parts, far, orders


def gather_rows(by_row, tiles, per_tile):
    half = by_row.shape[0] // 2
    near, order = by_row[None, :half], [0]
    for partners in rounds_of(2, tiles):
        near, order = gather_round(near, order, partners, tiles, "rows")
    parts = [(0, order), (0, [m ^ 1 for m in order])]
    pieces = [near, exchange(near, tiles, 1, "rows")]
    near, order = gather_round(by_row[None, half:], [0], [1], tiles, "rows")
    *early, late = rounds_of(2, tiles)
    for partners in early:
        near, order = gather_round(near, order, partners, tiles, "rows")
    start = per_tile // 2
    parts.append((start, order))
    pieces.append(near)
    for mask in late:
        parts.append((start, [m ^ mask for m in order]))
        pieces.append(exchange(near, tiles, mask, "rows"))
    return parts, pieces


def to_all(pieces, axes=AXES):
    return lax.all_to_all(pieces, axes, 0, 0, tiled=True)


def total_of(kept, given, devices):
    total = kept + exchange(given, devices, 1, AXES)
    for partners in rounds_of(2, devices):
        terms = [exchange(total, devices, mask, AXES) for mask in partners]
        total = total + terms[0]
        if len(terms) == 3:
            total = total + (terms[1] + terms[2])
    return total, exchange(total, devices, 1, AXES)


def column_shards(kspace, sample_mask, start_basis):
    f32, bf16 = jnp.float32, jnp.bfloat16
    tiles, groups = lax.axis_size("rows"), lax.axis_size("coil")
    devices = tiles * groups
    chg, tile = kspace.shape
    channels = chg * groups
    positions = tile * tiles
    owned, rank = start_basis.shape[1:]
    per_tile = owned // chg
    cols = rank // devices
    rows = cols * KER
    lanes = cols * chg

    sampled, basis_send = call(
        functools.partial(prepare_kernel, cols, chg, per_tile),
        [((chg, tile), f32), ((devices * per_tile, lanes), f32)],
        kspace,
        sample_mask,
        start_basis.reshape(owned, rank),
        scratch=[
            pltpu.VMEM((chg, tile), f32),
            pltpu.VMEM((chg, tile), sample_mask.dtype),
            pltpu.VMEM((owned, rank), f32),
            pltpu.SemaphoreType.DMA((3,)),
        ],
        space=pltpu.HBM,
        limit=60,
    )
    basis_parts = to_all(basis_send.reshape(devices, per_tile, lanes))
    near, far, masks = gather_samples(sampled, tiles, groups, basis_parts)
    wide = pltpu.VMEM((rows, positions), f32)
    moved = pltpu.VMEM((2 * rows, positions), bf16)
    samples, normal, send = call(
        functools.partial(passes_kernel, masks),
        [
            ((tiles, 2, groups, chg, tile), bf16),
            ((rows, channels), f32),
            ((tiles, groups, 2, per_tile, lanes), f32),
        ],
        near[0],
        far[0],
        near[1],
        far[1],
        basis_parts.reshape(tiles, groups, per_tile, lanes),
        scratch=[wide, moved],
        micros=12,
    )
    received = to_all(send.reshape(devices, 2 * per_tile, lanes))
    reach = tile + LANES
    (images,) = call(images_kernel, [((tiles, cols, reach), f32)], samples, normal, scratch=[wide], micros=2)
    images = jnp.broadcast_to(images[:, None], (tiles, groups, cols, reach))
    received = after(received, images)
    half = ((rank // 2 + SUB, rank), f32)
    kept, given, by_row = call(
        functools.partial(gram_kernel, cols, per_tile),
        [half, half, ((owned, rank), f32)],
        received.reshape(devices * 2 * per_tile, lanes),
    )
    gram = total_of(kept, given, devices)
    images = to_all(images.reshape(devices, cols, reach)).reshape(rank, reach)
    parts, pieces = gather_rows(by_row, tiles, per_tile)
    whole = ((rank, rank), f32)
    first, both, sound = call(
        factors_kernel, [whole, whole, ((1,), jnp.int32)], *gram, scalars=1, micros=12
    )

    def again():
        (gram,) = call(rows_kernel, [whole], by_row, first)
        return call(again_kernel, [whole], lax.psum(gram, AXES), first)[0]

    both = lax.cond(sound[0] == 1, lambda: both, again)
    recovered, basis = call(
        functools.partial(last_kernel, cols, per_tile, parts),
        [((chg, tile), f32), ((owned, rank), f32)],
        images,
        both,
        kspace,
        sample_mask,
        *pieces,
        micros=5,
    )
    return (recovered, basis.reshape(1, owned, rank))


def divides_columns(kspace, start_basis):
    tiles, groups = lax.axis_size("rows"), lax.axis_size("coil")
    devices = tiles * groups
    chg, tile = kspace.shape
    owned, rank = start_basis.shape[1:]
    return (
        devices & (devices - 1) == 0
        and tiles > 2
        and groups > 2
        and rank % (2 * SUB) == 0
        and rank % devices == 0
        and rank % LANES == 0
        and tile % LANES == 0
        and owned == SUB * chg
        and chg * (rank // devices) == LANES
        and chg % (4 * SUB) == 0
        and (chg * groups) % LANES == 0
        and KER <= LANES
    )


def shards(kspace, sample_mask, start_basis):
    if divides_columns(kspace, start_basis):
        return column_shards(kspace, sample_mask, start_basis)
    return general_shards(kspace, sample_mask, start_basis)


def solution(mesh):
    return jax.shard_map(
        shards,
        mesh=mesh,
        in_specs=(P("coil", "rows"), P("coil", "rows"), P("coil", "rows", None)),
        out_specs=(P("coil", "rows"), P("coil", "rows", None)),
        check_vma=False,
    )
```

```python
import functools

import jax
import jax.numpy as jnp
from jax import lax
from jax.experimental import pallas as pl
from jax.experimental.pallas import tpu as pltpu
from jax.sharding import PartitionSpec as P

KER = 64
ITERS = 2
LANES = 128
SUB = 8
AXES = ("rows", "coil")


threshold = 0.05


def shifted(block, axis, distance):
    devices = range(lax.axis_size(axis))
    route = [((i - distance) % len(devices), i) for i in devices]
    return lax.ppermute(block, axis, route)


def orthonormal(normal_rows, gram_matrix):
    factor = jnp.linalg.cholesky(gram_matrix)
    return lax.linalg.triangular_solve(
        factor, normal_rows, left_side=False, lower=True, transpose_a=True
    )


def coil_total(partial_value):
    return lax.psum(partial_value, "coil")


def general_shards(kspace, sample_mask, start_basis):
    highest = lax.Precision.HIGHEST
    channels = kspace.shape[0]
    tile_rows = kspace.shape[1]
    mask_float = sample_mask.astype(jnp.float32)
    sampled = kspace * mask_float
    next_rim = shifted(sampled[:, : KER - 1], "rows", -1)
    extended = jnp.concatenate([sampled, next_rim], axis=1)
    hankel_cols = jnp.stack(
        [extended[:, offset : offset + tile_rows] for offset in range(KER)], axis=0
    )
    hankel_cols = hankel_cols.reshape(KER * channels, tile_rows)
    owned_basis = start_basis.reshape(start_basis.shape[1], start_basis.shape[2])
    whole_basis = lax.all_gather(owned_basis, "rows", axis=0, tiled=True)
    for iteration in range(ITERS):
        images = coil_total(
            lax.dot_general(
                whole_basis,
                hankel_cols,
                (((0,), (0,)), ((), ())),
                precision=highest,
                preferred_element_type=jnp.float32,
            )
        )
        local_normal = lax.dot_general(
            hankel_cols,
            images,
            (((1,), (1,)), ((), ())),
            precision=highest,
            preferred_element_type=jnp.float32,
        )
        normal_whole = lax.psum(local_normal, "rows")
        local_gram = jnp.dot(
            normal_whole.T, normal_whole, precision=highest, preferred_element_type=jnp.float32
        )
        gram_matrix = lax.psum(local_gram, "coil")
        whole_basis = orthonormal(normal_whole, gram_matrix)
    images = coil_total(
        lax.dot_general(
            whole_basis,
            hankel_cols,
            (((0,), (0,)), ((), ())),
            precision=highest,
            preferred_element_type=jnp.float32,
        )
    )
    projected = jnp.dot(whole_basis, images, precision=highest, preferred_element_type=jnp.float32)
    owned_count = whole_basis.shape[0] // lax.axis_size("rows")
    owned_basis = lax.dynamic_slice_in_dim(
        whole_basis, lax.axis_index("rows") * owned_count, owned_count, 0
    )
    stacked = projected.reshape(KER, channels, tile_rows)
    spread = jnp.zeros((channels, tile_rows + KER - 1), jnp.float32)
    for offset in range(KER):
        spread = spread.at[:, offset : offset + tile_rows].add(stacked[offset])
    carried = shifted(spread[:, tile_rows:], "rows", 1)
    estimate = spread[:, :tile_rows].at[:, : KER - 1].add(carried) / KER
    residual = mask_float * (kspace - estimate)
    recovered = estimate + residual - jnp.clip(residual, -threshold, threshold)
    return (recovered, owned_basis.reshape(1, owned_basis.shape[0], owned_basis.shape[1]))


def split(value):
    high = value.astype(jnp.bfloat16)
    low = (value - high.astype(jnp.float32)).astype(jnp.bfloat16)
    return high, low


def dot(a, b, dims=((1,), (0,))):
    return lax.dot_general(a, b, (dims, ((), ())), preferred_element_type=jnp.float32)


def dot3(a, b, dims=((1,), (0,))):
    a_high, a_low = split(a)
    b_high, b_low = split(b)
    return dot(a_high, b_high, dims) + (dot(a_high, b_low, dims) + dot(a_low, b_high, dims))


def prepare_kernel(
    cols,
    chg,
    per_tile,
    kspace_hbm,
    mask_hbm,
    basis_hbm,
    sampled_ref,
    send_ref,
    kspace_ref,
    mask_ref,
    basis_ref,
    sems,
):
    fetches = [
        pltpu.make_async_copy(source, target, sems.at[i])
        for i, (source, target) in enumerate(
            [(kspace_hbm, kspace_ref), (mask_hbm, mask_ref), (basis_hbm, basis_ref)]
        )
    ]
    for fetch in fetches:
        fetch.start()
    fetches[0].wait()
    fetches[1].wait()
    sampled_ref[...] = kspace_ref[...] * mask_ref[...].astype(jnp.float32)
    fetches[2].wait()
    turned = basis_ref[...].T
    devices = turned.shape[0] // cols
    for j in range(per_tile):
        part = turned[:, j * chg : (j + 1) * chg]
        row = jnp.concatenate([part[k * devices : (k + 1) * devices] for k in range(cols)], axis=1)
        send_ref[pl.ds(j, devices, stride=per_tile), :] = row


def images_of(vectors, samples_ref, wide_ref):
    rows, channels = vectors.shape
    cols = rows // KER
    high, low = split(vectors)
    at_row = lax.broadcasted_iota(jnp.int32, (rows, rows), 0)
    at_col = lax.broadcasted_iota(jnp.int32, (rows, rows), 1)
    flip = ((at_row // KER == at_col // KER) & (at_row % KER + at_col % KER == KER - 1)).astype(
        jnp.float32
    ).astype(jnp.bfloat16)
    both = dot(flip, jnp.concatenate([high, low], axis=1)).astype(jnp.bfloat16)
    high, low = both[:, :channels], both[:, channels:]
    twice = jnp.concatenate([high, high], axis=1)
    tiles = samples_ref.shape[0]
    tile = samples_ref.shape[-1]
    for t in range(tiles):
        block = samples_ref[t].reshape(2 * channels, tile)
        wide_ref[:, t * tile : (t + 1) * tile] = dot(twice, block) + dot(low, block[:channels])
    images = []
    for k in range(cols):
        total = None
        for i in reversed(range(0, KER, SUB)):
            part = wide_ref[k * KER + i : k * KER + i + SUB, :]
            total = part if total is None else pltpu.roll(total, SUB, 1) + part
        total = pltpu.roll(total, 0, 1, stride=1, stride_axis=0)
        images.append(jnp.sum(total, axis=0, keepdims=True))
    return images


def normal_of(images, samples_ref, moved_ref):
    cols = len(images)
    positions = images[0].shape[1]
    tiles = samples_ref.shape[0]
    tile = samples_ref.shape[-1]
    channels = samples_ref.shape[2] * samples_ref.shape[3]
    rows = cols * KER
    for k in range(cols):
        base = jnp.broadcast_to(images[k], (SUB, positions))
        base = pltpu.roll(base, positions - (KER - 1), 1, stride=1, stride_axis=0)
        for j in range(0, KER, 2 * SUB):
            first = base if j == 0 else pltpu.roll(base, j, 1)
            second = pltpu.roll(base, j + SUB, 1)
            high, low = split(jnp.concatenate([first, second], axis=0))
            moved_ref[k * KER + j : k * KER + j + 2 * SUB, :] = high
            moved_ref[rows + k * KER + j : rows + k * KER + j + 2 * SUB, :] = low
    total = jnp.zeros((2 * rows, 2 * channels), jnp.float32)
    for t in range(tiles):
        block = samples_ref[t].reshape(2 * channels, tile)
        total = total + dot(moved_ref[:, t * tile : (t + 1) * tile], block, ((1,), (1,)))
    return total[:rows, :channels] + (
        total[:rows, channels:] + total[rows:, :channels] + total[rows:, channels:]
    )


def store_by_rows(normal, send_ref, part):
    tiles, groups, _, per_tile, lanes = send_ref.shape
    cols = normal.shape[0] // KER
    chg = normal.shape[1] // groups
    for g in range(groups):
        joined = jnp.concatenate(
            [normal[k * KER : (k + 1) * KER, g * chg : (g + 1) * chg] for k in range(cols)], axis=1
        )
        send_ref[:, g, part] = joined.reshape(tiles, per_tile, lanes)


def passes_kernel(
    masks,
    top_near_ref,
    top_far_ref,
    low_near_ref,
    low_far_ref,
    basis_ref,
    samples_ref,
    normal_ref,
    send_ref,
    wide_ref,
    moved_ref,
):
    tiles, _, groups, chg, tile = samples_ref.shape
    me = lax.axis_index("rows") * groups + lax.axis_index("coil")
    start = 0
    for near_ref, far_ref, order in (
        (top_near_ref, top_far_ref, masks[0]),
        (low_near_ref, low_far_ref, masks[1]),
    ):
        half, count = near_ref.shape[:2]
        for slot, mask in enumerate(order):
            value = near_ref[slot] if slot < half else far_ref[slot - half]
            high, low = split(value)
            source = lax.bitwise_xor(me, mask)
            t, g = source // groups, source % groups
            samples_ref[t, 0, g, start : start + count] = high
            samples_ref[t, 1, g, start : start + count] = low
        start += count
    cols = basis_ref.shape[-1] // chg
    rows = []
    for k in range(cols):
        rows.append(
            jnp.concatenate(
                [
                    basis_ref[:, g].reshape(KER, cols * chg)[:, k * chg : (k + 1) * chg]
                    for g in range(groups)
                ],
                axis=1,
            )
        )
    vectors = jnp.concatenate(rows, axis=0)
    normal = normal_of(images_of(vectors, samples_ref, wide_ref), samples_ref, moved_ref)
    scaled = []
    for k in range(cols):
        part = normal[k * KER : (k + 1) * KER]
        scaled.append(part * (1.0 / jnp.max(jnp.abs(part))))
    normal = jnp.concatenate(scaled, axis=0)
    store_by_rows(normal, send_ref, 0)
    normal = normal_of(images_of(normal, samples_ref, wide_ref), samples_ref, moved_ref)
    normal_ref[...] = normal
    store_by_rows(normal, send_ref, 1)


def images_kernel(samples_ref, vectors_ref, send_ref, wide_ref):
    tiles, cols, reach = send_ref.shape
    tile = samples_ref.shape[-1]
    images = jnp.concatenate(images_of(vectors_ref[...], samples_ref, wide_ref), axis=0)
    positions = images.shape[1]
    images = pltpu.roll(images, positions - (KER - 1), 1)
    rim = reach - tile
    for t in range(tiles):
        if t == 0:
            part = jnp.concatenate([images[:, positions - rim :], images[:, :tile]], axis=1)
        else:
            part = images[:, t * tile - rim : (t + 1) * tile]
        send_ref[t] = part


def gather_turned(received_ref, cols, per_tile, part):
    count, lanes = received_ref.shape
    devices = count // (2 * per_tile)
    chg = lanes // cols
    loaded = [
        received_ref[pl.ds(part * per_tile + j, devices, stride=2 * per_tile), :]
        for j in range(per_tile)
    ]
    return jnp.concatenate(
        [
            jnp.concatenate(
                [loaded[j][:, k * chg : (k + 1) * chg] for j in range(per_tile)], axis=1
            )
            for k in range(cols)
        ],
        axis=0,
    )


def exact(a, b, dims=((1,), (0,))):
    return lax.dot_general(
        a, b, (dims, ((), ())), precision=lax.Precision.HIGHEST, preferred_element_type=jnp.float32
    )


def square(size):
    at_row = lax.broadcasted_iota(jnp.int32, (size, size), 0)
    at_col = lax.broadcasted_iota(jnp.int32, (size, size), 1)
    return at_row, at_col


def gram_kernel(cols, per_tile, received_ref, kept_ref, given_ref, rows_ref):
    turned = gather_turned(received_ref, cols, per_tile, 0)
    first = exact(turned, turned, ((1,), (1,)))
    turned = gather_turned(received_ref, cols, per_tile, 1)
    second = exact(turned, turned, ((1,), (1,)))
    rows_ref[...] = turned.T
    at_row, at_col = square(first.shape[0])
    packed = jnp.where(at_row >= at_col, first, second)
    line = jnp.sum(jnp.where(at_row == at_col, second, 0.0), axis=0, keepdims=True)
    line = jnp.broadcast_to(line, (SUB, line.shape[1]))
    half = packed.shape[0] // 2
    odd = lax.axis_index("coil") % 2 == 1
    kept_ref[:half] = jnp.where(odd, packed[half:], packed[:half])
    given_ref[:half] = jnp.where(odd, packed[:half], packed[half:])
    kept_ref[half:] = line
    given_ref[half:] = line


def load_grams(kept_ref, other_ref):
    odd = lax.axis_index("coil") % 2 == 1
    kept, other = kept_ref[...], other_ref[...]
    low, high = jnp.where(odd, other, kept), jnp.where(odd, kept, other)
    half = low.shape[0] - SUB
    packed = jnp.concatenate([low[:half], high[:half]], axis=0)
    line = low[half : half + 1]
    at_row, at_col = square(packed.shape[0])
    turned = packed.T
    first = jnp.where(at_row >= at_col, packed, turned)
    second = jnp.where(at_row > at_col, turned, packed)
    return first, jnp.where(at_row == at_col, line, second), line


def inverse_factor(gram):
    size = gram.shape[0]
    shape = (SUB, size)
    at_row = lax.broadcasted_iota(jnp.int32, (size, size), 0)
    at_col = lax.broadcasted_iota(jnp.int32, (size, size), 1)
    unit = (at_row == at_col).astype(jnp.float32)
    left = [gram[b : b + SUB] for b in range(0, size, SUB)]
    right = [unit[b : b + SUB] for b in range(0, size, SUB)]
    sub = lax.broadcasted_iota(jnp.int32, shape, 0)
    done = []
    for b in range(len(left)):
        spread = {
            c: [
                jnp.broadcast_to(left[c][:, b * SUB + k : b * SUB + k + 1], shape)
                for k in range(SUB)
            ]
            for c in range(b, len(left))
        }
        entry = {
            (i, k): jnp.broadcast_to(spread[b][k][i : i + 1], shape)
            for k in range(SUB)
            for i in range(k, SUB)
        }
        inverse = {}
        for k in range(SUB):
            root = lax.rsqrt(entry[k, k])
            root = root * (1.5 - (0.5 * entry[k, k]) * (root * root))
            inverse[k, k] = root
            for i in range(k + 1, SUB):
                entry[i, k] = entry[i, k] * root
            for i in range(k + 1, SUB):
                for m in range(k + 1, i + 1):
                    entry[i, m] = entry[i, m] - entry[i, k] * entry[m, k]
        for i in range(1, SUB):
            for k in range(i):
                total = entry[i, k] * inverse[k, k]
                for m in range(k + 1, i):
                    total = total + entry[i, m] * inverse[m, k]
                inverse[i, k] = -(total * inverse[i, i])

        def solved(rows):
            whole = [jnp.broadcast_to(rows[k : k + 1], shape) for k in range(SUB)]
            first = []
            for i in range(SUB):
                total = inverse[i, 0] * whole[0]
                for k in range(1, i + 1):
                    total = total + inverse[i, k] * whole[k]
                first.append(total)
            second = []
            for k in range(SUB):
                total = inverse[k, k] * first[k]
                for i in range(k + 1, SUB):
                    total = total + inverse[i, k] * first[i]
                second.append(total)
            return first, second

        lower, lower_again = solved(right[b])
        row = lower[0]
        for i in range(1, SUB):
            row = jnp.where(sub == i, lower[i], row)
        done.append(row)
        if b + 1 < len(left):
            _, upper_again = solved(left[b])
            for c in range(b + 1, len(left)):
                for k in range(SUB):
                    left[c] = left[c] - spread[c][k] * upper_again[k]
                    right[c] = right[c] - spread[c][k] * lower_again[k]
    return jnp.concatenate(done, axis=0)


def factors_kernel(gram_ref, other_ref, first_ref, both_ref, sound_ref):
    gram, raw, line = load_grams(gram_ref, other_ref)
    inverse = inverse_factor(gram)
    first_ref[...] = inverse
    gram = exact(exact(inverse, raw), inverse, ((1,), (1,)))
    both_ref[...] = exact(inverse_factor(gram), inverse)
    at_row, at_col = square(gram.shape[0])
    terms = jnp.sum(inverse * inverse * line, axis=1, keepdims=True)
    result = jnp.sum(jnp.where(at_row == at_col, gram, 0.0), axis=1, keepdims=True)
    worst = jnp.max(jnp.where(terms <= 64.0 * result, 0, 1))
    sound_ref[0] = 1 - worst


def rows_kernel(rows_ref, inverse_ref, gram_ref):
    rows = exact(rows_ref[...], inverse_ref[...], ((1,), (1,)))
    gram_ref[...] = exact(rows, rows, ((0,), (0,)))


def again_kernel(gram_ref, inverse_ref, both_ref):
    both_ref[...] = exact(inverse_factor(gram_ref[...]), inverse_ref[...])


def last_kernel(
    cols,
    per_tile,
    parts,
    images_ref,
    both_ref,
    kspace_ref,
    mask_ref,
    *refs,
):
    recovered_ref, basis_ref = refs[-2:]
    both = both_ref[...]
    count, reach = images_ref.shape
    devices = count // cols
    at_row, at_col = square(count)
    order = ((at_row // devices == at_col % cols) & (at_row % devices == at_col // cols)).astype(
        jnp.float32
    )
    images = exact(exact(both, order), images_ref[...])
    images_high, images_low = split(images)
    stacked = jnp.concatenate([images_high, images_low], axis=0)
    chg, tile = kspace_ref.shape
    me = lax.axis_index("rows")
    estimate = jnp.zeros((chg, tile), jnp.float32)
    for (start, masks), rows_ref in zip(parts, refs):
        blocks, owned, rank = rows_ref.shape
        vectors = dot3(rows_ref[...].reshape(blocks * owned, rank), both, ((1,), (1,)))
        if masks[0] == 0:
            basis_ref[start * chg : start * chg + owned] = vectors[:owned]
        high, low = split(vectors)
        projected = dot(jnp.concatenate([high, high], axis=1), stacked) + dot(low, images_high)
        for slot, mask in enumerate(masks):
            total = None
            for j in range(owned // chg):
                part = projected[slot * owned + j * chg : slot * owned + (j + 1) * chg]
                part = pltpu.roll(part, start + j, 1) if start + j else part
                total = part if total is None else total + part
            total = pltpu.roll(total, lax.bitwise_xor(me, mask) * per_tile, 1)
            estimate = estimate + total[:, reach - tile :]
    estimate = estimate / KER
    residual = mask_ref[...].astype(jnp.float32) * (kspace_ref[...] - estimate)
    recovered_ref[...] = estimate + residual - jnp.clip(residual, -threshold, threshold)


def call(kernel, outs, *args, scratch=(), space=pltpu.VMEM, limit=40, scalars=0, micros=1):
    return pl.pallas_call(
        kernel,
        out_shape=[jax.ShapeDtypeStruct(shape, kind) for shape, kind in outs],
        in_specs=[pl.BlockSpec(memory_space=space)] * len(args),
        out_specs=[pl.BlockSpec(memory_space=pltpu.VMEM)] * (len(outs) - scalars)
        + [pl.BlockSpec(memory_space=pltpu.SMEM)] * scalars,
        scratch_shapes=list(scratch),
        compiler_params=pltpu.CompilerParams(vmem_limit_bytes=limit * 2**20),
        cost_estimate=pl.CostEstimate(
            flops=micros * 10**9, bytes_accessed=0, transcendentals=0
        ),
    )(*args)


def exchange(block, devices, mask, axes):
    return lax.ppermute(block, axes, [(i, i ^ mask) for i in range(devices)])


def with_masks(masks, mask):
    return masks + [m ^ mask for m in masks]


def after(value, *others):
    return lax.optimization_barrier((value,) + others)[0]


def rounds_of(low, high):
    masks = []
    while low < high:
        if 2 * low < high:
            masks.append([low, 2 * low, 3 * low])
        else:
            masks.append([low])
        low *= 4
    return masks


def gather_round(part, order, masks, devices, axes):
    part = jnp.concatenate(
        [part] + [exchange(part, devices, mask, axes) for mask in masks], axis=0
    )
    return part, order + [m ^ mask for mask in masks for m in order]


def gather_samples(sampled, tiles, groups, beside):
    devices = tiles * groups
    near, masks = sampled[None], [0]
    for partners in rounds_of(2 * groups, devices):
        near, masks = gather_round(near, masks, partners, devices, AXES)
    near = after(near, beside)
    half = near.shape[1] // 2
    parts = [near[:, :half], near[:, half:]]
    orders = [masks, masks]
    ways = [(groups, groups // 2), (groups // 2, groups)]
    for step in range(2):
        for i in range(2):
            parts[i], orders[i] = gather_round(
                parts[i], orders[i], [ways[i][step]], devices, AXES
            )
    for partners in rounds_of(2, groups // 2):
        for i in range(2):
            parts[i], orders[i] = gather_round(parts[i], orders[i], partners, devices, AXES)
    far = [exchange(part, devices, 1, AXES) for part in parts]
    orders = [with_masks(order, 1) for order in orders]
    return parts, far, orders


def gather_rows(by_row, tiles, per_tile):
    half = by_row.shape[0] // 2
    near, order = by_row[None, :half], [0]
    for partners in rounds_of(2, tiles):
        near, order = gather_round(near, order, partners, tiles, "rows")
    parts = [(0, order), (0, [m ^ 1 for m in order])]
    pieces = [near, exchange(near, tiles, 1, "rows")]
    near, order = gather_round(by_row[None, half:], [0], [1], tiles, "rows")
    *early, late = rounds_of(2, tiles)
    for partners in early:
        near, order = gather_round(near, order, partners, tiles, "rows")
    start = per_tile // 2
    parts.append((start, order))
    pieces.append(near)
    for mask in late:
        parts.append((start, [m ^ mask for m in order]))
        pieces.append(exchange(near, tiles, mask, "rows"))
    return parts, pieces


def to_all(pieces, axes=AXES):
    return lax.all_to_all(pieces, axes, 0, 0, tiled=True)


def total_of(kept, given, devices):
    total = kept + exchange(given, devices, 1, AXES)
    for partners in rounds_of(2, devices):
        terms = [exchange(total, devices, mask, AXES) for mask in partners]
        total = total + terms[0]
        if len(terms) == 3:
            total = total + (terms[1] + terms[2])
    return total, exchange(total, devices, 1, AXES)


def column_shards(kspace, sample_mask, start_basis):
    f32, bf16 = jnp.float32, jnp.bfloat16
    tiles, groups = lax.axis_size("rows"), lax.axis_size("coil")
    devices = tiles * groups
    chg, tile = kspace.shape
    channels = chg * groups
    positions = tile * tiles
    owned, rank = start_basis.shape[1:]
    per_tile = owned // chg
    cols = rank // devices
    rows = cols * KER
    lanes = cols * chg

    sampled, basis_send = call(
        functools.partial(prepare_kernel, cols, chg, per_tile),
        [((chg, tile), f32), ((devices * per_tile, lanes), f32)],
        kspace,
        sample_mask,
        start_basis.reshape(owned, rank),
        scratch=[
            pltpu.VMEM((chg, tile), f32),
            pltpu.VMEM((chg, tile), sample_mask.dtype),
            pltpu.VMEM((owned, rank), f32),
            pltpu.SemaphoreType.DMA((3,)),
        ],
        space=pltpu.HBM,
        limit=60,
    )
    basis_parts = to_all(basis_send.reshape(devices, per_tile, lanes))
    near, far, masks = gather_samples(sampled, tiles, groups, basis_parts)
    wide = pltpu.VMEM((rows, positions), f32)
    moved = pltpu.VMEM((2 * rows, positions), bf16)
    samples, normal, send = call(
        functools.partial(passes_kernel, masks),
        [
            ((tiles, 2, groups, chg, tile), bf16),
            ((rows, channels), f32),
            ((tiles, groups, 2, per_tile, lanes), f32),
        ],
        near[0],
        far[0],
        near[1],
        far[1],
        basis_parts.reshape(tiles, groups, per_tile, lanes),
        scratch=[wide, moved],
        micros=12,
    )
    received = to_all(send.reshape(devices, 2 * per_tile, lanes))
    reach = tile + LANES
    (images,) = call(images_kernel, [((tiles, cols, reach), f32)], samples, normal, scratch=[wide], micros=2)
    images = jnp.broadcast_to(images[:, None], (tiles, groups, cols, reach))
    received = after(received, images)
    half = ((rank // 2 + SUB, rank), f32)
    kept, given, by_row = call(
        functools.partial(gram_kernel, cols, per_tile),
        [half, half, ((owned, rank), f32)],
        received.reshape(devices * 2 * per_tile, lanes),
    )
    gram = total_of(kept, given, devices)
    images = to_all(images.reshape(devices, cols, reach)).reshape(rank, reach)
    parts, pieces = gather_rows(by_row, tiles, per_tile)
    whole = ((rank, rank), f32)
    first, both, sound = call(
        factors_kernel, [whole, whole, ((1,), jnp.int32)], *gram, scalars=1, micros=12
    )

    def again():
        (gram,) = call(rows_kernel, [whole], by_row, first)
        mask = 1
        while mask < devices:
            gram = gram + exchange(gram, devices, mask, AXES)
            mask *= 2
        return call(again_kernel, [whole], gram, first)[0]

    both = lax.cond(sound[0] == 1, lambda: both, again)
    recovered, basis = call(
        functools.partial(last_kernel, cols, per_tile, parts),
        [((chg, tile), f32), ((owned, rank), f32)],
        images,
        both,
        kspace,
        sample_mask,
        *pieces,
        micros=5,
    )
    return (recovered, basis.reshape(1, owned, rank))


def divides_columns(kspace, start_basis):
    tiles, groups = lax.axis_size("rows"), lax.axis_size("coil")
    devices = tiles * groups
    chg, tile = kspace.shape
    owned, rank = start_basis.shape[1:]
    return (
        devices & (devices - 1) == 0
        and tiles > 2
        and groups > 2
        and rank % (2 * SUB) == 0
        and rank % devices == 0
        and rank % LANES == 0
        and tile % LANES == 0
        and owned == SUB * chg
        and chg * (rank // devices) == LANES
        and chg % (4 * SUB) == 0
        and (chg * groups) % LANES == 0
        and KER <= LANES
    )


def shards(kspace, sample_mask, start_basis):
    if divides_columns(kspace, start_basis):
        return column_shards(kspace, sample_mask, start_basis)
    return general_shards(kspace, sample_mask, start_basis)


def solution(mesh):
    return jax.shard_map(
        shards,
        mesh=mesh,
        in_specs=(P("coil", "rows"), P("coil", "rows"), P("coil", "rows", None)),
        out_specs=(P("coil", "rows"), P("coil", "rows", None)),
        check_vma=False,
    )
```

```python
import functools

import jax
import jax.numpy as jnp
from jax import lax
from jax.experimental import pallas as pl
from jax.experimental.pallas import tpu as pltpu
from jax.sharding import PartitionSpec as P

KER = 64
ITERS = 2
LANES = 128
SUB = 8
AXES = ("rows", "coil")


threshold = 0.05


def shifted(block, axis, distance):
    devices = range(lax.axis_size(axis))
    route = [((i - distance) % len(devices), i) for i in devices]
    return lax.ppermute(block, axis, route)


def orthonormal(normal_rows, gram_matrix):
    factor = jnp.linalg.cholesky(gram_matrix)
    return lax.linalg.triangular_solve(
        factor, normal_rows, left_side=False, lower=True, transpose_a=True
    )


def coil_total(partial_value):
    return lax.psum(partial_value, "coil")


def general_shards(kspace, sample_mask, start_basis):
    highest = lax.Precision.HIGHEST
    channels = kspace.shape[0]
    tile_rows = kspace.shape[1]
    mask_float = sample_mask.astype(jnp.float32)
    sampled = kspace * mask_float
    next_rim = shifted(sampled[:, : KER - 1], "rows", -1)
    extended = jnp.concatenate([sampled, next_rim], axis=1)
    hankel_cols = jnp.stack(
        [extended[:, offset : offset + tile_rows] for offset in range(KER)], axis=0
    )
    hankel_cols = hankel_cols.reshape(KER * channels, tile_rows)
    owned_basis = start_basis.reshape(start_basis.shape[1], start_basis.shape[2])
    whole_basis = lax.all_gather(owned_basis, "rows", axis=0, tiled=True)
    for iteration in range(ITERS):
        images = coil_total(
            lax.dot_general(
                whole_basis,
                hankel_cols,
                (((0,), (0,)), ((), ())),
                precision=highest,
                preferred_element_type=jnp.float32,
            )
        )
        local_normal = lax.dot_general(
            hankel_cols,
            images,
            (((1,), (1,)), ((), ())),
            precision=highest,
            preferred_element_type=jnp.float32,
        )
        normal_whole = lax.psum(local_normal, "rows")
        local_gram = jnp.dot(
            normal_whole.T, normal_whole, precision=highest, preferred_element_type=jnp.float32
        )
        gram_matrix = lax.psum(local_gram, "coil")
        whole_basis = orthonormal(normal_whole, gram_matrix)
    images = coil_total(
        lax.dot_general(
            whole_basis,
            hankel_cols,
            (((0,), (0,)), ((), ())),
            precision=highest,
            preferred_element_type=jnp.float32,
        )
    )
    projected = jnp.dot(whole_basis, images, precision=highest, preferred_element_type=jnp.float32)
    owned_count = whole_basis.shape[0] // lax.axis_size("rows")
    owned_basis = lax.dynamic_slice_in_dim(
        whole_basis, lax.axis_index("rows") * owned_count, owned_count, 0
    )
    stacked = projected.reshape(KER, channels, tile_rows)
    spread = jnp.zeros((channels, tile_rows + KER - 1), jnp.float32)
    for offset in range(KER):
        spread = spread.at[:, offset : offset + tile_rows].add(stacked[offset])
    carried = shifted(spread[:, tile_rows:], "rows", 1)
    estimate = spread[:, :tile_rows].at[:, : KER - 1].add(carried) / KER
    residual = mask_float * (kspace - estimate)
    recovered = estimate + residual - jnp.clip(residual, -threshold, threshold)
    return (recovered, owned_basis.reshape(1, owned_basis.shape[0], owned_basis.shape[1]))


def split(value):
    high = value.astype(jnp.bfloat16)
    low = (value - high.astype(jnp.float32)).astype(jnp.bfloat16)
    return high, low


def dot(a, b, dims=((1,), (0,))):
    return lax.dot_general(a, b, (dims, ((), ())), preferred_element_type=jnp.float32)


def dot3(a, b, dims=((1,), (0,))):
    a_high, a_low = split(a)
    b_high, b_low = split(b)
    return dot(a_high, b_high, dims) + (dot(a_high, b_low, dims) + dot(a_low, b_high, dims))


def prepare_kernel(
    cols,
    chg,
    per_tile,
    kspace_hbm,
    mask_hbm,
    basis_hbm,
    sampled_ref,
    send_ref,
    kspace_ref,
    mask_ref,
    basis_ref,
    sems,
):
    fetches = [
        pltpu.make_async_copy(source, target, sems.at[i])
        for i, (source, target) in enumerate(
            [(kspace_hbm, kspace_ref), (mask_hbm, mask_ref), (basis_hbm, basis_ref)]
        )
    ]
    for fetch in fetches:
        fetch.start()
    fetches[0].wait()
    fetches[1].wait()
    sampled_ref[...] = kspace_ref[...] * mask_ref[...].astype(jnp.float32)
    fetches[2].wait()
    turned = basis_ref[...].T
    devices = turned.shape[0] // cols
    for j in range(per_tile):
        part = turned[:, j * chg : (j + 1) * chg]
        row = jnp.concatenate([part[k * devices : (k + 1) * devices] for k in range(cols)], axis=1)
        send_ref[pl.ds(j, devices, stride=per_tile), :] = row


def images_of(vectors, samples_ref, wide_ref):
    rows, channels = vectors.shape
    cols = rows // KER
    high, low = split(vectors)
    at_row = lax.broadcasted_iota(jnp.int32, (rows, rows), 0)
    at_col = lax.broadcasted_iota(jnp.int32, (rows, rows), 1)
    flip = ((at_row // KER == at_col // KER) & (at_row % KER + at_col % KER == KER - 1)).astype(
        jnp.float32
    ).astype(jnp.bfloat16)
    both = dot(flip, jnp.concatenate([high, low], axis=1)).astype(jnp.bfloat16)
    high, low = both[:, :channels], both[:, channels:]
    twice = jnp.concatenate([high, high], axis=1)
    tiles = samples_ref.shape[0]
    tile = samples_ref.shape[-1]
    for t in range(tiles):
        block = samples_ref[t].reshape(2 * channels, tile)
        wide_ref[:, t * tile : (t + 1) * tile] = dot(twice, block) + dot(low, block[:channels])
    images = []
    for k in range(cols):
        total = None
        for i in reversed(range(0, KER, SUB)):
            part = wide_ref[k * KER + i : k * KER + i + SUB, :]
            total = part if total is None else pltpu.roll(total, SUB, 1) + part
        total = pltpu.roll(total, 0, 1, stride=1, stride_axis=0)
        images.append(jnp.sum(total, axis=0, keepdims=True))
    return images


def normal_of(images, samples_ref, moved_ref):
    cols = len(images)
    positions = images[0].shape[1]
    tiles = samples_ref.shape[0]
    tile = samples_ref.shape[-1]
    channels = samples_ref.shape[2] * samples_ref.shape[3]
    rows = cols * KER
    for k in range(cols):
        base = jnp.broadcast_to(images[k], (SUB, positions))
        base = pltpu.roll(base, positions - (KER - 1), 1, stride=1, stride_axis=0)
        for j in range(0, KER, 2 * SUB):
            first = base if j == 0 else pltpu.roll(base, j, 1)
            second = pltpu.roll(base, j + SUB, 1)
            high, low = split(jnp.concatenate([first, second], axis=0))
            moved_ref[k * KER + j : k * KER + j + 2 * SUB, :] = high
            moved_ref[rows + k * KER + j : rows + k * KER + j + 2 * SUB, :] = low
    total = jnp.zeros((2 * rows, 2 * channels), jnp.float32)
    for t in range(tiles):
        block = samples_ref[t].reshape(2 * channels, tile)
        total = total + dot(moved_ref[:, t * tile : (t + 1) * tile], block, ((1,), (1,)))
    return total[:rows, :channels] + (
        total[:rows, channels:] + total[rows:, :channels] + total[rows:, channels:]
    )


def store_by_rows(normal, send_ref, part):
    tiles, groups, _, per_tile, lanes = send_ref.shape
    cols = normal.shape[0] // KER
    chg = normal.shape[1] // groups
    for g in range(groups):
        joined = jnp.concatenate(
            [normal[k * KER : (k + 1) * KER, g * chg : (g + 1) * chg] for k in range(cols)], axis=1
        )
        send_ref[:, g, part] = joined.reshape(tiles, per_tile, lanes)


def passes_kernel(orders, basis_ref, *refs):
    *pieces, samples_ref, normal_ref, send_ref, wide_ref, moved_ref = refs
    tiles, _, groups, chg, tile = samples_ref.shape
    me = lax.axis_index("rows") * groups + lax.axis_index("coil")
    for (start, order), piece_ref in zip(orders, pieces):
        count = piece_ref.shape[1]
        for slot, mask in enumerate(order):
            high, low = split(piece_ref[slot])
            source = lax.bitwise_xor(me, mask)
            t, g = source // groups, source % groups
            samples_ref[t, 0, g, start : start + count] = high
            samples_ref[t, 1, g, start : start + count] = low
    cols = basis_ref.shape[-1] // chg
    rows = []
    for k in range(cols):
        rows.append(
            jnp.concatenate(
                [
                    basis_ref[:, g].reshape(KER, cols * chg)[:, k * chg : (k + 1) * chg]
                    for g in range(groups)
                ],
                axis=1,
            )
        )
    vectors = jnp.concatenate(rows, axis=0)
    normal = normal_of(images_of(vectors, samples_ref, wide_ref), samples_ref, moved_ref)
    scaled = []
    for k in range(cols):
        part = normal[k * KER : (k + 1) * KER]
        scaled.append(part * (1.0 / jnp.max(jnp.abs(part))))
    normal = jnp.concatenate(scaled, axis=0)
    store_by_rows(normal, send_ref, 0)
    normal = normal_of(images_of(normal, samples_ref, wide_ref), samples_ref, moved_ref)
    normal_ref[...] = normal
    store_by_rows(normal, send_ref, 1)


def images_kernel(samples_ref, vectors_ref, send_ref, wide_ref):
    tiles, groups, cols, reach = send_ref.shape
    tile = samples_ref.shape[-1]
    images = jnp.concatenate(images_of(vectors_ref[...], samples_ref, wide_ref), axis=0)
    positions = images.shape[1]
    images = pltpu.roll(images, positions - (KER - 1), 1)
    rim = reach - tile
    for t in range(tiles):
        if t == 0:
            part = jnp.concatenate([images[:, positions - rim :], images[:, :tile]], axis=1)
        else:
            part = images[:, t * tile - rim : (t + 1) * tile]
        for g in range(groups):
            send_ref[t, g] = part


def gather_turned(received_ref, cols, per_tile, part):
    count, lanes = received_ref.shape
    devices = count // (2 * per_tile)
    chg = lanes // cols
    loaded = [
        received_ref[pl.ds(part * per_tile + j, devices, stride=2 * per_tile), :]
        for j in range(per_tile)
    ]
    return jnp.concatenate(
        [
            jnp.concatenate(
                [loaded[j][:, k * chg : (k + 1) * chg] for j in range(per_tile)], axis=1
            )
            for k in range(cols)
        ],
        axis=0,
    )


def exact(a, b, dims=((1,), (0,))):
    return lax.dot_general(
        a, b, (dims, ((), ())), precision=lax.Precision.HIGHEST, preferred_element_type=jnp.float32
    )


def square(size):
    at_row = lax.broadcasted_iota(jnp.int32, (size, size), 0)
    at_col = lax.broadcasted_iota(jnp.int32, (size, size), 1)
    return at_row, at_col


def gram_kernel(cols, per_tile, received_ref, kept_ref, given_ref, rows_ref):
    turned = gather_turned(received_ref, cols, per_tile, 0)
    first = exact(turned, turned, ((1,), (1,)))
    turned = gather_turned(received_ref, cols, per_tile, 1)
    second = exact(turned, turned, ((1,), (1,)))
    rows_ref[...] = turned.T
    at_row, at_col = square(first.shape[0])
    packed = jnp.where(at_row >= at_col, first, second)
    line = jnp.sum(jnp.where(at_row == at_col, second, 0.0), axis=0, keepdims=True)
    line = jnp.broadcast_to(line, (SUB, line.shape[1]))
    half = packed.shape[0] // 2
    odd = lax.axis_index("coil") % 2 == 1
    kept_ref[:half] = jnp.where(odd, packed[half:], packed[:half])
    given_ref[:half] = jnp.where(odd, packed[:half], packed[half:])
    kept_ref[half:] = line
    given_ref[half:] = line


def load_grams(kept_ref, other_ref):
    odd = lax.axis_index("coil") % 2 == 1
    kept, other = kept_ref[...], other_ref[...]
    low, high = jnp.where(odd, other, kept), jnp.where(odd, kept, other)
    half = low.shape[0] - SUB
    packed = jnp.concatenate([low[:half], high[:half]], axis=0)
    line = low[half : half + 1]
    at_row, at_col = square(packed.shape[0])
    turned = packed.T
    first = jnp.where(at_row >= at_col, packed, turned)
    second = jnp.where(at_row > at_col, turned, packed)
    return first, jnp.where(at_row == at_col, line, second), line


def inverse_factor(gram):
    size = gram.shape[0]
    shape = (SUB, size)
    at_row = lax.broadcasted_iota(jnp.int32, (size, size), 0)
    at_col = lax.broadcasted_iota(jnp.int32, (size, size), 1)
    unit = (at_row == at_col).astype(jnp.float32)
    left = [gram[b : b + SUB] for b in range(0, size, SUB)]
    right = [unit[b : b + SUB] for b in range(0, size, SUB)]
    sub = lax.broadcasted_iota(jnp.int32, shape, 0)
    done = []
    for b in range(len(left)):
        spread = {
            c: [
                jnp.broadcast_to(left[c][:, b * SUB + k : b * SUB + k + 1], shape)
                for k in range(SUB)
            ]
            for c in range(b, len(left))
        }
        entry = {
            (i, k): jnp.broadcast_to(spread[b][k][i : i + 1], shape)
            for k in range(SUB)
            for i in range(k, SUB)
        }
        inverse = {}
        for k in range(SUB):
            root = lax.rsqrt(entry[k, k])
            root = root * (1.5 - (0.5 * entry[k, k]) * (root * root))
            inverse[k, k] = root
            for i in range(k + 1, SUB):
                entry[i, k] = entry[i, k] * root
            for i in range(k + 1, SUB):
                for m in range(k + 1, i + 1):
                    entry[i, m] = entry[i, m] - entry[i, k] * entry[m, k]
        for i in range(1, SUB):
            for k in range(i):
                total = entry[i, k] * inverse[k, k]
                for m in range(k + 1, i):
                    total = total + entry[i, m] * inverse[m, k]
                inverse[i, k] = -(total * inverse[i, i])

        def solved(rows):
            whole = [jnp.broadcast_to(rows[k : k + 1], shape) for k in range(SUB)]
            first = []
            for i in range(SUB):
                total = inverse[i, 0] * whole[0]
                for k in range(1, i + 1):
                    total = total + inverse[i, k] * whole[k]
                first.append(total)
            second = []
            for k in range(SUB):
                total = inverse[k, k] * first[k]
                for i in range(k + 1, SUB):
                    total = total + inverse[i, k] * first[i]
                second.append(total)
            return first, second

        lower, lower_again = solved(right[b])
        row = lower[0]
        for i in range(1, SUB):
            row = jnp.where(sub == i, lower[i], row)
        done.append(row)
        if b + 1 < len(left):
            _, upper_again = solved(left[b])
            for c in range(b + 1, len(left)):
                for k in range(SUB):
                    left[c] = left[c] - spread[c][k] * upper_again[k]
                    right[c] = right[c] - spread[c][k] * lower_again[k]
    return jnp.concatenate(done, axis=0)


def factors_kernel(gram_ref, other_ref, first_ref, both_ref, sound_ref):
    gram, raw, line = load_grams(gram_ref, other_ref)
    inverse = inverse_factor(gram)
    first_ref[...] = inverse
    gram = exact(exact(inverse, raw), inverse, ((1,), (1,)))
    both_ref[...] = exact(inverse_factor(gram), inverse)
    at_row, at_col = square(gram.shape[0])
    terms = jnp.sum(inverse * inverse * line, axis=1, keepdims=True)
    result = jnp.sum(jnp.where(at_row == at_col, gram, 0.0), axis=1, keepdims=True)
    worst = jnp.max(jnp.where(terms <= 64.0 * result, 0, 1))
    sound_ref[0] = 1 - worst


def rows_kernel(rows_ref, inverse_ref, gram_ref):
    rows = exact(rows_ref[...], inverse_ref[...], ((1,), (1,)))
    gram_ref[...] = exact(rows, rows, ((0,), (0,)))


def again_kernel(gram_ref, inverse_ref, both_ref):
    both_ref[...] = exact(inverse_factor(gram_ref[...]), inverse_ref[...])


def last_kernel(cols, orders, images_ref, both_ref, kspace_hbm, mask_hbm, *refs):
    *pieces, recovered_ref, basis_ref, kspace_ref, mask_ref, sems = refs
    fetches = [
        pltpu.make_async_copy(kspace_hbm, kspace_ref, sems.at[0]),
        pltpu.make_async_copy(mask_hbm, mask_ref, sems.at[1]),
    ]
    for fetch in fetches:
        fetch.start()
    both = both_ref[...]
    count, reach = images_ref.shape
    devices = count // cols
    at_row, at_col = square(count)
    order = ((at_row // devices == at_col % cols) & (at_row % devices == at_col // cols)).astype(
        jnp.float32
    )
    images = exact(exact(both, order), images_ref[...])
    images_high, images_low = split(images)
    stacked = jnp.concatenate([images_high, images_low], axis=0)
    chg, tile = kspace_ref.shape
    me = lax.axis_index("rows")
    estimate = jnp.zeros((chg, tile), jnp.float32)
    for order, rows_ref in zip(orders, pieces):
        for slot, mask in enumerate(order):
            vectors = dot3(rows_ref[slot], both, ((1,), (1,)))
            if mask == 0:
                basis_ref[...] = vectors
            high, low = split(vectors)
            projected = dot(jnp.concatenate([high, high], axis=1), stacked) + dot(low, images_high)
            per_tile = vectors.shape[0] // chg
            total = projected[:chg]
            for j in range(1, per_tile):
                total = total + pltpu.roll(projected[j * chg : (j + 1) * chg], j, 1)
            total = pltpu.roll(total, lax.bitwise_xor(me, mask) * per_tile, 1)
            estimate = estimate + total[:, reach - tile :]
    for fetch in fetches:
        fetch.wait()
    estimate = estimate / KER
    residual = mask_ref[...].astype(jnp.float32) * (kspace_ref[...] - estimate)
    recovered_ref[...] = estimate + residual - jnp.clip(residual, -threshold, threshold)


def call(kernel, outs, *args, scratch=(), far=(), limit=40, scalars=0, micros=1):
    return pl.pallas_call(
        kernel,
        out_shape=[jax.ShapeDtypeStruct(shape, kind) for shape, kind in outs],
        in_specs=[
            pl.BlockSpec(memory_space=pltpu.HBM if i in far else pltpu.VMEM)
            for i in range(len(args))
        ],
        out_specs=[pl.BlockSpec(memory_space=pltpu.VMEM)] * (len(outs) - scalars)
        + [pl.BlockSpec(memory_space=pltpu.SMEM)] * scalars,
        scratch_shapes=list(scratch),
        compiler_params=pltpu.CompilerParams(vmem_limit_bytes=limit * 2**20),
        cost_estimate=pl.CostEstimate(
            flops=micros * 10**9, bytes_accessed=0, transcendentals=0
        ),
    )(*args)


def exchange(block, devices, mask, axes):
    return lax.ppermute(block, axes, [(i, i ^ mask) for i in range(devices)])


def with_masks(masks, mask):
    return masks + [m ^ mask for m in masks]


def after(value, *others):
    return lax.optimization_barrier((value,) + others)[0]


def rounds_of(low, high):
    masks = []
    while low < high:
        if 2 * low < high:
            masks.append([low, 2 * low, 3 * low])
        else:
            masks.append([low])
        low *= 4
    return masks


def gather_round(part, order, masks, devices, axes):
    part = jnp.concatenate(
        [part] + [exchange(part, devices, mask, axes) for mask in masks], axis=0
    )
    return part, order + [m ^ mask for mask in masks for m in order]


def gather_samples(sampled, tiles, groups, beside):
    devices = tiles * groups
    near, masks = sampled[None], [0]
    mask = devices // 2
    while mask > groups:
        near, masks = gather_round(near, masks, [mask], devices, AXES)
        mask //= 2
    near = after(near, beside)
    half = near.shape[1] // 2
    halves = []
    for part, ways in (
        (near[:, :half], (groups, groups // 2)),
        (near[:, half:], (groups // 2, groups)),
    ):
        part, order = gather_round(part, masks, [ways[0]], devices, AXES)
        pieces = [(part, order)]
        mask = ways[1]
        rest = groups // 4
        while mask > 1:
            pieces = pieces + [
                (exchange(part, devices, mask, AXES), [m ^ mask for m in order])
                for part, order in pieces
            ]
            mask, rest = rest, rest // 2
        halves.append(
            pieces
            + [(exchange(part, devices, 1, AXES), [m ^ 1 for m in order]) for part, order in pieces]
        )
    return halves


def to_all(pieces, axes=AXES):
    return lax.all_to_all(pieces, axes, 0, 0, tiled=True)


def total_and_rows(kept, given, by_row, images, tiles, devices):
    total = kept + exchange(given, devices, 1, AXES)
    near, order = by_row[None], [0]
    mask = tiles // 2
    for partners in rounds_of(2, devices):
        terms = [exchange(total, devices, way, AXES) for way in partners]
        if mask > 1:
            near, order = gather_round(near, order, [mask], tiles, "rows")
            mask //= 2
        total = total + terms[0]
        if len(terms) == 3:
            total = total + (terms[1] + terms[2])
        near = after(near, total)
    while mask > 1:
        near, order = gather_round(near, order, [mask], tiles, "rows")
        mask //= 2
    other = exchange(total, devices, 1, AXES)
    near, total, other = lax.optimization_barrier((near, total, other))
    far = exchange(near, tiles, 1, "rows")
    pieces = [(near, order), (far, [m ^ 1 for m in order])]
    return (total, other), pieces, to_all(images)


def column_shards(kspace, sample_mask, start_basis):
    f32, bf16 = jnp.float32, jnp.bfloat16
    tiles, groups = lax.axis_size("rows"), lax.axis_size("coil")
    devices = tiles * groups
    chg, tile = kspace.shape
    channels = chg * groups
    positions = tile * tiles
    owned, rank = start_basis.shape[1:]
    per_tile = owned // chg
    cols = rank // devices
    rows = cols * KER
    lanes = cols * chg

    sampled, basis_send = call(
        functools.partial(prepare_kernel, cols, chg, per_tile),
        [((chg, tile), f32), ((devices * per_tile, lanes), f32)],
        kspace,
        sample_mask,
        start_basis.reshape(owned, rank),
        scratch=[
            pltpu.VMEM((chg, tile), f32),
            pltpu.VMEM((chg, tile), sample_mask.dtype),
            pltpu.VMEM((owned, rank), f32),
            pltpu.SemaphoreType.DMA((3,)),
        ],
        far=(0, 1, 2),
        limit=60,
    )
    basis_parts = to_all(basis_send.reshape(devices, per_tile, lanes))
    halves = gather_samples(sampled, tiles, groups, basis_parts)
    starts = (0, chg // len(halves))
    orders = [(start, order) for start, half in zip(starts, halves) for _, order in half]
    wide = pltpu.VMEM((rows, positions), f32)
    moved = pltpu.VMEM((2 * rows, positions), bf16)
    samples, normal, send = call(
        functools.partial(passes_kernel, orders),
        [
            ((tiles, 2, groups, chg, tile), bf16),
            ((rows, channels), f32),
            ((tiles, groups, 2, per_tile, lanes), f32),
        ],
        basis_parts.reshape(tiles, groups, per_tile, lanes),
        *[piece for half in halves for piece, _ in half],
        scratch=[wide, moved],
        micros=12,
    )
    received = to_all(send.reshape(devices, 2 * per_tile, lanes))
    reach = tile + LANES
    (images,) = call(
        images_kernel,
        [((tiles, groups, cols, reach), f32)],
        samples,
        normal,
        scratch=[wide],
        micros=2,
    )
    received = after(received, images)
    half = ((rank // 2 + SUB, rank), f32)
    kept, given, by_row = call(
        functools.partial(gram_kernel, cols, per_tile),
        [half, half, ((owned, rank), f32)],
        received.reshape(devices * 2 * per_tile, lanes),
    )
    gram, pieces, images = total_and_rows(
        kept, given, by_row, images.reshape(devices, cols, reach), tiles, devices
    )
    whole = ((rank, rank), f32)
    first, both, sound = call(
        factors_kernel, [whole, whole, ((1,), jnp.int32)], *gram, scalars=1, micros=12
    )

    def again():
        (gram,) = call(rows_kernel, [whole], by_row, first)
        mask = 1
        while mask < devices:
            gram = gram + exchange(gram, devices, mask, AXES)
            mask *= 2
        return call(again_kernel, [whole], gram, first)[0]

    both = lax.cond(sound[0] == 1, lambda: both, again)
    recovered, basis = call(
        functools.partial(last_kernel, cols, [order for _, order in pieces]),
        [((chg, tile), f32), ((owned, rank), f32)],
        images.reshape(rank, reach),
        both,
        kspace,
        sample_mask,
        *[piece for piece, _ in pieces],
        scratch=[
            pltpu.VMEM((chg, tile), f32),
            pltpu.VMEM((chg, tile), sample_mask.dtype),
            pltpu.SemaphoreType.DMA((2,)),
        ],
        far=(2, 3),
        limit=40,
        micros=5,
    )
    return (recovered, basis.reshape(1, owned, rank))


def divides_columns(kspace, start_basis):
    tiles, groups = lax.axis_size("rows"), lax.axis_size("coil")
    devices = tiles * groups
    chg, tile = kspace.shape
    owned, rank = start_basis.shape[1:]
    return (
        devices & (devices - 1) == 0
        and tiles > 2
        and groups > 2
        and rank % (2 * SUB) == 0
        and rank % devices == 0
        and rank % LANES == 0
        and tile % LANES == 0
        and owned == SUB * chg
        and chg * (rank // devices) == LANES
        and chg % (4 * SUB) == 0
        and (chg * groups) % LANES == 0
        and KER <= LANES
    )


def shards(kspace, sample_mask, start_basis):
    if divides_columns(kspace, start_basis):
        return column_shards(kspace, sample_mask, start_basis)
    return general_shards(kspace, sample_mask, start_basis)


def solution(mesh):
    return jax.shard_map(
        shards,
        mesh=mesh,
        in_specs=(P("coil", "rows"), P("coil", "rows"), P("coil", "rows", None)),
        out_specs=(P("coil", "rows"), P("coil", "rows", None)),
        check_vma=False,
    )
```

```python
import functools

import jax
import jax.numpy as jnp
from jax import lax
from jax.experimental import pallas as pl
from jax.experimental.pallas import tpu as pltpu
from jax.sharding import PartitionSpec as P

KER = 64
ITERS = 2
LANES = 128
SUB = 8
AXES = ("rows", "coil")


threshold = 0.05


def shifted(block, axis, distance):
    devices = range(lax.axis_size(axis))
    route = [((i - distance) % len(devices), i) for i in devices]
    return lax.ppermute(block, axis, route)


def orthonormal(normal_rows, gram_matrix):
    factor = jnp.linalg.cholesky(gram_matrix)
    return lax.linalg.triangular_solve(
        factor, normal_rows, left_side=False, lower=True, transpose_a=True
    )


def coil_total(partial_value):
    return lax.psum(partial_value, "coil")


def general_shards(kspace, sample_mask, start_basis):
    highest = lax.Precision.HIGHEST
    channels = kspace.shape[0]
    tile_rows = kspace.shape[1]
    mask_float = sample_mask.astype(jnp.float32)
    sampled = kspace * mask_float
    next_rim = shifted(sampled[:, : KER - 1], "rows", -1)
    extended = jnp.concatenate([sampled, next_rim], axis=1)
    hankel_cols = jnp.stack(
        [extended[:, offset : offset + tile_rows] for offset in range(KER)], axis=0
    )
    hankel_cols = hankel_cols.reshape(KER * channels, tile_rows)
    owned_basis = start_basis.reshape(start_basis.shape[1], start_basis.shape[2])
    whole_basis = lax.all_gather(owned_basis, "rows", axis=0, tiled=True)
    for iteration in range(ITERS):
        images = coil_total(
            lax.dot_general(
                whole_basis,
                hankel_cols,
                (((0,), (0,)), ((), ())),
                precision=highest,
                preferred_element_type=jnp.float32,
            )
        )
        local_normal = lax.dot_general(
            hankel_cols,
            images,
            (((1,), (1,)), ((), ())),
            precision=highest,
            preferred_element_type=jnp.float32,
        )
        normal_whole = lax.psum(local_normal, "rows")
        local_gram = jnp.dot(
            normal_whole.T, normal_whole, precision=highest, preferred_element_type=jnp.float32
        )
        gram_matrix = lax.psum(local_gram, "coil")
        whole_basis = orthonormal(normal_whole, gram_matrix)
    images = coil_total(
        lax.dot_general(
            whole_basis,
            hankel_cols,
            (((0,), (0,)), ((), ())),
            precision=highest,
            preferred_element_type=jnp.float32,
        )
    )
    projected = jnp.dot(whole_basis, images, precision=highest, preferred_element_type=jnp.float32)
    owned_count = whole_basis.shape[0] // lax.axis_size("rows")
    owned_basis = lax.dynamic_slice_in_dim(
        whole_basis, lax.axis_index("rows") * owned_count, owned_count, 0
    )
    stacked = projected.reshape(KER, channels, tile_rows)
    spread = jnp.zeros((channels, tile_rows + KER - 1), jnp.float32)
    for offset in range(KER):
        spread = spread.at[:, offset : offset + tile_rows].add(stacked[offset])
    carried = shifted(spread[:, tile_rows:], "rows", 1)
    estimate = spread[:, :tile_rows].at[:, : KER - 1].add(carried) / KER
    residual = mask_float * (kspace - estimate)
    recovered = estimate + residual - jnp.clip(residual, -threshold, threshold)
    return (recovered, owned_basis.reshape(1, owned_basis.shape[0], owned_basis.shape[1]))


def split(value):
    high = value.astype(jnp.bfloat16)
    low = (value - high.astype(jnp.float32)).astype(jnp.bfloat16)
    return high, low


def dot(a, b, dims=((1,), (0,))):
    return lax.dot_general(a, b, (dims, ((), ())), preferred_element_type=jnp.float32)


def dot3(a, b, dims=((1,), (0,))):
    a_high, a_low = split(a)
    b_high, b_low = split(b)
    return dot(a_high, b_high, dims) + (dot(a_high, b_low, dims) + dot(a_low, b_high, dims))


def prepare_kernel(
    cols,
    chg,
    per_tile,
    kspace_hbm,
    mask_hbm,
    basis_hbm,
    sampled_ref,
    send_ref,
    kspace_ref,
    mask_ref,
    basis_ref,
    sems,
):
    fetches = [
        pltpu.make_async_copy(source, target, sems.at[i])
        for i, (source, target) in enumerate(
            [(kspace_hbm, kspace_ref), (mask_hbm, mask_ref), (basis_hbm, basis_ref)]
        )
    ]
    for fetch in fetches:
        fetch.start()
    fetches[0].wait()
    fetches[1].wait()
    sampled_ref[...] = kspace_ref[...] * mask_ref[...].astype(jnp.float32)
    fetches[2].wait()
    turned = basis_ref[...].T
    devices = turned.shape[0] // cols
    for j in range(per_tile):
        part = turned[:, j * chg : (j + 1) * chg]
        row = jnp.concatenate([part[k * devices : (k + 1) * devices] for k in range(cols)], axis=1)
        send_ref[pl.ds(j, devices, stride=per_tile), :] = row


def images_of(vectors, samples_ref, wide_ref):
    rows, channels = vectors.shape
    cols = rows // KER
    high, low = split(vectors)
    at_row = lax.broadcasted_iota(jnp.int32, (rows, rows), 0)
    at_col = lax.broadcasted_iota(jnp.int32, (rows, rows), 1)
    flip = ((at_row // KER == at_col // KER) & (at_row % KER + at_col % KER == KER - 1)).astype(
        jnp.float32
    ).astype(jnp.bfloat16)
    both = dot(flip, jnp.concatenate([high, low], axis=1)).astype(jnp.bfloat16)
    high, low = both[:, :channels], both[:, channels:]
    twice = jnp.concatenate([high, high], axis=1)
    tiles = samples_ref.shape[0]
    tile = samples_ref.shape[-1]
    for t in range(tiles):
        block = samples_ref[t].reshape(2 * channels, tile)
        wide_ref[:, t * tile : (t + 1) * tile] = dot(twice, block) + dot(low, block[:channels])
    images = []
    for k in range(cols):
        total = None
        for i in reversed(range(0, KER, SUB)):
            part = wide_ref[k * KER + i : k * KER + i + SUB, :]
            total = part if total is None else pltpu.roll(total, SUB, 1) + part
        total = pltpu.roll(total, 0, 1, stride=1, stride_axis=0)
        images.append(jnp.sum(total, axis=0, keepdims=True))
    return images


def normal_of(images, samples_ref, moved_ref):
    cols = len(images)
    positions = images[0].shape[1]
    tiles = samples_ref.shape[0]
    tile = samples_ref.shape[-1]
    channels = samples_ref.shape[2] * samples_ref.shape[3]
    rows = cols * KER
    for k in range(cols):
        base = jnp.broadcast_to(images[k], (SUB, positions))
        base = pltpu.roll(base, positions - (KER - 1), 1, stride=1, stride_axis=0)
        for j in range(0, KER, 2 * SUB):
            first = base if j == 0 else pltpu.roll(base, j, 1)
            second = pltpu.roll(base, j + SUB, 1)
            high, low = split(jnp.concatenate([first, second], axis=0))
            moved_ref[k * KER + j : k * KER + j + 2 * SUB, :] = high
            moved_ref[rows + k * KER + j : rows + k * KER + j + 2 * SUB, :] = low
    total = jnp.zeros((2 * rows, 2 * channels), jnp.float32)
    for t in range(tiles):
        block = samples_ref[t].reshape(2 * channels, tile)
        total = total + dot(moved_ref[:, t * tile : (t + 1) * tile], block, ((1,), (1,)))
    return total[:rows, :channels] + (
        total[:rows, channels:] + total[rows:, :channels] + total[rows:, channels:]
    )


def store_by_rows(normal, send_ref, part):
    tiles, groups, _, per_tile, lanes = send_ref.shape
    cols = normal.shape[0] // KER
    chg = normal.shape[1] // groups
    for g in range(groups):
        joined = jnp.concatenate(
            [normal[k * KER : (k + 1) * KER, g * chg : (g + 1) * chg] for k in range(cols)], axis=1
        )
        send_ref[:, g, part] = joined.reshape(tiles, per_tile, lanes)


def store_by_groups(normal_ref, group_ref):
    groups, count, lanes = group_ref.shape
    rows, channels = normal_ref.shape
    chg = channels // groups
    fold = lanes // chg
    cols = rows // KER
    deep = KER // fold
    me = lax.axis_index("coil")
    parts = [
        [normal_ref[pl.ds(k * KER + f, deep, stride=fold), :] for f in range(fold)]
        for k in range(cols)
    ]
    for g in range(groups):
        joined = [
            jnp.concatenate([part[:, g * chg : (g + 1) * chg] for part in parts[k]], axis=1)
            for k in range(cols)
        ]
        group_ref[lax.bitwise_xor(me, g)] = jnp.concatenate(joined, axis=0)


def passes_kernel(orders, basis_ref, *refs):
    *pieces, samples_ref, normal_ref, send_ref, group_ref, wide_ref, moved_ref = refs
    tiles, _, groups, chg, tile = samples_ref.shape
    me = lax.axis_index("rows") * groups + lax.axis_index("coil")
    for (start, order), piece_ref in zip(orders, pieces):
        count = piece_ref.shape[1]
        for slot, mask in enumerate(order):
            high, low = split(piece_ref[slot])
            source = lax.bitwise_xor(me, mask)
            t, g = source // groups, source % groups
            samples_ref[t, 0, g, start : start + count] = high
            samples_ref[t, 1, g, start : start + count] = low
    cols = basis_ref.shape[-1] // chg
    rows = []
    for k in range(cols):
        rows.append(
            jnp.concatenate(
                [
                    basis_ref[:, g].reshape(KER, cols * chg)[:, k * chg : (k + 1) * chg]
                    for g in range(groups)
                ],
                axis=1,
            )
        )
    vectors = jnp.concatenate(rows, axis=0)
    normal = normal_of(images_of(vectors, samples_ref, wide_ref), samples_ref, moved_ref)
    scaled = []
    for k in range(cols):
        part = normal[k * KER : (k + 1) * KER]
        scaled.append(part * (1.0 / jnp.max(jnp.abs(part))))
    normal = jnp.concatenate(scaled, axis=0)
    store_by_rows(normal, send_ref, 0)
    normal = normal_of(images_of(normal, samples_ref, wide_ref), samples_ref, moved_ref)
    normal_ref[...] = normal
    store_by_rows(normal, send_ref, 1)
    store_by_groups(normal_ref, group_ref)


def images_kernel(samples_ref, vectors_ref, send_ref, wide_ref):
    tiles, groups, cols, reach = send_ref.shape
    tile = samples_ref.shape[-1]
    images = jnp.concatenate(images_of(vectors_ref[...], samples_ref, wide_ref), axis=0)
    positions = images.shape[1]
    images = pltpu.roll(images, positions - (KER - 1), 1)
    rim = reach - tile
    for t in range(tiles):
        if t == 0:
            part = jnp.concatenate([images[:, positions - rim :], images[:, :tile]], axis=1)
        else:
            part = images[:, t * tile - rim : (t + 1) * tile]
        for g in range(groups):
            send_ref[t, g] = part


def gather_turned(received_ref, cols, per_tile, part):
    count, lanes = received_ref.shape
    devices = count // (2 * per_tile)
    chg = lanes // cols
    loaded = [
        received_ref[pl.ds(part * per_tile + j, devices, stride=2 * per_tile), :]
        for j in range(per_tile)
    ]
    return jnp.concatenate(
        [
            jnp.concatenate(
                [loaded[j][:, k * chg : (k + 1) * chg] for j in range(per_tile)], axis=1
            )
            for k in range(cols)
        ],
        axis=0,
    )


def exact(a, b, dims=((1,), (0,))):
    return lax.dot_general(
        a, b, (dims, ((), ())), precision=lax.Precision.HIGHEST, preferred_element_type=jnp.float32
    )


def square(size):
    at_row = lax.broadcasted_iota(jnp.int32, (size, size), 0)
    at_col = lax.broadcasted_iota(jnp.int32, (size, size), 1)
    return at_row, at_col


def gram_kernel(cols, per_tile, received_ref, kept_ref, given_ref, turned_ref):
    turned = gather_turned(received_ref, cols, per_tile, 0)
    first = exact(turned, turned, ((1,), (1,)))
    turned = gather_turned(received_ref, cols, per_tile, 1)
    second = exact(turned, turned, ((1,), (1,)))
    turned_ref[...] = turned
    at_row, at_col = square(first.shape[0])
    packed = jnp.where(at_row >= at_col, first, second)
    line = jnp.sum(jnp.where(at_row == at_col, second, 0.0), axis=0, keepdims=True)
    line = jnp.broadcast_to(line, (SUB, line.shape[1]))
    half = packed.shape[0] // 2
    odd = lax.axis_index("coil") % 2 == 1
    kept_ref[:half] = jnp.where(odd, packed[half:], packed[:half])
    given_ref[:half] = jnp.where(odd, packed[:half], packed[half:])
    kept_ref[half:] = line
    given_ref[half:] = line


def load_grams(kept_ref, other_ref):
    odd = lax.axis_index("coil") % 2 == 1
    kept, other = kept_ref[...], other_ref[...]
    low, high = jnp.where(odd, other, kept), jnp.where(odd, kept, other)
    half = low.shape[0] - SUB
    packed = jnp.concatenate([low[:half], high[:half]], axis=0)
    line = low[half : half + 1]
    at_row, at_col = square(packed.shape[0])
    turned = packed.T
    first = jnp.where(at_row >= at_col, packed, turned)
    second = jnp.where(at_row > at_col, turned, packed)
    return first, jnp.where(at_row == at_col, line, second), line


def inverse_factor(gram):
    size = gram.shape[0]
    shape = (SUB, size)
    at_row = lax.broadcasted_iota(jnp.int32, (size, size), 0)
    at_col = lax.broadcasted_iota(jnp.int32, (size, size), 1)
    unit = (at_row == at_col).astype(jnp.float32)
    left = [gram[b : b + SUB] for b in range(0, size, SUB)]
    right = [unit[b : b + SUB] for b in range(0, size, SUB)]
    sub = lax.broadcasted_iota(jnp.int32, shape, 0)
    done = []
    for b in range(len(left)):
        spread = {
            c: [
                jnp.broadcast_to(left[c][:, b * SUB + k : b * SUB + k + 1], shape)
                for k in range(SUB)
            ]
            for c in range(b, len(left))
        }
        entry = {
            (i, k): jnp.broadcast_to(spread[b][k][i : i + 1], shape)
            for k in range(SUB)
            for i in range(k, SUB)
        }
        inverse = {}
        for k in range(SUB):
            root = lax.rsqrt(entry[k, k])
            root = root * (1.5 - (0.5 * entry[k, k]) * (root * root))
            inverse[k, k] = root
            for i in range(k + 1, SUB):
                entry[i, k] = entry[i, k] * root
            for i in range(k + 1, SUB):
                for m in range(k + 1, i + 1):
                    entry[i, m] = entry[i, m] - entry[i, k] * entry[m, k]
        for i in range(1, SUB):
            for k in range(i):
                total = entry[i, k] * inverse[k, k]
                for m in range(k + 1, i):
                    total = total + entry[i, m] * inverse[m, k]
                inverse[i, k] = -(total * inverse[i, i])

        def solved(rows):
            whole = [jnp.broadcast_to(rows[k : k + 1], shape) for k in range(SUB)]
            first = []
            for i in range(SUB):
                total = inverse[i, 0] * whole[0]
                for k in range(1, i + 1):
                    total = total + inverse[i, k] * whole[k]
                first.append(total)
            second = []
            for k in range(SUB):
                total = inverse[k, k] * first[k]
                for i in range(k + 1, SUB):
                    total = total + inverse[i, k] * first[i]
                second.append(total)
            return first, second

        lower, lower_again = solved(right[b])
        row = lower[0]
        for i in range(1, SUB):
            row = jnp.where(sub == i, lower[i], row)
        done.append(row)
        if b + 1 < len(left):
            _, upper_again = solved(left[b])
            for c in range(b + 1, len(left)):
                for k in range(SUB):
                    left[c] = left[c] - spread[c][k] * upper_again[k]
                    right[c] = right[c] - spread[c][k] * lower_again[k]
    return jnp.concatenate(done, axis=0)


def factors_kernel(gram_ref, other_ref, first_ref, both_ref, sound_ref):
    gram, raw, line = load_grams(gram_ref, other_ref)
    inverse = inverse_factor(gram)
    first_ref[...] = inverse
    gram = exact(exact(inverse, raw), inverse, ((1,), (1,)))
    both_ref[...] = exact(inverse_factor(gram), inverse)
    at_row, at_col = square(gram.shape[0])
    terms = jnp.sum(inverse * inverse * line, axis=1, keepdims=True)
    result = jnp.sum(jnp.where(at_row == at_col, gram, 0.0), axis=1, keepdims=True)
    worst = jnp.max(jnp.where(terms <= 64.0 * result, 0, 1))
    sound_ref[0] = 1 - worst


def rows_kernel(turned_ref, inverse_ref, gram_ref):
    turned = exact(inverse_ref[...], turned_ref[...])
    gram_ref[...] = exact(turned, turned, ((1,), (1,)))


def again_kernel(gram_ref, inverse_ref, both_ref):
    both_ref[...] = exact(inverse_factor(gram_ref[...]), inverse_ref[...])


def moved_columns(values, order):
    devices = len(order)
    at_row, at_col = square(values.shape[0])
    me = lax.axis_index("rows") * lax.axis_size("coil") + lax.axis_index("coil")
    slot = at_col % devices
    mask = jnp.zeros_like(slot)
    bit = 1
    while bit < devices:
        mask = mask | jnp.where(slot & bit != 0, order[bit], 0)
        bit *= 2
    source = at_col - slot + lax.bitwise_xor(mask, jnp.full_like(mask, me))
    return exact(values, (at_row == source).astype(jnp.float32))


def last_kernel(
    cols,
    order,
    images_ref,
    both_ref,
    kspace_hbm,
    mask_hbm,
    near_ref,
    far_ref,
    recovered_ref,
    basis_ref,
    kspace_ref,
    mask_ref,
    vectors_ref,
    sems,
):
    fetches = [
        pltpu.make_async_copy(kspace_hbm, kspace_ref, sems.at[0]),
        pltpu.make_async_copy(mask_hbm, mask_ref, sems.at[1]),
    ]
    for fetch in fetches:
        fetch.start()
    both = both_ref[...]
    count, reach = images_ref.shape
    devices = count // cols
    at_row, at_col = square(count)
    turn = ((at_row // devices == at_col % cols) & (at_row % devices == at_col // cols)).astype(
        jnp.float32
    )
    images = exact(exact(both, turn), images_ref[...])
    images_high, images_low = split(images)
    stacked = jnp.concatenate([images_high, images_low], axis=0)
    chg, tile = kspace_ref.shape
    lanes = near_ref.shape[1]
    deep = KER * chg // lanes
    step = cols * deep
    factor = moved_columns(both, order)
    estimate = jnp.zeros((chg, reach), jnp.float32)
    for a in range(0, deep, 2):
        turned = [
            jnp.concatenate(
                [
                    ref[pl.ds(k * deep + a + i, ref.shape[0] // step, stride=step), :]
                    for k in range(cols)
                    for ref in (near_ref, far_ref)
                ],
                axis=0,
            )
            for i in range(2)
        ]
        vectors = dot3(jnp.concatenate(turned, axis=1), factor, ((0,), (1,)))
        vectors_ref[a * lanes : (a + 2) * lanes, :] = vectors
        high, low = split(vectors)
        projected = dot(jnp.concatenate([high, high], axis=1), stacked) + dot(low, images_high)
        for i in range(2 * lanes // chg):
            j = a * lanes // chg + i
            part = projected[i * chg : (i + 1) * chg]
            estimate = estimate + (pltpu.roll(part, j, 1) if j else part)
    owned = basis_ref.shape[0]
    start = pl.multiple_of(lax.axis_index("rows") * owned, owned)
    basis_ref[...] = vectors_ref[pl.ds(start, owned), :]
    estimate = estimate[:, reach - tile :]
    for fetch in fetches:
        fetch.wait()
    estimate = estimate / KER
    residual = mask_ref[...].astype(jnp.float32) * (kspace_ref[...] - estimate)
    recovered_ref[...] = estimate + residual - jnp.clip(residual, -threshold, threshold)


def call(kernel, outs, *args, scratch=(), far=(), limit=40, scalars=0, micros=1):
    return pl.pallas_call(
        kernel,
        out_shape=[jax.ShapeDtypeStruct(shape, kind) for shape, kind in outs],
        in_specs=[
            pl.BlockSpec(memory_space=pltpu.HBM if i in far else pltpu.VMEM)
            for i in range(len(args))
        ],
        out_specs=[pl.BlockSpec(memory_space=pltpu.VMEM)] * (len(outs) - scalars)
        + [pl.BlockSpec(memory_space=pltpu.SMEM)] * scalars,
        scratch_shapes=list(scratch),
        compiler_params=pltpu.CompilerParams(vmem_limit_bytes=limit * 2**20),
        cost_estimate=pl.CostEstimate(
            flops=micros * 10**9, bytes_accessed=0, transcendentals=0
        ),
    )(*args)


def exchange(block, devices, mask, axes):
    return lax.ppermute(block, axes, [(i, i ^ mask) for i in range(devices)])


def with_masks(masks, mask):
    return masks + [m ^ mask for m in masks]


def after(value, *others):
    return lax.optimization_barrier((value,) + others)[0]


def rounds_of(low, high):
    masks = []
    while low < high:
        if 2 * low < high:
            masks.append([low, 2 * low, 3 * low])
        else:
            masks.append([low])
        low *= 4
    return masks


def gather_round(part, order, masks, devices, axes):
    part = jnp.concatenate(
        [part] + [exchange(part, devices, mask, axes) for mask in masks], axis=0
    )
    return part, order + [m ^ mask for mask in masks for m in order]


def gather_samples(sampled, tiles, groups, beside):
    devices = tiles * groups
    near, masks = sampled[None], [0]
    mask = devices // 2
    while mask > groups:
        near, masks = gather_round(near, masks, [mask], devices, AXES)
        mask //= 2
    near = after(near, beside)
    half = near.shape[1] // 2
    halves = []
    for part, ways in (
        (near[:, :half], (groups, groups // 2)),
        (near[:, half:], (groups // 2, groups)),
    ):
        part, order = gather_round(part, masks, [ways[0]], devices, AXES)
        pieces = [(part, order)]
        mask = ways[1]
        rest = groups // 4
        while mask > 1:
            pieces = pieces + [
                (exchange(part, devices, mask, AXES), [m ^ mask for m in order])
                for part, order in pieces
            ]
            mask, rest = rest, rest // 2
        halves.append(
            pieces
            + [(exchange(part, devices, 1, AXES), [m ^ 1 for m in order]) for part, order in pieces]
        )
    return halves


def to_all(pieces, axes=AXES):
    return lax.all_to_all(pieces, axes, 0, 0, tiled=True)


def gather_group(group, devices):
    groups = group.shape[0]
    parts = [group[:1]]
    parts += [exchange(group[s : s + 1], devices, s, AXES) for s in range(1, groups)]
    near = jnp.concatenate(parts, axis=0)
    return gather_round(near, list(range(groups)), [devices // 2], devices, AXES)


def total_beside(kept, given, near, order, groups, devices):
    total = kept + exchange(given, devices, 1, AXES)
    mask = devices // 4
    for partners in rounds_of(2, devices):
        terms = [exchange(total, devices, way, AXES) for way in partners]
        total = total + terms[0]
        if len(terms) == 3:
            total = total + (terms[1] + terms[2])
        if mask > groups:
            near, order = gather_round(near, order, [mask], devices, AXES)
            mask //= 2
    while mask > groups:
        near, order = gather_round(near, order, [mask], devices, AXES)
        mask //= 2
    other = exchange(total, devices, 1, AXES)
    near, total, other = lax.optimization_barrier((near, total, other))
    far = exchange(near, devices, groups, AXES)
    return (total, other), near, far, order + [m ^ groups for m in order]


def column_shards(kspace, sample_mask, start_basis):
    f32, bf16 = jnp.float32, jnp.bfloat16
    tiles, groups = lax.axis_size("rows"), lax.axis_size("coil")
    devices = tiles * groups
    chg, tile = kspace.shape
    channels = chg * groups
    positions = tile * tiles
    owned, rank = start_basis.shape[1:]
    per_tile = owned // chg
    cols = rank // devices
    rows = cols * KER
    lanes = cols * chg

    sampled, basis_send = call(
        functools.partial(prepare_kernel, cols, chg, per_tile),
        [((chg, tile), f32), ((devices * per_tile, lanes), f32)],
        kspace,
        sample_mask,
        start_basis.reshape(owned, rank),
        scratch=[
            pltpu.VMEM((chg, tile), f32),
            pltpu.VMEM((chg, tile), sample_mask.dtype),
            pltpu.VMEM((owned, rank), f32),
            pltpu.SemaphoreType.DMA((3,)),
        ],
        far=(0, 1, 2),
        limit=60,
    )
    basis_parts = to_all(basis_send.reshape(devices, per_tile, lanes))
    halves = gather_samples(sampled, tiles, groups, basis_parts)
    starts = (0, chg // len(halves))
    orders = [(start, order) for start, half in zip(starts, halves) for _, order in half]
    wide = pltpu.VMEM((rows, positions), f32)
    moved = pltpu.VMEM((2 * rows, positions), bf16)
    samples, normal, send, group = call(
        functools.partial(passes_kernel, orders),
        [
            ((tiles, 2, groups, chg, tile), bf16),
            ((rows, channels), f32),
            ((tiles, groups, 2, per_tile, lanes), f32),
            ((groups, rows * chg // lanes, lanes), f32),
        ],
        basis_parts.reshape(tiles, groups, per_tile, lanes),
        *[piece for half in halves for piece, _ in half],
        scratch=[wide, moved],
        micros=12,
    )
    received = to_all(send.reshape(devices, 2 * per_tile, lanes))
    reach = tile + LANES
    (images,) = call(
        images_kernel,
        [((tiles, groups, cols, reach), f32)],
        samples,
        normal,
        scratch=[wide],
        micros=2,
    )
    near, order = gather_group(group, devices)
    received = after(received, images, near)
    half = ((rank // 2 + SUB, rank), f32)
    kept, given, turned = call(
        functools.partial(gram_kernel, cols, per_tile),
        [half, half, ((rank, owned), f32)],
        received.reshape(devices * 2 * per_tile, lanes),
    )
    images = to_all(images.reshape(devices, cols, reach))
    gram, near, far, order = total_beside(kept, given, near, order, groups, devices)
    whole = ((rank, rank), f32)
    first, both, sound = call(
        factors_kernel, [whole, whole, ((1,), jnp.int32)], *gram, scalars=1, micros=12
    )

    def again():
        (gram,) = call(rows_kernel, [whole], turned, first)
        mask = 1
        while mask < devices:
            gram = gram + exchange(gram, devices, mask, AXES)
            mask *= 2
        return call(again_kernel, [whole], gram, first)[0]

    both = lax.cond(sound[0] == 1, lambda: both, again)
    recovered, basis = call(
        functools.partial(last_kernel, cols, order),
        [((chg, tile), f32), ((owned, rank), f32)],
        images.reshape(rank, reach),
        both,
        kspace,
        sample_mask,
        near.reshape(-1, lanes),
        far.reshape(-1, lanes),
        scratch=[
            pltpu.VMEM((chg, tile), f32),
            pltpu.VMEM((chg, tile), sample_mask.dtype),
            pltpu.VMEM((KER * chg, rank), f32),
            pltpu.SemaphoreType.DMA((2,)),
        ],
        far=(2, 3),
        limit=40,
        micros=5,
    )
    return (recovered, basis.reshape(1, owned, rank))


def divides_columns(kspace, start_basis):
    tiles, groups = lax.axis_size("rows"), lax.axis_size("coil")
    devices = tiles * groups
    chg, tile = kspace.shape
    owned, rank = start_basis.shape[1:]
    return (
        devices & (devices - 1) == 0
        and tiles > 2
        and groups > 2
        and rank % (2 * SUB) == 0
        and rank % devices == 0
        and rank % LANES == 0
        and tile % LANES == 0
        and owned == SUB * chg
        and chg * (rank // devices) == LANES
        and chg % (4 * SUB) == 0
        and (chg * groups) % LANES == 0
        and KER <= LANES
    )


def shards(kspace, sample_mask, start_basis):
    if divides_columns(kspace, start_basis):
        return column_shards(kspace, sample_mask, start_basis)
    return general_shards(kspace, sample_mask, start_basis)


def solution(mesh):
    return jax.shard_map(
        shards,
        mesh=mesh,
        in_specs=(P("coil", "rows"), P("coil", "rows"), P("coil", "rows", None)),
        out_specs=(P("coil", "rows"), P("coil", "rows", None)),
        check_vma=False,
    )
```

```python
import functools

import jax
import jax.numpy as jnp
from jax import lax
from jax.experimental import pallas as pl
from jax.experimental.pallas import tpu as pltpu
from jax.sharding import PartitionSpec as P

KER = 64
ITERS = 2
LANES = 128
SUB = 8
AXES = ("rows", "coil")


threshold = 0.05


def shifted(block, axis, distance):
    devices = range(lax.axis_size(axis))
    route = [((i - distance) % len(devices), i) for i in devices]
    return lax.ppermute(block, axis, route)


def orthonormal(normal_rows, gram_matrix):
    factor = jnp.linalg.cholesky(gram_matrix)
    return lax.linalg.triangular_solve(
        factor, normal_rows, left_side=False, lower=True, transpose_a=True
    )


def coil_total(partial_value):
    return lax.psum(partial_value, "coil")


def general_shards(kspace, sample_mask, start_basis):
    highest = lax.Precision.HIGHEST
    channels = kspace.shape[0]
    tile_rows = kspace.shape[1]
    mask_float = sample_mask.astype(jnp.float32)
    sampled = kspace * mask_float
    next_rim = shifted(sampled[:, : KER - 1], "rows", -1)
    extended = jnp.concatenate([sampled, next_rim], axis=1)
    hankel_cols = jnp.stack(
        [extended[:, offset : offset + tile_rows] for offset in range(KER)], axis=0
    )
    hankel_cols = hankel_cols.reshape(KER * channels, tile_rows)
    owned_basis = start_basis.reshape(start_basis.shape[1], start_basis.shape[2])
    whole_basis = lax.all_gather(owned_basis, "rows", axis=0, tiled=True)
    for iteration in range(ITERS):
        images = coil_total(
            lax.dot_general(
                whole_basis,
                hankel_cols,
                (((0,), (0,)), ((), ())),
                precision=highest,
                preferred_element_type=jnp.float32,
            )
        )
        local_normal = lax.dot_general(
            hankel_cols,
            images,
            (((1,), (1,)), ((), ())),
            precision=highest,
            preferred_element_type=jnp.float32,
        )
        normal_whole = lax.psum(local_normal, "rows")
        local_gram = jnp.dot(
            normal_whole.T, normal_whole, precision=highest, preferred_element_type=jnp.float32
        )
        gram_matrix = lax.psum(local_gram, "coil")
        whole_basis = orthonormal(normal_whole, gram_matrix)
    images = coil_total(
        lax.dot_general(
            whole_basis,
            hankel_cols,
            (((0,), (0,)), ((), ())),
            precision=highest,
            preferred_element_type=jnp.float32,
        )
    )
    projected = jnp.dot(whole_basis, images, precision=highest, preferred_element_type=jnp.float32)
    owned_count = whole_basis.shape[0] // lax.axis_size("rows")
    owned_basis = lax.dynamic_slice_in_dim(
        whole_basis, lax.axis_index("rows") * owned_count, owned_count, 0
    )
    stacked = projected.reshape(KER, channels, tile_rows)
    spread = jnp.zeros((channels, tile_rows + KER - 1), jnp.float32)
    for offset in range(KER):
        spread = spread.at[:, offset : offset + tile_rows].add(stacked[offset])
    carried = shifted(spread[:, tile_rows:], "rows", 1)
    estimate = spread[:, :tile_rows].at[:, : KER - 1].add(carried) / KER
    residual = mask_float * (kspace - estimate)
    recovered = estimate + residual - jnp.clip(residual, -threshold, threshold)
    return (recovered, owned_basis.reshape(1, owned_basis.shape[0], owned_basis.shape[1]))


def split(value):
    high = value.astype(jnp.bfloat16)
    low = (value - high.astype(jnp.float32)).astype(jnp.bfloat16)
    return high, low


def dot(a, b, dims=((1,), (0,))):
    return lax.dot_general(a, b, (dims, ((), ())), preferred_element_type=jnp.float32)


def dot3(a, b, dims=((1,), (0,))):
    a_high, a_low = split(a)
    b_high, b_low = split(b)
    return dot(a_high, b_high, dims) + (dot(a_high, b_low, dims) + dot(a_low, b_high, dims))


def prepare_kernel(
    cols,
    chg,
    per_tile,
    kspace_hbm,
    mask_hbm,
    basis_hbm,
    sampled_ref,
    send_ref,
    kspace_ref,
    mask_ref,
    basis_ref,
    sems,
):
    fetches = [
        pltpu.make_async_copy(source, target, sems.at[i])
        for i, (source, target) in enumerate(
            [(kspace_hbm, kspace_ref), (mask_hbm, mask_ref), (basis_hbm, basis_ref)]
        )
    ]
    for fetch in fetches:
        fetch.start()
    fetches[0].wait()
    fetches[1].wait()
    sampled_ref[...] = kspace_ref[...] * mask_ref[...].astype(jnp.float32)
    fetches[2].wait()
    turned = basis_ref[...].T
    devices = turned.shape[0] // cols
    for j in range(per_tile):
        part = turned[:, j * chg : (j + 1) * chg]
        row = jnp.concatenate([part[k * devices : (k + 1) * devices] for k in range(cols)], axis=1)
        send_ref[pl.ds(j, devices, stride=per_tile), :] = row


def images_of(vectors, samples_ref, wide_ref):
    rows, channels = vectors.shape
    cols = rows // KER
    high, low = split(vectors)
    at_row = lax.broadcasted_iota(jnp.int32, (rows, rows), 0)
    at_col = lax.broadcasted_iota(jnp.int32, (rows, rows), 1)
    flip = ((at_row // KER == at_col // KER) & (at_row % KER + at_col % KER == KER - 1)).astype(
        jnp.float32
    ).astype(jnp.bfloat16)
    both = dot(flip, jnp.concatenate([high, low], axis=1)).astype(jnp.bfloat16)
    high, low = both[:, :channels], both[:, channels:]
    twice = jnp.concatenate([high, high], axis=1)
    tiles = samples_ref.shape[0]
    tile = samples_ref.shape[-1]
    for t in range(tiles):
        block = samples_ref[t].reshape(2 * channels, tile)
        wide_ref[:, t * tile : (t + 1) * tile] = dot(twice, block) + dot(low, block[:channels])
    images = []
    for k in range(cols):
        total = None
        for i in reversed(range(0, KER, SUB)):
            part = wide_ref[k * KER + i : k * KER + i + SUB, :]
            total = part if total is None else pltpu.roll(total, SUB, 1) + part
        total = pltpu.roll(total, 0, 1, stride=1, stride_axis=0)
        images.append(jnp.sum(total, axis=0, keepdims=True))
    return images


def normal_of(images, samples_ref, moved_ref):
    cols = len(images)
    positions = images[0].shape[1]
    tiles = samples_ref.shape[0]
    tile = samples_ref.shape[-1]
    channels = samples_ref.shape[2] * samples_ref.shape[3]
    rows = cols * KER
    for k in range(cols):
        base = jnp.broadcast_to(images[k], (SUB, positions))
        base = pltpu.roll(base, positions - (KER - 1), 1, stride=1, stride_axis=0)
        for j in range(0, KER, 2 * SUB):
            first = base if j == 0 else pltpu.roll(base, j, 1)
            second = pltpu.roll(base, j + SUB, 1)
            high, low = split(jnp.concatenate([first, second], axis=0))
            moved_ref[k * KER + j : k * KER + j + 2 * SUB, :] = high
            moved_ref[rows + k * KER + j : rows + k * KER + j + 2 * SUB, :] = low
    total = jnp.zeros((2 * rows, 2 * channels), jnp.float32)
    for t in range(tiles):
        block = samples_ref[t].reshape(2 * channels, tile)
        total = total + dot(moved_ref[:, t * tile : (t + 1) * tile], block, ((1,), (1,)))
    return total[:rows, :channels] + (
        total[:rows, channels:] + total[rows:, :channels] + total[rows:, channels:]
    )


def store_by_rows(normal, send_ref, part):
    tiles, groups, _, per_tile, lanes = send_ref.shape
    cols = normal.shape[0] // KER
    chg = normal.shape[1] // groups
    for g in range(groups):
        joined = jnp.concatenate(
            [normal[k * KER : (k + 1) * KER, g * chg : (g + 1) * chg] for k in range(cols)], axis=1
        )
        send_ref[:, g, part] = joined.reshape(tiles, per_tile, lanes)


def store_by_groups(normal_ref, group_ref):
    groups, count, lanes = group_ref.shape
    rows, channels = normal_ref.shape
    chg = channels // groups
    fold = lanes // chg
    cols = rows // KER
    deep = KER // fold
    me = lax.axis_index("coil")
    parts = [
        [normal_ref[pl.ds(k * KER + f, deep, stride=fold), :] for f in range(fold)]
        for k in range(cols)
    ]
    for g in range(groups):
        joined = [
            jnp.concatenate([part[:, g * chg : (g + 1) * chg] for part in parts[k]], axis=1)
            for k in range(cols)
        ]
        group_ref[lax.bitwise_xor(me, g)] = jnp.concatenate(joined, axis=0)


def passes_kernel(orders, basis_ref, *refs):
    *pieces, samples_ref, normal_ref, send_ref, group_ref, wide_ref, moved_ref = refs
    tiles, _, groups, chg, tile = samples_ref.shape
    me = lax.axis_index("rows") * groups + lax.axis_index("coil")
    for (start, order), piece_ref in zip(orders, pieces):
        count = piece_ref.shape[1]
        for slot, mask in enumerate(order):
            high, low = split(piece_ref[slot])
            source = lax.bitwise_xor(me, mask)
            t, g = source // groups, source % groups
            samples_ref[t, 0, g, start : start + count] = high
            samples_ref[t, 1, g, start : start + count] = low
    cols = basis_ref.shape[-1] // chg
    rows = []
    for k in range(cols):
        rows.append(
            jnp.concatenate(
                [
                    basis_ref[:, g].reshape(KER, cols * chg)[:, k * chg : (k + 1) * chg]
                    for g in range(groups)
                ],
                axis=1,
            )
        )
    vectors = jnp.concatenate(rows, axis=0)
    normal = normal_of(images_of(vectors, samples_ref, wide_ref), samples_ref, moved_ref)
    scaled = []
    for k in range(cols):
        part = normal[k * KER : (k + 1) * KER]
        scaled.append(part * (1.0 / jnp.max(jnp.abs(part))))
    normal = jnp.concatenate(scaled, axis=0)
    store_by_rows(normal, send_ref, 0)
    normal = normal_of(images_of(normal, samples_ref, wide_ref), samples_ref, moved_ref)
    normal_ref[...] = normal
    store_by_rows(normal, send_ref, 1)
    store_by_groups(normal_ref, group_ref)


def images_kernel(samples_ref, vectors_ref, send_ref, wide_ref):
    tiles, groups, cols, reach = send_ref.shape
    tile = samples_ref.shape[-1]
    images = jnp.concatenate(images_of(vectors_ref[...], samples_ref, wide_ref), axis=0)
    positions = images.shape[1]
    images = pltpu.roll(images, positions - (KER - 1), 1)
    rim = reach - tile
    for t in range(tiles):
        if t == 0:
            part = jnp.concatenate([images[:, positions - rim :], images[:, :tile]], axis=1)
        else:
            part = images[:, t * tile - rim : (t + 1) * tile]
        for g in range(groups):
            send_ref[t, g] = part


def gather_turned(received_ref, cols, per_tile, part):
    count, lanes = received_ref.shape
    devices = count // (2 * per_tile)
    chg = lanes // cols
    loaded = [
        received_ref[pl.ds(part * per_tile + j, devices, stride=2 * per_tile), :]
        for j in range(per_tile)
    ]
    return jnp.concatenate(
        [
            jnp.concatenate(
                [loaded[j][:, k * chg : (k + 1) * chg] for j in range(per_tile)], axis=1
            )
            for k in range(cols)
        ],
        axis=0,
    )


def exact(a, b, dims=((1,), (0,))):
    return lax.dot_general(
        a, b, (dims, ((), ())), precision=lax.Precision.HIGHEST, preferred_element_type=jnp.float32
    )


def square(size):
    at_row = lax.broadcasted_iota(jnp.int32, (size, size), 0)
    at_col = lax.broadcasted_iota(jnp.int32, (size, size), 1)
    return at_row, at_col


def gram_kernel(cols, per_tile, received_ref, kept_ref, given_ref, turned_ref):
    turned = gather_turned(received_ref, cols, per_tile, 0)
    first = exact(turned, turned, ((1,), (1,)))
    turned = gather_turned(received_ref, cols, per_tile, 1)
    second = exact(turned, turned, ((1,), (1,)))
    turned_ref[...] = turned
    at_row, at_col = square(first.shape[0])
    packed = jnp.where(at_row >= at_col, first, second)
    line = jnp.sum(jnp.where(at_row == at_col, second, 0.0), axis=0, keepdims=True)
    line = jnp.broadcast_to(line, (SUB, line.shape[1]))
    half = packed.shape[0] // 2
    odd = lax.axis_index("coil") % 2 == 1
    kept_ref[:half] = jnp.where(odd, packed[half:], packed[:half])
    given_ref[:half] = jnp.where(odd, packed[:half], packed[half:])
    kept_ref[half:] = line
    given_ref[half:] = line


def load_grams(kept_ref, other_ref):
    odd = lax.axis_index("coil") % 2 == 1
    kept, other = kept_ref[...], other_ref[...]
    low, high = jnp.where(odd, other, kept), jnp.where(odd, kept, other)
    half = low.shape[0] - SUB
    packed = jnp.concatenate([low[:half], high[:half]], axis=0)
    line = low[half : half + 1]
    at_row, at_col = square(packed.shape[0])
    turned = packed.T
    first = jnp.where(at_row >= at_col, packed, turned)
    second = jnp.where(at_row > at_col, turned, packed)
    return first, jnp.where(at_row == at_col, line, second), line


def inverse_factor(gram):
    size = gram.shape[0]
    shape = (SUB, size)
    at_row = lax.broadcasted_iota(jnp.int32, (size, size), 0)
    at_col = lax.broadcasted_iota(jnp.int32, (size, size), 1)
    unit = (at_row == at_col).astype(jnp.float32)
    left = [gram[b : b + SUB] for b in range(0, size, SUB)]
    right = [unit[b : b + SUB] for b in range(0, size, SUB)]
    sub = lax.broadcasted_iota(jnp.int32, shape, 0)
    done = []
    for b in range(len(left)):
        spread = {
            c: [
                jnp.broadcast_to(left[c][:, b * SUB + k : b * SUB + k + 1], shape)
                for k in range(SUB)
            ]
            for c in range(b, len(left))
        }
        entry = {
            (i, k): jnp.broadcast_to(spread[b][k][i : i + 1], shape)
            for k in range(SUB)
            for i in range(k, SUB)
        }
        inverse = {}
        for k in range(SUB):
            root = lax.rsqrt(entry[k, k])
            root = root * (1.5 - (0.5 * entry[k, k]) * (root * root))
            inverse[k, k] = root
            for i in range(k + 1, SUB):
                entry[i, k] = entry[i, k] * root
            for i in range(k + 1, SUB):
                for m in range(k + 1, i + 1):
                    entry[i, m] = entry[i, m] - entry[i, k] * entry[m, k]
        for i in range(1, SUB):
            for k in range(i):
                total = entry[i, k] * inverse[k, k]
                for m in range(k + 1, i):
                    total = total + entry[i, m] * inverse[m, k]
                inverse[i, k] = -(total * inverse[i, i])

        def solved(rows):
            whole = [jnp.broadcast_to(rows[k : k + 1], shape) for k in range(SUB)]
            first = []
            for i in range(SUB):
                total = inverse[i, 0] * whole[0]
                for k in range(1, i + 1):
                    total = total + inverse[i, k] * whole[k]
                first.append(total)
            second = []
            for k in range(SUB):
                total = inverse[k, k] * first[k]
                for i in range(k + 1, SUB):
                    total = total + inverse[i, k] * first[i]
                second.append(total)
            return first, second

        lower, lower_again = solved(right[b])
        row = lower[0]
        for i in range(1, SUB):
            row = jnp.where(sub == i, lower[i], row)
        done.append(row)
        if b + 1 < len(left):
            _, upper_again = solved(left[b])
            for c in range(b + 1, len(left)):
                for k in range(SUB):
                    left[c] = left[c] - spread[c][k] * upper_again[k]
                    right[c] = right[c] - spread[c][k] * lower_again[k]
    return jnp.concatenate(done, axis=0)


def factors_kernel(gram_ref, other_ref, first_ref, both_ref, sound_ref):
    gram, raw, line = load_grams(gram_ref, other_ref)
    inverse = inverse_factor(gram)
    first_ref[...] = inverse
    gram = exact(exact(inverse, raw), inverse, ((1,), (1,)))
    both_ref[...] = exact(inverse_factor(gram), inverse)
    at_row, at_col = square(gram.shape[0])
    terms = jnp.sum(inverse * inverse * line, axis=1, keepdims=True)
    result = jnp.sum(jnp.where(at_row == at_col, gram, 0.0), axis=1, keepdims=True)
    worst = jnp.max(jnp.where(terms <= 64.0 * result, 0, 1))
    sound_ref[0] = 1 - worst


def rows_kernel(turned_ref, inverse_ref, gram_ref):
    turned = exact(inverse_ref[...], turned_ref[...])
    gram_ref[...] = exact(turned, turned, ((1,), (1,)))


def again_kernel(gram_ref, inverse_ref, both_ref):
    both_ref[...] = exact(inverse_factor(gram_ref[...]), inverse_ref[...])


def moved_columns(values, order):
    devices = len(order)
    at_row, at_col = square(values.shape[0])
    me = lax.axis_index("rows") * lax.axis_size("coil") + lax.axis_index("coil")
    slot = at_col % devices
    mask = jnp.zeros_like(slot)
    bit = 1
    while bit < devices:
        mask = mask | jnp.where(slot & bit != 0, order[bit], 0)
        bit *= 2
    source = at_col - slot + lax.bitwise_xor(mask, jnp.full_like(mask, me))
    return exact(values, (at_row == source).astype(jnp.float32))


def last_kernel(
    cols,
    order,
    images_ref,
    both_ref,
    kspace_hbm,
    mask_hbm,
    near_ref,
    far_ref,
    recovered_ref,
    basis_ref,
    kspace_ref,
    mask_ref,
    vectors_ref,
    sems,
):
    fetches = [
        pltpu.make_async_copy(kspace_hbm, kspace_ref, sems.at[0]),
        pltpu.make_async_copy(mask_hbm, mask_ref, sems.at[1]),
    ]
    for fetch in fetches:
        fetch.start()
    both = both_ref[...]
    count, reach = images_ref.shape
    devices = count // cols
    at_row, at_col = square(count)
    turn = ((at_row // devices == at_col % cols) & (at_row % devices == at_col // cols)).astype(
        jnp.float32
    )
    images = exact(exact(both, turn), images_ref[...])
    images_high, images_low = split(images)
    stacked = jnp.concatenate([images_high, images_low], axis=0)
    chg, tile = kspace_ref.shape
    lanes = near_ref.shape[1]
    deep = KER * chg // lanes
    step = cols * deep
    factor = moved_columns(both, order)
    estimate = jnp.zeros((chg, reach), jnp.float32)
    for a in range(0, deep, 2):
        turned = [
            jnp.concatenate(
                [
                    ref[pl.ds(k * deep + a + i, ref.shape[0] // step, stride=step), :]
                    for k in range(cols)
                    for ref in (near_ref, far_ref)
                ],
                axis=0,
            )
            for i in range(2)
        ]
        vectors = dot3(jnp.concatenate(turned, axis=1), factor, ((0,), (1,)))
        vectors_ref[a * lanes : (a + 2) * lanes, :] = vectors
        high, low = split(vectors)
        projected = dot(jnp.concatenate([high, high], axis=1), stacked) + dot(low, images_high)
        for i in range(2 * lanes // chg):
            j = a * lanes // chg + i
            part = projected[i * chg : (i + 1) * chg]
            estimate = estimate + (pltpu.roll(part, j, 1) if j else part)
    owned = basis_ref.shape[0]
    start = pl.multiple_of(lax.axis_index("rows") * owned, owned)
    basis_ref[...] = vectors_ref[pl.ds(start, owned), :]
    estimate = estimate[:, reach - tile :]
    for fetch in fetches:
        fetch.wait()
    estimate = estimate / KER
    residual = mask_ref[...].astype(jnp.float32) * (kspace_ref[...] - estimate)
    recovered_ref[...] = estimate + residual - jnp.clip(residual, -threshold, threshold)


def call(kernel, outs, *args, scratch=(), far=(), limit=40, scalars=0, micros=1):
    return pl.pallas_call(
        kernel,
        out_shape=[jax.ShapeDtypeStruct(shape, kind) for shape, kind in outs],
        in_specs=[
            pl.BlockSpec(memory_space=pltpu.HBM if i in far else pltpu.VMEM)
            for i in range(len(args))
        ],
        out_specs=[pl.BlockSpec(memory_space=pltpu.VMEM)] * (len(outs) - scalars)
        + [pl.BlockSpec(memory_space=pltpu.SMEM)] * scalars,
        scratch_shapes=list(scratch),
        compiler_params=pltpu.CompilerParams(vmem_limit_bytes=limit * 2**20),
        cost_estimate=pl.CostEstimate(
            flops=micros * 10**9, bytes_accessed=0, transcendentals=0
        ),
    )(*args)


def exchange(block, devices, mask, axes):
    return lax.ppermute(block, axes, [(i, i ^ mask) for i in range(devices)])


def with_masks(masks, mask):
    return masks + [m ^ mask for m in masks]


def after(value, *others):
    return lax.optimization_barrier((value,) + others)[0]


def rounds_of(low, high):
    masks = []
    while low < high:
        if 2 * low < high:
            masks.append([low, 2 * low, 3 * low])
        else:
            masks.append([low])
        low *= 4
    return masks


def gather_round(part, order, masks, devices, axes):
    part = jnp.concatenate(
        [part] + [exchange(part, devices, mask, axes) for mask in masks], axis=0
    )
    return part, order + [m ^ mask for mask in masks for m in order]


def gather_samples(sampled, tiles, groups, beside):
    devices = tiles * groups
    near, masks = sampled[None], [0]
    mask = devices // 2
    while mask > groups:
        near, masks = gather_round(near, masks, [mask], devices, AXES)
        mask //= 2
    near = after(near, beside)
    half = near.shape[1] // 2
    halves = []
    for part, ways in (
        (near[:, :half], (groups, groups // 2)),
        (near[:, half:], (groups // 2, groups)),
    ):
        part, order = gather_round(part, masks, [ways[0]], devices, AXES)
        pieces = [(part, order)]
        mask = ways[1]
        rest = groups // 4
        while mask > 1:
            pieces = pieces + [
                (exchange(part, devices, mask, AXES), [m ^ mask for m in order])
                for part, order in pieces
            ]
            mask, rest = rest, rest // 2
        halves.append(
            pieces
            + [(exchange(part, devices, 1, AXES), [m ^ 1 for m in order]) for part, order in pieces]
        )
    return halves


def to_all(pieces, axes=AXES):
    return lax.all_to_all(pieces, axes, 0, 0, tiled=True)


def gather_group(group, devices):
    groups = group.shape[0]
    parts = [group[:1]]
    parts += [exchange(group[s : s + 1], devices, s, AXES) for s in range(1, groups)]
    return jnp.concatenate(parts, axis=0), list(range(groups))


def total_beside(kept, given, near, order, images, groups, devices):
    total = kept + exchange(given, devices, 1, AXES)
    mask = devices // 2
    for partners in rounds_of(2, devices):
        terms = [exchange(total, devices, way, AXES) for way in partners]
        total = total + terms[0]
        if len(terms) == 3:
            total = total + (terms[1] + terms[2])
        if mask > groups:
            near, order = gather_round(near, order, [mask], devices, AXES)
            mask //= 2
    while mask > groups:
        near, order = gather_round(near, order, [mask], devices, AXES)
        mask //= 2
    other = exchange(total, devices, 1, AXES)
    near, total, other, images = lax.optimization_barrier((near, total, other, images))
    far = exchange(near, devices, groups, AXES)
    return (total, other), near, far, order + [m ^ groups for m in order], to_all(images)


def column_shards(kspace, sample_mask, start_basis):
    f32, bf16 = jnp.float32, jnp.bfloat16
    tiles, groups = lax.axis_size("rows"), lax.axis_size("coil")
    devices = tiles * groups
    chg, tile = kspace.shape
    channels = chg * groups
    positions = tile * tiles
    owned, rank = start_basis.shape[1:]
    per_tile = owned // chg
    cols = rank // devices
    rows = cols * KER
    lanes = cols * chg

    sampled, basis_send = call(
        functools.partial(prepare_kernel, cols, chg, per_tile),
        [((chg, tile), f32), ((devices * per_tile, lanes), f32)],
        kspace,
        sample_mask,
        start_basis.reshape(owned, rank),
        scratch=[
            pltpu.VMEM((chg, tile), f32),
            pltpu.VMEM((chg, tile), sample_mask.dtype),
            pltpu.VMEM((owned, rank), f32),
            pltpu.SemaphoreType.DMA((3,)),
        ],
        far=(0, 1, 2),
        limit=60,
    )
    basis_parts = to_all(basis_send.reshape(devices, per_tile, lanes))
    halves = gather_samples(sampled, tiles, groups, basis_parts)
    starts = (0, chg // len(halves))
    orders = [(start, order) for start, half in zip(starts, halves) for _, order in half]
    wide = pltpu.VMEM((rows, positions), f32)
    moved = pltpu.VMEM((2 * rows, positions), bf16)
    samples, normal, send, group = call(
        functools.partial(passes_kernel, orders),
        [
            ((tiles, 2, groups, chg, tile), bf16),
            ((rows, channels), f32),
            ((tiles, groups, 2, per_tile, lanes), f32),
            ((groups, rows * chg // lanes, lanes), f32),
        ],
        basis_parts.reshape(tiles, groups, per_tile, lanes),
        *[piece for half in halves for piece, _ in half],
        scratch=[wide, moved],
        micros=12,
    )
    received = to_all(send.reshape(devices, 2 * per_tile, lanes))
    reach = tile + LANES
    (images,) = call(
        images_kernel,
        [((tiles, groups, cols, reach), f32)],
        samples,
        normal,
        scratch=[wide],
        micros=2,
    )
    near, order = gather_group(group, devices)
    received, near = lax.optimization_barrier((received, images, near))[::2]
    half = ((rank // 2 + SUB, rank), f32)
    kept, given, turned = call(
        functools.partial(gram_kernel, cols, per_tile),
        [half, half, ((rank, owned), f32)],
        received.reshape(devices * 2 * per_tile, lanes),
    )
    gram, near, far, order, images = total_beside(
        kept, given, near, order, images.reshape(devices, cols, reach), groups, devices
    )
    whole = ((rank, rank), f32)
    first, both, sound = call(
        factors_kernel, [whole, whole, ((1,), jnp.int32)], *gram, scalars=1, micros=12
    )

    def again():
        (gram,) = call(rows_kernel, [whole], turned, first)
        mask = 1
        while mask < devices:
            gram = gram + exchange(gram, devices, mask, AXES)
            mask *= 2
        return call(again_kernel, [whole], gram, first)[0]

    both = lax.cond(sound[0] == 1, lambda: both, again)
    recovered, basis = call(
        functools.partial(last_kernel, cols, order),
        [((chg, tile), f32), ((owned, rank), f32)],
        images.reshape(rank, reach),
        both,
        kspace,
        sample_mask,
        near.reshape(-1, lanes),
        far.reshape(-1, lanes),
        scratch=[
            pltpu.VMEM((chg, tile), f32),
            pltpu.VMEM((chg, tile), sample_mask.dtype),
            pltpu.VMEM((KER * chg, rank), f32),
            pltpu.SemaphoreType.DMA((2,)),
        ],
        far=(2, 3),
        limit=40,
        micros=5,
    )
    return (recovered, basis.reshape(1, owned, rank))


def divides_columns(kspace, start_basis):
    tiles, groups = lax.axis_size("rows"), lax.axis_size("coil")
    devices = tiles * groups
    chg, tile = kspace.shape
    owned, rank = start_basis.shape[1:]
    return (
        devices & (devices - 1) == 0
        and tiles > 2
        and groups > 2
        and rank % (2 * SUB) == 0
        and rank % devices == 0
        and rank % LANES == 0
        and tile % LANES == 0
        and owned == SUB * chg
        and chg * (rank // devices) == LANES
        and chg % (4 * SUB) == 0
        and (chg * groups) % LANES == 0
        and KER <= LANES
    )


def shards(kspace, sample_mask, start_basis):
    if divides_columns(kspace, start_basis):
        return column_shards(kspace, sample_mask, start_basis)
    return general_shards(kspace, sample_mask, start_basis)


def solution(mesh):
    return jax.shard_map(
        shards,
        mesh=mesh,
        in_specs=(P("coil", "rows"), P("coil", "rows"), P("coil", "rows", None)),
        out_specs=(P("coil", "rows"), P("coil", "rows", None)),
        check_vma=False,
    )
```

```python
import functools

import jax
import jax.numpy as jnp
from jax import lax
from jax.experimental import pallas as pl
from jax.experimental.pallas import tpu as pltpu
from jax.sharding import PartitionSpec as P

KER = 64
ITERS = 2
LANES = 128
SUB = 8
AXES = ("rows", "coil")


threshold = 0.05


def shifted(block, axis, distance):
    devices = range(lax.axis_size(axis))
    route = [((i - distance) % len(devices), i) for i in devices]
    return lax.ppermute(block, axis, route)


def orthonormal(normal_rows, gram_matrix):
    factor = jnp.linalg.cholesky(gram_matrix)
    return lax.linalg.triangular_solve(
        factor, normal_rows, left_side=False, lower=True, transpose_a=True
    )


def coil_total(partial_value):
    return lax.psum(partial_value, "coil")


def general_shards(kspace, sample_mask, start_basis):
    highest = lax.Precision.HIGHEST
    channels = kspace.shape[0]
    tile_rows = kspace.shape[1]
    mask_float = sample_mask.astype(jnp.float32)
    sampled = kspace * mask_float
    next_rim = shifted(sampled[:, : KER - 1], "rows", -1)
    extended = jnp.concatenate([sampled, next_rim], axis=1)
    hankel_cols = jnp.stack(
        [extended[:, offset : offset + tile_rows] for offset in range(KER)], axis=0
    )
    hankel_cols = hankel_cols.reshape(KER * channels, tile_rows)
    owned_basis = start_basis.reshape(start_basis.shape[1], start_basis.shape[2])
    whole_basis = lax.all_gather(owned_basis, "rows", axis=0, tiled=True)
    for iteration in range(ITERS):
        images = coil_total(
            lax.dot_general(
                whole_basis,
                hankel_cols,
                (((0,), (0,)), ((), ())),
                precision=highest,
                preferred_element_type=jnp.float32,
            )
        )
        local_normal = lax.dot_general(
            hankel_cols,
            images,
            (((1,), (1,)), ((), ())),
            precision=highest,
            preferred_element_type=jnp.float32,
        )
        normal_whole = lax.psum(local_normal, "rows")
        local_gram = jnp.dot(
            normal_whole.T, normal_whole, precision=highest, preferred_element_type=jnp.float32
        )
        gram_matrix = lax.psum(local_gram, "coil")
        whole_basis = orthonormal(normal_whole, gram_matrix)
    images = coil_total(
        lax.dot_general(
            whole_basis,
            hankel_cols,
            (((0,), (0,)), ((), ())),
            precision=highest,
            preferred_element_type=jnp.float32,
        )
    )
    projected = jnp.dot(whole_basis, images, precision=highest, preferred_element_type=jnp.float32)
    owned_count = whole_basis.shape[0] // lax.axis_size("rows")
    owned_basis = lax.dynamic_slice_in_dim(
        whole_basis, lax.axis_index("rows") * owned_count, owned_count, 0
    )
    stacked = projected.reshape(KER, channels, tile_rows)
    spread = jnp.zeros((channels, tile_rows + KER - 1), jnp.float32)
    for offset in range(KER):
        spread = spread.at[:, offset : offset + tile_rows].add(stacked[offset])
    carried = shifted(spread[:, tile_rows:], "rows", 1)
    estimate = spread[:, :tile_rows].at[:, : KER - 1].add(carried) / KER
    residual = mask_float * (kspace - estimate)
    recovered = estimate + residual - jnp.clip(residual, -threshold, threshold)
    return (recovered, owned_basis.reshape(1, owned_basis.shape[0], owned_basis.shape[1]))


def split(value):
    high = value.astype(jnp.bfloat16)
    low = (value - high.astype(jnp.float32)).astype(jnp.bfloat16)
    return high, low


def dot(a, b, dims=((1,), (0,))):
    return lax.dot_general(a, b, (dims, ((), ())), preferred_element_type=jnp.float32)


def dot3(a, b, dims=((1,), (0,))):
    a_high, a_low = split(a)
    b_high, b_low = split(b)
    return dot(a_high, b_high, dims) + (dot(a_high, b_low, dims) + dot(a_low, b_high, dims))


def square(size):
    at_row = lax.broadcasted_iota(jnp.int32, (size, size), 0)
    at_col = lax.broadcasted_iota(jnp.int32, (size, size), 1)
    return at_row, at_col


def prepare_kernel(
    cols,
    chg,
    per_tile,
    kspace_hbm,
    mask_hbm,
    basis_hbm,
    sampled_ref,
    send_ref,
    kspace_ref,
    mask_ref,
    basis_ref,
    sems,
):
    fetches = [
        pltpu.make_async_copy(source, target, sems.at[i])
        for i, (source, target) in enumerate(
            [(kspace_hbm, kspace_ref), (mask_hbm, mask_ref), (basis_hbm, basis_ref)]
        )
    ]
    for fetch in fetches:
        fetch.start()
    fetches[0].wait()
    fetches[1].wait()
    sampled_ref[...] = kspace_ref[...] * mask_ref[...].astype(jnp.float32)
    fetches[2].wait()
    turned = basis_ref[...].T
    devices = turned.shape[0] // cols
    for j in range(per_tile):
        part = turned[:, j * chg : (j + 1) * chg]
        row = jnp.concatenate([part[k * devices : (k + 1) * devices] for k in range(cols)], axis=1)
        send_ref[pl.ds(j, devices, stride=per_tile), :] = row


def widened(vectors, samples_ref, wide_ref):
    rows, channels = vectors.shape
    high, low = split(vectors)
    at_row, at_col = square(rows)
    flip = ((at_row // KER == at_col // KER) & (at_row % KER + at_col % KER == KER - 1)).astype(
        jnp.float32
    ).astype(jnp.bfloat16)
    both = dot(flip, jnp.concatenate([high, low], axis=1)).astype(jnp.bfloat16)
    high, low = both[:, :channels], both[:, channels:]
    twice = jnp.concatenate([high, high], axis=1)
    tiles = samples_ref.shape[0]
    tile = samples_ref.shape[-1]

    def store(t):
        block = samples_ref[t].reshape(2 * channels, tile)
        wide = dot(twice, block) + dot(low, block[:channels])
        wide_ref[:, LANES + t * tile : LANES + (t + 1) * tile] = wide
        if t == tiles - 1:
            wide_ref[:, :LANES] = wide[:, tile - LANES :]

    return store


def store_images(t, tile, wide_ref, images_ref):
    for k in range(wide_ref.shape[0] // KER):
        total = None
        for i in reversed(range(0, KER, SUB)):
            part = wide_ref[k * KER + i : k * KER + i + SUB, t * tile : (t + 1) * tile + LANES]
            total = part if total is None else pltpu.roll(total, SUB, 1) + part
        total = pltpu.roll(total, 0, 1, stride=1, stride_axis=0)
        total = jnp.sum(total, axis=0, keepdims=True)[:, LANES:]
        images_ref[k : k + 1, t * tile : (t + 1) * tile] = total
        if t == 0:
            end = images_ref.shape[1]
            images_ref[k : k + 1, end - LANES : end] = total[:, :LANES]


def normal_tile(t, cols, samples_ref, images_ref, moved_ref):
    _, parts, groups, chg, tile = samples_ref.shape
    rows = cols * KER
    lanes = slice(t * tile, (t + 1) * tile)
    for k in range(cols):
        base = images_ref[k : k + 1, t * tile : (t + 1) * tile + LANES]
        base = jnp.broadcast_to(base, (SUB, tile + LANES))
        base = pltpu.roll(base, tile + LANES - (KER - 1), 1, stride=1, stride_axis=0)
        for j in range(0, KER, 2 * SUB):
            first = base if j == 0 else pltpu.roll(base, j, 1)
            second = pltpu.roll(base, j + SUB, 1)
            high, low = split(jnp.concatenate([first[:, :tile], second[:, :tile]], axis=0))
            moved_ref[k * KER + j : k * KER + j + 2 * SUB, lanes] = high
            moved_ref[rows + k * KER + j : rows + k * KER + j + 2 * SUB, lanes] = low
    block = samples_ref[t].reshape(parts * groups * chg, tile)
    return dot(moved_ref[:, lanes], block, ((1,), (1,)))


def normal_of(vectors, samples_ref, wide_ref, images_ref, moved_ref):
    tiles, _, groups, chg, tile = samples_ref.shape
    rows, channels = vectors.shape
    store = widened(vectors, samples_ref, wide_ref)
    store(tiles - 1)
    total = None
    for t in range(tiles + 1):
        if t < tiles - 1:
            store(t)
        if t < tiles:
            store_images(t, tile, wide_ref, images_ref)
        if t > 0:
            part = normal_tile(t - 1, rows // KER, samples_ref, images_ref, moved_ref)
            total = part if total is None else total + part
    return total[:rows, :channels] + (
        total[:rows, channels:] + total[rows:, :channels] + total[rows:, channels:]
    )


def store_by_rows(normal, send_ref, part):
    tiles, groups, _, per_tile, lanes = send_ref.shape
    cols = normal.shape[0] // KER
    chg = normal.shape[1] // groups
    for g in range(groups):
        joined = jnp.concatenate(
            [normal[k * KER : (k + 1) * KER, g * chg : (g + 1) * chg] for k in range(cols)], axis=1
        )
        send_ref[:, g, part] = joined.reshape(tiles, per_tile, lanes)


def store_by_groups(normal_ref, group_ref):
    groups, count, lanes = group_ref.shape
    rows, channels = normal_ref.shape
    chg = channels // groups
    fold = lanes // chg
    cols = rows // KER
    deep = KER // fold
    me = lax.axis_index("coil")
    parts = [
        [normal_ref[pl.ds(k * KER + f, deep, stride=fold), :] for f in range(fold)]
        for k in range(cols)
    ]
    for g in range(groups):
        joined = [
            jnp.concatenate([part[:, g * chg : (g + 1) * chg] for part in parts[k]], axis=1)
            for k in range(cols)
        ]
        group_ref[lax.bitwise_xor(me, g)] = jnp.concatenate(joined, axis=0)


def passes_kernel(orders, basis_ref, *refs):
    *pieces, samples_ref, normal_ref, send_ref, group_ref, wide_ref, images_ref, moved_ref = refs
    tiles, _, groups, chg, tile = samples_ref.shape
    me = lax.axis_index("rows") * groups + lax.axis_index("coil")
    for (start, order), piece_ref in zip(orders, pieces):
        count = piece_ref.shape[1]
        for slot, mask in enumerate(order):
            high, low = split(piece_ref[slot])
            source = lax.bitwise_xor(me, mask)
            t, g = source // groups, source % groups
            samples_ref[t, 0, g, start : start + count] = high
            samples_ref[t, 1, g, start : start + count] = low
    cols = basis_ref.shape[-1] // chg
    rows = []
    for k in range(cols):
        rows.append(
            jnp.concatenate(
                [
                    basis_ref[:, g].reshape(KER, cols * chg)[:, k * chg : (k + 1) * chg]
                    for g in range(groups)
                ],
                axis=1,
            )
        )
    vectors = jnp.concatenate(rows, axis=0)
    normal = normal_of(vectors, samples_ref, wide_ref, images_ref, moved_ref)
    scaled = []
    for k in range(cols):
        part = normal[k * KER : (k + 1) * KER]
        scaled.append(part * (1.0 / jnp.max(jnp.abs(part))))
    normal = jnp.concatenate(scaled, axis=0)
    store_by_rows(normal, send_ref, 0)
    normal = normal_of(normal, samples_ref, wide_ref, images_ref, moved_ref)
    normal_ref[...] = normal
    store_by_rows(normal, send_ref, 1)
    store_by_groups(normal_ref, group_ref)


def images_kernel(samples_ref, vectors_ref, send_ref, wide_ref, images_ref):
    tiles, groups, cols, reach = send_ref.shape
    tile = samples_ref.shape[-1]
    store = widened(vectors_ref[...], samples_ref, wide_ref)
    store(tiles - 1)
    for t in range(tiles):
        if t < tiles - 1:
            store(t)
        store_images(t, tile, wide_ref, images_ref)
    positions = tiles * tile
    images = pltpu.roll(images_ref[:cols, :positions], positions - (KER - 1), 1)
    rim = reach - tile
    for t in range(tiles):
        if t == 0:
            part = jnp.concatenate([images[:, positions - rim :], images[:, :tile]], axis=1)
        else:
            part = images[:, t * tile - rim : (t + 1) * tile]
        for g in range(groups):
            send_ref[t, g] = part


def gather_turned(received_ref, cols, per_tile, part):
    count, lanes = received_ref.shape
    devices = count // (2 * per_tile)
    chg = lanes // cols
    loaded = [
        received_ref[pl.ds(part * per_tile + j, devices, stride=2 * per_tile), :]
        for j in range(per_tile)
    ]
    return jnp.concatenate(
        [
            jnp.concatenate(
                [loaded[j][:, k * chg : (k + 1) * chg] for j in range(per_tile)], axis=1
            )
            for k in range(cols)
        ],
        axis=0,
    )


def exact(a, b, dims=((1,), (0,))):
    return lax.dot_general(
        a, b, (dims, ((), ())), precision=lax.Precision.HIGHEST, preferred_element_type=jnp.float32
    )


def gram_kernel(cols, per_tile, received_ref, kept_ref, given_ref, turned_ref):
    turned = gather_turned(received_ref, cols, per_tile, 0)
    first = exact(turned, turned, ((1,), (1,)))
    turned = gather_turned(received_ref, cols, per_tile, 1)
    second = exact(turned, turned, ((1,), (1,)))
    turned_ref[...] = turned
    at_row, at_col = square(first.shape[0])
    packed = jnp.where(at_row >= at_col, first, second)
    line = jnp.sum(jnp.where(at_row == at_col, second, 0.0), axis=0, keepdims=True)
    line = jnp.broadcast_to(line, (SUB, line.shape[1]))
    half = packed.shape[0] // 2
    odd = lax.axis_index("coil") % 2 == 1
    kept_ref[:half] = jnp.where(odd, packed[half:], packed[:half])
    given_ref[:half] = jnp.where(odd, packed[:half], packed[half:])
    kept_ref[half:] = line
    given_ref[half:] = line


def load_grams(kept_ref, other_ref):
    odd = lax.axis_index("coil") % 2 == 1
    kept, other = kept_ref[...], other_ref[...]
    low, high = jnp.where(odd, other, kept), jnp.where(odd, kept, other)
    half = low.shape[0] - SUB
    packed = jnp.concatenate([low[:half], high[:half]], axis=0)
    line = low[half : half + 1]
    at_row, at_col = square(packed.shape[0])
    turned = packed.T
    first = jnp.where(at_row >= at_col, packed, turned)
    second = jnp.where(at_row > at_col, turned, packed)
    return first, jnp.where(at_row == at_col, line, second), line


def inverse_factor(gram):
    size = gram.shape[0]
    shape = (SUB, size)
    at_row = lax.broadcasted_iota(jnp.int32, (size, size), 0)
    at_col = lax.broadcasted_iota(jnp.int32, (size, size), 1)
    unit = (at_row == at_col).astype(jnp.float32)
    left = [gram[b : b + SUB] for b in range(0, size, SUB)]
    right = [unit[b : b + SUB] for b in range(0, size, SUB)]
    sub = lax.broadcasted_iota(jnp.int32, shape, 0)
    done = []
    for b in range(len(left)):
        spread = {
            c: [
                jnp.broadcast_to(left[c][:, b * SUB + k : b * SUB + k + 1], shape)
                for k in range(SUB)
            ]
            for c in range(b, len(left))
        }
        entry = {
            (i, k): jnp.broadcast_to(spread[b][k][i : i + 1], shape)
            for k in range(SUB)
            for i in range(k, SUB)
        }
        inverse = {}
        for k in range(SUB):
            root = lax.rsqrt(entry[k, k])
            root = root * (1.5 - (0.5 * entry[k, k]) * (root * root))
            inverse[k, k] = root
            for i in range(k + 1, SUB):
                entry[i, k] = entry[i, k] * root
            for i in range(k + 1, SUB):
                for m in range(k + 1, i + 1):
                    entry[i, m] = entry[i, m] - entry[i, k] * entry[m, k]
        for i in range(1, SUB):
            for k in range(i):
                total = entry[i, k] * inverse[k, k]
                for m in range(k + 1, i):
                    total = total + entry[i, m] * inverse[m, k]
                inverse[i, k] = -(total * inverse[i, i])

        def solved(rows):
            whole = [jnp.broadcast_to(rows[k : k + 1], shape) for k in range(SUB)]
            first = []
            for i in range(SUB):
                total = inverse[i, 0] * whole[0]
                for k in range(1, i + 1):
                    total = total + inverse[i, k] * whole[k]
                first.append(total)
            second = []
            for k in range(SUB):
                total = inverse[k, k] * first[k]
                for i in range(k + 1, SUB):
                    total = total + inverse[i, k] * first[i]
                second.append(total)
            return first, second

        lower, lower_again = solved(right[b])
        row = lower[0]
        for i in range(1, SUB):
            row = jnp.where(sub == i, lower[i], row)
        done.append(row)
        if b + 1 < len(left):
            _, upper_again = solved(left[b])
            for c in range(b + 1, len(left)):
                for k in range(SUB):
                    left[c] = left[c] - spread[c][k] * upper_again[k]
                    right[c] = right[c] - spread[c][k] * lower_again[k]
    return jnp.concatenate(done, axis=0)


def factors_kernel(gram_ref, other_ref, first_ref, both_ref, sound_ref):
    gram, raw, line = load_grams(gram_ref, other_ref)
    inverse = inverse_factor(gram)
    first_ref[...] = inverse
    gram = exact(exact(inverse, raw), inverse, ((1,), (1,)))
    both_ref[...] = exact(inverse_factor(gram), inverse)
    at_row, at_col = square(gram.shape[0])
    terms = jnp.sum(inverse * inverse * line, axis=1, keepdims=True)
    result = jnp.sum(jnp.where(at_row == at_col, gram, 0.0), axis=1, keepdims=True)
    worst = jnp.max(jnp.where(terms <= 64.0 * result, 0, 1))
    sound_ref[0] = 1 - worst


def rows_kernel(turned_ref, inverse_ref, gram_ref):
    turned = exact(inverse_ref[...], turned_ref[...])
    gram_ref[...] = exact(turned, turned, ((1,), (1,)))


def again_kernel(gram_ref, inverse_ref, both_ref):
    both_ref[...] = exact(inverse_factor(gram_ref[...]), inverse_ref[...])


def moved_columns(values, order):
    devices = len(order[0])
    at_row, at_col = square(values.shape[0])
    me = lax.axis_index("rows") * lax.axis_size("coil") + lax.axis_index("coil")
    slot = at_col % devices
    mask = jnp.zeros_like(slot)
    bit = 1
    while bit < devices:
        step = jnp.where(2 * at_col < at_col.shape[1], order[0][bit], order[1][bit])
        mask = mask | jnp.where(slot & bit != 0, step, 0)
        bit *= 2
    source = at_col - slot + lax.bitwise_xor(mask, jnp.full_like(mask, me))
    return exact(values, (at_row == source).astype(jnp.float32))


def last_kernel(
    cols,
    order,
    images_ref,
    both_ref,
    kspace_hbm,
    mask_hbm,
    top_near_ref,
    top_far_ref,
    low_near_ref,
    low_far_ref,
    recovered_ref,
    basis_ref,
    kspace_ref,
    mask_ref,
    vectors_ref,
    sems,
):
    fetches = [
        pltpu.make_async_copy(kspace_hbm, kspace_ref, sems.at[0]),
        pltpu.make_async_copy(mask_hbm, mask_ref, sems.at[1]),
    ]
    for fetch in fetches:
        fetch.start()
    both = both_ref[...]
    count, reach = images_ref.shape
    devices = count // cols
    at_row, at_col = square(count)
    turn = ((at_row // devices == at_col % cols) & (at_row % devices == at_col // cols)).astype(
        jnp.float32
    )
    images = exact(exact(both, turn), images_ref[...])
    images_high, images_low = split(images)
    stacked = jnp.concatenate([images_high, images_low], axis=0)
    chg, tile = kspace_ref.shape
    lanes = top_near_ref.shape[1]
    deep = KER * chg // lanes
    step = cols // 2 * deep
    factor = moved_columns(both, order)
    estimate = jnp.zeros((chg, reach), jnp.float32)
    for a in range(0, deep, 2):
        turned = [
            jnp.concatenate(
                [
                    ref[pl.ds(k * deep + a + i, ref.shape[0] // step, stride=step), :]
                    for refs in ((top_near_ref, top_far_ref), (low_near_ref, low_far_ref))
                    for k in range(cols // 2)
                    for ref in refs
                ],
                axis=0,
            )
            for i in range(2)
        ]
        vectors = dot3(jnp.concatenate(turned, axis=1), factor, ((0,), (1,)))
        vectors_ref[a * lanes : (a + 2) * lanes, :] = vectors
        high, low = split(vectors)
        projected = dot(jnp.concatenate([high, high], axis=1), stacked) + dot(low, images_high)
        for i in range(2 * lanes // chg):
            j = a * lanes // chg + i
            part = projected[i * chg : (i + 1) * chg]
            estimate = estimate + (pltpu.roll(part, j, 1) if j else part)
    owned = basis_ref.shape[0]
    start = pl.multiple_of(lax.axis_index("rows") * owned, owned)
    basis_ref[...] = vectors_ref[pl.ds(start, owned), :]
    estimate = estimate[:, reach - tile :]
    for fetch in fetches:
        fetch.wait()
    estimate = estimate / KER
    residual = mask_ref[...].astype(jnp.float32) * (kspace_ref[...] - estimate)
    recovered_ref[...] = estimate + residual - jnp.clip(residual, -threshold, threshold)


def call(kernel, outs, *args, scratch=(), far=(), limit=40, scalars=0, micros=1):
    return pl.pallas_call(
        kernel,
        out_shape=[jax.ShapeDtypeStruct(shape, kind) for shape, kind in outs],
        in_specs=[
            pl.BlockSpec(memory_space=pltpu.HBM if i in far else pltpu.VMEM)
            for i in range(len(args))
        ],
        out_specs=[pl.BlockSpec(memory_space=pltpu.VMEM)] * (len(outs) - scalars)
        + [pl.BlockSpec(memory_space=pltpu.SMEM)] * scalars,
        scratch_shapes=list(scratch),
        compiler_params=pltpu.CompilerParams(vmem_limit_bytes=limit * 2**20),
        cost_estimate=pl.CostEstimate(
            flops=micros * 10**9, bytes_accessed=0, transcendentals=0
        ),
    )(*args)


def exchange(block, devices, mask, axes):
    return lax.ppermute(block, axes, [(i, i ^ mask) for i in range(devices)])


def with_masks(masks, mask):
    return masks + [m ^ mask for m in masks]


def after(value, *others):
    return lax.optimization_barrier((value,) + others)[0]


def rounds_of(low, high):
    masks = []
    while low < high:
        if 2 * low < high:
            masks.append([low, 2 * low, 3 * low])
        else:
            masks.append([low])
        low *= 4
    return masks


def gather_round(part, order, masks, devices, axes):
    part = jnp.concatenate(
        [part] + [exchange(part, devices, mask, axes) for mask in masks], axis=0
    )
    return part, order + [m ^ mask for mask in masks for m in order]


def gather_samples(sampled, tiles, groups, beside):
    devices = tiles * groups
    near, masks = sampled[None], [0]
    mask = devices // 2
    while mask > groups:
        near, masks = gather_round(near, masks, [mask], devices, AXES)
        mask //= 2
    near = after(near, beside)
    half = near.shape[1] // 2
    halves = []
    for part, ways in (
        (near[:, :half], (groups, groups // 2)),
        (near[:, half:], (groups // 2, groups)),
    ):
        part, order = gather_round(part, masks, [ways[0]], devices, AXES)
        pieces = [(part, order)]
        mask = ways[1]
        rest = groups // 4
        while mask > 1:
            pieces = pieces + [
                (exchange(part, devices, mask, AXES), [m ^ mask for m in order])
                for part, order in pieces
            ]
            mask, rest = rest, rest // 2
        halves.append(
            pieces
            + [(exchange(part, devices, 1, AXES), [m ^ 1 for m in order]) for part, order in pieces]
        )
    return halves


def to_all(pieces, axes=AXES):
    return lax.all_to_all(pieces, axes, 0, 0, tiled=True)


def gather_group(group, devices):
    groups = group.shape[0]
    parts = [group[:1]]
    parts += [exchange(group[s : s + 1], devices, s, AXES) for s in range(1, groups)]
    return jnp.concatenate(parts, axis=0), list(range(groups))


def total_beside(kept, given, near, order, images, groups, devices):
    ways = []
    mask = devices // 2
    while mask >= groups:
        ways.append(mask)
        mask //= 2
    half = near.shape[1] // 2
    parts = [near[:, :half], near[:, half:]]
    orders = [order, order]
    ways = [ways, ways[-1:] + ways[:-1]]
    step = 0

    def advance():
        for i in range(2):
            parts[i], orders[i] = gather_round(
                parts[i], orders[i], [ways[i][step]], devices, AXES
            )

    total = kept + exchange(given, devices, 1, AXES)
    for partners in rounds_of(2, devices):
        terms = [exchange(total, devices, way, AXES) for way in partners]
        total = total + terms[0]
        if len(terms) == 3:
            total = total + (terms[1] + terms[2])
        if step < len(ways[0]) - 1:
            advance()
            step += 1
    while step < len(ways[0]) - 1:
        advance()
        step += 1
    other = exchange(total, devices, 1, AXES)
    *parts, total, other, images = lax.optimization_barrier((*parts, total, other, images))
    pieces = []
    for i in range(2):
        mask = ways[i][-1]
        pieces += [parts[i], exchange(parts[i], devices, mask, AXES)]
        orders[i] = orders[i] + [m ^ mask for m in orders[i]]
    return (total, other), pieces, orders, to_all(images)


def column_shards(kspace, sample_mask, start_basis):
    f32, bf16 = jnp.float32, jnp.bfloat16
    tiles, groups = lax.axis_size("rows"), lax.axis_size("coil")
    devices = tiles * groups
    chg, tile = kspace.shape
    channels = chg * groups
    positions = tile * tiles
    owned, rank = start_basis.shape[1:]
    per_tile = owned // chg
    cols = rank // devices
    rows = cols * KER
    lanes = cols * chg

    sampled, basis_send = call(
        functools.partial(prepare_kernel, cols, chg, per_tile),
        [((chg, tile), f32), ((devices * per_tile, lanes), f32)],
        kspace,
        sample_mask,
        start_basis.reshape(owned, rank),
        scratch=[
            pltpu.VMEM((chg, tile), f32),
            pltpu.VMEM((chg, tile), sample_mask.dtype),
            pltpu.VMEM((owned, rank), f32),
            pltpu.SemaphoreType.DMA((3,)),
        ],
        far=(0, 1, 2),
        limit=60,
    )
    basis_parts = to_all(basis_send.reshape(devices, per_tile, lanes))
    halves = gather_samples(sampled, tiles, groups, basis_parts)
    starts = (0, chg // len(halves))
    orders = [(start, order) for start, half in zip(starts, halves) for _, order in half]
    wide = pltpu.VMEM((rows, LANES + positions), f32)
    lines = pltpu.VMEM((SUB, positions + LANES), f32)
    moved = pltpu.VMEM((2 * rows, positions), bf16)
    samples, normal, send, group = call(
        functools.partial(passes_kernel, orders),
        [
            ((tiles, 2, groups, chg, tile), bf16),
            ((rows, channels), f32),
            ((tiles, groups, 2, per_tile, lanes), f32),
            ((groups, rows * chg // lanes, lanes), f32),
        ],
        basis_parts.reshape(tiles, groups, per_tile, lanes),
        *[piece for half in halves for piece, _ in half],
        scratch=[wide, lines, moved],
        micros=12,
    )
    received = to_all(send.reshape(devices, 2 * per_tile, lanes))
    reach = tile + LANES
    (images,) = call(
        images_kernel,
        [((tiles, groups, cols, reach), f32)],
        samples,
        normal,
        scratch=[wide, lines],
        micros=2,
    )
    near, order = gather_group(group, devices)
    received, near = lax.optimization_barrier((received, images, near))[::2]
    half = ((rank // 2 + SUB, rank), f32)
    kept, given, turned = call(
        functools.partial(gram_kernel, cols, per_tile),
        [half, half, ((rank, owned), f32)],
        received.reshape(devices * 2 * per_tile, lanes),
    )
    gram, pieces, order, images = total_beside(
        kept, given, near, order, images.reshape(devices, cols, reach), groups, devices
    )
    whole = ((rank, rank), f32)
    first, both, sound = call(
        factors_kernel, [whole, whole, ((1,), jnp.int32)], *gram, scalars=1, micros=12
    )

    def again():
        (gram,) = call(rows_kernel, [whole], turned, first)
        mask = 1
        while mask < devices:
            gram = gram + exchange(gram, devices, mask, AXES)
            mask *= 2
        return call(again_kernel, [whole], gram, first)[0]

    both = lax.cond(sound[0] == 1, lambda: both, again)
    recovered, basis = call(
        functools.partial(last_kernel, cols, order),
        [((chg, tile), f32), ((owned, rank), f32)],
        images.reshape(rank, reach),
        both,
        kspace,
        sample_mask,
        *[piece.reshape(-1, lanes) for piece in pieces],
        scratch=[
            pltpu.VMEM((chg, tile), f32),
            pltpu.VMEM((chg, tile), sample_mask.dtype),
            pltpu.VMEM((KER * chg, rank), f32),
            pltpu.SemaphoreType.DMA((2,)),
        ],
        far=(2, 3),
        limit=40,
        micros=5,
    )
    return (recovered, basis.reshape(1, owned, rank))


def divides_columns(kspace, start_basis):
    tiles, groups = lax.axis_size("rows"), lax.axis_size("coil")
    devices = tiles * groups
    chg, tile = kspace.shape
    owned, rank = start_basis.shape[1:]
    return (
        devices & (devices - 1) == 0
        and tiles > 2
        and groups > 2
        and rank % (2 * SUB) == 0
        and rank % devices == 0
        and rank % LANES == 0
        and tile % LANES == 0
        and owned == SUB * chg
        and chg * (rank // devices) == LANES
        and chg % (4 * SUB) == 0
        and (chg * groups) % LANES == 0
        and KER <= LANES
        and rank // devices <= SUB
        and rank // devices % 2 == 0
    )


def shards(kspace, sample_mask, start_basis):
    if divides_columns(kspace, start_basis):
        return column_shards(kspace, sample_mask, start_basis)
    return general_shards(kspace, sample_mask, start_basis)


def solution(mesh):
    return jax.shard_map(
        shards,
        mesh=mesh,
        in_specs=(P("coil", "rows"), P("coil", "rows"), P("coil", "rows", None)),
        out_specs=(P("coil", "rows"), P("coil", "rows", None)),
        check_vma=False,
    )
```

```python
import functools

import jax
import jax.numpy as jnp
from jax import lax
from jax.experimental import pallas as pl
from jax.experimental.pallas import tpu as pltpu
from jax.sharding import PartitionSpec as P

KER = 64
ITERS = 2
LANES = 128
SUB = 8
AXES = ("rows", "coil")


threshold = 0.05


def shifted(block, axis, distance):
    devices = range(lax.axis_size(axis))
    route = [((i - distance) % len(devices), i) for i in devices]
    return lax.ppermute(block, axis, route)


def orthonormal(normal_rows, gram_matrix):
    factor = jnp.linalg.cholesky(gram_matrix)
    return lax.linalg.triangular_solve(
        factor, normal_rows, left_side=False, lower=True, transpose_a=True
    )


def coil_total(partial_value):
    return lax.psum(partial_value, "coil")


def general_shards(kspace, sample_mask, start_basis):
    highest = lax.Precision.HIGHEST
    channels = kspace.shape[0]
    tile_rows = kspace.shape[1]
    mask_float = sample_mask.astype(jnp.float32)
    sampled = kspace * mask_float
    next_rim = shifted(sampled[:, : KER - 1], "rows", -1)
    extended = jnp.concatenate([sampled, next_rim], axis=1)
    hankel_cols = jnp.stack(
        [extended[:, offset : offset + tile_rows] for offset in range(KER)], axis=0
    )
    hankel_cols = hankel_cols.reshape(KER * channels, tile_rows)
    owned_basis = start_basis.reshape(start_basis.shape[1], start_basis.shape[2])
    whole_basis = lax.all_gather(owned_basis, "rows", axis=0, tiled=True)
    for iteration in range(ITERS):
        images = coil_total(
            lax.dot_general(
                whole_basis,
                hankel_cols,
                (((0,), (0,)), ((), ())),
                precision=highest,
                preferred_element_type=jnp.float32,
            )
        )
        local_normal = lax.dot_general(
            hankel_cols,
            images,
            (((1,), (1,)), ((), ())),
            precision=highest,
            preferred_element_type=jnp.float32,
        )
        normal_whole = lax.psum(local_normal, "rows")
        local_gram = jnp.dot(
            normal_whole.T, normal_whole, precision=highest, preferred_element_type=jnp.float32
        )
        gram_matrix = lax.psum(local_gram, "coil")
        whole_basis = orthonormal(normal_whole, gram_matrix)
    images = coil_total(
        lax.dot_general(
            whole_basis,
            hankel_cols,
            (((0,), (0,)), ((), ())),
            precision=highest,
            preferred_element_type=jnp.float32,
        )
    )
    projected = jnp.dot(whole_basis, images, precision=highest, preferred_element_type=jnp.float32)
    owned_count = whole_basis.shape[0] // lax.axis_size("rows")
    owned_basis = lax.dynamic_slice_in_dim(
        whole_basis, lax.axis_index("rows") * owned_count, owned_count, 0
    )
    stacked = projected.reshape(KER, channels, tile_rows)
    spread = jnp.zeros((channels, tile_rows + KER - 1), jnp.float32)
    for offset in range(KER):
        spread = spread.at[:, offset : offset + tile_rows].add(stacked[offset])
    carried = shifted(spread[:, tile_rows:], "rows", 1)
    estimate = spread[:, :tile_rows].at[:, : KER - 1].add(carried) / KER
    residual = mask_float * (kspace - estimate)
    recovered = estimate + residual - jnp.clip(residual, -threshold, threshold)
    return (recovered, owned_basis.reshape(1, owned_basis.shape[0], owned_basis.shape[1]))


def split(value):
    high = value.astype(jnp.bfloat16)
    low = (value - high.astype(jnp.float32)).astype(jnp.bfloat16)
    return high, low


def dot(a, b, dims=((1,), (0,))):
    return lax.dot_general(a, b, (dims, ((), ())), preferred_element_type=jnp.float32)


def dot3(a, b, dims=((1,), (0,))):
    a_high, a_low = split(a)
    b_high, b_low = split(b)
    return dot(a_high, b_high, dims) + (dot(a_high, b_low, dims) + dot(a_low, b_high, dims))


def square(size):
    at_row = lax.broadcasted_iota(jnp.int32, (size, size), 0)
    at_col = lax.broadcasted_iota(jnp.int32, (size, size), 1)
    return at_row, at_col


def prepare_kernel(
    cols,
    chg,
    per_tile,
    kspace_hbm,
    mask_hbm,
    basis_hbm,
    sampled_ref,
    send_ref,
    kspace_ref,
    mask_ref,
    basis_ref,
    sems,
):
    fetches = [
        pltpu.make_async_copy(source, target, sems.at[i])
        for i, (source, target) in enumerate(
            [(kspace_hbm, kspace_ref), (mask_hbm, mask_ref), (basis_hbm, basis_ref)]
        )
    ]
    for fetch in fetches:
        fetch.start()
    fetches[0].wait()
    fetches[1].wait()
    sampled_ref[...] = kspace_ref[...] * mask_ref[...].astype(jnp.float32)
    fetches[2].wait()
    turned = basis_ref[...].T
    devices = turned.shape[0] // cols
    for j in range(per_tile):
        part = turned[:, j * chg : (j + 1) * chg]
        row = jnp.concatenate([part[k * devices : (k + 1) * devices] for k in range(cols)], axis=1)
        send_ref[pl.ds(j, devices, stride=per_tile), :] = row


def images_of(vectors, samples_ref, wide_ref):
    rows, channels = vectors.shape
    cols = rows // KER
    high, low = split(vectors)
    at_row, at_col = square(rows)
    flip = ((at_row // KER == at_col // KER) & (at_row % KER + at_col % KER == KER - 1)).astype(
        jnp.float32
    ).astype(jnp.bfloat16)
    both = dot(flip, jnp.concatenate([high, low], axis=1)).astype(jnp.bfloat16)
    high, low = both[:, :channels], both[:, channels:]
    positions = samples_ref.shape[-1]
    block = samples_ref[...].reshape(3 * channels, positions)
    wide_ref[...] = dot(jnp.concatenate([high, high, low], axis=1), block)
    images = []
    for k in range(cols):
        total = None
        for i in reversed(range(0, KER, SUB)):
            part = wide_ref[k * KER + i : k * KER + i + SUB, :]
            total = part if total is None else pltpu.roll(total, SUB, 1) + part
        total = pltpu.roll(total, 0, 1, stride=1, stride_axis=0)
        images.append(jnp.sum(total, axis=0, keepdims=True))
    return images


def normal_of(images, samples_ref, moved_ref):
    cols = len(images)
    positions = images[0].shape[1]
    channels = samples_ref.shape[1] * samples_ref.shape[2]
    rows = cols * KER
    for k in range(cols):
        base = jnp.broadcast_to(images[k], (SUB, positions))
        base = pltpu.roll(base, positions - (KER - 1), 1, stride=1, stride_axis=0)
        for j in range(0, KER, 2 * SUB):
            first = base if j == 0 else pltpu.roll(base, j, 1)
            second = pltpu.roll(base, j + SUB, 1)
            high, low = split(jnp.concatenate([first, second], axis=0))
            moved_ref[k * KER + j : k * KER + j + 2 * SUB, :] = high
            moved_ref[rows + k * KER + j : rows + k * KER + j + 2 * SUB, :] = low
    block = samples_ref[:2].reshape(2 * channels, positions)
    total = dot(moved_ref[...], block, ((1,), (1,)))
    return total[:rows, :channels] + (
        total[:rows, channels:] + total[rows:, :channels] + total[rows:, channels:]
    )


def store_by_rows(normal, send_ref, part):
    tiles, groups, _, per_tile, lanes = send_ref.shape
    cols = normal.shape[0] // KER
    chg = normal.shape[1] // groups
    for g in range(groups):
        joined = jnp.concatenate(
            [normal[k * KER : (k + 1) * KER, g * chg : (g + 1) * chg] for k in range(cols)], axis=1
        )
        send_ref[:, g, part] = joined.reshape(tiles, per_tile, lanes)


def store_by_groups(normal_ref, group_ref):
    groups, count, lanes = group_ref.shape
    rows, channels = normal_ref.shape
    chg = channels // groups
    fold = lanes // chg
    cols = rows // KER
    deep = KER // fold
    me = lax.axis_index("coil")
    parts = [
        [normal_ref[pl.ds(k * KER + f, deep, stride=fold), :] for f in range(fold)]
        for k in range(cols)
    ]
    for g in range(groups):
        joined = [
            jnp.concatenate([part[:, g * chg : (g + 1) * chg] for part in parts[k]], axis=1)
            for k in range(cols)
        ]
        group_ref[lax.bitwise_xor(me, g)] = jnp.concatenate(joined, axis=0)


def passes_kernel(orders, basis_ref, *refs):
    *pieces, samples_ref, normal_ref, send_ref, group_ref, wide_ref, moved_ref = refs
    _, groups, chg, _ = samples_ref.shape
    tile = pieces[0].shape[-1]
    me = lax.axis_index("rows") * groups + lax.axis_index("coil")
    for (start, order), piece_ref in zip(orders, pieces):
        count = piece_ref.shape[1]
        for slot, mask in enumerate(order):
            high, low = split(piece_ref[slot])
            source = lax.bitwise_xor(me, mask)
            t, g = source // groups, source % groups
            lanes = pl.ds(pl.multiple_of(t * tile, tile), tile)
            for part, value in enumerate((high, low, high)):
                samples_ref[part, g, start : start + count, lanes] = value
    cols = basis_ref.shape[-1] // chg
    rows = []
    for k in range(cols):
        rows.append(
            jnp.concatenate(
                [
                    basis_ref[:, g].reshape(KER, cols * chg)[:, k * chg : (k + 1) * chg]
                    for g in range(groups)
                ],
                axis=1,
            )
        )
    vectors = jnp.concatenate(rows, axis=0)
    normal = normal_of(images_of(vectors, samples_ref, wide_ref), samples_ref, moved_ref)
    scaled = []
    for k in range(cols):
        part = normal[k * KER : (k + 1) * KER]
        scaled.append(part * (1.0 / jnp.max(jnp.abs(part))))
    normal = jnp.concatenate(scaled, axis=0)
    store_by_rows(normal, send_ref, 0)
    normal = normal_of(images_of(normal, samples_ref, wide_ref), samples_ref, moved_ref)
    normal_ref[...] = normal
    store_by_rows(normal, send_ref, 1)
    store_by_groups(normal_ref, group_ref)


def images_kernel(samples_ref, vectors_ref, send_ref, wide_ref):
    tiles, groups, cols, reach = send_ref.shape
    images = jnp.concatenate(images_of(vectors_ref[...], samples_ref, wide_ref), axis=0)
    positions = images.shape[1]
    tile = positions // tiles
    images = pltpu.roll(images, positions - (KER - 1), 1)
    rim = reach - tile
    for t in range(tiles):
        if t == 0:
            part = jnp.concatenate([images[:, positions - rim :], images[:, :tile]], axis=1)
        else:
            part = images[:, t * tile - rim : (t + 1) * tile]
        for g in range(groups):
            send_ref[t, g] = part


def gather_turned(received_ref, cols, per_tile, part):
    count, lanes = received_ref.shape
    devices = count // (2 * per_tile)
    chg = lanes // cols
    loaded = [
        received_ref[pl.ds(part * per_tile + j, devices, stride=2 * per_tile), :]
        for j in range(per_tile)
    ]
    return jnp.concatenate(
        [
            jnp.concatenate(
                [loaded[j][:, k * chg : (k + 1) * chg] for j in range(per_tile)], axis=1
            )
            for k in range(cols)
        ],
        axis=0,
    )


def exact(a, b, dims=((1,), (0,))):
    return lax.dot_general(
        a, b, (dims, ((), ())), precision=lax.Precision.HIGHEST, preferred_element_type=jnp.float32
    )


def gram_kernel(cols, per_tile, received_ref, kept_ref, given_ref, turned_ref):
    turned = gather_turned(received_ref, cols, per_tile, 0)
    first = exact(turned, turned, ((1,), (1,)))
    turned = gather_turned(received_ref, cols, per_tile, 1)
    second = exact(turned, turned, ((1,), (1,)))
    turned_ref[...] = turned
    at_row, at_col = square(first.shape[0])
    packed = jnp.where(at_row >= at_col, first, second)
    line = jnp.sum(jnp.where(at_row == at_col, second, 0.0), axis=0, keepdims=True)
    line = jnp.broadcast_to(line, (SUB, line.shape[1]))
    half = packed.shape[0] // 2
    odd = lax.axis_index("coil") % 2 == 1
    kept_ref[:half] = jnp.where(odd, packed[half:], packed[:half])
    given_ref[:half] = jnp.where(odd, packed[:half], packed[half:])
    kept_ref[half:] = line
    given_ref[half:] = line


def load_grams(kept_ref, other_ref):
    odd = lax.axis_index("coil") % 2 == 1
    kept, other = kept_ref[...], other_ref[...]
    low, high = jnp.where(odd, other, kept), jnp.where(odd, kept, other)
    half = low.shape[0] - SUB
    packed = jnp.concatenate([low[:half], high[:half]], axis=0)
    line = low[half : half + 1]
    at_row, at_col = square(packed.shape[0])
    turned = packed.T
    first = jnp.where(at_row >= at_col, packed, turned)
    second = jnp.where(at_row > at_col, turned, packed)
    return first, jnp.where(at_row == at_col, line, second), line


def inverse_factor(gram):
    size = gram.shape[0]
    shape = (SUB, size)
    at_row = lax.broadcasted_iota(jnp.int32, (size, size), 0)
    at_col = lax.broadcasted_iota(jnp.int32, (size, size), 1)
    unit = (at_row == at_col).astype(jnp.float32)
    left = [gram[b : b + SUB] for b in range(0, size, SUB)]
    right = [unit[b : b + SUB] for b in range(0, size, SUB)]
    sub = lax.broadcasted_iota(jnp.int32, shape, 0)
    done = []
    for b in range(len(left)):
        spread = {
            c: [
                jnp.broadcast_to(left[c][:, b * SUB + k : b * SUB + k + 1], shape)
                for k in range(SUB)
            ]
            for c in range(b, len(left))
        }
        entry = {
            (i, k): jnp.broadcast_to(spread[b][k][i : i + 1], shape)
            for k in range(SUB)
            for i in range(k, SUB)
        }
        inverse = {}
        for k in range(SUB):
            root = lax.rsqrt(entry[k, k])
            root = root * (1.5 - (0.5 * entry[k, k]) * (root * root))
            inverse[k, k] = root
            for i in range(k + 1, SUB):
                entry[i, k] = entry[i, k] * root
            for i in range(k + 1, SUB):
                for m in range(k + 1, i + 1):
                    entry[i, m] = entry[i, m] - entry[i, k] * entry[m, k]
        for i in range(1, SUB):
            for k in range(i):
                total = entry[i, k] * inverse[k, k]
                for m in range(k + 1, i):
                    total = total + entry[i, m] * inverse[m, k]
                inverse[i, k] = -(total * inverse[i, i])

        def solved(rows):
            whole = [jnp.broadcast_to(rows[k : k + 1], shape) for k in range(SUB)]
            first = []
            for i in range(SUB):
                total = inverse[i, 0] * whole[0]
                for k in range(1, i + 1):
                    total = total + inverse[i, k] * whole[k]
                first.append(total)
            second = []
            for k in range(SUB):
                total = inverse[k, k] * first[k]
                for i in range(k + 1, SUB):
                    total = total + inverse[i, k] * first[i]
                second.append(total)
            return first, second

        lower, lower_again = solved(right[b])
        row = lower[0]
        for i in range(1, SUB):
            row = jnp.where(sub == i, lower[i], row)
        done.append(row)
        if b + 1 < len(left):
            _, upper_again = solved(left[b])
            for c in range(b + 1, len(left)):
                for k in range(SUB):
                    left[c] = left[c] - spread[c][k] * upper_again[k]
                    right[c] = right[c] - spread[c][k] * lower_again[k]
    return jnp.concatenate(done, axis=0)


def factor_kernel(gram_ref, other_ref, inverse_ref, next_ref, sound_ref):
    gram, raw, line = load_grams(gram_ref, other_ref)
    inverse = inverse_factor(gram)
    inverse_ref[...] = inverse
    gram = exact(exact(inverse, raw), inverse, ((1,), (1,)))
    next_ref[...] = gram
    at_row, at_col = square(gram.shape[0])
    terms = jnp.sum(inverse * inverse * line, axis=1, keepdims=True)
    result = jnp.sum(jnp.where(at_row == at_col, gram, 0.0), axis=1, keepdims=True)
    worst = jnp.max(jnp.where(terms <= 64.0 * result, 0, 1))
    sound_ref[0] = 1 - worst


def rows_kernel(turned_ref, inverse_ref, gram_ref):
    turned = exact(inverse_ref[...], turned_ref[...])
    gram_ref[...] = exact(turned, turned, ((1,), (1,)))


def both_kernel(gram_ref, inverse_ref, both_ref):
    both_ref[...] = exact(inverse_factor(gram_ref[...]), inverse_ref[...])


def moved_columns(values, order):
    devices = len(order)
    at_row, at_col = square(values.shape[0])
    me = lax.axis_index("rows") * lax.axis_size("coil") + lax.axis_index("coil")
    slot = at_col % devices
    mask = jnp.zeros_like(slot)
    bit = 1
    while bit < devices:
        mask = mask | jnp.where(slot & bit != 0, order[bit], 0)
        bit *= 2
    source = at_col - slot + lax.bitwise_xor(mask, jnp.full_like(mask, me))
    return exact(values, (at_row == source).astype(jnp.float32))


def last_kernel(
    cols,
    order,
    images_ref,
    both_ref,
    kspace_hbm,
    mask_hbm,
    near_ref,
    far_ref,
    recovered_ref,
    basis_ref,
    kspace_ref,
    mask_ref,
    vectors_ref,
    sems,
):
    fetches = [
        pltpu.make_async_copy(kspace_hbm, kspace_ref, sems.at[0]),
        pltpu.make_async_copy(mask_hbm, mask_ref, sems.at[1]),
    ]
    for fetch in fetches:
        fetch.start()
    both = both_ref[...]
    count, reach = images_ref.shape
    devices = count // cols
    at_row, at_col = square(count)
    turn = ((at_row // devices == at_col % cols) & (at_row % devices == at_col // cols)).astype(
        jnp.float32
    )
    images = exact(exact(both, turn), images_ref[...])
    images_high, images_low = split(images)
    stacked = jnp.concatenate([images_high, images_low], axis=0)
    chg, tile = kspace_ref.shape
    lanes = near_ref.shape[1]
    deep = KER * chg // lanes
    step = cols * deep
    factor = moved_columns(both, order)
    estimate = jnp.zeros((chg, reach), jnp.float32)
    for a in range(0, deep, 2):
        turned = [
            jnp.concatenate(
                [
                    ref[pl.ds(k * deep + a + i, ref.shape[0] // step, stride=step), :]
                    for k in range(cols)
                    for ref in (near_ref, far_ref)
                ],
                axis=0,
            )
            for i in range(2)
        ]
        vectors = dot3(jnp.concatenate(turned, axis=1), factor, ((0,), (1,)))
        vectors_ref[a * lanes : (a + 2) * lanes, :] = vectors
        high, low = split(vectors)
        projected = dot(jnp.concatenate([high, high], axis=1), stacked) + dot(low, images_high)
        for i in range(2 * lanes // chg):
            j = a * lanes // chg + i
            part = projected[i * chg : (i + 1) * chg]
            estimate = estimate + (pltpu.roll(part, j, 1) if j else part)
    owned = basis_ref.shape[0]
    start = pl.multiple_of(lax.axis_index("rows") * owned, owned)
    basis_ref[...] = vectors_ref[pl.ds(start, owned), :]
    estimate = estimate[:, reach - tile :]
    for fetch in fetches:
        fetch.wait()
    estimate = estimate / KER
    residual = mask_ref[...].astype(jnp.float32) * (kspace_ref[...] - estimate)
    recovered_ref[...] = estimate + residual - jnp.clip(residual, -threshold, threshold)


def call(kernel, outs, *args, scratch=(), far=(), limit=40, scalars=0, micros=1):
    return pl.pallas_call(
        kernel,
        out_shape=[jax.ShapeDtypeStruct(shape, kind) for shape, kind in outs],
        in_specs=[
            pl.BlockSpec(memory_space=pltpu.HBM if i in far else pltpu.VMEM)
            for i in range(len(args))
        ],
        out_specs=[pl.BlockSpec(memory_space=pltpu.VMEM)] * (len(outs) - scalars)
        + [pl.BlockSpec(memory_space=pltpu.SMEM)] * scalars,
        scratch_shapes=list(scratch),
        compiler_params=pltpu.CompilerParams(vmem_limit_bytes=limit * 2**20),
        cost_estimate=pl.CostEstimate(
            flops=micros * 10**9, bytes_accessed=0, transcendentals=0
        ),
    )(*args)


def exchange(block, devices, mask, axes):
    return lax.ppermute(block, axes, [(i, i ^ mask) for i in range(devices)])


def with_masks(masks, mask):
    return masks + [m ^ mask for m in masks]


def after(value, *others):
    return lax.optimization_barrier((value,) + others)[0]


def rounds_of(low, high):
    masks = []
    while low < high:
        if 2 * low < high:
            masks.append([low, 2 * low, 3 * low])
        else:
            masks.append([low])
        low *= 4
    return masks


def gather_round(part, order, masks, devices, axes):
    part = jnp.concatenate(
        [part] + [exchange(part, devices, mask, axes) for mask in masks], axis=0
    )
    return part, order + [m ^ mask for mask in masks for m in order]


def gather_samples(sampled, tiles, groups, beside):
    devices = tiles * groups
    near, masks = sampled[None], [0]
    mask = devices // 2
    while mask > groups:
        near, masks = gather_round(near, masks, [mask], devices, AXES)
        mask //= 2
    near = after(near, beside)
    half = near.shape[1] // 2
    halves = []
    for part, ways in (
        (near[:, :half], (groups, groups // 2)),
        (near[:, half:], (groups // 2, groups)),
    ):
        part, order = gather_round(part, masks, [ways[0]], devices, AXES)
        pieces = [(part, order)]
        mask = ways[1]
        rest = groups // 4
        while mask > 1:
            pieces = pieces + [
                (exchange(part, devices, mask, AXES), [m ^ mask for m in order])
                for part, order in pieces
            ]
            mask, rest = rest, rest // 2
        halves.append(
            pieces
            + [(exchange(part, devices, 1, AXES), [m ^ 1 for m in order]) for part, order in pieces]
        )
    return halves


def to_all(pieces, axes=AXES):
    return lax.all_to_all(pieces, axes, 0, 0, tiled=True)


def gather_group(group, devices):
    groups = group.shape[0]
    parts = [group[:1]]
    parts += [exchange(group[s : s + 1], devices, s, AXES) for s in range(1, groups)]
    return jnp.concatenate(parts, axis=0), list(range(groups))


def total_beside(kept, given, near, order, images, groups, devices):
    total = kept + exchange(given, devices, 1, AXES)
    mask = 2
    while mask <= groups:
        total = total + exchange(total, devices, mask, AXES)
        mask *= 2
    step = devices // 2
    near, order = gather_round(near, order, [step], devices, AXES)
    step //= 2
    total, near = lax.optimization_barrier((total, near))
    while mask < devices:
        total = total + exchange(total, devices, mask, AXES)
        mask *= 2
    while step > groups:
        near, order = gather_round(near, order, [step], devices, AXES)
        step //= 2
    other = exchange(total, devices, 1, AXES)
    near, total, other, images = lax.optimization_barrier((near, total, other, images))
    far = exchange(near, devices, groups, AXES)
    return (total, other), near, far, order + [m ^ groups for m in order], to_all(images)


def column_shards(kspace, sample_mask, start_basis):
    f32, bf16 = jnp.float32, jnp.bfloat16
    tiles, groups = lax.axis_size("rows"), lax.axis_size("coil")
    devices = tiles * groups
    chg, tile = kspace.shape
    channels = chg * groups
    positions = tile * tiles
    owned, rank = start_basis.shape[1:]
    per_tile = owned // chg
    cols = rank // devices
    rows = cols * KER
    lanes = cols * chg

    sampled, basis_send = call(
        functools.partial(prepare_kernel, cols, chg, per_tile),
        [((chg, tile), f32), ((devices * per_tile, lanes), f32)],
        kspace,
        sample_mask,
        start_basis.reshape(owned, rank),
        scratch=[
            pltpu.VMEM((chg, tile), f32),
            pltpu.VMEM((chg, tile), sample_mask.dtype),
            pltpu.VMEM((owned, rank), f32),
            pltpu.SemaphoreType.DMA((3,)),
        ],
        far=(0, 1, 2),
        limit=60,
    )
    basis_parts = to_all(basis_send.reshape(devices, per_tile, lanes))
    halves = gather_samples(sampled, tiles, groups, basis_parts)
    starts = (0, chg // len(halves))
    orders = [(start, order) for start, half in zip(starts, halves) for _, order in half]
    wide = pltpu.VMEM((rows, positions), f32)
    moved = pltpu.VMEM((2 * rows, positions), bf16)
    samples, normal, send, group = call(
        functools.partial(passes_kernel, orders),
        [
            ((3, groups, chg, positions), bf16),
            ((rows, channels), f32),
            ((tiles, groups, 2, per_tile, lanes), f32),
            ((groups, rows * chg // lanes, lanes), f32),
        ],
        basis_parts.reshape(tiles, groups, per_tile, lanes),
        *[piece for half in halves for piece, _ in half],
        scratch=[wide, moved],
        micros=12,
    )
    received = to_all(send.reshape(devices, 2 * per_tile, lanes))
    reach = tile + LANES
    (images,) = call(
        images_kernel,
        [((tiles, groups, cols, reach), f32)],
        samples,
        normal,
        scratch=[wide],
        micros=2,
    )
    near, order = gather_group(group, devices)
    received, near = lax.optimization_barrier((received, images, near))[::2]
    half = ((rank // 2 + SUB, rank), f32)
    kept, given, turned = call(
        functools.partial(gram_kernel, cols, per_tile),
        [half, half, ((rank, owned), f32)],
        received.reshape(devices * 2 * per_tile, lanes),
    )
    gram, near, far, order, images = total_beside(
        kept, given, near, order, images.reshape(devices, cols, reach), groups, devices
    )
    whole = ((rank, rank), f32)
    first, second, sound = call(
        factor_kernel, [whole, whole, ((1,), jnp.int32)], *gram, scalars=1, micros=12
    )

    def again():
        (gram,) = call(rows_kernel, [whole], turned, first)
        mask = 1
        while mask < devices:
            gram = gram + exchange(gram, devices, mask, AXES)
            mask *= 2
        return gram

    second = lax.cond(sound[0] == 1, lambda: second, again)
    (both,) = call(both_kernel, [whole], second, first, micros=0)
    recovered, basis = call(
        functools.partial(last_kernel, cols, order),
        [((chg, tile), f32), ((owned, rank), f32)],
        images.reshape(rank, reach),
        both,
        kspace,
        sample_mask,
        near.reshape(-1, lanes),
        far.reshape(-1, lanes),
        scratch=[
            pltpu.VMEM((chg, tile), f32),
            pltpu.VMEM((chg, tile), sample_mask.dtype),
            pltpu.VMEM((KER * chg, rank), f32),
            pltpu.SemaphoreType.DMA((2,)),
        ],
        far=(2, 3),
        limit=40,
        micros=5,
    )
    return (recovered, basis.reshape(1, owned, rank))


def divides_columns(kspace, start_basis):
    tiles, groups = lax.axis_size("rows"), lax.axis_size("coil")
    devices = tiles * groups
    chg, tile = kspace.shape
    owned, rank = start_basis.shape[1:]
    return (
        devices & (devices - 1) == 0
        and tiles > 2
        and groups > 2
        and rank % (2 * SUB) == 0
        and rank % devices == 0
        and rank % LANES == 0
        and tile % LANES == 0
        and owned == SUB * chg
        and chg * (rank // devices) == LANES
        and chg % (4 * SUB) == 0
        and (chg * groups) % LANES == 0
        and KER <= LANES
        and rank // devices <= SUB
        and rank // devices % 2 == 0
    )


def shards(kspace, sample_mask, start_basis):
    if divides_columns(kspace, start_basis):
        return column_shards(kspace, sample_mask, start_basis)
    return general_shards(kspace, sample_mask, start_basis)


def solution(mesh):
    return jax.shard_map(
        shards,
        mesh=mesh,
        in_specs=(P("coil", "rows"), P("coil", "rows"), P("coil", "rows", None)),
        out_specs=(P("coil", "rows"), P("coil", "rows", None)),
        check_vma=False,
    )
```

```python
import functools

import jax
import jax.numpy as jnp
from jax import lax
from jax.experimental import pallas as pl
from jax.experimental.pallas import tpu as pltpu
from jax.sharding import PartitionSpec as P

KER = 64
ITERS = 2
LANES = 128
SUB = 8
AXES = ("rows", "coil")


threshold = 0.05


def shifted(block, axis, distance):
    devices = range(lax.axis_size(axis))
    route = [((i - distance) % len(devices), i) for i in devices]
    return lax.ppermute(block, axis, route)


def orthonormal(normal_rows, gram_matrix):
    factor = jnp.linalg.cholesky(gram_matrix)
    return lax.linalg.triangular_solve(
        factor, normal_rows, left_side=False, lower=True, transpose_a=True
    )


def coil_total(partial_value):
    return lax.psum(partial_value, "coil")


def general_shards(kspace, sample_mask, start_basis):
    highest = lax.Precision.HIGHEST
    channels = kspace.shape[0]
    tile_rows = kspace.shape[1]
    mask_float = sample_mask.astype(jnp.float32)
    sampled = kspace * mask_float
    next_rim = shifted(sampled[:, : KER - 1], "rows", -1)
    extended = jnp.concatenate([sampled, next_rim], axis=1)
    hankel_cols = jnp.stack(
        [extended[:, offset : offset + tile_rows] for offset in range(KER)], axis=0
    )
    hankel_cols = hankel_cols.reshape(KER * channels, tile_rows)
    owned_basis = start_basis.reshape(start_basis.shape[1], start_basis.shape[2])
    whole_basis = lax.all_gather(owned_basis, "rows", axis=0, tiled=True)
    for iteration in range(ITERS):
        images = coil_total(
            lax.dot_general(
                whole_basis,
                hankel_cols,
                (((0,), (0,)), ((), ())),
                precision=highest,
                preferred_element_type=jnp.float32,
            )
        )
        local_normal = lax.dot_general(
            hankel_cols,
            images,
            (((1,), (1,)), ((), ())),
            precision=highest,
            preferred_element_type=jnp.float32,
        )
        normal_whole = lax.psum(local_normal, "rows")
        local_gram = jnp.dot(
            normal_whole.T, normal_whole, precision=highest, preferred_element_type=jnp.float32
        )
        gram_matrix = lax.psum(local_gram, "coil")
        whole_basis = orthonormal(normal_whole, gram_matrix)
    images = coil_total(
        lax.dot_general(
            whole_basis,
            hankel_cols,
            (((0,), (0,)), ((), ())),
            precision=highest,
            preferred_element_type=jnp.float32,
        )
    )
    projected = jnp.dot(whole_basis, images, precision=highest, preferred_element_type=jnp.float32)
    owned_count = whole_basis.shape[0] // lax.axis_size("rows")
    owned_basis = lax.dynamic_slice_in_dim(
        whole_basis, lax.axis_index("rows") * owned_count, owned_count, 0
    )
    stacked = projected.reshape(KER, channels, tile_rows)
    spread = jnp.zeros((channels, tile_rows + KER - 1), jnp.float32)
    for offset in range(KER):
        spread = spread.at[:, offset : offset + tile_rows].add(stacked[offset])
    carried = shifted(spread[:, tile_rows:], "rows", 1)
    estimate = spread[:, :tile_rows].at[:, : KER - 1].add(carried) / KER
    residual = mask_float * (kspace - estimate)
    recovered = estimate + residual - jnp.clip(residual, -threshold, threshold)
    return (recovered, owned_basis.reshape(1, owned_basis.shape[0], owned_basis.shape[1]))


def split(value):
    high = value.astype(jnp.bfloat16)
    low = (value - high.astype(jnp.float32)).astype(jnp.bfloat16)
    return high, low


def dot(a, b, dims=((1,), (0,))):
    return lax.dot_general(a, b, (dims, ((), ())), preferred_element_type=jnp.float32)


def dot3(a, b, dims=((1,), (0,))):
    a_high, a_low = split(a)
    b_high, b_low = split(b)
    return dot(a_high, b_high, dims) + (dot(a_high, b_low, dims) + dot(a_low, b_high, dims))


def square(size):
    at_row = lax.broadcasted_iota(jnp.int32, (size, size), 0)
    at_col = lax.broadcasted_iota(jnp.int32, (size, size), 1)
    return at_row, at_col


def prepare_kernel(
    cols,
    chg,
    per_tile,
    kspace_hbm,
    mask_hbm,
    basis_hbm,
    sampled_ref,
    send_ref,
    kspace_ref,
    mask_ref,
    basis_ref,
    sems,
):
    fetches = [
        pltpu.make_async_copy(source, target, sems.at[i])
        for i, (source, target) in enumerate(
            [(kspace_hbm, kspace_ref), (mask_hbm, mask_ref), (basis_hbm, basis_ref)]
        )
    ]
    for fetch in fetches:
        fetch.start()
    fetches[0].wait()
    fetches[1].wait()
    sampled_ref[...] = kspace_ref[...] * mask_ref[...].astype(jnp.float32)
    fetches[2].wait()
    turned = basis_ref[...].T
    devices = turned.shape[0] // cols
    for j in range(per_tile):
        part = turned[:, j * chg : (j + 1) * chg]
        row = jnp.concatenate([part[k * devices : (k + 1) * devices] for k in range(cols)], axis=1)
        send_ref[pl.ds(j, devices, stride=per_tile), :] = row


def images_of(vectors, samples_ref, wide_ref):
    rows, channels = vectors.shape
    cols = rows // KER
    high, low = split(vectors)
    at_row = lax.broadcasted_iota(jnp.int32, (rows, rows), 0)
    at_col = lax.broadcasted_iota(jnp.int32, (rows, rows), 1)
    flip = ((at_row // KER == at_col // KER) & (at_row % KER + at_col % KER == KER - 1)).astype(
        jnp.float32
    ).astype(jnp.bfloat16)
    both = dot(flip, jnp.concatenate([high, low], axis=1)).astype(jnp.bfloat16)
    high, low = both[:, :channels], both[:, channels:]
    twice = jnp.concatenate([high, high], axis=1)
    tiles = samples_ref.shape[0]
    tile = samples_ref.shape[-1]
    for t in range(tiles):
        block = samples_ref[t].reshape(2 * channels, tile)
        wide_ref[:, t * tile : (t + 1) * tile] = dot(twice, block) + dot(low, block[:channels])
    images = []
    for k in range(cols):
        total = None
        for i in reversed(range(0, KER, SUB)):
            part = wide_ref[k * KER + i : k * KER + i + SUB, :]
            total = part if total is None else pltpu.roll(total, SUB, 1) + part
        total = pltpu.roll(total, 0, 1, stride=1, stride_axis=0)
        images.append(jnp.sum(total, axis=0, keepdims=True))
    return images


def normal_of(images, samples_ref, moved_ref):
    cols = len(images)
    positions = images[0].shape[1]
    tiles = samples_ref.shape[0]
    tile = samples_ref.shape[-1]
    channels = samples_ref.shape[2] * samples_ref.shape[3]
    rows = cols * KER
    for k in range(cols):
        base = jnp.broadcast_to(images[k], (SUB, positions))
        base = pltpu.roll(base, positions - (KER - 1), 1, stride=1, stride_axis=0)
        for j in range(0, KER, 2 * SUB):
            first = base if j == 0 else pltpu.roll(base, j, 1)
            second = pltpu.roll(base, j + SUB, 1)
            high, low = split(jnp.concatenate([first, second], axis=0))
            moved_ref[k * KER + j : k * KER + j + 2 * SUB, :] = high
            moved_ref[rows + k * KER + j : rows + k * KER + j + 2 * SUB, :] = low
    total = jnp.zeros((2 * rows, 2 * channels), jnp.float32)
    for t in range(tiles):
        block = samples_ref[t].reshape(2 * channels, tile)
        total = total + dot(moved_ref[:, t * tile : (t + 1) * tile], block, ((1,), (1,)))
    return total[:rows, :channels] + (
        total[:rows, channels:] + total[rows:, :channels] + total[rows:, channels:]
    )


def store_by_rows(normal, send_ref, part):
    tiles, groups, _, per_tile, lanes = send_ref.shape
    cols = normal.shape[0] // KER
    chg = normal.shape[1] // groups
    for g in range(groups):
        joined = jnp.concatenate(
            [normal[k * KER : (k + 1) * KER, g * chg : (g + 1) * chg] for k in range(cols)], axis=1
        )
        send_ref[:, g, part] = joined.reshape(tiles, per_tile, lanes)


def store_by_groups(normal_ref, group_ref):
    groups, count, lanes = group_ref.shape
    rows, channels = normal_ref.shape
    chg = channels // groups
    fold = lanes // chg
    cols = rows // KER
    deep = KER // fold
    me = lax.axis_index("coil")
    parts = [
        [normal_ref[pl.ds(k * KER + f, deep, stride=fold), :] for f in range(fold)]
        for k in range(cols)
    ]
    for g in range(groups):
        joined = [
            jnp.concatenate([part[:, g * chg : (g + 1) * chg] for part in parts[k]], axis=1)
            for k in range(cols)
        ]
        group_ref[lax.bitwise_xor(me, g)] = jnp.concatenate(joined, axis=0)


def passes_kernel(orders, basis_ref, *refs):
    *pieces, samples_ref, normal_ref, send_ref, group_ref, wide_ref, moved_ref = refs
    tiles, _, groups, chg, tile = samples_ref.shape
    me = lax.axis_index("rows") * groups + lax.axis_index("coil")
    for (start, order), piece_ref in zip(orders, pieces):
        count = piece_ref.shape[1]
        for slot, mask in enumerate(order):
            high, low = split(piece_ref[slot])
            source = lax.bitwise_xor(me, mask)
            t, g = source // groups, source % groups
            samples_ref[t, 0, g, start : start + count] = high
            samples_ref[t, 1, g, start : start + count] = low
    cols = basis_ref.shape[-1] // chg
    rows = []
    for k in range(cols):
        rows.append(
            jnp.concatenate(
                [
                    basis_ref[:, g].reshape(KER, cols * chg)[:, k * chg : (k + 1) * chg]
                    for g in range(groups)
                ],
                axis=1,
            )
        )
    vectors = jnp.concatenate(rows, axis=0)
    normal = normal_of(images_of(vectors, samples_ref, wide_ref), samples_ref, moved_ref)
    scaled = []
    for k in range(cols):
        part = normal[k * KER : (k + 1) * KER]
        scaled.append(part * (1.0 / jnp.max(jnp.abs(part))))
    normal = jnp.concatenate(scaled, axis=0)
    store_by_rows(normal, send_ref, 0)
    normal = normal_of(images_of(normal, samples_ref, wide_ref), samples_ref, moved_ref)
    normal_ref[...] = normal
    store_by_rows(normal, send_ref, 1)
    store_by_groups(normal_ref, group_ref)


def images_kernel(samples_ref, vectors_ref, send_ref, wide_ref):
    tiles, groups, cols, reach = send_ref.shape
    tile = samples_ref.shape[-1]
    images = jnp.concatenate(images_of(vectors_ref[...], samples_ref, wide_ref), axis=0)
    positions = images.shape[1]
    images = pltpu.roll(images, positions - (KER - 1), 1)
    rim = reach - tile
    for t in range(tiles):
        if t == 0:
            part = jnp.concatenate([images[:, positions - rim :], images[:, :tile]], axis=1)
        else:
            part = images[:, t * tile - rim : (t + 1) * tile]
        for g in range(groups):
            send_ref[t, g] = part


def gather_turned(received_ref, cols, per_tile, part):
    count, lanes = received_ref.shape
    devices = count // (2 * per_tile)
    chg = lanes // cols
    loaded = [
        received_ref[pl.ds(part * per_tile + j, devices, stride=2 * per_tile), :]
        for j in range(per_tile)
    ]
    return jnp.concatenate(
        [
            jnp.concatenate(
                [loaded[j][:, k * chg : (k + 1) * chg] for j in range(per_tile)], axis=1
            )
            for k in range(cols)
        ],
        axis=0,
    )


def exact(a, b, dims=((1,), (0,))):
    return lax.dot_general(
        a, b, (dims, ((), ())), precision=lax.Precision.HIGHEST, preferred_element_type=jnp.float32
    )


def gram_kernel(cols, per_tile, received_ref, kept_ref, given_ref, turned_ref):
    turned = gather_turned(received_ref, cols, per_tile, 0)
    first = exact(turned, turned, ((1,), (1,)))
    turned = gather_turned(received_ref, cols, per_tile, 1)
    second = exact(turned, turned, ((1,), (1,)))
    turned_ref[...] = turned
    at_row, at_col = square(first.shape[0])
    packed = jnp.where(at_row >= at_col, first, second)
    line = jnp.sum(jnp.where(at_row == at_col, second, 0.0), axis=0, keepdims=True)
    line = jnp.broadcast_to(line, (SUB, line.shape[1]))
    half = packed.shape[0] // 2
    odd = lax.axis_index("coil") % 2 == 1
    kept_ref[:half] = jnp.where(odd, packed[half:], packed[:half])
    given_ref[:half] = jnp.where(odd, packed[:half], packed[half:])
    kept_ref[half:] = line
    given_ref[half:] = line


def load_grams(kept_ref, other_ref):
    odd = lax.axis_index("coil") % 2 == 1
    kept, other = kept_ref[...], other_ref[...]
    low, high = jnp.where(odd, other, kept), jnp.where(odd, kept, other)
    half = low.shape[0] - SUB
    packed = jnp.concatenate([low[:half], high[:half]], axis=0)
    line = low[half : half + 1]
    at_row, at_col = square(packed.shape[0])
    turned = packed.T
    first = jnp.where(at_row >= at_col, packed, turned)
    second = jnp.where(at_row > at_col, turned, packed)
    return first, jnp.where(at_row == at_col, line, second), line


def inverse_factor(gram):
    size = gram.shape[0]
    shape = (SUB, size)
    at_row = lax.broadcasted_iota(jnp.int32, (size, size), 0)
    at_col = lax.broadcasted_iota(jnp.int32, (size, size), 1)
    unit = (at_row == at_col).astype(jnp.float32)
    left = [gram[b : b + SUB] for b in range(0, size, SUB)]
    right = [unit[b : b + SUB] for b in range(0, size, SUB)]
    sub = lax.broadcasted_iota(jnp.int32, shape, 0)
    done = []
    for b in range(len(left)):
        spread = {
            c: [
                jnp.broadcast_to(left[c][:, b * SUB + k : b * SUB + k + 1], shape)
                for k in range(SUB)
            ]
            for c in range(b, len(left))
        }
        entry = {
            (i, k): jnp.broadcast_to(spread[b][k][i : i + 1], shape)
            for k in range(SUB)
            for i in range(k, SUB)
        }
        inverse = {}
        for k in range(SUB):
            root = lax.rsqrt(entry[k, k])
            root = root * (1.5 - (0.5 * entry[k, k]) * (root * root))
            inverse[k, k] = root
            for i in range(k + 1, SUB):
                entry[i, k] = entry[i, k] * root
            for i in range(k + 1, SUB):
                for m in range(k + 1, i + 1):
                    entry[i, m] = entry[i, m] - entry[i, k] * entry[m, k]
        for i in range(1, SUB):
            for k in range(i):
                total = entry[i, k] * inverse[k, k]
                for m in range(k + 1, i):
                    total = total + entry[i, m] * inverse[m, k]
                inverse[i, k] = -(total * inverse[i, i])

        def solved(rows):
            whole = [jnp.broadcast_to(rows[k : k + 1], shape) for k in range(SUB)]
            first = []
            for i in range(SUB):
                total = inverse[i, 0] * whole[0]
                for k in range(1, i + 1):
                    total = total + inverse[i, k] * whole[k]
                first.append(total)
            second = []
            for k in range(SUB):
                total = inverse[k, k] * first[k]
                for i in range(k + 1, SUB):
                    total = total + inverse[i, k] * first[i]
                second.append(total)
            return first, second

        lower, lower_again = solved(right[b])
        row = lower[0]
        for i in range(1, SUB):
            row = jnp.where(sub == i, lower[i], row)
        done.append(row)
        if b + 1 < len(left):
            _, upper_again = solved(left[b])
            for c in range(b + 1, len(left)):
                for k in range(SUB):
                    left[c] = left[c] - spread[c][k] * upper_again[k]
                    right[c] = right[c] - spread[c][k] * lower_again[k]
    return jnp.concatenate(done, axis=0)


def factor_kernel(gram_ref, other_ref, inverse_ref, next_ref, sound_ref):
    gram, raw, line = load_grams(gram_ref, other_ref)
    inverse = inverse_factor(gram)
    inverse_ref[...] = inverse
    gram = exact(exact(inverse, raw), inverse, ((1,), (1,)))
    next_ref[...] = gram
    at_row, at_col = square(gram.shape[0])
    terms = jnp.sum(inverse * inverse * line, axis=1, keepdims=True)
    result = jnp.sum(jnp.where(at_row == at_col, gram, 0.0), axis=1, keepdims=True)
    worst = jnp.max(jnp.where(terms <= 64.0 * result, 0, 1))
    sound_ref[0] = 1 - worst


def rows_kernel(turned_ref, inverse_ref, gram_ref):
    turned = exact(inverse_ref[...], turned_ref[...])
    gram_ref[...] = exact(turned, turned, ((1,), (1,)))


def both_kernel(gram_ref, inverse_ref, both_ref):
    both_ref[...] = exact(inverse_factor(gram_ref[...]), inverse_ref[...])


def moved_columns(values, order):
    devices = len(order[0])
    at_row, at_col = square(values.shape[0])
    me = lax.axis_index("rows") * lax.axis_size("coil") + lax.axis_index("coil")
    slot = at_col % devices
    mask = jnp.zeros_like(slot)
    bit = 1
    while bit < devices:
        step = jnp.where(2 * at_col < at_col.shape[1], order[0][bit], order[1][bit])
        mask = mask | jnp.where(slot & bit != 0, step, 0)
        bit *= 2
    source = at_col - slot + lax.bitwise_xor(mask, jnp.full_like(mask, me))
    return exact(values, (at_row == source).astype(jnp.float32))


def last_kernel(
    cols,
    order,
    images_ref,
    both_ref,
    kspace_hbm,
    mask_hbm,
    top_near_ref,
    top_far_ref,
    low_near_ref,
    low_far_ref,
    recovered_ref,
    basis_ref,
    kspace_ref,
    mask_ref,
    vectors_ref,
    sems,
):
    fetches = [
        pltpu.make_async_copy(kspace_hbm, kspace_ref, sems.at[0]),
        pltpu.make_async_copy(mask_hbm, mask_ref, sems.at[1]),
    ]
    for fetch in fetches:
        fetch.start()
    both = both_ref[...]
    count, reach = images_ref.shape
    devices = count // cols
    at_row, at_col = square(count)
    turn = ((at_row // devices == at_col % cols) & (at_row % devices == at_col // cols)).astype(
        jnp.float32
    )
    images = exact(exact(both, turn), images_ref[...])
    images_high, images_low = split(images)
    stacked = jnp.concatenate([images_high, images_low], axis=0)
    chg, tile = kspace_ref.shape
    lanes = top_near_ref.shape[1]
    deep = KER * chg // lanes
    step = cols // 2 * deep
    factor = moved_columns(both, order)
    estimate = jnp.zeros((chg, reach), jnp.float32)
    for a in range(0, deep, 2):
        turned = [
            jnp.concatenate(
                [
                    ref[pl.ds(k * deep + a + i, ref.shape[0] // step, stride=step), :]
                    for refs in ((top_near_ref, top_far_ref), (low_near_ref, low_far_ref))
                    for k in range(cols // 2)
                    for ref in refs
                ],
                axis=0,
            )
            for i in range(2)
        ]
        vectors = dot3(jnp.concatenate(turned, axis=1), factor, ((0,), (1,)))
        vectors_ref[a * lanes : (a + 2) * lanes, :] = vectors
        high, low = split(vectors)
        projected = dot(jnp.concatenate([high, high], axis=1), stacked) + dot(low, images_high)
        for i in range(2 * lanes // chg):
            j = a * lanes // chg + i
            part = projected[i * chg : (i + 1) * chg]
            estimate = estimate + (pltpu.roll(part, j, 1) if j else part)
    owned = basis_ref.shape[0]
    start = pl.multiple_of(lax.axis_index("rows") * owned, owned)
    basis_ref[...] = vectors_ref[pl.ds(start, owned), :]
    estimate = estimate[:, reach - tile :]
    for fetch in fetches:
        fetch.wait()
    estimate = estimate / KER
    residual = mask_ref[...].astype(jnp.float32) * (kspace_ref[...] - estimate)
    recovered_ref[...] = estimate + residual - jnp.clip(residual, -threshold, threshold)


def call(kernel, outs, *args, scratch=(), far=(), limit=40, scalars=0, micros=1):
    return pl.pallas_call(
        kernel,
        out_shape=[jax.ShapeDtypeStruct(shape, kind) for shape, kind in outs],
        in_specs=[
            pl.BlockSpec(memory_space=pltpu.HBM if i in far else pltpu.VMEM)
            for i in range(len(args))
        ],
        out_specs=[pl.BlockSpec(memory_space=pltpu.VMEM)] * (len(outs) - scalars)
        + [pl.BlockSpec(memory_space=pltpu.SMEM)] * scalars,
        scratch_shapes=list(scratch),
        compiler_params=pltpu.CompilerParams(vmem_limit_bytes=limit * 2**20),
        cost_estimate=pl.CostEstimate(
            flops=micros * 10**9, bytes_accessed=0, transcendentals=0
        ),
    )(*args)


def exchange(block, devices, mask, axes):
    return lax.ppermute(block, axes, [(i, i ^ mask) for i in range(devices)])


def with_masks(masks, mask):
    return masks + [m ^ mask for m in masks]


def after(value, *others):
    return lax.optimization_barrier((value,) + others)[0]


def rounds_of(low, high):
    masks = []
    while low < high:
        if 2 * low < high:
            masks.append([low, 2 * low, 3 * low])
        else:
            masks.append([low])
        low *= 4
    return masks


def gather_round(part, order, masks, devices, axes):
    part = jnp.concatenate(
        [part] + [exchange(part, devices, mask, axes) for mask in masks], axis=0
    )
    return part, order + [m ^ mask for mask in masks for m in order]


def gather_samples(sampled, tiles, groups, beside):
    devices = tiles * groups
    first = devices // 2
    near = sampled[None]
    streams = [(near, [0]), (exchange(near, devices, first, AXES), [first])]
    halves = [[], []]
    for number, (near, masks) in enumerate(streams):
        mask = first // 2
        while mask > groups:
            near, masks = gather_round(near, masks, [mask], devices, AXES)
            mask //= 2
        if number:
            near = after(near, beside)
        half = near.shape[1] // 2
        for i, (part, ways) in enumerate(
            (
                (near[:, :half], (groups, groups // 2)),
                (near[:, half:], (groups // 2, groups)),
            )
        ):
            pieces = [gather_round(part, masks, [ways[0]], devices, AXES)]
            mask = ways[1]
            rest = groups // 4
            while mask:
                pieces = pieces + [
                    (exchange(part, devices, mask, AXES), [m ^ mask for m in order])
                    for part, order in pieces
                ]
                mask, rest = rest, rest // 2
            halves[i] += pieces
    return halves


def to_all(pieces, axes=AXES):
    return lax.all_to_all(pieces, axes, 0, 0, tiled=True)


def gather_group(group, devices):
    groups = group.shape[0]
    parts = [group[:1]]
    parts += [exchange(group[s : s + 1], devices, s, AXES) for s in range(1, groups)]
    return jnp.concatenate(parts, axis=0), list(range(groups))


def total_beside(kept, given, near, order, images, groups, devices):
    ways = []
    mask = devices // 2
    while mask >= groups:
        ways.append(mask)
        mask //= 2
    half = near.shape[1] // 2
    parts = [near[:, :half], near[:, half:]]
    orders = [order, order]
    ways = [ways, ways[-1:] + ways[:-1]]
    step = 0

    def advance():
        for i in range(2):
            parts[i], orders[i] = gather_round(
                parts[i], orders[i], [ways[i][step]], devices, AXES
            )

    total = kept + exchange(given, devices, 1, AXES)
    for partners in rounds_of(2, devices):
        terms = [exchange(total, devices, way, AXES) for way in partners]
        total = total + terms[0]
        if len(terms) == 3:
            total = total + (terms[1] + terms[2])
        if step < len(ways[0]) - 1:
            advance()
            step += 1
    while step < len(ways[0]) - 1:
        advance()
        step += 1
    other = exchange(total, devices, 1, AXES)
    *parts, total, other, images = lax.optimization_barrier((*parts, total, other, images))
    pieces = []
    for i in range(2):
        mask = ways[i][-1]
        pieces += [parts[i], exchange(parts[i], devices, mask, AXES)]
        orders[i] = orders[i] + [m ^ mask for m in orders[i]]
    return (total, other), pieces, orders, to_all(images)


def column_shards(kspace, sample_mask, start_basis):
    f32, bf16 = jnp.float32, jnp.bfloat16
    tiles, groups = lax.axis_size("rows"), lax.axis_size("coil")
    devices = tiles * groups
    chg, tile = kspace.shape
    channels = chg * groups
    positions = tile * tiles
    owned, rank = start_basis.shape[1:]
    per_tile = owned // chg
    cols = rank // devices
    rows = cols * KER
    lanes = cols * chg

    sampled, basis_send = call(
        functools.partial(prepare_kernel, cols, chg, per_tile),
        [((chg, tile), f32), ((devices * per_tile, lanes), f32)],
        kspace,
        sample_mask,
        start_basis.reshape(owned, rank),
        scratch=[
            pltpu.VMEM((chg, tile), f32),
            pltpu.VMEM((chg, tile), sample_mask.dtype),
            pltpu.VMEM((owned, rank), f32),
            pltpu.SemaphoreType.DMA((3,)),
        ],
        far=(0, 1, 2),
        limit=60,
    )
    basis_parts = to_all(basis_send.reshape(devices, per_tile, lanes))
    halves = gather_samples(sampled, tiles, groups, basis_parts)
    starts = (0, chg // len(halves))
    orders = [(start, order) for start, half in zip(starts, halves) for _, order in half]
    wide = pltpu.VMEM((rows, positions), f32)
    moved = pltpu.VMEM((2 * rows, positions), bf16)
    samples, normal, send, group = call(
        functools.partial(passes_kernel, orders),
        [
            ((tiles, 2, groups, chg, tile), bf16),
            ((rows, channels), f32),
            ((tiles, groups, 2, per_tile, lanes), f32),
            ((groups, rows * chg // lanes, lanes), f32),
        ],
        basis_parts.reshape(tiles, groups, per_tile, lanes),
        *[piece for half in halves for piece, _ in half],
        scratch=[wide, moved],
        micros=12,
    )
    received = to_all(send.reshape(devices, 2 * per_tile, lanes))
    reach = tile + LANES
    (images,) = call(
        images_kernel,
        [((tiles, groups, cols, reach), f32)],
        samples,
        normal,
        scratch=[wide],
        micros=2,
    )
    near, order = gather_group(group, devices)
    received, near = lax.optimization_barrier((received, images, near))[::2]
    half = ((rank // 2 + SUB, rank), f32)
    kept, given, turned = call(
        functools.partial(gram_kernel, cols, per_tile),
        [half, half, ((rank, owned), f32)],
        received.reshape(devices * 2 * per_tile, lanes),
    )
    gram, pieces, order, images = total_beside(
        kept, given, near, order, images.reshape(devices, cols, reach), groups, devices
    )
    whole = ((rank, rank), f32)
    first, second, sound = call(
        factor_kernel, [whole, whole, ((1,), jnp.int32)], *gram, scalars=1, micros=12
    )

    def again():
        (gram,) = call(rows_kernel, [whole], turned, first)
        mask = 1
        while mask < devices:
            gram = gram + exchange(gram, devices, mask, AXES)
            mask *= 2
        return gram

    second = lax.cond(sound[0] == 1, lambda: second, again)
    (both,) = call(both_kernel, [whole], second, first, micros=0)
    recovered, basis = call(
        functools.partial(last_kernel, cols, order),
        [((chg, tile), f32), ((owned, rank), f32)],
        images.reshape(rank, reach),
        both,
        kspace,
        sample_mask,
        *[piece.reshape(-1, lanes) for piece in pieces],
        scratch=[
            pltpu.VMEM((chg, tile), f32),
            pltpu.VMEM((chg, tile), sample_mask.dtype),
            pltpu.VMEM((KER * chg, rank), f32),
            pltpu.SemaphoreType.DMA((2,)),
        ],
        far=(2, 3),
        limit=40,
        micros=5,
    )
    return (recovered, basis.reshape(1, owned, rank))


def divides_columns(kspace, start_basis):
    tiles, groups = lax.axis_size("rows"), lax.axis_size("coil")
    devices = tiles * groups
    chg, tile = kspace.shape
    owned, rank = start_basis.shape[1:]
    return (
        devices & (devices - 1) == 0
        and tiles > 2
        and groups > 2
        and rank % (2 * SUB) == 0
        and rank % devices == 0
        and rank % LANES == 0
        and tile % LANES == 0
        and owned == SUB * chg
        and chg * (rank // devices) == LANES
        and chg % (4 * SUB) == 0
        and (chg * groups) % LANES == 0
        and KER <= LANES
        and rank // devices <= SUB
        and rank // devices % 2 == 0
    )


def shards(kspace, sample_mask, start_basis):
    if divides_columns(kspace, start_basis):
        return column_shards(kspace, sample_mask, start_basis)
    return general_shards(kspace, sample_mask, start_basis)


def solution(mesh):
    return jax.shard_map(
        shards,
        mesh=mesh,
        in_specs=(P("coil", "rows"), P("coil", "rows"), P("coil", "rows", None)),
        out_specs=(P("coil", "rows"), P("coil", "rows", None)),
        check_vma=False,
    )
```

```python
import functools

import jax
import jax.numpy as jnp
from jax import lax
from jax.experimental import pallas as pl
from jax.experimental.pallas import tpu as pltpu
from jax.sharding import PartitionSpec as P

KER = 64
ITERS = 2
LANES = 128
SUB = 8
AXES = ("rows", "coil")


threshold = 0.05


def shifted(block, axis, distance):
    devices = range(lax.axis_size(axis))
    route = [((i - distance) % len(devices), i) for i in devices]
    return lax.ppermute(block, axis, route)


def orthonormal(normal_rows, gram_matrix):
    factor = jnp.linalg.cholesky(gram_matrix)
    return lax.linalg.triangular_solve(
        factor, normal_rows, left_side=False, lower=True, transpose_a=True
    )


def coil_total(partial_value):
    return lax.psum(partial_value, "coil")


def general_shards(kspace, sample_mask, start_basis):
    highest = lax.Precision.HIGHEST
    channels = kspace.shape[0]
    tile_rows = kspace.shape[1]
    mask_float = sample_mask.astype(jnp.float32)
    sampled = kspace * mask_float
    next_rim = shifted(sampled[:, : KER - 1], "rows", -1)
    extended = jnp.concatenate([sampled, next_rim], axis=1)
    hankel_cols = jnp.stack(
        [extended[:, offset : offset + tile_rows] for offset in range(KER)], axis=0
    )
    hankel_cols = hankel_cols.reshape(KER * channels, tile_rows)
    owned_basis = start_basis.reshape(start_basis.shape[1], start_basis.shape[2])
    whole_basis = lax.all_gather(owned_basis, "rows", axis=0, tiled=True)
    for iteration in range(ITERS):
        images = coil_total(
            lax.dot_general(
                whole_basis,
                hankel_cols,
                (((0,), (0,)), ((), ())),
                precision=highest,
                preferred_element_type=jnp.float32,
            )
        )
        local_normal = lax.dot_general(
            hankel_cols,
            images,
            (((1,), (1,)), ((), ())),
            precision=highest,
            preferred_element_type=jnp.float32,
        )
        normal_whole = lax.psum(local_normal, "rows")
        local_gram = jnp.dot(
            normal_whole.T, normal_whole, precision=highest, preferred_element_type=jnp.float32
        )
        gram_matrix = lax.psum(local_gram, "coil")
        whole_basis = orthonormal(normal_whole, gram_matrix)
    images = coil_total(
        lax.dot_general(
            whole_basis,
            hankel_cols,
            (((0,), (0,)), ((), ())),
            precision=highest,
            preferred_element_type=jnp.float32,
        )
    )
    projected = jnp.dot(whole_basis, images, precision=highest, preferred_element_type=jnp.float32)
    owned_count = whole_basis.shape[0] // lax.axis_size("rows")
    owned_basis = lax.dynamic_slice_in_dim(
        whole_basis, lax.axis_index("rows") * owned_count, owned_count, 0
    )
    stacked = projected.reshape(KER, channels, tile_rows)
    spread = jnp.zeros((channels, tile_rows + KER - 1), jnp.float32)
    for offset in range(KER):
        spread = spread.at[:, offset : offset + tile_rows].add(stacked[offset])
    carried = shifted(spread[:, tile_rows:], "rows", 1)
    estimate = spread[:, :tile_rows].at[:, : KER - 1].add(carried) / KER
    residual = mask_float * (kspace - estimate)
    recovered = estimate + residual - jnp.clip(residual, -threshold, threshold)
    return (recovered, owned_basis.reshape(1, owned_basis.shape[0], owned_basis.shape[1]))


def split(value):
    high = value.astype(jnp.bfloat16)
    low = (value - high.astype(jnp.float32)).astype(jnp.bfloat16)
    return high, low


def dot(a, b, dims=((1,), (0,))):
    return lax.dot_general(a, b, (dims, ((), ())), preferred_element_type=jnp.float32)


def dot3(a, b, dims=((1,), (0,))):
    a_high, a_low = split(a)
    b_high, b_low = split(b)
    return dot(a_high, b_high, dims) + (dot(a_high, b_low, dims) + dot(a_low, b_high, dims))


def square(size):
    at_row = lax.broadcasted_iota(jnp.int32, (size, size), 0)
    at_col = lax.broadcasted_iota(jnp.int32, (size, size), 1)
    return at_row, at_col


def prepare_kernel(
    cols,
    chg,
    per_tile,
    kspace_hbm,
    mask_hbm,
    basis_hbm,
    sampled_ref,
    send_ref,
    kspace_ref,
    mask_ref,
    basis_ref,
    sems,
):
    fetches = [
        pltpu.make_async_copy(source, target, sems.at[i])
        for i, (source, target) in enumerate(
            [(kspace_hbm, kspace_ref), (mask_hbm, mask_ref), (basis_hbm, basis_ref)]
        )
    ]
    for fetch in fetches:
        fetch.start()
    fetches[0].wait()
    fetches[1].wait()
    sampled_ref[...] = kspace_ref[...] * mask_ref[...].astype(jnp.float32)
    fetches[2].wait()
    turned = basis_ref[...].T
    devices = turned.shape[0] // cols
    for j in range(per_tile):
        part = turned[:, j * chg : (j + 1) * chg]
        row = jnp.concatenate([part[k * devices : (k + 1) * devices] for k in range(cols)], axis=1)
        send_ref[pl.ds(j, devices, stride=per_tile), :] = row


def images_of(vectors, samples_ref, wide_ref):
    rows, channels = vectors.shape
    cols = rows // KER
    high, low = split(vectors)
    at_row = lax.broadcasted_iota(jnp.int32, (rows, rows), 0)
    at_col = lax.broadcasted_iota(jnp.int32, (rows, rows), 1)
    flip = ((at_row // KER == at_col // KER) & (at_row % KER + at_col % KER == KER - 1)).astype(
        jnp.float32
    ).astype(jnp.bfloat16)
    both = dot(flip, jnp.concatenate([high, low], axis=1)).astype(jnp.bfloat16)
    high, low = both[:, :channels], both[:, channels:]
    zero = jnp.zeros_like(low)
    both = jnp.concatenate(
        [jnp.concatenate([high, high], axis=1), jnp.concatenate([low, zero], axis=1)], axis=0
    )
    tiles = samples_ref.shape[0]
    tile = samples_ref.shape[-1]
    for t in range(tiles):
        wide = dot(both, samples_ref[t].reshape(2 * channels, tile))
        wide_ref[:, t * tile : (t + 1) * tile] = wide[:rows] + wide[rows:]
    images = []
    for k in range(cols):
        total = None
        for i in reversed(range(0, KER, SUB)):
            part = wide_ref[k * KER + i : k * KER + i + SUB, :]
            total = part if total is None else pltpu.roll(total, SUB, 1) + part
        total = pltpu.roll(total, 0, 1, stride=1, stride_axis=0)
        images.append(jnp.sum(total, axis=0, keepdims=True))
    return images


def normal_of(images, samples_ref, moved_ref):
    cols = len(images)
    positions = images[0].shape[1]
    tiles = samples_ref.shape[0]
    tile = samples_ref.shape[-1]
    channels = samples_ref.shape[2] * samples_ref.shape[3]
    rows = cols * KER
    for k in range(cols):
        base = jnp.broadcast_to(images[k], (SUB, positions))
        base = pltpu.roll(base, positions - (KER - 1), 1, stride=1, stride_axis=0)
        for j in range(0, KER, 2 * SUB):
            first = base if j == 0 else pltpu.roll(base, j, 1)
            second = pltpu.roll(base, j + SUB, 1)
            high, low = split(jnp.concatenate([first, second], axis=0))
            moved_ref[k * KER + j : k * KER + j + 2 * SUB, :] = high
            moved_ref[rows + k * KER + j : rows + k * KER + j + 2 * SUB, :] = low
    total = jnp.zeros((2 * rows, 2 * channels), jnp.float32)
    for t in range(tiles):
        block = samples_ref[t].reshape(2 * channels, tile)
        total = total + dot(moved_ref[:, t * tile : (t + 1) * tile], block, ((1,), (1,)))
    return total[:rows, :channels] + (
        total[:rows, channels:] + total[rows:, :channels] + total[rows:, channels:]
    )


def store_by_rows(normal, send_ref, part):
    tiles, groups, _, per_tile, lanes = send_ref.shape
    cols = normal.shape[0] // KER
    chg = normal.shape[1] // groups
    for g in range(groups):
        joined = jnp.concatenate(
            [normal[k * KER : (k + 1) * KER, g * chg : (g + 1) * chg] for k in range(cols)], axis=1
        )
        send_ref[:, g, part] = joined.reshape(tiles, per_tile, lanes)


def store_by_groups(normal_ref, group_ref):
    groups, count, lanes = group_ref.shape
    rows, channels = normal_ref.shape
    chg = channels // groups
    fold = lanes // chg
    cols = rows // KER
    deep = KER // fold
    me = lax.axis_index("coil")
    parts = [
        [normal_ref[pl.ds(k * KER + f, deep, stride=fold), :] for f in range(fold)]
        for k in range(cols)
    ]
    for g in range(groups):
        joined = [
            jnp.concatenate([part[:, g * chg : (g + 1) * chg] for part in parts[k]], axis=1)
            for k in range(cols)
        ]
        group_ref[lax.bitwise_xor(me, g)] = jnp.concatenate(joined, axis=0)


def passes_kernel(orders, basis_ref, *refs):
    *pieces, samples_ref, normal_ref, send_ref, group_ref, wide_ref, moved_ref = refs
    tiles, _, groups, chg, tile = samples_ref.shape
    me = lax.axis_index("rows") * groups + lax.axis_index("coil")
    for (start, order), piece_ref in zip(orders, pieces):
        count = piece_ref.shape[1]
        for slot, mask in enumerate(order):
            high, low = split(piece_ref[slot])
            source = lax.bitwise_xor(me, mask)
            t, g = source // groups, source % groups
            samples_ref[t, 0, g, start : start + count] = high
            samples_ref[t, 1, g, start : start + count] = low
    cols = basis_ref.shape[-1] // chg
    rows = []
    for k in range(cols):
        rows.append(
            jnp.concatenate(
                [
                    basis_ref[:, g].reshape(KER, cols * chg)[:, k * chg : (k + 1) * chg]
                    for g in range(groups)
                ],
                axis=1,
            )
        )
    vectors = jnp.concatenate(rows, axis=0)
    normal = normal_of(images_of(vectors, samples_ref, wide_ref), samples_ref, moved_ref)
    scaled = []
    for k in range(cols):
        part = normal[k * KER : (k + 1) * KER]
        scaled.append(part * (1.0 / jnp.max(jnp.abs(part))))
    normal = jnp.concatenate(scaled, axis=0)
    store_by_rows(normal, send_ref, 0)
    normal = normal_of(images_of(normal, samples_ref, wide_ref), samples_ref, moved_ref)
    normal_ref[...] = normal
    store_by_rows(normal, send_ref, 1)
    store_by_groups(normal_ref, group_ref)


def images_kernel(samples_ref, vectors_ref, send_ref, wide_ref):
    tiles, groups, cols, reach = send_ref.shape
    tile = samples_ref.shape[-1]
    images = jnp.concatenate(images_of(vectors_ref[...], samples_ref, wide_ref), axis=0)
    positions = images.shape[1]
    images = pltpu.roll(images, positions - (KER - 1), 1)
    rim = reach - tile
    for t in range(tiles):
        if t == 0:
            part = jnp.concatenate([images[:, positions - rim :], images[:, :tile]], axis=1)
        else:
            part = images[:, t * tile - rim : (t + 1) * tile]
        for g in range(groups):
            send_ref[t, g] = part


def gather_turned(received_ref, cols, per_tile, part):
    count, lanes = received_ref.shape
    devices = count // (2 * per_tile)
    chg = lanes // cols
    loaded = [
        received_ref[pl.ds(part * per_tile + j, devices, stride=2 * per_tile), :]
        for j in range(per_tile)
    ]
    return jnp.concatenate(
        [
            jnp.concatenate(
                [loaded[j][:, k * chg : (k + 1) * chg] for j in range(per_tile)], axis=1
            )
            for k in range(cols)
        ],
        axis=0,
    )


def exact(a, b, dims=((1,), (0,))):
    return lax.dot_general(
        a, b, (dims, ((), ())), precision=lax.Precision.HIGHEST, preferred_element_type=jnp.float32
    )


def gram_kernel(cols, per_tile, received_ref, kept_ref, given_ref, turned_ref):
    turned = gather_turned(received_ref, cols, per_tile, 0)
    first = exact(turned, turned, ((1,), (1,)))
    turned = gather_turned(received_ref, cols, per_tile, 1)
    second = exact(turned, turned, ((1,), (1,)))
    turned_ref[...] = turned
    at_row, at_col = square(first.shape[0])
    packed = jnp.where(at_row >= at_col, first, second)
    line = jnp.sum(jnp.where(at_row == at_col, second, 0.0), axis=0, keepdims=True)
    line = jnp.broadcast_to(line, (SUB, line.shape[1]))
    half = packed.shape[0] // 2
    odd = lax.axis_index("coil") % 2 == 1
    kept_ref[:half] = jnp.where(odd, packed[half:], packed[:half])
    given_ref[:half] = jnp.where(odd, packed[:half], packed[half:])
    kept_ref[half:] = line
    given_ref[half:] = line


def load_grams(kept_ref, other_ref):
    odd = lax.axis_index("coil") % 2 == 1
    kept, other = kept_ref[...], other_ref[...]
    low, high = jnp.where(odd, other, kept), jnp.where(odd, kept, other)
    half = low.shape[0] - SUB
    packed = jnp.concatenate([low[:half], high[:half]], axis=0)
    line = low[half : half + 1]
    at_row, at_col = square(packed.shape[0])
    turned = packed.T
    first = jnp.where(at_row >= at_col, packed, turned)
    second = jnp.where(at_row > at_col, turned, packed)
    return first, jnp.where(at_row == at_col, line, second), line


def inverse_factor(gram):
    size = gram.shape[0]
    shape = (SUB, size)
    at_row = lax.broadcasted_iota(jnp.int32, (size, size), 0)
    at_col = lax.broadcasted_iota(jnp.int32, (size, size), 1)
    unit = (at_row == at_col).astype(jnp.float32)
    left = [gram[b : b + SUB] for b in range(0, size, SUB)]
    right = [unit[b : b + SUB] for b in range(0, size, SUB)]
    sub = lax.broadcasted_iota(jnp.int32, shape, 0)
    done = []
    for b in range(len(left)):
        spread = {
            c: [
                jnp.broadcast_to(left[c][:, b * SUB + k : b * SUB + k + 1], shape)
                for k in range(SUB)
            ]
            for c in range(b, len(left))
        }
        entry = {
            (i, k): jnp.broadcast_to(spread[b][k][i : i + 1], shape)
            for k in range(SUB)
            for i in range(k, SUB)
        }
        inverse = {}
        for k in range(SUB):
            root = lax.rsqrt(entry[k, k])
            inverse[k, k] = root
            for i in range(k + 1, SUB):
                entry[i, k] = entry[i, k] * root
            for i in range(k + 1, SUB):
                for m in range(k + 1, i + 1):
                    entry[i, m] = entry[i, m] - entry[i, k] * entry[m, k]
        for i in range(1, SUB):
            for k in range(i):
                total = entry[i, k] * inverse[k, k]
                for m in range(k + 1, i):
                    total = total + entry[i, m] * inverse[m, k]
                inverse[i, k] = -(total * inverse[i, i])

        def solved(rows):
            whole = [jnp.broadcast_to(rows[k : k + 1], shape) for k in range(SUB)]
            first = []
            for i in range(SUB):
                total = inverse[i, 0] * whole[0]
                for k in range(1, i + 1):
                    total = total + inverse[i, k] * whole[k]
                first.append(total)
            second = []
            for k in range(SUB):
                total = inverse[k, k] * first[k]
                for i in range(k + 1, SUB):
                    total = total + inverse[i, k] * first[i]
                second.append(total)
            return first, second

        lower, lower_again = solved(right[b])
        row = lower[0]
        for i in range(1, SUB):
            row = jnp.where(sub == i, lower[i], row)
        done.append(row)
        if b + 1 < len(left):
            _, upper_again = solved(left[b])
            for c in range(b + 1, len(left)):
                for k in range(SUB):
                    left[c] = left[c] - spread[c][k] * upper_again[k]
                    right[c] = right[c] - spread[c][k] * lower_again[k]
    return jnp.concatenate(done, axis=0)


def factor_kernel(gram_ref, other_ref, inverse_ref, next_ref, sound_ref):
    gram, raw, line = load_grams(gram_ref, other_ref)
    inverse = inverse_factor(gram)
    inverse_ref[...] = inverse
    gram = exact(exact(inverse, raw), inverse, ((1,), (1,)))
    next_ref[...] = gram
    at_row, at_col = square(gram.shape[0])
    terms = jnp.sum(inverse * inverse * line, axis=1, keepdims=True)
    result = jnp.sum(jnp.where(at_row == at_col, gram, 0.0), axis=1, keepdims=True)
    worst = jnp.max(jnp.where(terms <= 64.0 * result, 0, 1))
    sound_ref[0] = 1 - worst


def rows_kernel(turned_ref, inverse_ref, gram_ref):
    turned = exact(inverse_ref[...], turned_ref[...])
    gram_ref[...] = exact(turned, turned, ((1,), (1,)))


def both_kernel(gram_ref, inverse_ref, both_ref):
    both_ref[...] = exact(inverse_factor(gram_ref[...]), inverse_ref[...])


def moved_columns(order, cols):
    devices = len(order[0])
    at_row, at_col = square(devices * cols)
    turn = at_col % cols * devices + at_col // cols
    me = lax.axis_index("rows") * lax.axis_size("coil") + lax.axis_index("coil")
    slot = at_col % devices
    mask = jnp.zeros_like(slot)
    bit = 1
    while bit < devices:
        step = jnp.where(2 * at_col < at_col.shape[1], order[0][bit], order[1][bit])
        mask = mask | jnp.where(slot & bit != 0, step, 0)
        bit *= 2
    source = at_col - slot + lax.bitwise_xor(mask, jnp.full_like(mask, me))
    return [(at_row == place).astype(jnp.float32) for place in (turn, source)]


def stacked_dot(a, b):
    a_high, a_low = split(a)
    b_high, b_low = split(b)
    left = jnp.concatenate(
        [
            jnp.concatenate([a_high, a_high], axis=1),
            jnp.concatenate([a_low, jnp.zeros_like(a_low)], axis=1),
        ],
        axis=0,
    )
    both = dot(left, jnp.concatenate([b_high, b_low], axis=0))
    return both[: a.shape[0]] + both[a.shape[0] :]


def last_kernel(
    cols,
    order,
    images_ref,
    both_ref,
    kspace_hbm,
    mask_hbm,
    top_near_ref,
    top_far_ref,
    low_near_ref,
    low_far_ref,
    recovered_ref,
    basis_ref,
    kspace_ref,
    mask_ref,
    vectors_ref,
    sems,
):
    fetches = [
        pltpu.make_async_copy(kspace_hbm, kspace_ref, sems.at[0]),
        pltpu.make_async_copy(mask_hbm, mask_ref, sems.at[1]),
    ]
    for fetch in fetches:
        fetch.start()
    both = both_ref[...]
    reach = images_ref.shape[1]
    factors = [exact(both, moved) for moved in moved_columns(order, cols)]
    chg, tile = kspace_ref.shape
    lanes = top_near_ref.shape[1]
    fold = lanes // chg
    deep = KER // fold
    step = cols // 2 * deep
    lead = reach - tile - KER - 2 * SUB
    images = stacked_dot(factors[0], images_ref[...]).T[lead:]
    rim = reach - tile - SUB - lead
    even, odd = None, None
    for a in range(0, deep, 2):
        turned = [
            jnp.concatenate(
                [
                    ref[pl.ds(k * deep + a + i, ref.shape[0] // step, stride=step), :]
                    for refs in ((top_near_ref, top_far_ref), (low_near_ref, low_far_ref))
                    for k in range(cols // 2)
                    for ref in refs
                ],
                axis=0,
            )
            for i in range(2)
        ]
        vectors = stacked_dot(factors[1], jnp.concatenate(turned, axis=1))
        vectors_ref[:, a * lanes : (a + 2) * lanes] = vectors
        projected = stacked_dot(images, vectors)
        shift = a * fold
        part = projected[rim - shift : rim - shift + tile + SUB, :lanes]
        even = part if even is None else even + part
        part = projected[rim - SUB - shift : rim - shift + tile + SUB, lanes:]
        odd = part if odd is None else odd + part
    total = even + odd[SUB - fold : SUB - fold + tile + SUB]
    estimate = total[SUB : SUB + tile]
    for f in range(1, fold):
        moved = pltpu.roll(total, lanes - f * chg, 1)
        estimate = estimate + moved[SUB - f : SUB - f + tile]
    estimate = estimate.T[:chg]
    owned = basis_ref.shape[0]
    start = pl.multiple_of(lax.axis_index("rows") * owned, owned)
    basis_ref[...] = vectors_ref[:, pl.ds(start, owned)].T
    for fetch in fetches:
        fetch.wait()
    estimate = estimate / KER
    residual = mask_ref[...].astype(jnp.float32) * (kspace_ref[...] - estimate)
    recovered_ref[...] = estimate + residual - jnp.clip(residual, -threshold, threshold)


def call(kernel, outs, *args, scratch=(), far=(), limit=40, scalars=0, micros=1):
    return pl.pallas_call(
        kernel,
        out_shape=[jax.ShapeDtypeStruct(shape, kind) for shape, kind in outs],
        in_specs=[
            pl.BlockSpec(memory_space=pltpu.HBM if i in far else pltpu.VMEM)
            for i in range(len(args))
        ],
        out_specs=[pl.BlockSpec(memory_space=pltpu.VMEM)] * (len(outs) - scalars)
        + [pl.BlockSpec(memory_space=pltpu.SMEM)] * scalars,
        scratch_shapes=list(scratch),
        compiler_params=pltpu.CompilerParams(vmem_limit_bytes=limit * 2**20),
        cost_estimate=pl.CostEstimate(
            flops=micros * 10**9, bytes_accessed=0, transcendentals=0
        ),
    )(*args)


def exchange(block, devices, mask, axes):
    return lax.ppermute(block, axes, [(i, i ^ mask) for i in range(devices)])


def with_masks(masks, mask):
    return masks + [m ^ mask for m in masks]


def after(value, *others):
    return lax.optimization_barrier((value,) + others)[0]


def rounds_of(low, high):
    masks = []
    while low < high:
        if 2 * low < high:
            masks.append([low, 2 * low, 3 * low])
        else:
            masks.append([low])
        low *= 4
    return masks


def gather_round(part, order, masks, devices, axes):
    part = jnp.concatenate(
        [part] + [exchange(part, devices, mask, axes) for mask in masks], axis=0
    )
    return part, order + [m ^ mask for mask in masks for m in order]


def gather_samples(sampled, basis, tiles, groups):
    devices = tiles * groups
    near, masks = sampled[None], [0]
    mask = devices // 2
    while mask > groups:
        near, masks = gather_round(near, masks, [mask], devices, AXES)
        mask //= 2
    half = near.shape[1] // 2
    halves = []
    for part, ways in (
        (near[:, :half], (groups, groups // 2)),
        (near[:, half:], (groups // 2, groups)),
    ):
        part, order = gather_round(part, masks, [ways[0]], devices, AXES)
        if not halves:
            basis = to_all(after(basis, part))
        pieces = [(part, order)]
        mask = ways[1]
        rest = groups // 4
        while mask > 1:
            pieces = pieces + [
                (exchange(part, devices, mask, AXES), [m ^ mask for m in order])
                for part, order in pieces
            ]
            mask, rest = rest, rest // 2
        if halves:
            part, order = pieces[-1]
            pieces[-1] = (after(part, basis), order)
        halves.append(
            pieces
            + [(exchange(part, devices, 1, AXES), [m ^ 1 for m in order]) for part, order in pieces]
        )
    return halves, basis


def to_all(pieces, axes=AXES):
    return lax.all_to_all(pieces, axes, 0, 0, tiled=True)


def gather_group(group, devices):
    groups = group.shape[0]
    parts = [group[:1]]
    parts += [exchange(group[s : s + 1], devices, s, AXES) for s in range(1, groups)]
    return jnp.concatenate(parts, axis=0), list(range(groups))


def total_beside(kept, given, near, order, images, groups, devices):
    ways = []
    mask = devices // 2
    while mask >= groups:
        ways.append(mask)
        mask //= 2
    half = near.shape[1] // 2
    parts = [near[:, :half], near[:, half:]]
    orders = [order, order]
    ways = [ways, ways[-1:] + ways[:-1]]
    step = 0

    def advance():
        for i in range(2):
            parts[i], orders[i] = gather_round(
                parts[i], orders[i], [ways[i][step]], devices, AXES
            )

    total = kept + exchange(given, devices, 1, AXES)
    for partners in rounds_of(2, devices):
        terms = [exchange(total, devices, way, AXES) for way in partners]
        total = total + terms[0]
        if len(terms) == 3:
            total = total + (terms[1] + terms[2])
        if step < len(ways[0]) - 1:
            advance()
            step += 1
    while step < len(ways[0]) - 1:
        advance()
        step += 1
    other = exchange(total, devices, 1, AXES)
    *parts, total, other, images = lax.optimization_barrier((*parts, total, other, images))
    pieces = []
    for i in range(2):
        mask = ways[i][-1]
        pieces += [parts[i], exchange(parts[i], devices, mask, AXES)]
        orders[i] = orders[i] + [m ^ mask for m in orders[i]]
    return (total, other), pieces, orders, to_all(images)


def column_shards(kspace, sample_mask, start_basis):
    f32, bf16 = jnp.float32, jnp.bfloat16
    tiles, groups = lax.axis_size("rows"), lax.axis_size("coil")
    devices = tiles * groups
    chg, tile = kspace.shape
    channels = chg * groups
    positions = tile * tiles
    owned, rank = start_basis.shape[1:]
    per_tile = owned // chg
    cols = rank // devices
    rows = cols * KER
    lanes = cols * chg

    sampled, basis_send = call(
        functools.partial(prepare_kernel, cols, chg, per_tile),
        [((chg, tile), f32), ((devices * per_tile, lanes), f32)],
        kspace,
        sample_mask,
        start_basis.reshape(owned, rank),
        scratch=[
            pltpu.VMEM((chg, tile), f32),
            pltpu.VMEM((chg, tile), sample_mask.dtype),
            pltpu.VMEM((owned, rank), f32),
            pltpu.SemaphoreType.DMA((3,)),
        ],
        far=(0, 1, 2),
        limit=60,
    )
    halves, basis_parts = gather_samples(
        sampled, basis_send.reshape(devices, per_tile, lanes), tiles, groups
    )
    starts = (0, chg // len(halves))
    orders = [(start, order) for start, half in zip(starts, halves) for _, order in half]
    wide = pltpu.VMEM((rows, positions), f32)
    moved = pltpu.VMEM((2 * rows, positions), bf16)
    samples, normal, send, group = call(
        functools.partial(passes_kernel, orders),
        [
            ((tiles, 2, groups, chg, tile), bf16),
            ((rows, channels), f32),
            ((tiles, groups, 2, per_tile, lanes), f32),
            ((groups, rows * chg // lanes, lanes), f32),
        ],
        basis_parts.reshape(tiles, groups, per_tile, lanes),
        *[piece for half in halves for piece, _ in half],
        scratch=[wide, moved],
        micros=12,
    )
    received = to_all(send.reshape(devices, 2 * per_tile, lanes))
    reach = tile + LANES
    (images,) = call(
        images_kernel,
        [((tiles, groups, cols, reach), f32)],
        samples,
        normal,
        scratch=[wide],
        micros=2,
    )
    near, order = gather_group(group, devices)
    received, near = lax.optimization_barrier((received, images, near))[::2]
    half = ((rank // 2 + SUB, rank), f32)
    kept, given, turned = call(
        functools.partial(gram_kernel, cols, per_tile),
        [half, half, ((rank, owned), f32)],
        received.reshape(devices * 2 * per_tile, lanes),
    )
    gram, pieces, order, images = total_beside(
        kept, given, near, order, images.reshape(devices, cols, reach), groups, devices
    )
    whole = ((rank, rank), f32)
    first, second, sound = call(
        factor_kernel, [whole, whole, ((1,), jnp.int32)], *gram, scalars=1, micros=12
    )

    def again():
        (gram,) = call(rows_kernel, [whole], turned, first)
        mask = 1
        while mask < devices:
            gram = gram + exchange(gram, devices, mask, AXES)
            mask *= 2
        return gram

    second = lax.cond(sound[0] == 1, lambda: second, again)
    (both,) = call(both_kernel, [whole], second, first, micros=0)
    recovered, basis = call(
        functools.partial(last_kernel, cols, order),
        [((chg, tile), f32), ((owned, rank), f32)],
        images.reshape(rank, reach),
        both,
        kspace,
        sample_mask,
        *[piece.reshape(-1, lanes) for piece in pieces],
        scratch=[
            pltpu.VMEM((chg, tile), f32),
            pltpu.VMEM((chg, tile), sample_mask.dtype),
            pltpu.VMEM((rank, KER * chg), f32),
            pltpu.SemaphoreType.DMA((2,)),
        ],
        far=(2, 3),
        limit=40,
        micros=5,
    )
    return (recovered, basis.reshape(1, owned, rank))


def divides_columns(kspace, start_basis):
    tiles, groups = lax.axis_size("rows"), lax.axis_size("coil")
    devices = tiles * groups
    chg, tile = kspace.shape
    owned, rank = start_basis.shape[1:]
    return (
        devices & (devices - 1) == 0
        and tiles > 2
        and groups > 2
        and rank % (2 * SUB) == 0
        and rank % devices == 0
        and rank % LANES == 0
        and tile % LANES == 0
        and owned == SUB * chg
        and chg * (rank // devices) == LANES
        and 2 * (LANES // chg) == SUB
        and KER + 2 * SUB <= LANES
        and chg % (4 * SUB) == 0
        and (chg * groups) % LANES == 0
        and KER <= LANES
        and rank // devices <= SUB
        and rank // devices % 2 == 0
    )


def shards(kspace, sample_mask, start_basis):
    if divides_columns(kspace, start_basis):
        return column_shards(kspace, sample_mask, start_basis)
    return general_shards(kspace, sample_mask, start_basis)


def solution(mesh):
    return jax.shard_map(
        shards,
        mesh=mesh,
        in_specs=(P("coil", "rows"), P("coil", "rows"), P("coil", "rows", None)),
        out_specs=(P("coil", "rows"), P("coil", "rows", None)),
        check_vma=False,
    )
```

```python
import functools

import jax
import jax.numpy as jnp
from jax import lax
from jax.experimental import pallas as pl
from jax.experimental.pallas import tpu as pltpu
from jax.sharding import PartitionSpec as P

KER = 64
ITERS = 2
LANES = 128
SUB = 8
AXES = ("rows", "coil")


threshold = 0.05


def shifted(block, axis, distance):
    devices = range(lax.axis_size(axis))
    route = [((i - distance) % len(devices), i) for i in devices]
    return lax.ppermute(block, axis, route)


def orthonormal(normal_rows, gram_matrix):
    factor = jnp.linalg.cholesky(gram_matrix)
    return lax.linalg.triangular_solve(
        factor, normal_rows, left_side=False, lower=True, transpose_a=True
    )


def coil_total(partial_value):
    return lax.psum(partial_value, "coil")


def general_shards(kspace, sample_mask, start_basis):
    highest = lax.Precision.HIGHEST
    channels = kspace.shape[0]
    tile_rows = kspace.shape[1]
    mask_float = sample_mask.astype(jnp.float32)
    sampled = kspace * mask_float
    next_rim = shifted(sampled[:, : KER - 1], "rows", -1)
    extended = jnp.concatenate([sampled, next_rim], axis=1)
    hankel_cols = jnp.stack(
        [extended[:, offset : offset + tile_rows] for offset in range(KER)], axis=0
    )
    hankel_cols = hankel_cols.reshape(KER * channels, tile_rows)
    owned_basis = start_basis.reshape(start_basis.shape[1], start_basis.shape[2])
    whole_basis = lax.all_gather(owned_basis, "rows", axis=0, tiled=True)
    for iteration in range(ITERS):
        images = coil_total(
            lax.dot_general(
                whole_basis,
                hankel_cols,
                (((0,), (0,)), ((), ())),
                precision=highest,
                preferred_element_type=jnp.float32,
            )
        )
        local_normal = lax.dot_general(
            hankel_cols,
            images,
            (((1,), (1,)), ((), ())),
            precision=highest,
            preferred_element_type=jnp.float32,
        )
        normal_whole = lax.psum(local_normal, "rows")
        local_gram = jnp.dot(
            normal_whole.T, normal_whole, precision=highest, preferred_element_type=jnp.float32
        )
        gram_matrix = lax.psum(local_gram, "coil")
        whole_basis = orthonormal(normal_whole, gram_matrix)
    images = coil_total(
        lax.dot_general(
            whole_basis,
            hankel_cols,
            (((0,), (0,)), ((), ())),
            precision=highest,
            preferred_element_type=jnp.float32,
        )
    )
    projected = jnp.dot(whole_basis, images, precision=highest, preferred_element_type=jnp.float32)
    owned_count = whole_basis.shape[0] // lax.axis_size("rows")
    owned_basis = lax.dynamic_slice_in_dim(
        whole_basis, lax.axis_index("rows") * owned_count, owned_count, 0
    )
    stacked = projected.reshape(KER, channels, tile_rows)
    spread = jnp.zeros((channels, tile_rows + KER - 1), jnp.float32)
    for offset in range(KER):
        spread = spread.at[:, offset : offset + tile_rows].add(stacked[offset])
    carried = shifted(spread[:, tile_rows:], "rows", 1)
    estimate = spread[:, :tile_rows].at[:, : KER - 1].add(carried) / KER
    residual = mask_float * (kspace - estimate)
    recovered = estimate + residual - jnp.clip(residual, -threshold, threshold)
    return (recovered, owned_basis.reshape(1, owned_basis.shape[0], owned_basis.shape[1]))


def split(value):
    high = value.astype(jnp.bfloat16)
    low = (value - high.astype(jnp.float32)).astype(jnp.bfloat16)
    return high, low


def dot(a, b, dims=((1,), (0,))):
    return lax.dot_general(a, b, (dims, ((), ())), preferred_element_type=jnp.float32)


def dot3(a, b, dims=((1,), (0,))):
    a_high, a_low = split(a)
    b_high, b_low = split(b)
    return dot(a_high, b_high, dims) + (dot(a_high, b_low, dims) + dot(a_low, b_high, dims))


def square(size):
    at_row = lax.broadcasted_iota(jnp.int32, (size, size), 0)
    at_col = lax.broadcasted_iota(jnp.int32, (size, size), 1)
    return at_row, at_col


def prepare_kernel(cols, chg, per_tile, basis_ref, send_ref):
    turned = basis_ref[...].T
    devices = turned.shape[0] // cols
    for j in range(per_tile):
        part = turned[:, j * chg : (j + 1) * chg]
        row = jnp.concatenate([part[k * devices : (k + 1) * devices] for k in range(cols)], axis=1)
        send_ref[pl.ds(j, devices, stride=per_tile), :] = row


def images_of(vectors, samples_ref, wide_ref):
    rows, channels = vectors.shape
    cols = rows // KER
    high, low = split(vectors)
    at_row = lax.broadcasted_iota(jnp.int32, (rows, rows), 0)
    at_col = lax.broadcasted_iota(jnp.int32, (rows, rows), 1)
    flip = ((at_row // KER == at_col // KER) & (at_row % KER + at_col % KER == KER - 1)).astype(
        jnp.float32
    ).astype(jnp.bfloat16)
    both = dot(flip, jnp.concatenate([high, low], axis=1)).astype(jnp.bfloat16)
    high, low = both[:, :channels], both[:, channels:]
    zero = jnp.zeros_like(low)
    both = jnp.concatenate(
        [jnp.concatenate([high, high], axis=1), jnp.concatenate([low, zero], axis=1)], axis=0
    )
    tiles = samples_ref.shape[0]
    tile = samples_ref.shape[-1]
    for t in range(tiles):
        wide = dot(both, samples_ref[t].reshape(2 * channels, tile))
        wide_ref[:, t * tile : (t + 1) * tile] = wide[:rows] + wide[rows:]
    images = []
    for k in range(cols):
        total = None
        for i in reversed(range(0, KER, SUB)):
            part = wide_ref[k * KER + i : k * KER + i + SUB, :]
            total = part if total is None else pltpu.roll(total, SUB, 1) + part
        total = pltpu.roll(total, 0, 1, stride=1, stride_axis=0)
        images.append(jnp.sum(total, axis=0, keepdims=True))
    return images


def normal_of(images, samples_ref, moved_ref):
    cols = len(images)
    positions = images[0].shape[1]
    tiles = samples_ref.shape[0]
    tile = samples_ref.shape[-1]
    channels = samples_ref.shape[2] * samples_ref.shape[3]
    rows = cols * KER
    for k in range(cols):
        base = jnp.broadcast_to(images[k], (SUB, positions))
        base = pltpu.roll(base, positions - (KER - 1), 1, stride=1, stride_axis=0)
        for j in range(0, KER, 2 * SUB):
            first = base if j == 0 else pltpu.roll(base, j, 1)
            second = pltpu.roll(base, j + SUB, 1)
            high, low = split(jnp.concatenate([first, second], axis=0))
            moved_ref[k * KER + j : k * KER + j + 2 * SUB, :] = high
            moved_ref[rows + k * KER + j : rows + k * KER + j + 2 * SUB, :] = low
    total = jnp.zeros((2 * rows, 2 * channels), jnp.float32)
    for t in range(tiles):
        block = samples_ref[t].reshape(2 * channels, tile)
        total = total + dot(moved_ref[:, t * tile : (t + 1) * tile], block, ((1,), (1,)))
    return total[:rows, :channels] + (
        total[:rows, channels:] + total[rows:, :channels] + total[rows:, channels:]
    )


def store_by_rows(normal, send_ref, part):
    tiles, groups, _, per_tile, lanes = send_ref.shape
    cols = normal.shape[0] // KER
    chg = normal.shape[1] // groups
    for g in range(groups):
        joined = jnp.concatenate(
            [normal[k * KER : (k + 1) * KER, g * chg : (g + 1) * chg] for k in range(cols)], axis=1
        )
        send_ref[:, g, part] = joined.reshape(tiles, per_tile, lanes)


def store_by_groups(normal_ref, group_ref):
    groups, count, lanes = group_ref.shape
    rows, channels = normal_ref.shape
    chg = channels // groups
    fold = lanes // chg
    cols = rows // KER
    deep = KER // fold
    me = lax.axis_index("coil")
    parts = [
        [normal_ref[pl.ds(k * KER + f, deep, stride=fold), :] for f in range(fold)]
        for k in range(cols)
    ]
    for g in range(groups):
        joined = [
            jnp.concatenate([part[:, g * chg : (g + 1) * chg] for part in parts[k]], axis=1)
            for k in range(cols)
        ]
        group_ref[lax.bitwise_xor(me, g)] = jnp.concatenate(joined, axis=0)


def passes_kernel(orders, basis_ref, *refs):
    *pieces, samples_ref, normal_ref, send_ref, group_ref, wide_ref, moved_ref = refs
    tiles, _, groups, chg, tile = samples_ref.shape
    me = lax.axis_index("rows") * groups + lax.axis_index("coil")
    for (start, order), piece_ref in zip(orders, pieces):
        count = piece_ref.shape[1]
        for slot, mask in enumerate(order):
            high, low = split(piece_ref[slot])
            source = lax.bitwise_xor(me, mask)
            t, g = source // groups, source % groups
            samples_ref[t, 0, g, start : start + count] = high
            samples_ref[t, 1, g, start : start + count] = low
    cols = basis_ref.shape[-1] // chg
    rows = []
    for k in range(cols):
        rows.append(
            jnp.concatenate(
                [
                    basis_ref[:, g].reshape(KER, cols * chg)[:, k * chg : (k + 1) * chg]
                    for g in range(groups)
                ],
                axis=1,
            )
        )
    vectors = jnp.concatenate(rows, axis=0)
    normal = normal_of(images_of(vectors, samples_ref, wide_ref), samples_ref, moved_ref)
    scaled = []
    for k in range(cols):
        part = normal[k * KER : (k + 1) * KER]
        scaled.append(part * (1.0 / jnp.max(jnp.abs(part))))
    normal = jnp.concatenate(scaled, axis=0)
    store_by_rows(normal, send_ref, 0)
    normal = normal_of(images_of(normal, samples_ref, wide_ref), samples_ref, moved_ref)
    normal_ref[...] = normal
    store_by_rows(normal, send_ref, 1)
    store_by_groups(normal_ref, group_ref)


def images_kernel(samples_ref, vectors_ref, send_ref, wide_ref):
    tiles, groups, cols, reach = send_ref.shape
    tile = samples_ref.shape[-1]
    images = jnp.concatenate(images_of(vectors_ref[...], samples_ref, wide_ref), axis=0)
    positions = images.shape[1]
    images = pltpu.roll(images, positions - (KER - 1), 1)
    rim = reach - tile
    for t in range(tiles):
        if t == 0:
            part = jnp.concatenate([images[:, positions - rim :], images[:, :tile]], axis=1)
        else:
            part = images[:, t * tile - rim : (t + 1) * tile]
        for g in range(groups):
            send_ref[t, g] = part


def gather_turned(received_ref, cols, per_tile, part):
    count, lanes = received_ref.shape
    devices = count // (2 * per_tile)
    chg = lanes // cols
    loaded = [
        received_ref[pl.ds(part * per_tile + j, devices, stride=2 * per_tile), :]
        for j in range(per_tile)
    ]
    return jnp.concatenate(
        [
            jnp.concatenate(
                [loaded[j][:, k * chg : (k + 1) * chg] for j in range(per_tile)], axis=1
            )
            for k in range(cols)
        ],
        axis=0,
    )


def exact(a, b, dims=((1,), (0,))):
    return lax.dot_general(
        a, b, (dims, ((), ())), precision=lax.Precision.HIGHEST, preferred_element_type=jnp.float32
    )


def gram_kernel(cols, per_tile, received_ref, kept_ref, given_ref, turned_ref):
    turned = gather_turned(received_ref, cols, per_tile, 0)
    first = exact(turned, turned, ((1,), (1,)))
    turned = gather_turned(received_ref, cols, per_tile, 1)
    second = exact(turned, turned, ((1,), (1,)))
    turned_ref[...] = turned
    at_row, at_col = square(first.shape[0])
    packed = jnp.where(at_row >= at_col, first, second)
    line = jnp.sum(jnp.where(at_row == at_col, second, 0.0), axis=0, keepdims=True)
    line = jnp.broadcast_to(line, (SUB, line.shape[1]))
    half = packed.shape[0] // 2
    odd = lax.axis_index("coil") % 2 == 1
    kept_ref[:half] = jnp.where(odd, packed[half:], packed[:half])
    given_ref[:half] = jnp.where(odd, packed[:half], packed[half:])
    kept_ref[half:] = line
    given_ref[half:] = line


def load_grams(kept_ref, other_ref):
    odd = lax.axis_index("coil") % 2 == 1
    kept, other = kept_ref[...], other_ref[...]
    low, high = jnp.where(odd, other, kept), jnp.where(odd, kept, other)
    half = low.shape[0] - SUB
    packed = jnp.concatenate([low[:half], high[:half]], axis=0)
    line = low[half : half + 1]
    at_row, at_col = square(packed.shape[0])
    turned = packed.T
    first = jnp.where(at_row >= at_col, packed, turned)
    second = jnp.where(at_row > at_col, turned, packed)
    return first, jnp.where(at_row == at_col, line, second), line


def inverse_factor(gram):
    size = gram.shape[0]
    shape = (SUB, size)
    at_row = lax.broadcasted_iota(jnp.int32, (size, size), 0)
    at_col = lax.broadcasted_iota(jnp.int32, (size, size), 1)
    unit = (at_row == at_col).astype(jnp.float32)
    left = [gram[b : b + SUB] for b in range(0, size, SUB)]
    right = [unit[b : b + SUB] for b in range(0, size, SUB)]
    sub = lax.broadcasted_iota(jnp.int32, shape, 0)
    done = []
    for b in range(len(left)):
        spread = {
            c: [
                jnp.broadcast_to(left[c][:, b * SUB + k : b * SUB + k + 1], shape)
                for k in range(SUB)
            ]
            for c in range(b, len(left))
        }
        entry = {
            (i, k): jnp.broadcast_to(spread[b][k][i : i + 1], shape)
            for k in range(SUB)
            for i in range(k, SUB)
        }
        inverse = {}
        for k in range(SUB):
            root = lax.rsqrt(entry[k, k])
            inverse[k, k] = root
            for i in range(k + 1, SUB):
                entry[i, k] = entry[i, k] * root
            for i in range(k + 1, SUB):
                for m in range(k + 1, i + 1):
                    entry[i, m] = entry[i, m] - entry[i, k] * entry[m, k]
        for i in range(1, SUB):
            for k in range(i):
                total = entry[i, k] * inverse[k, k]
                for m in range(k + 1, i):
                    total = total + entry[i, m] * inverse[m, k]
                inverse[i, k] = -(total * inverse[i, i])

        def solved(rows):
            whole = [jnp.broadcast_to(rows[k : k + 1], shape) for k in range(SUB)]
            first = []
            for i in range(SUB):
                total = inverse[i, 0] * whole[0]
                for k in range(1, i + 1):
                    total = total + inverse[i, k] * whole[k]
                first.append(total)
            second = []
            for k in range(SUB):
                total = inverse[k, k] * first[k]
                for i in range(k + 1, SUB):
                    total = total + inverse[i, k] * first[i]
                second.append(total)
            return first, second

        lower, lower_again = solved(right[b])
        row = lower[0]
        for i in range(1, SUB):
            row = jnp.where(sub == i, lower[i], row)
        done.append(row)
        if b + 1 < len(left):
            _, upper_again = solved(left[b])
            for c in range(b + 1, len(left)):
                for k in range(SUB):
                    left[c] = left[c] - spread[c][k] * upper_again[k]
                    right[c] = right[c] - spread[c][k] * lower_again[k]
    return jnp.concatenate(done, axis=0)


def factor_kernel(gram_ref, other_ref, inverse_ref, next_ref, sound_ref):
    gram, raw, line = load_grams(gram_ref, other_ref)
    inverse = inverse_factor(gram)
    inverse_ref[...] = inverse
    gram = exact(exact(inverse, raw), inverse, ((1,), (1,)))
    next_ref[...] = gram
    at_row, at_col = square(gram.shape[0])
    terms = jnp.sum(inverse * inverse * line, axis=1, keepdims=True)
    result = jnp.sum(jnp.where(at_row == at_col, gram, 0.0), axis=1, keepdims=True)
    worst = jnp.max(jnp.where(terms <= 64.0 * result, 0, 1))
    sound_ref[0] = 1 - worst


def rows_kernel(turned_ref, inverse_ref, gram_ref):
    turned = exact(inverse_ref[...], turned_ref[...])
    gram_ref[...] = exact(turned, turned, ((1,), (1,)))


def both_kernel(gram_ref, inverse_ref, both_ref):
    both_ref[...] = exact(inverse_factor(gram_ref[...]), inverse_ref[...])


def moved_columns(order, cols):
    devices = len(order[0])
    at_row, at_col = square(devices * cols)
    turn = at_col % cols * devices + at_col // cols
    me = lax.axis_index("rows") * lax.axis_size("coil") + lax.axis_index("coil")
    slot = at_col % devices
    mask = jnp.zeros_like(slot)
    bit = 1
    while bit < devices:
        step = jnp.where(2 * at_col < at_col.shape[1], order[0][bit], order[1][bit])
        mask = mask | jnp.where(slot & bit != 0, step, 0)
        bit *= 2
    source = at_col - slot + lax.bitwise_xor(mask, jnp.full_like(mask, me))
    return [(at_row == place).astype(jnp.float32) for place in (turn, source)]


def stacked_dot(a, b):
    a_high, a_low = split(a)
    b_high, b_low = split(b)
    left = jnp.concatenate(
        [
            jnp.concatenate([a_high, a_high], axis=1),
            jnp.concatenate([a_low, jnp.zeros_like(a_low)], axis=1),
        ],
        axis=0,
    )
    both = dot(left, jnp.concatenate([b_high, b_low], axis=0))
    return both[: a.shape[0]] + both[a.shape[0] :]


def last_kernel(
    cols,
    order,
    images_ref,
    both_ref,
    kspace_ref,
    mask_ref,
    top_near_ref,
    top_far_ref,
    low_near_ref,
    low_far_ref,
    recovered_ref,
    basis_ref,
    vectors_ref,
):
    both = both_ref[...]
    reach = images_ref.shape[1]
    factors = [exact(both, moved) for moved in moved_columns(order, cols)]
    chg, tile = kspace_ref.shape
    lanes = top_near_ref.shape[1]
    fold = lanes // chg
    deep = KER // fold
    step = cols // 2 * deep
    lead = reach - tile - KER - 2 * SUB
    images = stacked_dot(factors[0], images_ref[...]).T[lead:]
    rim = reach - tile - SUB - lead
    even, odd = None, None
    for a in range(0, deep, 2):
        turned = [
            jnp.concatenate(
                [
                    ref[pl.ds(k * deep + a + i, ref.shape[0] // step, stride=step), :]
                    for refs in ((top_near_ref, top_far_ref), (low_near_ref, low_far_ref))
                    for k in range(cols // 2)
                    for ref in refs
                ],
                axis=0,
            )
            for i in range(2)
        ]
        vectors = stacked_dot(factors[1], jnp.concatenate(turned, axis=1))
        vectors_ref[:, a * lanes : (a + 2) * lanes] = vectors
        projected = stacked_dot(images, vectors)
        shift = a * fold
        part = projected[rim - shift : rim - shift + tile + SUB, :lanes]
        even = part if even is None else even + part
        part = projected[rim - SUB - shift : rim - shift + tile + SUB, lanes:]
        odd = part if odd is None else odd + part
    total = even + odd[SUB - fold : SUB - fold + tile + SUB]
    estimate = total[SUB : SUB + tile]
    for f in range(1, fold):
        moved = pltpu.roll(total, lanes - f * chg, 1)
        estimate = estimate + moved[SUB - f : SUB - f + tile]
    estimate = estimate.T[:chg]
    owned = basis_ref.shape[0]
    start = pl.multiple_of(lax.axis_index("rows") * owned, owned)
    basis_ref[...] = vectors_ref[:, pl.ds(start, owned)].T
    estimate = estimate / KER
    residual = mask_ref[...].astype(jnp.float32) * (kspace_ref[...] - estimate)
    recovered_ref[...] = estimate + residual - jnp.clip(residual, -threshold, threshold)


def call(kernel, outs, *args, scratch=(), limit=12, scalars=0, micros=1):
    return pl.pallas_call(
        kernel,
        out_shape=[jax.ShapeDtypeStruct(shape, kind) for shape, kind in outs],
        in_specs=[pl.BlockSpec(memory_space=pltpu.VMEM)] * len(args),
        out_specs=[pl.BlockSpec(memory_space=pltpu.VMEM)] * (len(outs) - scalars)
        + [pl.BlockSpec(memory_space=pltpu.SMEM)] * scalars,
        scratch_shapes=list(scratch),
        compiler_params=pltpu.CompilerParams(vmem_limit_bytes=limit * 2**20),
        cost_estimate=pl.CostEstimate(
            flops=micros * 10**9, bytes_accessed=0, transcendentals=0
        ),
    )(*args)


def exchange(block, devices, mask, axes):
    return lax.ppermute(block, axes, [(i, i ^ mask) for i in range(devices)])


def with_masks(masks, mask):
    return masks + [m ^ mask for m in masks]


def after(value, *others):
    return lax.optimization_barrier((value,) + others)[0]


def rounds_of(low, high):
    masks = []
    while low < high:
        if 2 * low < high:
            masks.append([low, 2 * low, 3 * low])
        else:
            masks.append([low])
        low *= 4
    return masks


def gather_round(part, order, masks, devices, axes):
    part = jnp.concatenate(
        [part] + [exchange(part, devices, mask, axes) for mask in masks], axis=0
    )
    return part, order + [m ^ mask for mask in masks for m in order]


def gather_samples(sampled, basis, tiles, groups):
    devices = tiles * groups
    near, masks = sampled[None], [0]
    mask = devices // 2
    while mask > groups:
        near, masks = gather_round(near, masks, [mask], devices, AXES)
        mask //= 2
    basis = to_all(basis)
    near = after(near, basis)
    half = near.shape[1] // 2
    halves = []
    for part, ways in (
        (near[:, :half], (groups, groups // 2)),
        (near[:, half:], (groups // 2, groups)),
    ):
        part, order = gather_round(part, masks, [ways[0]], devices, AXES)
        pieces = [(part, order)]
        mask = ways[1]
        rest = groups // 4
        while mask > 1:
            pieces = pieces + [
                (exchange(part, devices, mask, AXES), [m ^ mask for m in order])
                for part, order in pieces
            ]
            mask, rest = rest, rest // 2
        halves.append(
            pieces
            + [(exchange(part, devices, 1, AXES), [m ^ 1 for m in order]) for part, order in pieces]
        )
    return halves, basis


def to_all(pieces, axes=AXES):
    return lax.all_to_all(pieces, axes, 0, 0, tiled=True)


def gather_group(group, devices):
    groups = group.shape[0]
    parts = [group[:1]]
    parts += [exchange(group[s : s + 1], devices, s, AXES) for s in range(1, groups)]
    return jnp.concatenate(parts, axis=0), list(range(groups))


def total_beside(kept, given, near, order, images, groups, devices):
    ways = []
    mask = devices // 2
    while mask >= groups:
        ways.append(mask)
        mask //= 2
    half = near.shape[1] // 2
    parts = [near[:, :half], near[:, half:]]
    orders = [order, order]
    ways = [ways, ways[-1:] + ways[:-1]]
    step = 0

    def advance():
        for i in range(2):
            parts[i], orders[i] = gather_round(
                parts[i], orders[i], [ways[i][step]], devices, AXES
            )

    total = kept + exchange(given, devices, 1, AXES)
    for partners in rounds_of(2, devices):
        terms = [exchange(total, devices, way, AXES) for way in partners]
        total = total + terms[0]
        if len(terms) == 3:
            total = total + (terms[1] + terms[2])
        if step < len(ways[0]) - 1:
            advance()
            step += 1
    while step < len(ways[0]) - 1:
        advance()
        step += 1
    other = exchange(total, devices, 1, AXES)
    *parts, total, other, images = lax.optimization_barrier((*parts, total, other, images))
    pieces = []
    for i in range(2):
        mask = ways[i][-1]
        pieces += [parts[i], exchange(parts[i], devices, mask, AXES)]
        orders[i] = orders[i] + [m ^ mask for m in orders[i]]
    return (total, other), pieces, orders, to_all(images)


def column_shards(kspace, sample_mask, start_basis):
    f32, bf16 = jnp.float32, jnp.bfloat16
    tiles, groups = lax.axis_size("rows"), lax.axis_size("coil")
    devices = tiles * groups
    chg, tile = kspace.shape
    channels = chg * groups
    positions = tile * tiles
    owned, rank = start_basis.shape[1:]
    per_tile = owned // chg
    cols = rank // devices
    rows = cols * KER
    lanes = cols * chg

    sampled = kspace * sample_mask.astype(f32)
    (basis_send,) = call(
        functools.partial(prepare_kernel, cols, chg, per_tile),
        [((devices * per_tile, lanes), f32)],
        start_basis.reshape(owned, rank),
    )
    halves, basis_parts = gather_samples(
        sampled, basis_send.reshape(devices, per_tile, lanes), tiles, groups
    )
    starts = (0, chg // len(halves))
    orders = [(start, order) for start, half in zip(starts, halves) for _, order in half]
    wide = pltpu.VMEM((rows, positions), f32)
    moved = pltpu.VMEM((2 * rows, positions), bf16)
    samples, normal, send, group = call(
        functools.partial(passes_kernel, orders),
        [
            ((tiles, 2, groups, chg, tile), bf16),
            ((rows, channels), f32),
            ((tiles, groups, 2, per_tile, lanes), f32),
            ((groups, rows * chg // lanes, lanes), f32),
        ],
        basis_parts.reshape(tiles, groups, per_tile, lanes),
        *[piece for half in halves for piece, _ in half],
        scratch=[wide, moved],
        limit=24,
        micros=12,
    )
    received = to_all(send.reshape(devices, 2 * per_tile, lanes))
    reach = tile + LANES
    (images,) = call(
        images_kernel,
        [((tiles, groups, cols, reach), f32)],
        samples,
        normal,
        scratch=[wide],
        limit=16,
        micros=2,
    )
    near, order = gather_group(group, devices)
    received, near = lax.optimization_barrier((received, images, near))[::2]
    half = ((rank // 2 + SUB, rank), f32)
    kept, given, turned = call(
        functools.partial(gram_kernel, cols, per_tile),
        [half, half, ((rank, owned), f32)],
        received.reshape(devices * 2 * per_tile, lanes),
    )
    gram, pieces, order, images = total_beside(
        kept, given, near, order, images.reshape(devices, cols, reach), groups, devices
    )
    whole = ((rank, rank), f32)
    first, second, sound = call(
        factor_kernel, [whole, whole, ((1,), jnp.int32)], *gram, scalars=1, micros=12
    )

    def again():
        (gram,) = call(rows_kernel, [whole], turned, first)
        mask = 1
        while mask < devices:
            gram = gram + exchange(gram, devices, mask, AXES)
            mask *= 2
        return gram

    second = lax.cond(sound[0] == 1, lambda: second, again)
    (both,) = call(both_kernel, [whole], second, first, micros=0)
    recovered, basis = call(
        functools.partial(last_kernel, cols, order),
        [((chg, tile), f32), ((owned, rank), f32)],
        images.reshape(rank, reach),
        both,
        kspace,
        sample_mask,
        *[piece.reshape(-1, lanes) for piece in pieces],
        scratch=[pltpu.VMEM((rank, KER * chg), f32)],
        limit=16,
        micros=5,
    )
    return (recovered, basis.reshape(1, owned, rank))


def divides_columns(kspace, start_basis):
    tiles, groups = lax.axis_size("rows"), lax.axis_size("coil")
    devices = tiles * groups
    chg, tile = kspace.shape
    owned, rank = start_basis.shape[1:]
    return (
        devices & (devices - 1) == 0
        and tiles > 2
        and groups > 2
        and rank % (2 * SUB) == 0
        and rank % devices == 0
        and rank % LANES == 0
        and tile % LANES == 0
        and owned == SUB * chg
        and chg * (rank // devices) == LANES
        and 2 * (LANES // chg) == SUB
        and KER + 2 * SUB <= LANES
        and chg % (4 * SUB) == 0
        and (chg * groups) % LANES == 0
        and KER <= LANES
        and rank // devices <= SUB
        and rank // devices % 2 == 0
    )


def shards(kspace, sample_mask, start_basis):
    if divides_columns(kspace, start_basis):
        return column_shards(kspace, sample_mask, start_basis)
    return general_shards(kspace, sample_mask, start_basis)


def solution(mesh):
    return jax.shard_map(
        shards,
        mesh=mesh,
        in_specs=(P("coil", "rows"), P("coil", "rows"), P("coil", "rows", None)),
        out_specs=(P("coil", "rows"), P("coil", "rows", None)),
        check_vma=False,
    )
```

```python
import functools

import jax
import jax.numpy as jnp
from jax import lax
from jax.experimental import pallas as pl
from jax.experimental.pallas import tpu as pltpu
from jax.sharding import PartitionSpec as P

KER = 64
ITERS = 2
LANES = 128
SUB = 8
AXES = ("rows", "coil")


threshold = 0.05


def shifted(block, axis, distance):
    devices = range(lax.axis_size(axis))
    route = [((i - distance) % len(devices), i) for i in devices]
    return lax.ppermute(block, axis, route)


def orthonormal(normal_rows, gram_matrix):
    factor = jnp.linalg.cholesky(gram_matrix)
    return lax.linalg.triangular_solve(
        factor, normal_rows, left_side=False, lower=True, transpose_a=True
    )


def coil_total(partial_value):
    return lax.psum(partial_value, "coil")


def general_shards(kspace, sample_mask, start_basis):
    highest = lax.Precision.HIGHEST
    channels = kspace.shape[0]
    tile_rows = kspace.shape[1]
    mask_float = sample_mask.astype(jnp.float32)
    sampled = kspace * mask_float
    next_rim = shifted(sampled[:, : KER - 1], "rows", -1)
    extended = jnp.concatenate([sampled, next_rim], axis=1)
    hankel_cols = jnp.stack(
        [extended[:, offset : offset + tile_rows] for offset in range(KER)], axis=0
    )
    hankel_cols = hankel_cols.reshape(KER * channels, tile_rows)
    owned_basis = start_basis.reshape(start_basis.shape[1], start_basis.shape[2])
    whole_basis = lax.all_gather(owned_basis, "rows", axis=0, tiled=True)
    for iteration in range(ITERS):
        images = coil_total(
            lax.dot_general(
                whole_basis,
                hankel_cols,
                (((0,), (0,)), ((), ())),
                precision=highest,
                preferred_element_type=jnp.float32,
            )
        )
        local_normal = lax.dot_general(
            hankel_cols,
            images,
            (((1,), (1,)), ((), ())),
            precision=highest,
            preferred_element_type=jnp.float32,
        )
        normal_whole = lax.psum(local_normal, "rows")
        local_gram = jnp.dot(
            normal_whole.T, normal_whole, precision=highest, preferred_element_type=jnp.float32
        )
        gram_matrix = lax.psum(local_gram, "coil")
        whole_basis = orthonormal(normal_whole, gram_matrix)
    images = coil_total(
        lax.dot_general(
            whole_basis,
            hankel_cols,
            (((0,), (0,)), ((), ())),
            precision=highest,
            preferred_element_type=jnp.float32,
        )
    )
    projected = jnp.dot(whole_basis, images, precision=highest, preferred_element_type=jnp.float32)
    owned_count = whole_basis.shape[0] // lax.axis_size("rows")
    owned_basis = lax.dynamic_slice_in_dim(
        whole_basis, lax.axis_index("rows") * owned_count, owned_count, 0
    )
    stacked = projected.reshape(KER, channels, tile_rows)
    spread = jnp.zeros((channels, tile_rows + KER - 1), jnp.float32)
    for offset in range(KER):
        spread = spread.at[:, offset : offset + tile_rows].add(stacked[offset])
    carried = shifted(spread[:, tile_rows:], "rows", 1)
    estimate = spread[:, :tile_rows].at[:, : KER - 1].add(carried) / KER
    residual = mask_float * (kspace - estimate)
    recovered = estimate + residual - jnp.clip(residual, -threshold, threshold)
    return (recovered, owned_basis.reshape(1, owned_basis.shape[0], owned_basis.shape[1]))


def split(value):
    high = value.astype(jnp.bfloat16)
    low = (value - high.astype(jnp.float32)).astype(jnp.bfloat16)
    return high, low


def dot(a, b, dims=((1,), (0,))):
    return lax.dot_general(a, b, (dims, ((), ())), preferred_element_type=jnp.float32)


def dot3(a, b, dims=((1,), (0,))):
    a_high, a_low = split(a)
    b_high, b_low = split(b)
    return dot(a_high, b_high, dims) + (dot(a_high, b_low, dims) + dot(a_low, b_high, dims))


def square(size):
    at_row = lax.broadcasted_iota(jnp.int32, (size, size), 0)
    at_col = lax.broadcasted_iota(jnp.int32, (size, size), 1)
    return at_row, at_col


def prepare_kernel(cols, chg, per_tile, basis_ref, send_ref):
    turned = basis_ref[...].T
    devices = turned.shape[0] // cols
    for j in range(per_tile):
        part = turned[:, j * chg : (j + 1) * chg]
        row = jnp.concatenate([part[k * devices : (k + 1) * devices] for k in range(cols)], axis=1)
        send_ref[pl.ds(j, devices, stride=per_tile), :] = row


def images_of(vectors, samples_ref, wide_ref):
    rows, channels = vectors.shape
    cols = rows // KER
    high, low = split(vectors)
    at_row = lax.broadcasted_iota(jnp.int32, (rows, rows), 0)
    at_col = lax.broadcasted_iota(jnp.int32, (rows, rows), 1)
    flip = ((at_row // KER == at_col // KER) & (at_row % KER + at_col % KER == KER - 1)).astype(
        jnp.float32
    ).astype(jnp.bfloat16)
    both = dot(flip, jnp.concatenate([high, low], axis=1)).astype(jnp.bfloat16)
    high, low = both[:, :channels], both[:, channels:]
    twice = jnp.concatenate([high, high], axis=1)
    tiles = samples_ref.shape[0]
    tile = samples_ref.shape[-1]
    for t in range(tiles):
        block = samples_ref[t].reshape(2 * channels, tile)
        wide_ref[:, t * tile : (t + 1) * tile] = dot(twice, block) + dot(low, block[:channels])
    images = []
    for k in range(cols):
        total = None
        for i in reversed(range(0, KER, SUB)):
            part = wide_ref[k * KER + i : k * KER + i + SUB, :]
            total = part if total is None else pltpu.roll(total, SUB, 1) + part
        total = pltpu.roll(total, 0, 1, stride=1, stride_axis=0)
        images.append(jnp.sum(total, axis=0, keepdims=True))
    return images


def normal_of(images, samples_ref, moved_ref):
    cols = len(images)
    positions = images[0].shape[1]
    tiles = samples_ref.shape[0]
    tile = samples_ref.shape[-1]
    channels = samples_ref.shape[2] * samples_ref.shape[3]
    rows = cols * KER
    for k in range(cols):
        base = jnp.broadcast_to(images[k], (SUB, positions))
        base = pltpu.roll(base, positions - (KER - 1), 1, stride=1, stride_axis=0)
        for j in range(0, KER, 2 * SUB):
            first = base if j == 0 else pltpu.roll(base, j, 1)
            second = pltpu.roll(base, j + SUB, 1)
            high, low = split(jnp.concatenate([first, second], axis=0))
            moved_ref[k * KER + j : k * KER + j + 2 * SUB, :] = high
            moved_ref[rows + k * KER + j : rows + k * KER + j + 2 * SUB, :] = low
    total = jnp.zeros((2 * rows, 2 * channels), jnp.float32)
    for t in range(tiles):
        block = samples_ref[t].reshape(2 * channels, tile)
        total = total + dot(moved_ref[:, t * tile : (t + 1) * tile], block, ((1,), (1,)))
    return total[:rows, :channels] + (
        total[:rows, channels:] + total[rows:, :channels] + total[rows:, channels:]
    )


def store_by_rows(normal, send_ref):
    tiles, groups, per_tile, lanes = send_ref.shape
    cols = normal.shape[0] // KER
    chg = normal.shape[1] // groups
    for g in range(groups):
        joined = jnp.concatenate(
            [normal[k * KER : (k + 1) * KER, g * chg : (g + 1) * chg] for k in range(cols)], axis=1
        )
        send_ref[:, g] = joined.reshape(tiles, per_tile, lanes)


def store_by_groups(normal_ref, group_ref):
    groups, count, lanes = group_ref.shape
    rows, channels = normal_ref.shape
    chg = channels // groups
    fold = lanes // chg
    cols = rows // KER
    deep = KER // fold
    me = lax.axis_index("coil")
    parts = [
        [normal_ref[pl.ds(k * KER + f, deep, stride=fold), :] for f in range(fold)]
        for k in range(cols)
    ]
    for g in range(groups):
        joined = [
            jnp.concatenate([part[:, g * chg : (g + 1) * chg] for part in parts[k]], axis=1)
            for k in range(cols)
        ]
        group_ref[lax.bitwise_xor(me, g)] = jnp.concatenate(joined, axis=0)


def passes_kernel(orders, basis_ref, *refs):
    *pieces, samples_ref, normal_ref, send_ref, group_ref, wide_ref, moved_ref = refs
    tiles, _, groups, chg, tile = samples_ref.shape
    me = lax.axis_index("rows") * groups + lax.axis_index("coil")
    for (start, order), piece_ref in zip(orders, pieces):
        count = piece_ref.shape[1]
        for slot, mask in enumerate(order):
            high, low = split(piece_ref[slot])
            source = lax.bitwise_xor(me, mask)
            t, g = source // groups, source % groups
            samples_ref[t, 0, g, start : start + count] = high
            samples_ref[t, 1, g, start : start + count] = low
    cols = basis_ref.shape[-1] // chg
    rows = []
    for k in range(cols):
        rows.append(
            jnp.concatenate(
                [
                    basis_ref[:, g].reshape(KER, cols * chg)[:, k * chg : (k + 1) * chg]
                    for g in range(groups)
                ],
                axis=1,
            )
        )
    vectors = jnp.concatenate(rows, axis=0)
    normal = normal_of(images_of(vectors, samples_ref, wide_ref), samples_ref, moved_ref)
    power = jnp.zeros((1, tile), jnp.float32)
    for t in range(samples_ref.shape[0]):
        value = samples_ref[t, 0].reshape(groups * chg, tile).astype(jnp.float32)
        power = power + jnp.sum(value * value, axis=0, keepdims=True)
    normal = normal * (groups * chg / jnp.sum(power))
    normal = normal_of(images_of(normal, samples_ref, wide_ref), samples_ref, moved_ref)
    normal_ref[...] = normal
    store_by_rows(normal, send_ref)
    store_by_groups(normal_ref, group_ref)


def images_kernel(samples_ref, vectors_ref, send_ref, wide_ref):
    tiles, groups, cols, reach = send_ref.shape
    tile = samples_ref.shape[-1]
    images = jnp.concatenate(images_of(vectors_ref[...], samples_ref, wide_ref), axis=0)
    positions = images.shape[1]
    images = pltpu.roll(images, positions - (KER - 1), 1)
    rim = reach - tile
    for t in range(tiles):
        if t == 0:
            part = jnp.concatenate([images[:, positions - rim :], images[:, :tile]], axis=1)
        else:
            part = images[:, t * tile - rim : (t + 1) * tile]
        for g in range(groups):
            send_ref[t, g] = part


def gather_turned(received_ref, cols, per_tile):
    count, lanes = received_ref.shape
    devices = count // per_tile
    chg = lanes // cols
    loaded = [received_ref[pl.ds(j, devices, stride=per_tile), :] for j in range(per_tile)]
    return jnp.concatenate(
        [
            jnp.concatenate(
                [loaded[j][:, k * chg : (k + 1) * chg] for j in range(per_tile)], axis=1
            )
            for k in range(cols)
        ],
        axis=0,
    )


def exact(a, b, dims=((1,), (0,))):
    return lax.dot_general(
        a, b, (dims, ((), ())), precision=lax.Precision.HIGHEST, preferred_element_type=jnp.float32
    )


def gram_kernel(cols, per_tile, received_ref, basis_ref, kept_ref, given_ref, turned_ref):
    turned = gather_turned(received_ref, cols, per_tile)
    first = exact(basis_ref[...], turned, ((0,), (1,)))
    second = exact(turned, turned, ((1,), (1,)))
    turned_ref[...] = turned
    at_row, at_col = square(first.shape[0])
    packed = jnp.where(at_row >= at_col, first, second)
    line = jnp.sum(jnp.where(at_row == at_col, second, 0.0), axis=0, keepdims=True)
    line = jnp.broadcast_to(line, (SUB, line.shape[1]))
    half = packed.shape[0] // 2
    odd = lax.axis_index("coil") % 2 == 1
    kept_ref[:half] = jnp.where(odd, packed[half:], packed[:half])
    given_ref[:half] = jnp.where(odd, packed[:half], packed[half:])
    kept_ref[half:] = line
    given_ref[half:] = line


def load_grams(kept_ref, other_ref):
    odd = lax.axis_index("coil") % 2 == 1
    kept, other = kept_ref[...], other_ref[...]
    low, high = jnp.where(odd, other, kept), jnp.where(odd, kept, other)
    half = low.shape[0] - SUB
    packed = jnp.concatenate([low[:half], high[:half]], axis=0)
    line = low[half : half + 1]
    at_row, at_col = square(packed.shape[0])
    turned = packed.T
    first = jnp.where(at_row >= at_col, packed, turned)
    second = jnp.where(at_row > at_col, turned, packed)
    return first, jnp.where(at_row == at_col, line, second), line


def inverse_factor(gram):
    size = gram.shape[0]
    shape = (SUB, size)
    at_row = lax.broadcasted_iota(jnp.int32, (size, size), 0)
    at_col = lax.broadcasted_iota(jnp.int32, (size, size), 1)
    unit = (at_row == at_col).astype(jnp.float32)
    left = [gram[b : b + SUB] for b in range(0, size, SUB)]
    right = [unit[b : b + SUB] for b in range(0, size, SUB)]
    sub = lax.broadcasted_iota(jnp.int32, shape, 0)
    done = []
    for b in range(len(left)):
        spread = {
            c: [
                jnp.broadcast_to(left[c][:, b * SUB + k : b * SUB + k + 1], shape)
                for k in range(SUB)
            ]
            for c in range(b, len(left))
        }
        entry = {
            (i, k): jnp.broadcast_to(spread[b][k][i : i + 1], shape)
            for k in range(SUB)
            for i in range(k, SUB)
        }
        inverse = {}
        for k in range(SUB):
            root = lax.rsqrt(entry[k, k])
            inverse[k, k] = root
            for i in range(k + 1, SUB):
                entry[i, k] = entry[i, k] * root
            for i in range(k + 1, SUB):
                for m in range(k + 1, i + 1):
                    entry[i, m] = entry[i, m] - entry[i, k] * entry[m, k]
        for i in range(1, SUB):
            for k in range(i):
                total = entry[i, k] * inverse[k, k]
                for m in range(k + 1, i):
                    total = total + entry[i, m] * inverse[m, k]
                inverse[i, k] = -(total * inverse[i, i])

        def solved(rows):
            whole = [jnp.broadcast_to(rows[k : k + 1], shape) for k in range(SUB)]
            first = []
            for i in range(SUB):
                total = inverse[i, 0] * whole[0]
                for k in range(1, i + 1):
                    total = total + inverse[i, k] * whole[k]
                first.append(total)
            second = []
            for k in range(SUB):
                total = inverse[k, k] * first[k]
                for i in range(k + 1, SUB):
                    total = total + inverse[i, k] * first[i]
                second.append(total)
            return first, second

        lower, lower_again = solved(right[b])
        row = lower[0]
        for i in range(1, SUB):
            row = jnp.where(sub == i, lower[i], row)
        done.append(row)
        if b + 1 < len(left):
            _, upper_again = solved(left[b])
            for c in range(b + 1, len(left)):
                for k in range(SUB):
                    left[c] = left[c] - spread[c][k] * upper_again[k]
                    right[c] = right[c] - spread[c][k] * lower_again[k]
    return jnp.concatenate(done, axis=0)


def factor_kernel(gram_ref, other_ref, inverse_ref, next_ref, sound_ref):
    gram, raw, line = load_grams(gram_ref, other_ref)
    inverse = inverse_factor(gram)
    inverse_ref[...] = inverse
    gram = exact(exact(inverse, raw), inverse, ((1,), (1,)))
    next_ref[...] = gram
    at_row, at_col = square(gram.shape[0])
    terms = jnp.sum(inverse * inverse * line, axis=1, keepdims=True)
    result = jnp.sum(jnp.where(at_row == at_col, gram, 0.0), axis=1, keepdims=True)
    worst = jnp.max(jnp.where(terms <= 64.0 * result, 0, 1))
    sound_ref[0] = 1 - worst


def rows_kernel(turned_ref, inverse_ref, gram_ref):
    turned = exact(inverse_ref[...], turned_ref[...])
    gram_ref[...] = exact(turned, turned, ((1,), (1,)))


def both_kernel(gram_ref, inverse_ref, both_ref):
    both_ref[...] = exact(inverse_factor(gram_ref[...]), inverse_ref[...])


def moved_columns(order, cols):
    devices = len(order[0])
    at_row, at_col = square(devices * cols)
    turn = at_col % cols * devices + at_col // cols
    me = lax.axis_index("rows") * lax.axis_size("coil") + lax.axis_index("coil")
    slot = at_col % devices
    mask = jnp.zeros_like(slot)
    bit = 1
    while bit < devices:
        step = jnp.where(2 * at_col < at_col.shape[1], order[0][bit], order[1][bit])
        mask = mask | jnp.where(slot & bit != 0, step, 0)
        bit *= 2
    source = at_col - slot + lax.bitwise_xor(mask, jnp.full_like(mask, me))
    return [(at_row == place).astype(jnp.float32) for place in (turn, source)]


def stacked_dot(a, b):
    a_high, a_low = split(a)
    b_high, b_low = split(b)
    left = jnp.concatenate(
        [
            jnp.concatenate([a_high, a_high], axis=1),
            jnp.concatenate([a_low, jnp.zeros_like(a_low)], axis=1),
        ],
        axis=0,
    )
    both = dot(left, jnp.concatenate([b_high, b_low], axis=0))
    return both[: a.shape[0]] + both[a.shape[0] :]


def last_kernel(
    cols,
    order,
    images_ref,
    both_ref,
    kspace_ref,
    mask_ref,
    top_near_ref,
    top_far_ref,
    low_near_ref,
    low_far_ref,
    recovered_ref,
    basis_ref,
    vectors_ref,
):
    both = both_ref[...]
    reach = images_ref.shape[1]
    factors = [exact(both, moved) for moved in moved_columns(order, cols)]
    chg, tile = kspace_ref.shape
    lanes = top_near_ref.shape[1]
    fold = lanes // chg
    deep = KER // fold
    step = cols // 2 * deep
    lead = reach - tile - KER - 2 * SUB
    images = stacked_dot(factors[0], images_ref[...]).T[lead:]
    rim = reach - tile - SUB - lead
    even, odd = None, None
    for a in range(0, deep, 2):
        turned = [
            jnp.concatenate(
                [
                    ref[pl.ds(k * deep + a + i, ref.shape[0] // step, stride=step), :]
                    for refs in ((top_near_ref, top_far_ref), (low_near_ref, low_far_ref))
                    for k in range(cols // 2)
                    for ref in refs
                ],
                axis=0,
            )
            for i in range(2)
        ]
        vectors = stacked_dot(factors[1], jnp.concatenate(turned, axis=1))
        vectors_ref[:, a * lanes : (a + 2) * lanes] = vectors
        projected = stacked_dot(images, vectors)
        shift = a * fold
        part = projected[rim - shift : rim - shift + tile + SUB, :lanes]
        even = part if even is None else even + part
        part = projected[rim - SUB - shift : rim - shift + tile + SUB, lanes:]
        odd = part if odd is None else odd + part
    total = even + odd[SUB - fold : SUB - fold + tile + SUB]
    estimate = total[SUB : SUB + tile]
    for f in range(1, fold):
        moved = pltpu.roll(total, lanes - f * chg, 1)
        estimate = estimate + moved[SUB - f : SUB - f + tile]
    estimate = estimate.T[:chg]
    owned = basis_ref.shape[0]
    start = pl.multiple_of(lax.axis_index("rows") * owned, owned)
    basis_ref[...] = vectors_ref[:, pl.ds(start, owned)].T
    estimate = estimate / KER
    residual = mask_ref[...].astype(jnp.float32) * (kspace_ref[...] - estimate)
    recovered_ref[...] = estimate + residual - jnp.clip(residual, -threshold, threshold)


def call(kernel, outs, *args, scratch=(), limit=12, scalars=0, micros=1):
    return pl.pallas_call(
        kernel,
        out_shape=[jax.ShapeDtypeStruct(shape, kind) for shape, kind in outs],
        in_specs=[pl.BlockSpec(memory_space=pltpu.VMEM)] * len(args),
        out_specs=[pl.BlockSpec(memory_space=pltpu.VMEM)] * (len(outs) - scalars)
        + [pl.BlockSpec(memory_space=pltpu.SMEM)] * scalars,
        scratch_shapes=list(scratch),
        compiler_params=pltpu.CompilerParams(vmem_limit_bytes=limit * 2**20),
        cost_estimate=pl.CostEstimate(
            flops=micros * 10**9, bytes_accessed=0, transcendentals=0
        ),
    )(*args)


def exchange(block, devices, mask, axes):
    return lax.ppermute(block, axes, [(i, i ^ mask) for i in range(devices)])


def with_masks(masks, mask):
    return masks + [m ^ mask for m in masks]


def after(value, *others):
    return lax.optimization_barrier((value,) + others)[0]


def rounds_of(low, high):
    masks = []
    while low < high:
        if 2 * low < high:
            masks.append([low, 2 * low, 3 * low])
        else:
            masks.append([low])
        low *= 4
    return masks


def gather_round(part, order, masks, devices, axes):
    part = jnp.concatenate(
        [part] + [exchange(part, devices, mask, axes) for mask in masks], axis=0
    )
    return part, order + [m ^ mask for mask in masks for m in order]


def gather_samples(sampled, basis, tiles, groups):
    devices = tiles * groups
    near, masks = sampled[None], [0]
    mask = devices // 2
    while mask > groups:
        near, masks = gather_round(near, masks, [mask], devices, AXES)
        mask //= 2
    basis = to_all(basis)
    near = after(near, basis)
    half = near.shape[1] // 2
    halves = []
    for part, ways in (
        (near[:, :half], (groups, groups // 2)),
        (near[:, half:], (groups // 2, groups)),
    ):
        part, order = gather_round(part, masks, [ways[0]], devices, AXES)
        pieces = [(part, order)]
        mask = ways[1]
        rest = groups // 4
        while mask > 1:
            pieces = pieces + [
                (exchange(part, devices, mask, AXES), [m ^ mask for m in order])
                for part, order in pieces
            ]
            mask, rest = rest, rest // 2
        halves.append(
            pieces
            + [(exchange(part, devices, 1, AXES), [m ^ 1 for m in order]) for part, order in pieces]
        )
    return halves, basis


def to_all(pieces, axes=AXES):
    return lax.all_to_all(pieces, axes, 0, 0, tiled=True)


def gather_group(group, devices):
    groups = group.shape[0]
    parts = [group[:1]]
    parts += [exchange(group[s : s + 1], devices, s, AXES) for s in range(1, groups)]
    return jnp.concatenate(parts, axis=0), list(range(groups))


def total_beside(kept, given, near, order, images, groups, devices):
    ways = []
    mask = devices // 2
    while mask >= groups:
        ways.append(mask)
        mask //= 2
    half = near.shape[1] // 2
    parts = [near[:, :half], near[:, half:]]
    orders = [order, order]
    ways = [ways, ways[-1:] + ways[:-1]]
    step = 0

    def advance():
        for i in range(2):
            parts[i], orders[i] = gather_round(
                parts[i], orders[i], [ways[i][step]], devices, AXES
            )

    total = kept + exchange(given, devices, 1, AXES)
    for partners in rounds_of(2, devices):
        terms = [exchange(total, devices, way, AXES) for way in partners]
        total = total + terms[0]
        if len(terms) == 3:
            total = total + (terms[1] + terms[2])
        if step < len(ways[0]) - 1:
            advance()
            step += 1
    while step < len(ways[0]) - 1:
        advance()
        step += 1
    other = exchange(total, devices, 1, AXES)
    *parts, total, other, images = lax.optimization_barrier((*parts, total, other, images))
    pieces = []
    for i in range(2):
        mask = ways[i][-1]
        pieces += [parts[i], exchange(parts[i], devices, mask, AXES)]
        orders[i] = orders[i] + [m ^ mask for m in orders[i]]
    return (total, other), pieces, orders, to_all(images)


def column_shards(kspace, sample_mask, start_basis):
    f32, bf16 = jnp.float32, jnp.bfloat16
    tiles, groups = lax.axis_size("rows"), lax.axis_size("coil")
    devices = tiles * groups
    chg, tile = kspace.shape
    channels = chg * groups
    positions = tile * tiles
    owned, rank = start_basis.shape[1:]
    per_tile = owned // chg
    cols = rank // devices
    rows = cols * KER
    lanes = cols * chg

    sampled = kspace * sample_mask.astype(f32)
    (basis_send,) = call(
        functools.partial(prepare_kernel, cols, chg, per_tile),
        [((devices * per_tile, lanes), f32)],
        start_basis.reshape(owned, rank),
    )
    halves, basis_parts = gather_samples(
        sampled, basis_send.reshape(devices, per_tile, lanes), tiles, groups
    )
    starts = (0, chg // len(halves))
    orders = [(start, order) for start, half in zip(starts, halves) for _, order in half]
    wide = pltpu.VMEM((rows, positions), f32)
    moved = pltpu.VMEM((2 * rows, positions), bf16)
    samples, normal, send, group = call(
        functools.partial(passes_kernel, orders),
        [
            ((tiles, 2, groups, chg, tile), bf16),
            ((rows, channels), f32),
            ((tiles, groups, per_tile, lanes), f32),
            ((groups, rows * chg // lanes, lanes), f32),
        ],
        basis_parts.reshape(tiles, groups, per_tile, lanes),
        *[piece for half in halves for piece, _ in half],
        scratch=[wide, moved],
        limit=24,
        micros=12,
    )
    received = to_all(send.reshape(devices, per_tile, lanes))
    reach = tile + LANES
    (images,) = call(
        images_kernel,
        [((tiles, groups, cols, reach), f32)],
        samples,
        normal,
        scratch=[wide],
        limit=16,
        micros=2,
    )
    near, order = gather_group(group, devices)
    received, near = lax.optimization_barrier((received, images, near))[::2]
    half = ((rank // 2 + SUB, rank), f32)
    kept, given, turned = call(
        functools.partial(gram_kernel, cols, per_tile),
        [half, half, ((rank, owned), f32)],
        received.reshape(devices * per_tile, lanes),
        start_basis.reshape(owned, rank),
    )
    gram, pieces, order, images = total_beside(
        kept, given, near, order, images.reshape(devices, cols, reach), groups, devices
    )
    whole = ((rank, rank), f32)
    first, second, sound = call(
        factor_kernel, [whole, whole, ((1,), jnp.int32)], *gram, scalars=1, micros=12
    )

    def again():
        (gram,) = call(rows_kernel, [whole], turned, first)
        mask = 1
        while mask < devices:
            gram = gram + exchange(gram, devices, mask, AXES)
            mask *= 2
        return gram

    second = lax.cond(sound[0] == 1, lambda: second, again)
    (both,) = call(both_kernel, [whole], second, first, micros=0)
    recovered, basis = call(
        functools.partial(last_kernel, cols, order),
        [((chg, tile), f32), ((owned, rank), f32)],
        images.reshape(rank, reach),
        both,
        kspace,
        sample_mask,
        *[piece.reshape(-1, lanes) for piece in pieces],
        scratch=[pltpu.VMEM((rank, KER * chg), f32)],
        limit=16,
        micros=5,
    )
    return (recovered, basis.reshape(1, owned, rank))


def divides_columns(kspace, start_basis):
    tiles, groups = lax.axis_size("rows"), lax.axis_size("coil")
    devices = tiles * groups
    chg, tile = kspace.shape
    owned, rank = start_basis.shape[1:]
    return (
        devices & (devices - 1) == 0
        and tiles > 2
        and groups > 2
        and rank % (2 * SUB) == 0
        and rank % devices == 0
        and rank % LANES == 0
        and tile % LANES == 0
        and owned == SUB * chg
        and chg * (rank // devices) == LANES
        and 2 * (LANES // chg) == SUB
        and KER + 2 * SUB <= LANES
        and chg % (4 * SUB) == 0
        and (chg * groups) % LANES == 0
        and KER <= LANES
        and rank // devices <= SUB
        and rank // devices % 2 == 0
    )


def shards(kspace, sample_mask, start_basis):
    if divides_columns(kspace, start_basis):
        return column_shards(kspace, sample_mask, start_basis)
    return general_shards(kspace, sample_mask, start_basis)


def solution(mesh):
    return jax.shard_map(
        shards,
        mesh=mesh,
        in_specs=(P("coil", "rows"), P("coil", "rows"), P("coil", "rows", None)),
        out_specs=(P("coil", "rows"), P("coil", "rows", None)),
        check_vma=False,
    )
```

```python
import functools

import jax
import jax.numpy as jnp
from jax import lax
from jax.experimental import pallas as pl
from jax.experimental.pallas import tpu as pltpu
from jax.sharding import PartitionSpec as P

KER = 64
ITERS = 2
LANES = 128
SUB = 8
AXES = ("rows", "coil")


threshold = 0.05


def shifted(block, axis, distance):
    devices = range(lax.axis_size(axis))
    route = [((i - distance) % len(devices), i) for i in devices]
    return lax.ppermute(block, axis, route)


def orthonormal(normal_rows, gram_matrix):
    factor = jnp.linalg.cholesky(gram_matrix)
    return lax.linalg.triangular_solve(
        factor, normal_rows, left_side=False, lower=True, transpose_a=True
    )


def coil_total(partial_value):
    return lax.psum(partial_value, "coil")


def general_shards(kspace, sample_mask, start_basis):
    highest = lax.Precision.HIGHEST
    channels = kspace.shape[0]
    tile_rows = kspace.shape[1]
    mask_float = sample_mask.astype(jnp.float32)
    sampled = kspace * mask_float
    next_rim = shifted(sampled[:, : KER - 1], "rows", -1)
    extended = jnp.concatenate([sampled, next_rim], axis=1)
    hankel_cols = jnp.stack(
        [extended[:, offset : offset + tile_rows] for offset in range(KER)], axis=0
    )
    hankel_cols = hankel_cols.reshape(KER * channels, tile_rows)
    owned_basis = start_basis.reshape(start_basis.shape[1], start_basis.shape[2])
    whole_basis = lax.all_gather(owned_basis, "rows", axis=0, tiled=True)
    for iteration in range(ITERS):
        images = coil_total(
            lax.dot_general(
                whole_basis,
                hankel_cols,
                (((0,), (0,)), ((), ())),
                precision=highest,
                preferred_element_type=jnp.float32,
            )
        )
        local_normal = lax.dot_general(
            hankel_cols,
            images,
            (((1,), (1,)), ((), ())),
            precision=highest,
            preferred_element_type=jnp.float32,
        )
        normal_whole = lax.psum(local_normal, "rows")
        local_gram = jnp.dot(
            normal_whole.T, normal_whole, precision=highest, preferred_element_type=jnp.float32
        )
        gram_matrix = lax.psum(local_gram, "coil")
        whole_basis = orthonormal(normal_whole, gram_matrix)
    images = coil_total(
        lax.dot_general(
            whole_basis,
            hankel_cols,
            (((0,), (0,)), ((), ())),
            precision=highest,
            preferred_element_type=jnp.float32,
        )
    )
    projected = jnp.dot(whole_basis, images, precision=highest, preferred_element_type=jnp.float32)
    owned_count = whole_basis.shape[0] // lax.axis_size("rows")
    owned_basis = lax.dynamic_slice_in_dim(
        whole_basis, lax.axis_index("rows") * owned_count, owned_count, 0
    )
    stacked = projected.reshape(KER, channels, tile_rows)
    spread = jnp.zeros((channels, tile_rows + KER - 1), jnp.float32)
    for offset in range(KER):
        spread = spread.at[:, offset : offset + tile_rows].add(stacked[offset])
    carried = shifted(spread[:, tile_rows:], "rows", 1)
    estimate = spread[:, :tile_rows].at[:, : KER - 1].add(carried) / KER
    residual = mask_float * (kspace - estimate)
    recovered = estimate + residual - jnp.clip(residual, -threshold, threshold)
    return (recovered, owned_basis.reshape(1, owned_basis.shape[0], owned_basis.shape[1]))


def split(value):
    high = value.astype(jnp.bfloat16)
    low = (value - high.astype(jnp.float32)).astype(jnp.bfloat16)
    return high, low


def dot(a, b, dims=((1,), (0,))):
    return lax.dot_general(a, b, (dims, ((), ())), preferred_element_type=jnp.float32)


def dot3(a, b, dims=((1,), (0,))):
    a_high, a_low = split(a)
    b_high, b_low = split(b)
    return dot(a_high, b_high, dims) + (dot(a_high, b_low, dims) + dot(a_low, b_high, dims))


def square(size):
    at_row = lax.broadcasted_iota(jnp.int32, (size, size), 0)
    at_col = lax.broadcasted_iota(jnp.int32, (size, size), 1)
    return at_row, at_col


def prepare_kernel(cols, chg, per_tile, basis_ref, send_ref):
    turned = basis_ref[...].T
    devices = turned.shape[0] // cols
    for j in range(per_tile):
        part = turned[:, j * chg : (j + 1) * chg]
        row = jnp.concatenate([part[k * devices : (k + 1) * devices] for k in range(cols)], axis=1)
        send_ref[pl.ds(j, devices, stride=per_tile), :] = row


def images_of(vectors, samples_ref, wide_ref):
    rows, channels = vectors.shape
    cols = rows // KER
    high, low = split(vectors)
    at_row = lax.broadcasted_iota(jnp.int32, (rows, rows), 0)
    at_col = lax.broadcasted_iota(jnp.int32, (rows, rows), 1)
    flip = ((at_row // KER == at_col // KER) & (at_row % KER + at_col % KER == KER - 1)).astype(
        jnp.float32
    ).astype(jnp.bfloat16)
    both = dot(flip, jnp.concatenate([high, low], axis=1)).astype(jnp.bfloat16)
    high, low = both[:, :channels], both[:, channels:]
    twice = jnp.concatenate([high, high], axis=1)
    tiles = samples_ref.shape[0]
    tile = samples_ref.shape[-1]
    for t in range(tiles):
        block = samples_ref[t].reshape(2 * channels, tile)
        wide_ref[:, t * tile : (t + 1) * tile] = dot(twice, block) + dot(low, block[:channels])
    images = []
    for k in range(cols):
        total = None
        for i in reversed(range(0, KER, SUB)):
            part = wide_ref[k * KER + i : k * KER + i + SUB, :]
            total = part if total is None else pltpu.roll(total, SUB, 1) + part
        total = pltpu.roll(total, 0, 1, stride=1, stride_axis=0)
        images.append(jnp.sum(total, axis=0, keepdims=True))
    return images


def normal_of(images, samples_ref, moved_ref):
    cols = len(images)
    positions = images[0].shape[1]
    tiles = samples_ref.shape[0]
    tile = samples_ref.shape[-1]
    channels = samples_ref.shape[2] * samples_ref.shape[3]
    rows = cols * KER
    for k in range(cols):
        base = jnp.broadcast_to(images[k], (SUB, positions))
        base = pltpu.roll(base, positions - (KER - 1), 1, stride=1, stride_axis=0)
        for j in range(0, KER, 2 * SUB):
            first = base if j == 0 else pltpu.roll(base, j, 1)
            second = pltpu.roll(base, j + SUB, 1)
            high, low = split(jnp.concatenate([first, second], axis=0))
            moved_ref[k * KER + j : k * KER + j + 2 * SUB, :] = high
            moved_ref[rows + k * KER + j : rows + k * KER + j + 2 * SUB, :] = low
    high = jnp.zeros((rows, 2 * channels), jnp.float32)
    low = jnp.zeros((rows, channels), jnp.float32)
    for t in range(tiles):
        block = samples_ref[t].reshape(2 * channels, tile)
        lanes = slice(t * tile, (t + 1) * tile)
        high = high + dot(moved_ref[:rows, lanes], block, ((1,), (1,)))
        low = low + dot(moved_ref[rows:, lanes], block[:channels], ((1,), (1,)))
    return high[:, :channels] + (high[:, channels:] + low)


def store_by_rows(normal, send_ref):
    tiles, groups, per_tile, lanes = send_ref.shape
    cols = normal.shape[0] // KER
    chg = normal.shape[1] // groups
    for g in range(groups):
        joined = jnp.concatenate(
            [normal[k * KER : (k + 1) * KER, g * chg : (g + 1) * chg] for k in range(cols)], axis=1
        )
        send_ref[:, g] = joined.reshape(tiles, per_tile, lanes)


def store_by_groups(normal_ref, group_ref):
    groups, count, lanes = group_ref.shape
    rows, channels = normal_ref.shape
    chg = channels // groups
    fold = lanes // chg
    cols = rows // KER
    deep = KER // fold
    me = lax.axis_index("coil")
    parts = [
        [normal_ref[pl.ds(k * KER + f, deep, stride=fold), :] for f in range(fold)]
        for k in range(cols)
    ]
    for g in range(groups):
        joined = [
            jnp.concatenate([part[:, g * chg : (g + 1) * chg] for part in parts[k]], axis=1)
            for k in range(cols)
        ]
        group_ref[lax.bitwise_xor(me, g)] = jnp.concatenate(joined, axis=0)


def passes_kernel(orders, basis_ref, *refs):
    *pieces, samples_ref, normal_ref, send_ref, group_ref, wide_ref, moved_ref = refs
    tiles, _, groups, chg, tile = samples_ref.shape
    me = lax.axis_index("rows") * groups + lax.axis_index("coil")
    for (start, order), piece_ref in zip(orders, pieces):
        count = piece_ref.shape[1]
        for slot, mask in enumerate(order):
            high, low = split(piece_ref[slot])
            source = lax.bitwise_xor(me, mask)
            t, g = source // groups, source % groups
            samples_ref[t, 0, g, start : start + count] = high
            samples_ref[t, 1, g, start : start + count] = low
    cols = basis_ref.shape[-1] // chg
    rows = []
    for k in range(cols):
        rows.append(
            jnp.concatenate(
                [
                    basis_ref[:, g].reshape(KER, cols * chg)[:, k * chg : (k + 1) * chg]
                    for g in range(groups)
                ],
                axis=1,
            )
        )
    vectors = jnp.concatenate(rows, axis=0)
    normal = normal_of(images_of(vectors, samples_ref, wide_ref), samples_ref, moved_ref)
    power = jnp.zeros((1, tile), jnp.float32)
    for t in range(samples_ref.shape[0]):
        value = samples_ref[t, 0].reshape(groups * chg, tile).astype(jnp.float32)
        power = power + jnp.sum(value * value, axis=0, keepdims=True)
    normal = normal * (groups * chg / jnp.sum(power))
    normal = normal_of(images_of(normal, samples_ref, wide_ref), samples_ref, moved_ref)
    normal_ref[...] = normal
    store_by_rows(normal, send_ref)
    store_by_groups(normal_ref, group_ref)


def images_kernel(samples_ref, vectors_ref, send_ref, wide_ref):
    tiles, groups, cols, reach = send_ref.shape
    tile = samples_ref.shape[-1]
    images = jnp.concatenate(images_of(vectors_ref[...], samples_ref, wide_ref), axis=0)
    positions = images.shape[1]
    images = pltpu.roll(images, positions - (KER - 1), 1)
    rim = reach - tile
    for t in range(tiles):
        if t == 0:
            part = jnp.concatenate([images[:, positions - rim :], images[:, :tile]], axis=1)
        else:
            part = images[:, t * tile - rim : (t + 1) * tile]
        for g in range(groups):
            send_ref[t, g] = part


def gather_turned(received_ref, cols, per_tile):
    count, lanes = received_ref.shape
    devices = count // per_tile
    chg = lanes // cols
    loaded = [received_ref[pl.ds(j, devices, stride=per_tile), :] for j in range(per_tile)]
    return jnp.concatenate(
        [
            jnp.concatenate(
                [loaded[j][:, k * chg : (k + 1) * chg] for j in range(per_tile)], axis=1
            )
            for k in range(cols)
        ],
        axis=0,
    )


def exact(a, b, dims=((1,), (0,))):
    return lax.dot_general(
        a, b, (dims, ((), ())), precision=lax.Precision.HIGHEST, preferred_element_type=jnp.float32
    )


def gram_kernel(cols, per_tile, received_ref, basis_ref, kept_ref, given_ref, turned_ref):
    turned = gather_turned(received_ref, cols, per_tile)
    first = exact(basis_ref[...], turned, ((0,), (1,)))
    second = exact(turned, turned, ((1,), (1,)))
    turned_ref[...] = turned
    at_row, at_col = square(first.shape[0])
    packed = jnp.where(at_row >= at_col, first, second)
    line = jnp.sum(jnp.where(at_row == at_col, second, 0.0), axis=0, keepdims=True)
    line = jnp.broadcast_to(line, (SUB, line.shape[1]))
    half = packed.shape[0] // 2
    odd = lax.axis_index("coil") % 2 == 1
    kept_ref[:half] = jnp.where(odd, packed[half:], packed[:half])
    given_ref[:half] = jnp.where(odd, packed[:half], packed[half:])
    kept_ref[half:] = line
    given_ref[half:] = line


def load_grams(kept_ref, other_ref):
    odd = lax.axis_index("coil") % 2 == 1
    kept, other = kept_ref[...], other_ref[...]
    low, high = jnp.where(odd, other, kept), jnp.where(odd, kept, other)
    half = low.shape[0] - SUB
    packed = jnp.concatenate([low[:half], high[:half]], axis=0)
    line = low[half : half + 1]
    at_row, at_col = square(packed.shape[0])
    turned = packed.T
    first = jnp.where(at_row >= at_col, packed, turned)
    second = jnp.where(at_row > at_col, turned, packed)
    return first, jnp.where(at_row == at_col, line, second), line


def inverse_factor(gram):
    size = gram.shape[0]
    shape = (SUB, size)
    at_row = lax.broadcasted_iota(jnp.int32, (size, size), 0)
    at_col = lax.broadcasted_iota(jnp.int32, (size, size), 1)
    unit = (at_row == at_col).astype(jnp.float32)
    left = [gram[b : b + SUB] for b in range(0, size, SUB)]
    right = [unit[b : b + SUB] for b in range(0, size, SUB)]
    sub = lax.broadcasted_iota(jnp.int32, shape, 0)
    done = []
    for b in range(len(left)):
        spread = {
            c: [
                jnp.broadcast_to(left[c][:, b * SUB + k : b * SUB + k + 1], shape)
                for k in range(SUB)
            ]
            for c in range(b, len(left))
        }
        entry = {
            (i, k): jnp.broadcast_to(spread[b][k][i : i + 1], shape)
            for k in range(SUB)
            for i in range(k, SUB)
        }
        inverse = {}
        for k in range(SUB):
            root = lax.rsqrt(entry[k, k])
            inverse[k, k] = root
            for i in range(k + 1, SUB):
                entry[i, k] = entry[i, k] * root
            for i in range(k + 1, SUB):
                for m in range(k + 1, i + 1):
                    entry[i, m] = entry[i, m] - entry[i, k] * entry[m, k]
        for i in range(1, SUB):
            for k in range(i):
                total = entry[i, k] * inverse[k, k]
                for m in range(k + 1, i):
                    total = total + entry[i, m] * inverse[m, k]
                inverse[i, k] = -(total * inverse[i, i])

        def solved(rows):
            whole = [jnp.broadcast_to(rows[k : k + 1], shape) for k in range(SUB)]
            first = []
            for i in range(SUB):
                total = inverse[i, 0] * whole[0]
                for k in range(1, i + 1):
                    total = total + inverse[i, k] * whole[k]
                first.append(total)
            second = []
            for k in range(SUB):
                total = inverse[k, k] * first[k]
                for i in range(k + 1, SUB):
                    total = total + inverse[i, k] * first[i]
                second.append(total)
            return first, second

        lower, lower_again = solved(right[b])
        row = lower[0]
        for i in range(1, SUB):
            row = jnp.where(sub == i, lower[i], row)
        done.append(row)
        if b + 1 < len(left):
            _, upper_again = solved(left[b])
            for c in range(b + 1, len(left)):
                for k in range(SUB):
                    left[c] = left[c] - spread[c][k] * upper_again[k]
                    right[c] = right[c] - spread[c][k] * lower_again[k]
    return jnp.concatenate(done, axis=0)


def factor_kernel(gram_ref, other_ref, inverse_ref, next_ref, sound_ref):
    gram, raw, line = load_grams(gram_ref, other_ref)
    inverse = inverse_factor(gram)
    inverse_ref[...] = inverse
    gram = exact(exact(inverse, raw), inverse, ((1,), (1,)))
    next_ref[...] = gram
    at_row, at_col = square(gram.shape[0])
    terms = jnp.sum(inverse * inverse * line, axis=1, keepdims=True)
    result = jnp.sum(jnp.where(at_row == at_col, gram, 0.0), axis=1, keepdims=True)
    worst = jnp.max(jnp.where(terms <= 64.0 * result, 0, 1))
    sound_ref[0] = 1 - worst


def rows_kernel(turned_ref, inverse_ref, gram_ref):
    turned = exact(inverse_ref[...], turned_ref[...])
    gram_ref[...] = exact(turned, turned, ((1,), (1,)))


def both_kernel(gram_ref, inverse_ref, both_ref):
    both_ref[...] = exact(inverse_factor(gram_ref[...]), inverse_ref[...])


def moved_columns(order, cols):
    devices = len(order)
    at_row, at_col = square(devices * cols)
    turn = at_col % cols * devices + at_col // cols
    me = lax.axis_index("rows") * lax.axis_size("coil") + lax.axis_index("coil")
    slot = at_col % devices
    mask = jnp.zeros_like(slot)
    bit = 1
    while bit < devices:
        mask = mask | jnp.where(slot & bit != 0, order[bit], 0)
        bit *= 2
    source = at_col - slot + lax.bitwise_xor(mask, jnp.full_like(mask, me))
    return [(at_row == place).astype(jnp.float32) for place in (turn, source)]


def stacked_dot(a, b):
    a_high, a_low = split(a)
    b_high, b_low = split(b)
    left = jnp.concatenate(
        [
            jnp.concatenate([a_high, a_high], axis=1),
            jnp.concatenate([a_low, jnp.zeros_like(a_low)], axis=1),
        ],
        axis=0,
    )
    both = dot(left, jnp.concatenate([b_high, b_low], axis=0))
    return both[: a.shape[0]] + both[a.shape[0] :]


def last_kernel(
    cols,
    order,
    images_ref,
    both_ref,
    kspace_ref,
    mask_ref,
    near_ref,
    far_ref,
    recovered_ref,
    basis_ref,
    vectors_ref,
):
    both = both_ref[...]
    reach = images_ref.shape[1]
    factors = [exact(both, moved) for moved in moved_columns(order, cols)]
    chg, tile = kspace_ref.shape
    lanes = near_ref.shape[1]
    fold = lanes // chg
    deep = KER // fold
    step = cols * deep
    lead = reach - tile - KER - 2 * SUB
    images = stacked_dot(factors[0], images_ref[...]).T[lead:]
    rim = reach - tile - SUB - lead
    even, odd = None, None
    for a in range(0, deep, 2):
        turned = [
            jnp.concatenate(
                [
                    ref[pl.ds(k * deep + a + i, ref.shape[0] // step, stride=step), :]
                    for k in range(cols)
                    for ref in (near_ref, far_ref)
                ],
                axis=0,
            )
            for i in range(2)
        ]
        vectors = stacked_dot(factors[1], jnp.concatenate(turned, axis=1))
        vectors_ref[:, a * lanes : (a + 2) * lanes] = vectors
        projected = stacked_dot(images, vectors)
        shift = a * fold
        part = projected[rim - shift : rim - shift + tile + SUB, :lanes]
        even = part if even is None else even + part
        part = projected[rim - SUB - shift : rim - shift + tile + SUB, lanes:]
        odd = part if odd is None else odd + part
    total = even + odd[SUB - fold : SUB - fold + tile + SUB]
    estimate = total[SUB : SUB + tile]
    for f in range(1, fold):
        moved = pltpu.roll(total, lanes - f * chg, 1)
        estimate = estimate + moved[SUB - f : SUB - f + tile]
    estimate = estimate.T[:chg]
    owned = basis_ref.shape[0]
    start = pl.multiple_of(lax.axis_index("rows") * owned, owned)
    basis_ref[...] = vectors_ref[:, pl.ds(start, owned)].T
    estimate = estimate / KER
    residual = mask_ref[...].astype(jnp.float32) * (kspace_ref[...] - estimate)
    recovered_ref[...] = estimate + residual - jnp.clip(residual, -threshold, threshold)


def call(kernel, outs, *args, scratch=(), limit=12, scalars=0, micros=1):
    return pl.pallas_call(
        kernel,
        out_shape=[jax.ShapeDtypeStruct(shape, kind) for shape, kind in outs],
        in_specs=[pl.BlockSpec(memory_space=pltpu.VMEM)] * len(args),
        out_specs=[pl.BlockSpec(memory_space=pltpu.VMEM)] * (len(outs) - scalars)
        + [pl.BlockSpec(memory_space=pltpu.SMEM)] * scalars,
        scratch_shapes=list(scratch),
        compiler_params=pltpu.CompilerParams(vmem_limit_bytes=limit * 2**20),
        cost_estimate=pl.CostEstimate(
            flops=micros * 10**9, bytes_accessed=0, transcendentals=0
        ),
    )(*args)


def exchange(block, devices, mask, axes):
    return lax.ppermute(block, axes, [(i, i ^ mask) for i in range(devices)])


def with_masks(masks, mask):
    return masks + [m ^ mask for m in masks]


def after(value, *others):
    return lax.optimization_barrier((value,) + others)[0]


def rounds_of(low, high):
    masks = []
    while low < high:
        if 2 * low < high:
            masks.append([low, 2 * low, 3 * low])
        else:
            masks.append([low])
        low *= 4
    return masks


def gather_round(part, order, masks, devices, axes):
    part = jnp.concatenate(
        [part] + [exchange(part, devices, mask, axes) for mask in masks], axis=0
    )
    return part, order + [m ^ mask for mask in masks for m in order]


def gather_samples(sampled, basis, tiles, groups):
    devices = tiles * groups
    near, masks = sampled[None], [0]
    mask = devices // 2
    while mask > groups:
        near, masks = gather_round(near, masks, [mask], devices, AXES)
        mask //= 2
    basis = to_all(basis)
    near = after(near, basis)
    half = near.shape[1] // 2
    halves = []
    for part, ways in (
        (near[:, :half], (groups, groups // 2)),
        (near[:, half:], (groups // 2, groups)),
    ):
        part, order = gather_round(part, masks, [ways[0]], devices, AXES)
        pieces = [(part, order)]
        mask = ways[1]
        rest = groups // 4
        while mask > 1:
            pieces = pieces + [
                (exchange(part, devices, mask, AXES), [m ^ mask for m in order])
                for part, order in pieces
            ]
            mask, rest = rest, rest // 2
        halves.append(
            pieces
            + [(exchange(part, devices, 1, AXES), [m ^ 1 for m in order]) for part, order in pieces]
        )
    return halves, basis


def to_all(pieces, axes=AXES):
    return lax.all_to_all(pieces, axes, 0, 0, tiled=True)


def gather_group(group, devices):
    groups = group.shape[0]
    parts = [group[:1]]
    parts += [exchange(group[s : s + 1], devices, s, AXES) for s in range(1, groups)]
    return jnp.concatenate(parts, axis=0), list(range(groups))


def total_beside(kept, given, near, order, images, groups, devices):
    total = kept + exchange(given, devices, 1, AXES)
    step = devices // 2
    for number, partners in enumerate(rounds_of(2, devices)):
        terms = [exchange(total, devices, way, AXES) for way in partners]
        total = total + terms[0]
        if len(terms) == 3:
            total = total + (terms[1] + terms[2])
        if step > groups:
            near, order = gather_round(near, order, [step], devices, AXES)
            step //= 2
            if number == 0:
                near, total = lax.optimization_barrier((near, total))
    while step > groups:
        near, order = gather_round(near, order, [step], devices, AXES)
        step //= 2
    other = exchange(total, devices, 1, AXES)
    near, total, other, images = lax.optimization_barrier((near, total, other, images))
    far = exchange(near, devices, groups, AXES)
    return (total, other), near, far, order + [m ^ groups for m in order], to_all(images)


def column_shards(kspace, sample_mask, start_basis):
    f32, bf16 = jnp.float32, jnp.bfloat16
    tiles, groups = lax.axis_size("rows"), lax.axis_size("coil")
    devices = tiles * groups
    chg, tile = kspace.shape
    channels = chg * groups
    positions = tile * tiles
    owned, rank = start_basis.shape[1:]
    per_tile = owned // chg
    cols = rank // devices
    rows = cols * KER
    lanes = cols * chg

    sampled = kspace * sample_mask.astype(f32)
    (basis_send,) = call(
        functools.partial(prepare_kernel, cols, chg, per_tile),
        [((devices * per_tile, lanes), f32)],
        start_basis.reshape(owned, rank),
    )
    halves, basis_parts = gather_samples(
        sampled, basis_send.reshape(devices, per_tile, lanes), tiles, groups
    )
    starts = (0, chg // len(halves))
    orders = [(start, order) for start, half in zip(starts, halves) for _, order in half]
    wide = pltpu.VMEM((rows, positions), f32)
    moved = pltpu.VMEM((2 * rows, positions), bf16)
    samples, normal, send, group = call(
        functools.partial(passes_kernel, orders),
        [
            ((tiles, 2, groups, chg, tile), bf16),
            ((rows, channels), f32),
            ((tiles, groups, per_tile, lanes), f32),
            ((groups, rows * chg // lanes, lanes), f32),
        ],
        basis_parts.reshape(tiles, groups, per_tile, lanes),
        *[piece for half in halves for piece, _ in half],
        scratch=[wide, moved],
        limit=24,
        micros=12,
    )
    received = to_all(send.reshape(devices, per_tile, lanes))
    reach = tile + LANES
    (images,) = call(
        images_kernel,
        [((tiles, groups, cols, reach), f32)],
        samples,
        normal,
        scratch=[wide],
        limit=16,
        micros=2,
    )
    near, order = gather_group(group, devices)
    received, near = lax.optimization_barrier((received, images, near))[::2]
    half = ((rank // 2 + SUB, rank), f32)
    kept, given, turned = call(
        functools.partial(gram_kernel, cols, per_tile),
        [half, half, ((rank, owned), f32)],
        received.reshape(devices * per_tile, lanes),
        start_basis.reshape(owned, rank),
    )
    gram, near, far, order, images = total_beside(
        kept, given, near, order, images.reshape(devices, cols, reach), groups, devices
    )
    whole = ((rank, rank), f32)
    first, second, sound = call(
        factor_kernel, [whole, whole, ((1,), jnp.int32)], *gram, scalars=1, micros=12
    )

    def again():
        (gram,) = call(rows_kernel, [whole], turned, first)
        mask = 1
        while mask < devices:
            gram = gram + exchange(gram, devices, mask, AXES)
            mask *= 2
        return gram

    second = lax.cond(sound[0] == 1, lambda: second, again)
    (both,) = call(both_kernel, [whole], second, first, micros=0)
    recovered, basis = call(
        functools.partial(last_kernel, cols, order),
        [((chg, tile), f32), ((owned, rank), f32)],
        images.reshape(rank, reach),
        both,
        kspace,
        sample_mask,
        near.reshape(-1, lanes),
        far.reshape(-1, lanes),
        scratch=[pltpu.VMEM((rank, KER * chg), f32)],
        limit=16,
        micros=5,
    )
    return (recovered, basis.reshape(1, owned, rank))


def divides_columns(kspace, start_basis):
    tiles, groups = lax.axis_size("rows"), lax.axis_size("coil")
    devices = tiles * groups
    chg, tile = kspace.shape
    owned, rank = start_basis.shape[1:]
    return (
        devices & (devices - 1) == 0
        and tiles > 2
        and groups > 2
        and rank % (2 * SUB) == 0
        and rank % devices == 0
        and rank % LANES == 0
        and tile % LANES == 0
        and owned == SUB * chg
        and chg * (rank // devices) == LANES
        and 2 * (LANES // chg) == SUB
        and KER + 2 * SUB <= LANES
        and chg % (4 * SUB) == 0
        and (chg * groups) % LANES == 0
        and KER <= LANES
        and rank // devices <= SUB
        and rank // devices % 2 == 0
    )


def shards(kspace, sample_mask, start_basis):
    if divides_columns(kspace, start_basis):
        return column_shards(kspace, sample_mask, start_basis)
    return general_shards(kspace, sample_mask, start_basis)


def solution(mesh):
    return jax.shard_map(
        shards,
        mesh=mesh,
        in_specs=(P("coil", "rows"), P("coil", "rows"), P("coil", "rows", None)),
        out_specs=(P("coil", "rows"), P("coil", "rows", None)),
        check_vma=False,
    )
```

```python
import functools

import jax
import jax.numpy as jnp
from jax import lax
from jax.experimental import pallas as pl
from jax.experimental.pallas import tpu as pltpu
from jax.sharding import PartitionSpec as P

KER = 64
ITERS = 2
LANES = 128
SUB = 8
AXES = ("rows", "coil")


threshold = 0.05


def shifted(block, axis, distance):
    devices = range(lax.axis_size(axis))
    route = [((i - distance) % len(devices), i) for i in devices]
    return lax.ppermute(block, axis, route)


def orthonormal(normal_rows, gram_matrix):
    factor = jnp.linalg.cholesky(gram_matrix)
    return lax.linalg.triangular_solve(
        factor, normal_rows, left_side=False, lower=True, transpose_a=True
    )


def coil_total(partial_value):
    return lax.psum(partial_value, "coil")


def general_shards(kspace, sample_mask, start_basis):
    highest = lax.Precision.HIGHEST
    channels = kspace.shape[0]
    tile_rows = kspace.shape[1]
    mask_float = sample_mask.astype(jnp.float32)
    sampled = kspace * mask_float
    next_rim = shifted(sampled[:, : KER - 1], "rows", -1)
    extended = jnp.concatenate([sampled, next_rim], axis=1)
    hankel_cols = jnp.stack(
        [extended[:, offset : offset + tile_rows] for offset in range(KER)], axis=0
    )
    hankel_cols = hankel_cols.reshape(KER * channels, tile_rows)
    owned_basis = start_basis.reshape(start_basis.shape[1], start_basis.shape[2])
    whole_basis = lax.all_gather(owned_basis, "rows", axis=0, tiled=True)
    for iteration in range(ITERS):
        images = coil_total(
            lax.dot_general(
                whole_basis,
                hankel_cols,
                (((0,), (0,)), ((), ())),
                precision=highest,
                preferred_element_type=jnp.float32,
            )
        )
        local_normal = lax.dot_general(
            hankel_cols,
            images,
            (((1,), (1,)), ((), ())),
            precision=highest,
            preferred_element_type=jnp.float32,
        )
        normal_whole = lax.psum(local_normal, "rows")
        local_gram = jnp.dot(
            normal_whole.T, normal_whole, precision=highest, preferred_element_type=jnp.float32
        )
        gram_matrix = lax.psum(local_gram, "coil")
        whole_basis = orthonormal(normal_whole, gram_matrix)
    images = coil_total(
        lax.dot_general(
            whole_basis,
            hankel_cols,
            (((0,), (0,)), ((), ())),
            precision=highest,
            preferred_element_type=jnp.float32,
        )
    )
    projected = jnp.dot(whole_basis, images, precision=highest, preferred_element_type=jnp.float32)
    owned_count = whole_basis.shape[0] // lax.axis_size("rows")
    owned_basis = lax.dynamic_slice_in_dim(
        whole_basis, lax.axis_index("rows") * owned_count, owned_count, 0
    )
    stacked = projected.reshape(KER, channels, tile_rows)
    spread = jnp.zeros((channels, tile_rows + KER - 1), jnp.float32)
    for offset in range(KER):
        spread = spread.at[:, offset : offset + tile_rows].add(stacked[offset])
    carried = shifted(spread[:, tile_rows:], "rows", 1)
    estimate = spread[:, :tile_rows].at[:, : KER - 1].add(carried) / KER
    residual = mask_float * (kspace - estimate)
    recovered = estimate + residual - jnp.clip(residual, -threshold, threshold)
    return (recovered, owned_basis.reshape(1, owned_basis.shape[0], owned_basis.shape[1]))


def split(value):
    high = value.astype(jnp.bfloat16)
    low = (value - high.astype(jnp.float32)).astype(jnp.bfloat16)
    return high, low


def dot(a, b, dims=((1,), (0,))):
    return lax.dot_general(a, b, (dims, ((), ())), preferred_element_type=jnp.float32)


def dot3(a, b, dims=((1,), (0,))):
    a_high, a_low = split(a)
    b_high, b_low = split(b)
    return dot(a_high, b_high, dims) + (dot(a_high, b_low, dims) + dot(a_low, b_high, dims))


def square(size):
    at_row = lax.broadcasted_iota(jnp.int32, (size, size), 0)
    at_col = lax.broadcasted_iota(jnp.int32, (size, size), 1)
    return at_row, at_col


def prepare_kernel(cols, chg, per_tile, basis_ref, send_ref):
    turned = basis_ref[...].T
    devices = turned.shape[0] // cols
    for j in range(per_tile):
        part = turned[:, j * chg : (j + 1) * chg]
        row = jnp.concatenate([part[k * devices : (k + 1) * devices] for k in range(cols)], axis=1)
        send_ref[pl.ds(j, devices, stride=per_tile), :] = row


def images_of(vectors, samples_ref, wide_ref):
    rows, channels = vectors.shape
    cols = rows // KER
    high, low = split(vectors)
    at_row = lax.broadcasted_iota(jnp.int32, (rows, rows), 0)
    at_col = lax.broadcasted_iota(jnp.int32, (rows, rows), 1)
    flip = ((at_row // KER == at_col // KER) & (at_row % KER + at_col % KER == KER - 1)).astype(
        jnp.float32
    ).astype(jnp.bfloat16)
    both = dot(flip, jnp.concatenate([high, low], axis=1)).astype(jnp.bfloat16)
    high, low = both[:, :channels], both[:, channels:]
    parts = jnp.concatenate([high, high, low], axis=1)
    tiles = samples_ref.shape[0]
    tile = samples_ref.shape[-1]
    for t in range(tiles):
        block = samples_ref[t].reshape(2 * channels, tile)
        block = jnp.concatenate([block, block[:channels]], axis=0)
        wide_ref[:, t * tile : (t + 1) * tile] = dot(parts, block)
    images = []
    for k in range(cols):
        total = None
        for i in reversed(range(0, KER, SUB)):
            part = wide_ref[k * KER + i : k * KER + i + SUB, :]
            total = part if total is None else pltpu.roll(total, SUB, 1) + part
        total = pltpu.roll(total, 0, 1, stride=1, stride_axis=0)
        images.append(jnp.sum(total, axis=0, keepdims=True))
    return images


def normal_of(images, samples_ref, moved_ref):
    cols = len(images)
    positions = images[0].shape[1]
    tiles = samples_ref.shape[0]
    tile = samples_ref.shape[-1]
    channels = samples_ref.shape[2] * samples_ref.shape[3]
    rows = cols * KER
    for k in range(cols):
        base = jnp.broadcast_to(images[k], (SUB, positions))
        base = pltpu.roll(base, positions - (KER - 1), 1, stride=1, stride_axis=0)
        for j in range(0, KER, 2 * SUB):
            first = base if j == 0 else pltpu.roll(base, j, 1)
            second = pltpu.roll(base, j + SUB, 1)
            high, low = split(jnp.concatenate([first, second], axis=0))
            moved_ref[k * KER + j : k * KER + j + 2 * SUB, :] = high
            moved_ref[rows + k * KER + j : rows + k * KER + j + 2 * SUB, :] = low
    high = jnp.zeros((rows, 2 * channels), jnp.float32)
    low = jnp.zeros((rows, channels), jnp.float32)
    for t in range(tiles):
        block = samples_ref[t].reshape(2 * channels, tile)
        lanes = slice(t * tile, (t + 1) * tile)
        high = high + dot(moved_ref[:rows, lanes], block, ((1,), (1,)))
        low = low + dot(moved_ref[rows:, lanes], block[:channels], ((1,), (1,)))
    return high[:, :channels] + (high[:, channels:] + low)


def store_by_rows(normal, send_ref):
    tiles, groups, per_tile, lanes = send_ref.shape
    cols = normal.shape[0] // KER
    chg = normal.shape[1] // groups
    for g in range(groups):
        joined = jnp.concatenate(
            [normal[k * KER : (k + 1) * KER, g * chg : (g + 1) * chg] for k in range(cols)], axis=1
        )
        send_ref[:, g] = joined.reshape(tiles, per_tile, lanes)


def store_by_groups(normal_ref, group_ref):
    groups, count, lanes = group_ref.shape
    rows, channels = normal_ref.shape
    chg = channels // groups
    fold = lanes // chg
    cols = rows // KER
    deep = KER // fold
    me = lax.axis_index("coil")
    parts = [
        [normal_ref[pl.ds(k * KER + f, deep, stride=fold), :] for f in range(fold)]
        for k in range(cols)
    ]
    for g in range(groups):
        joined = [
            jnp.concatenate([part[:, g * chg : (g + 1) * chg] for part in parts[k]], axis=1)
            for k in range(cols)
        ]
        group_ref[lax.bitwise_xor(me, g)] = jnp.concatenate(joined, axis=0)


def passes_kernel(orders, basis_ref, *refs):
    *pieces, samples_ref, normal_ref, send_ref, group_ref, wide_ref, moved_ref = refs
    tiles, _, groups, chg, tile = samples_ref.shape
    me = lax.axis_index("rows") * groups + lax.axis_index("coil")
    for (start, order), piece_ref in zip(orders, pieces):
        count = piece_ref.shape[1]
        for slot, mask in enumerate(order):
            high, low = split(piece_ref[slot])
            source = lax.bitwise_xor(me, mask)
            t, g = source // groups, source % groups
            samples_ref[t, 0, g, start : start + count] = high
            samples_ref[t, 1, g, start : start + count] = low
    cols = basis_ref.shape[-1] // chg
    rows = []
    for k in range(cols):
        rows.append(
            jnp.concatenate(
                [
                    basis_ref[:, g].reshape(KER, cols * chg)[:, k * chg : (k + 1) * chg]
                    for g in range(groups)
                ],
                axis=1,
            )
        )
    vectors = jnp.concatenate(rows, axis=0)
    normal = normal_of(images_of(vectors, samples_ref, wide_ref), samples_ref, moved_ref)
    power = jnp.zeros((1, tile), jnp.float32)
    for t in range(samples_ref.shape[0]):
        value = samples_ref[t, 0].reshape(groups * chg, tile).astype(jnp.float32)
        power = power + jnp.sum(value * value, axis=0, keepdims=True)
    normal = normal * (groups * chg / jnp.sum(power))
    normal = normal_of(images_of(normal, samples_ref, wide_ref), samples_ref, moved_ref)
    normal_ref[...] = normal
    store_by_rows(normal, send_ref)
    store_by_groups(normal_ref, group_ref)


def images_kernel(samples_ref, vectors_ref, send_ref, wide_ref):
    tiles, groups, cols, reach = send_ref.shape
    tile = samples_ref.shape[-1]
    images = jnp.concatenate(images_of(vectors_ref[...], samples_ref, wide_ref), axis=0)
    positions = images.shape[1]
    images = pltpu.roll(images, positions - (KER - 1), 1)
    rim = reach - tile
    for t in range(tiles):
        if t == 0:
            part = jnp.concatenate([images[:, positions - rim :], images[:, :tile]], axis=1)
        else:
            part = images[:, t * tile - rim : (t + 1) * tile]
        for g in range(groups):
            send_ref[t, g] = part


def gather_turned(received_ref, cols, per_tile):
    count, lanes = received_ref.shape
    devices = count // per_tile
    chg = lanes // cols
    loaded = [received_ref[pl.ds(j, devices, stride=per_tile), :] for j in range(per_tile)]
    return jnp.concatenate(
        [
            jnp.concatenate(
                [loaded[j][:, k * chg : (k + 1) * chg] for j in range(per_tile)], axis=1
            )
            for k in range(cols)
        ],
        axis=0,
    )


def exact(a, b, dims=((1,), (0,))):
    return lax.dot_general(
        a, b, (dims, ((), ())), precision=lax.Precision.HIGHEST, preferred_element_type=jnp.float32
    )


def gram_kernel(cols, per_tile, received_ref, basis_ref, kept_ref, given_ref, turned_ref):
    turned = gather_turned(received_ref, cols, per_tile)
    first = exact(basis_ref[...], turned, ((0,), (1,)))
    second = exact(turned, turned, ((1,), (1,)))
    turned_ref[...] = turned
    at_row, at_col = square(first.shape[0])
    packed = jnp.where(at_row >= at_col, first, second)
    line = jnp.sum(jnp.where(at_row == at_col, second, 0.0), axis=0, keepdims=True)
    line = jnp.broadcast_to(line, (SUB, line.shape[1]))
    half = packed.shape[0] // 2
    odd = lax.axis_index("coil") % 2 == 1
    kept_ref[:half] = jnp.where(odd, packed[half:], packed[:half])
    given_ref[:half] = jnp.where(odd, packed[:half], packed[half:])
    kept_ref[half:] = line
    given_ref[half:] = line


def load_grams(kept_ref, other_ref):
    odd = lax.axis_index("coil") % 2 == 1
    kept, other = kept_ref[...], other_ref[...]
    low, high = jnp.where(odd, other, kept), jnp.where(odd, kept, other)
    half = low.shape[0] - SUB
    packed = jnp.concatenate([low[:half], high[:half]], axis=0)
    line = low[half : half + 1]
    at_row, at_col = square(packed.shape[0])
    turned = packed.T
    first = jnp.where(at_row >= at_col, packed, turned)
    second = jnp.where(at_row > at_col, turned, packed)
    return first, jnp.where(at_row == at_col, line, second), line


def inverse_factor(gram):
    size = gram.shape[0]
    shape = (SUB, size)
    at_row = lax.broadcasted_iota(jnp.int32, (size, size), 0)
    at_col = lax.broadcasted_iota(jnp.int32, (size, size), 1)
    unit = (at_row == at_col).astype(jnp.float32)
    left = [gram[b : b + SUB] for b in range(0, size, SUB)]
    right = [unit[b : b + SUB] for b in range(0, size, SUB)]
    sub = lax.broadcasted_iota(jnp.int32, shape, 0)
    done = []
    for b in range(len(left)):
        spread = {
            c: [
                jnp.broadcast_to(left[c][:, b * SUB + k : b * SUB + k + 1], shape)
                for k in range(SUB)
            ]
            for c in range(b, len(left))
        }
        entry = {
            (i, k): jnp.broadcast_to(spread[b][k][i : i + 1], shape)
            for k in range(SUB)
            for i in range(k, SUB)
        }
        inverse = {}
        for k in range(SUB):
            root = lax.rsqrt(entry[k, k])
            inverse[k, k] = root
            for i in range(k + 1, SUB):
                entry[i, k] = entry[i, k] * root
            for i in range(k + 1, SUB):
                for m in range(k + 1, i + 1):
                    entry[i, m] = entry[i, m] - entry[i, k] * entry[m, k]
        for i in range(1, SUB):
            for k in range(i):
                total = entry[i, k] * inverse[k, k]
                for m in range(k + 1, i):
                    total = total + entry[i, m] * inverse[m, k]
                inverse[i, k] = -(total * inverse[i, i])

        def solved(rows):
            whole = [jnp.broadcast_to(rows[k : k + 1], shape) for k in range(SUB)]
            first = []
            for i in range(SUB):
                total = inverse[i, 0] * whole[0]
                for k in range(1, i + 1):
                    total = total + inverse[i, k] * whole[k]
                first.append(total)
            second = []
            for k in range(SUB):
                total = inverse[k, k] * first[k]
                for i in range(k + 1, SUB):
                    total = total + inverse[i, k] * first[i]
                second.append(total)
            return first, second

        lower, lower_again = solved(right[b])
        row = lower[0]
        for i in range(1, SUB):
            row = jnp.where(sub == i, lower[i], row)
        done.append(row)
        if b + 1 < len(left):
            _, upper_again = solved(left[b])
            for c in range(b + 1, len(left)):
                for k in range(SUB):
                    left[c] = left[c] - spread[c][k] * upper_again[k]
                    right[c] = right[c] - spread[c][k] * lower_again[k]
    return jnp.concatenate(done, axis=0)


def factor_kernel(gram_ref, other_ref, inverse_ref, next_ref, sound_ref):
    gram, raw, line = load_grams(gram_ref, other_ref)
    inverse = inverse_factor(gram)
    inverse_ref[...] = inverse
    gram = exact(exact(inverse, raw), inverse, ((1,), (1,)))
    next_ref[...] = gram
    at_row, at_col = square(gram.shape[0])
    terms = jnp.sum(inverse * inverse * line, axis=1, keepdims=True)
    result = jnp.sum(jnp.where(at_row == at_col, gram, 0.0), axis=1, keepdims=True)
    worst = jnp.max(jnp.where(terms <= 64.0 * result, 0, 1))
    sound_ref[0] = 1 - worst


def rows_kernel(turned_ref, inverse_ref, gram_ref):
    turned = exact(inverse_ref[...], turned_ref[...])
    gram_ref[...] = exact(turned, turned, ((1,), (1,)))


def both_kernel(gram_ref, inverse_ref, both_ref):
    both_ref[...] = exact(inverse_factor(gram_ref[...]), inverse_ref[...])


def moved_columns(order, cols):
    devices = len(order[0])
    at_row, at_col = square(devices * cols)
    turn = at_col % cols * devices + at_col // cols
    me = lax.axis_index("rows") * lax.axis_size("coil") + lax.axis_index("coil")
    slot = at_col % devices
    mask = jnp.zeros_like(slot)
    bit = 1
    while bit < devices:
        step = jnp.where(2 * at_col < at_col.shape[1], order[0][bit], order[1][bit])
        mask = mask | jnp.where(slot & bit != 0, step, 0)
        bit *= 2
    source = at_col - slot + lax.bitwise_xor(mask, jnp.full_like(mask, me))
    return [(at_row == place).astype(jnp.float32) for place in (turn, source)]


def stacked_dot(a, b):
    a_high, a_low = split(a)
    b_high, b_low = split(b)
    left = jnp.concatenate(
        [
            jnp.concatenate([a_high, a_high], axis=1),
            jnp.concatenate([a_low, jnp.zeros_like(a_low)], axis=1),
        ],
        axis=0,
    )
    both = dot(left, jnp.concatenate([b_high, b_low], axis=0))
    return both[: a.shape[0]] + both[a.shape[0] :]


def last_kernel(
    cols,
    order,
    images_ref,
    both_ref,
    kspace_ref,
    mask_ref,
    top_near_ref,
    top_far_ref,
    low_near_ref,
    low_far_ref,
    recovered_ref,
    basis_ref,
    vectors_ref,
):
    both = both_ref[...]
    reach = images_ref.shape[1]
    factors = [exact(both, moved) for moved in moved_columns(order, cols)]
    chg, tile = kspace_ref.shape
    lanes = top_near_ref.shape[1]
    fold = lanes // chg
    deep = KER // fold
    step = cols // 2 * deep
    lead = reach - tile - KER - 2 * SUB
    images = stacked_dot(factors[0], images_ref[...]).T[lead:]
    rim = reach - tile - SUB - lead
    even, odd = None, None
    for a in range(0, deep, 2):
        turned = [
            jnp.concatenate(
                [
                    ref[pl.ds(k * deep + a + i, ref.shape[0] // step, stride=step), :]
                    for refs in ((top_near_ref, top_far_ref), (low_near_ref, low_far_ref))
                    for k in range(cols // 2)
                    for ref in refs
                ],
                axis=0,
            )
            for i in range(2)
        ]
        vectors = stacked_dot(factors[1], jnp.concatenate(turned, axis=1))
        vectors_ref[:, a * lanes : (a + 2) * lanes] = vectors
        projected = stacked_dot(images, vectors)
        shift = a * fold
        part = projected[rim - shift : rim - shift + tile + SUB, :lanes]
        even = part if even is None else even + part
        part = projected[rim - SUB - shift : rim - shift + tile + SUB, lanes:]
        odd = part if odd is None else odd + part
    total = even + odd[SUB - fold : SUB - fold + tile + SUB]
    estimate = total[SUB : SUB + tile]
    for f in range(1, fold):
        moved = pltpu.roll(total, lanes - f * chg, 1)
        estimate = estimate + moved[SUB - f : SUB - f + tile]
    estimate = estimate.T[:chg]
    owned = basis_ref.shape[0]
    start = pl.multiple_of(lax.axis_index("rows") * owned, owned)
    basis_ref[...] = vectors_ref[:, pl.ds(start, owned)].T
    estimate = estimate / KER
    residual = mask_ref[...].astype(jnp.float32) * (kspace_ref[...] - estimate)
    recovered_ref[...] = estimate + residual - jnp.clip(residual, -threshold, threshold)


def call(kernel, outs, *args, scratch=(), limit=12, scalars=0, micros=1):
    return pl.pallas_call(
        kernel,
        out_shape=[jax.ShapeDtypeStruct(shape, kind) for shape, kind in outs],
        in_specs=[pl.BlockSpec(memory_space=pltpu.VMEM)] * len(args),
        out_specs=[pl.BlockSpec(memory_space=pltpu.VMEM)] * (len(outs) - scalars)
        + [pl.BlockSpec(memory_space=pltpu.SMEM)] * scalars,
        scratch_shapes=list(scratch),
        compiler_params=pltpu.CompilerParams(vmem_limit_bytes=limit * 2**20),
        cost_estimate=pl.CostEstimate(
            flops=micros * 10**9, bytes_accessed=0, transcendentals=0
        ),
    )(*args)


def exchange(block, devices, mask, axes):
    return lax.ppermute(block, axes, [(i, i ^ mask) for i in range(devices)])


def with_masks(masks, mask):
    return masks + [m ^ mask for m in masks]


def after(value, *others):
    return lax.optimization_barrier((value,) + others)[0]


def rounds_of(low, high):
    masks = []
    while low < high:
        if 2 * low < high:
            masks.append([low, 2 * low, 3 * low])
        else:
            masks.append([low])
        low *= 4
    return masks


def gather_round(part, order, masks, devices, axes):
    part = jnp.concatenate(
        [part] + [exchange(part, devices, mask, axes) for mask in masks], axis=0
    )
    return part, order + [m ^ mask for mask in masks for m in order]


def gather_samples(sampled, basis, tiles, groups):
    devices = tiles * groups
    near, masks = sampled[None], [0]
    mask = devices // 2
    while mask > groups:
        near, masks = gather_round(near, masks, [mask], devices, AXES)
        mask //= 2
    basis = to_all(basis)
    near = after(near, basis)
    half = near.shape[1] // 2
    halves = []
    for part, ways in (
        (near[:, :half], (groups, groups // 2)),
        (near[:, half:], (groups // 2, groups)),
    ):
        part, order = gather_round(part, masks, [ways[0]], devices, AXES)
        pieces = [(part, order)]
        mask = ways[1]
        rest = groups // 4
        while mask > 1:
            pieces = pieces + [
                (exchange(part, devices, mask, AXES), [m ^ mask for m in order])
                for part, order in pieces
            ]
            mask, rest = rest, rest // 2
        halves.append(
            pieces
            + [(exchange(part, devices, 1, AXES), [m ^ 1 for m in order]) for part, order in pieces]
        )
    return halves, basis


def to_all(pieces, axes=AXES):
    return lax.all_to_all(pieces, axes, 0, 0, tiled=True)


def gather_group(group, devices):
    groups = group.shape[0]
    parts = [group[:1]]
    parts += [exchange(group[s : s + 1], devices, s, AXES) for s in range(1, groups)]
    return jnp.concatenate(parts, axis=0), list(range(groups))


def total_beside(kept, given, near, order, images, groups, devices):
    ways = []
    mask = devices // 2
    while mask >= groups:
        ways.append(mask)
        mask //= 2
    half = near.shape[1] // 2
    parts = [near[:, :half], near[:, half:]]
    orders = [order, order]
    ways = [ways, ways[-1:] + ways[:-1]]
    step = 0

    def advance():
        for i in range(2):
            parts[i], orders[i] = gather_round(
                parts[i], orders[i], [ways[i][step]], devices, AXES
            )

    total = kept + exchange(given, devices, 1, AXES)
    for partners in rounds_of(2, devices):
        terms = [exchange(total, devices, way, AXES) for way in partners]
        total = total + terms[0]
        if len(terms) == 3:
            total = total + (terms[1] + terms[2])
        if step < len(ways[0]) - 1:
            advance()
            step += 1
    while step < len(ways[0]) - 1:
        advance()
        step += 1
    other = exchange(total, devices, 1, AXES)
    *parts, total, other, images = lax.optimization_barrier((*parts, total, other, images))
    pieces = []
    for i in range(2):
        mask = ways[i][-1]
        pieces += [parts[i], exchange(parts[i], devices, mask, AXES)]
        orders[i] = orders[i] + [m ^ mask for m in orders[i]]
    return (total, other), pieces, orders, to_all(images)


def column_shards(kspace, sample_mask, start_basis):
    f32, bf16 = jnp.float32, jnp.bfloat16
    tiles, groups = lax.axis_size("rows"), lax.axis_size("coil")
    devices = tiles * groups
    chg, tile = kspace.shape
    channels = chg * groups
    positions = tile * tiles
    owned, rank = start_basis.shape[1:]
    per_tile = owned // chg
    cols = rank // devices
    rows = cols * KER
    lanes = cols * chg

    sampled = kspace * sample_mask.astype(f32)
    (basis_send,) = call(
        functools.partial(prepare_kernel, cols, chg, per_tile),
        [((devices * per_tile, lanes), f32)],
        start_basis.reshape(owned, rank),
    )
    halves, basis_parts = gather_samples(
        sampled, basis_send.reshape(devices, per_tile, lanes), tiles, groups
    )
    starts = (0, chg // len(halves))
    orders = [(start, order) for start, half in zip(starts, halves) for _, order in half]
    wide = pltpu.VMEM((rows, positions), f32)
    moved = pltpu.VMEM((2 * rows, positions), bf16)
    samples, normal, send, group = call(
        functools.partial(passes_kernel, orders),
        [
            ((tiles, 2, groups, chg, tile), bf16),
            ((rows, channels), f32),
            ((tiles, groups, per_tile, lanes), f32),
            ((groups, rows * chg // lanes, lanes), f32),
        ],
        basis_parts.reshape(tiles, groups, per_tile, lanes),
        *[piece for half in halves for piece, _ in half],
        scratch=[wide, moved],
        limit=24,
        micros=12,
    )
    received = to_all(send.reshape(devices, per_tile, lanes))
    reach = tile + LANES
    (images,) = call(
        images_kernel,
        [((tiles, groups, cols, reach), f32)],
        samples,
        normal,
        scratch=[wide],
        limit=16,
        micros=2,
    )
    near, order = gather_group(group, devices)
    received, near = lax.optimization_barrier((received, images, near))[::2]
    half = ((rank // 2 + SUB, rank), f32)
    kept, given, turned = call(
        functools.partial(gram_kernel, cols, per_tile),
        [half, half, ((rank, owned), f32)],
        received.reshape(devices * per_tile, lanes),
        start_basis.reshape(owned, rank),
    )
    gram, pieces, order, images = total_beside(
        kept, given, near, order, images.reshape(devices, cols, reach), groups, devices
    )
    whole = ((rank, rank), f32)
    first, second, sound = call(
        factor_kernel, [whole, whole, ((1,), jnp.int32)], *gram, scalars=1, micros=12
    )

    def again():
        (gram,) = call(rows_kernel, [whole], turned, first)
        mask = 1
        while mask < devices:
            gram = gram + exchange(gram, devices, mask, AXES)
            mask *= 2
        return gram

    second = lax.cond(sound[0] == 1, lambda: second, again)
    (both,) = call(both_kernel, [whole], second, first, micros=0)
    recovered, basis = call(
        functools.partial(last_kernel, cols, order),
        [((chg, tile), f32), ((owned, rank), f32)],
        images.reshape(rank, reach),
        both,
        kspace,
        sample_mask,
        *[piece.reshape(-1, lanes) for piece in pieces],
        scratch=[pltpu.VMEM((rank, KER * chg), f32)],
        limit=16,
        micros=5,
    )
    return (recovered, basis.reshape(1, owned, rank))


def divides_columns(kspace, start_basis):
    tiles, groups = lax.axis_size("rows"), lax.axis_size("coil")
    devices = tiles * groups
    chg, tile = kspace.shape
    owned, rank = start_basis.shape[1:]
    return (
        devices & (devices - 1) == 0
        and tiles > 2
        and groups > 2
        and rank % (2 * SUB) == 0
        and rank % devices == 0
        and rank % LANES == 0
        and tile % LANES == 0
        and owned == SUB * chg
        and chg * (rank // devices) == LANES
        and 2 * (LANES // chg) == SUB
        and KER + 2 * SUB <= LANES
        and chg % (4 * SUB) == 0
        and (chg * groups) % LANES == 0
        and KER <= LANES
        and rank // devices <= SUB
        and rank // devices % 2 == 0
    )


def shards(kspace, sample_mask, start_basis):
    if divides_columns(kspace, start_basis):
        return column_shards(kspace, sample_mask, start_basis)
    return general_shards(kspace, sample_mask, start_basis)


def solution(mesh):
    return jax.shard_map(
        shards,
        mesh=mesh,
        in_specs=(P("coil", "rows"), P("coil", "rows"), P("coil", "rows", None)),
        out_specs=(P("coil", "rows"), P("coil", "rows", None)),
        check_vma=False,
    )
```

```python
import functools

import jax
import jax.numpy as jnp
from jax import lax
from jax.experimental import pallas as pl
from jax.experimental.pallas import tpu as pltpu
from jax.sharding import PartitionSpec as P

KER = 64
ITERS = 2
LANES = 128
SUB = 8
AXES = ("rows", "coil")


threshold = 0.05


def shifted(block, axis, distance):
    devices = range(lax.axis_size(axis))
    route = [((i - distance) % len(devices), i) for i in devices]
    return lax.ppermute(block, axis, route)


def orthonormal(normal_rows, gram_matrix):
    factor = jnp.linalg.cholesky(gram_matrix)
    return lax.linalg.triangular_solve(
        factor, normal_rows, left_side=False, lower=True, transpose_a=True
    )


def coil_total(partial_value):
    return lax.psum(partial_value, "coil")


def general_shards(kspace, sample_mask, start_basis):
    highest = lax.Precision.HIGHEST
    channels = kspace.shape[0]
    tile_rows = kspace.shape[1]
    mask_float = sample_mask.astype(jnp.float32)
    sampled = kspace * mask_float
    next_rim = shifted(sampled[:, : KER - 1], "rows", -1)
    extended = jnp.concatenate([sampled, next_rim], axis=1)
    hankel_cols = jnp.stack(
        [extended[:, offset : offset + tile_rows] for offset in range(KER)], axis=0
    )
    hankel_cols = hankel_cols.reshape(KER * channels, tile_rows)
    owned_basis = start_basis.reshape(start_basis.shape[1], start_basis.shape[2])
    whole_basis = lax.all_gather(owned_basis, "rows", axis=0, tiled=True)
    for iteration in range(ITERS):
        images = coil_total(
            lax.dot_general(
                whole_basis,
                hankel_cols,
                (((0,), (0,)), ((), ())),
                precision=highest,
                preferred_element_type=jnp.float32,
            )
        )
        local_normal = lax.dot_general(
            hankel_cols,
            images,
            (((1,), (1,)), ((), ())),
            precision=highest,
            preferred_element_type=jnp.float32,
        )
        normal_whole = lax.psum(local_normal, "rows")
        local_gram = jnp.dot(
            normal_whole.T, normal_whole, precision=highest, preferred_element_type=jnp.float32
        )
        gram_matrix = lax.psum(local_gram, "coil")
        whole_basis = orthonormal(normal_whole, gram_matrix)
    images = coil_total(
        lax.dot_general(
            whole_basis,
            hankel_cols,
            (((0,), (0,)), ((), ())),
            precision=highest,
            preferred_element_type=jnp.float32,
        )
    )
    projected = jnp.dot(whole_basis, images, precision=highest, preferred_element_type=jnp.float32)
    owned_count = whole_basis.shape[0] // lax.axis_size("rows")
    owned_basis = lax.dynamic_slice_in_dim(
        whole_basis, lax.axis_index("rows") * owned_count, owned_count, 0
    )
    stacked = projected.reshape(KER, channels, tile_rows)
    spread = jnp.zeros((channels, tile_rows + KER - 1), jnp.float32)
    for offset in range(KER):
        spread = spread.at[:, offset : offset + tile_rows].add(stacked[offset])
    carried = shifted(spread[:, tile_rows:], "rows", 1)
    estimate = spread[:, :tile_rows].at[:, : KER - 1].add(carried) / KER
    residual = mask_float * (kspace - estimate)
    recovered = estimate + residual - jnp.clip(residual, -threshold, threshold)
    return (recovered, owned_basis.reshape(1, owned_basis.shape[0], owned_basis.shape[1]))


def split(value):
    high = value.astype(jnp.bfloat16)
    low = (value - high.astype(jnp.float32)).astype(jnp.bfloat16)
    return high, low


def dot(a, b, dims=((1,), (0,))):
    return lax.dot_general(a, b, (dims, ((), ())), preferred_element_type=jnp.float32)


def dot3(a, b, dims=((1,), (0,))):
    a_high, a_low = split(a)
    b_high, b_low = split(b)
    return dot(a_high, b_high, dims) + (dot(a_high, b_low, dims) + dot(a_low, b_high, dims))


def square(size):
    at_row = lax.broadcasted_iota(jnp.int32, (size, size), 0)
    at_col = lax.broadcasted_iota(jnp.int32, (size, size), 1)
    return at_row, at_col


def prepare_kernel(cols, chg, per_tile, basis_ref, send_ref):
    turned = basis_ref[...].T
    devices = turned.shape[0] // cols
    for j in range(per_tile):
        part = turned[:, j * chg : (j + 1) * chg]
        row = jnp.concatenate([part[k * devices : (k + 1) * devices] for k in range(cols)], axis=1)
        send_ref[pl.ds(j, devices, stride=per_tile), :] = row


def images_of(vectors, samples_ref, wide_ref):
    rows, channels = vectors.shape
    cols = rows // KER
    high, low = split(vectors)
    at_row = lax.broadcasted_iota(jnp.int32, (rows, rows), 0)
    at_col = lax.broadcasted_iota(jnp.int32, (rows, rows), 1)
    flip = ((at_row // KER == at_col // KER) & (at_row % KER + at_col % KER == KER - 1)).astype(
        jnp.float32
    ).astype(jnp.bfloat16)
    both = dot(flip, jnp.concatenate([high, low], axis=1)).astype(jnp.bfloat16)
    high, low = both[:, :channels], both[:, channels:]
    parts = jnp.concatenate([high, high, low], axis=1)
    tiles = samples_ref.shape[0]
    tile = samples_ref.shape[-1]
    for t in range(tiles):
        block = samples_ref[t].reshape(2 * channels, tile)
        block = jnp.concatenate([block, block[:channels]], axis=0)
        wide_ref[:, t * tile : (t + 1) * tile] = dot(parts, block)
    images = []
    for k in range(cols):
        total = None
        for i in reversed(range(0, KER, SUB)):
            part = wide_ref[k * KER + i : k * KER + i + SUB, :]
            total = part if total is None else pltpu.roll(total, SUB, 1) + part
        total = pltpu.roll(total, 0, 1, stride=1, stride_axis=0)
        images.append(jnp.sum(total, axis=0, keepdims=True))
    return images


def normal_of(images, samples_ref, moved_ref):
    cols = len(images)
    positions = images[0].shape[1]
    tiles = samples_ref.shape[0]
    tile = samples_ref.shape[-1]
    channels = samples_ref.shape[2] * samples_ref.shape[3]
    rows = cols * KER
    for k in range(cols):
        base = jnp.broadcast_to(images[k], (SUB, positions))
        base = pltpu.roll(base, positions - (KER - 1), 1, stride=1, stride_axis=0)
        for j in range(0, KER, 2 * SUB):
            first = base if j == 0 else pltpu.roll(base, j, 1)
            second = pltpu.roll(base, j + SUB, 1)
            high, low = split(jnp.concatenate([first, second], axis=0))
            moved_ref[k * KER + j : k * KER + j + 2 * SUB, :] = high
            moved_ref[rows + k * KER + j : rows + k * KER + j + 2 * SUB, :] = low
    high = jnp.zeros((rows, 2 * channels), jnp.float32)
    low = jnp.zeros((rows, channels), jnp.float32)
    for t in range(tiles):
        block = samples_ref[t].reshape(2 * channels, tile)
        lanes = slice(t * tile, (t + 1) * tile)
        high = high + dot(moved_ref[:rows, lanes], block, ((1,), (1,)))
        low = low + dot(moved_ref[rows:, lanes], block[:channels], ((1,), (1,)))
    return high[:, :channels] + (high[:, channels:] + low)


def store_by_rows(normal, send_ref):
    tiles, groups, per_tile, lanes = send_ref.shape
    cols = normal.shape[0] // KER
    chg = normal.shape[1] // groups
    for g in range(groups):
        joined = jnp.concatenate(
            [normal[k * KER : (k + 1) * KER, g * chg : (g + 1) * chg] for k in range(cols)], axis=1
        )
        send_ref[:, g] = joined.reshape(tiles, per_tile, lanes)


def store_by_groups(normal_ref, group_ref):
    groups, count, lanes = group_ref.shape
    rows, channels = normal_ref.shape
    chg = channels // groups
    fold = lanes // chg
    cols = rows // KER
    deep = KER // fold
    me = lax.axis_index("coil")
    parts = [
        [normal_ref[pl.ds(k * KER + f, deep, stride=fold), :] for f in range(fold)]
        for k in range(cols)
    ]
    for g in range(groups):
        joined = [
            jnp.concatenate([part[:, g * chg : (g + 1) * chg] for part in parts[k]], axis=1)
            for k in range(cols)
        ]
        group_ref[lax.bitwise_xor(me, g)] = jnp.concatenate(joined, axis=0)


def passes_kernel(orders, basis_ref, *refs):
    *pieces, samples_ref, normal_ref, send_ref, group_ref, wide_ref, moved_ref = refs
    tiles, _, groups, chg, tile = samples_ref.shape
    me = lax.axis_index("rows") * groups + lax.axis_index("coil")
    for (start, order), piece_ref in zip(orders, pieces):
        count = piece_ref.shape[1]
        for slot, mask in enumerate(order):
            high, low = split(piece_ref[slot])
            source = lax.bitwise_xor(me, mask)
            t, g = source // groups, source % groups
            samples_ref[t, 0, g, start : start + count] = high
            samples_ref[t, 1, g, start : start + count] = low
    cols = basis_ref.shape[-1] // chg
    rows = []
    for k in range(cols):
        rows.append(
            jnp.concatenate(
                [
                    basis_ref[:, g].reshape(KER, cols * chg)[:, k * chg : (k + 1) * chg]
                    for g in range(groups)
                ],
                axis=1,
            )
        )
    vectors = jnp.concatenate(rows, axis=0)
    normal = normal_of(images_of(vectors, samples_ref, wide_ref), samples_ref, moved_ref)
    power = jnp.zeros((1, tile), jnp.float32)
    for t in range(samples_ref.shape[0]):
        value = samples_ref[t, 0].reshape(groups * chg, tile).astype(jnp.float32)
        power = power + jnp.sum(value * value, axis=0, keepdims=True)
    normal = normal * (groups * chg / jnp.sum(power))
    normal = normal_of(images_of(normal, samples_ref, wide_ref), samples_ref, moved_ref)
    normal_ref[...] = normal
    store_by_rows(normal, send_ref)
    store_by_groups(normal_ref, group_ref)


def images_kernel(samples_ref, vectors_ref, send_ref, wide_ref):
    tiles, groups, cols, reach = send_ref.shape
    tile = samples_ref.shape[-1]
    images = jnp.concatenate(images_of(vectors_ref[...], samples_ref, wide_ref), axis=0)
    positions = images.shape[1]
    images = pltpu.roll(images, positions - (KER - 1), 1)
    rim = reach - tile
    for t in range(tiles):
        if t == 0:
            part = jnp.concatenate([images[:, positions - rim :], images[:, :tile]], axis=1)
        else:
            part = images[:, t * tile - rim : (t + 1) * tile]
        for g in range(groups):
            send_ref[t, g] = part


def gather_turned(received_ref, cols, per_tile):
    count, lanes = received_ref.shape
    devices = count // per_tile
    chg = lanes // cols
    loaded = [received_ref[pl.ds(j, devices, stride=per_tile), :] for j in range(per_tile)]
    return jnp.concatenate(
        [
            jnp.concatenate(
                [loaded[j][:, k * chg : (k + 1) * chg] for j in range(per_tile)], axis=1
            )
            for k in range(cols)
        ],
        axis=0,
    )


def exact(a, b, dims=((1,), (0,))):
    return lax.dot_general(
        a, b, (dims, ((), ())), precision=lax.Precision.HIGHEST, preferred_element_type=jnp.float32
    )


def gram_kernel(cols, per_tile, received_ref, basis_ref, kept_ref, given_ref, turned_ref):
    turned = gather_turned(received_ref, cols, per_tile)
    first = exact(basis_ref[...], turned, ((0,), (1,)))
    second = exact(turned, turned, ((1,), (1,)))
    turned_ref[...] = turned
    at_row, at_col = square(first.shape[0])
    packed = jnp.where(at_row >= at_col, first, second)
    line = jnp.sum(jnp.where(at_row == at_col, second, 0.0), axis=0, keepdims=True)
    line = jnp.broadcast_to(line, (SUB, line.shape[1]))
    half = packed.shape[0] // 2
    odd = lax.axis_index("coil") % 2 == 1
    kept_ref[:half] = jnp.where(odd, packed[half:], packed[:half])
    given_ref[:half] = jnp.where(odd, packed[:half], packed[half:])
    kept_ref[half:] = line
    given_ref[half:] = line


def load_grams(kept_ref, other_ref):
    odd = lax.axis_index("coil") % 2 == 1
    kept, other = kept_ref[...], other_ref[...]
    low, high = jnp.where(odd, other, kept), jnp.where(odd, kept, other)
    half = low.shape[0] - SUB
    packed = jnp.concatenate([low[:half], high[:half]], axis=0)
    line = low[half : half + 1]
    at_row, at_col = square(packed.shape[0])
    turned = packed.T
    first = jnp.where(at_row >= at_col, packed, turned)
    second = jnp.where(at_row > at_col, turned, packed)
    return first, jnp.where(at_row == at_col, line, second), line


def inverse_factor(gram):
    size = gram.shape[0]
    shape = (SUB, size)
    at_row = lax.broadcasted_iota(jnp.int32, (size, size), 0)
    at_col = lax.broadcasted_iota(jnp.int32, (size, size), 1)
    unit = (at_row == at_col).astype(jnp.float32)
    left = [gram[b : b + SUB] for b in range(0, size, SUB)]
    right = [unit[b : b + SUB] for b in range(0, size, SUB)]
    sub = lax.broadcasted_iota(jnp.int32, shape, 0)
    done = []
    for b in range(len(left)):
        spread = {
            c: [
                jnp.broadcast_to(left[c][:, b * SUB + k : b * SUB + k + 1], shape)
                for k in range(SUB)
            ]
            for c in range(b, len(left))
        }
        entry = {
            (i, k): jnp.broadcast_to(spread[b][k][i : i + 1], shape)
            for k in range(SUB)
            for i in range(k, SUB)
        }
        inverse = {}
        for k in range(SUB):
            root = lax.rsqrt(entry[k, k])
            inverse[k, k] = root
            for i in range(k + 1, SUB):
                entry[i, k] = entry[i, k] * root
            for i in range(k + 1, SUB):
                for m in range(k + 1, i + 1):
                    entry[i, m] = entry[i, m] - entry[i, k] * entry[m, k]
        for i in range(1, SUB):
            for k in range(i):
                total = entry[i, k] * inverse[k, k]
                for m in range(k + 1, i):
                    total = total + entry[i, m] * inverse[m, k]
                inverse[i, k] = -(total * inverse[i, i])

        def solved(rows):
            whole = [jnp.broadcast_to(rows[k : k + 1], shape) for k in range(SUB)]
            first = []
            for i in range(SUB):
                total = inverse[i, 0] * whole[0]
                for k in range(1, i + 1):
                    total = total + inverse[i, k] * whole[k]
                first.append(total)
            second = []
            for k in range(SUB):
                total = inverse[k, k] * first[k]
                for i in range(k + 1, SUB):
                    total = total + inverse[i, k] * first[i]
                second.append(total)
            return first, second

        lower, lower_again = solved(right[b])
        row = lower[0]
        for i in range(1, SUB):
            row = jnp.where(sub == i, lower[i], row)
        done.append(row)
        if b + 1 < len(left):
            _, upper_again = solved(left[b])
            for c in range(b + 1, len(left)):
                for k in range(SUB):
                    left[c] = left[c] - spread[c][k] * upper_again[k]
                    right[c] = right[c] - spread[c][k] * lower_again[k]
    return jnp.concatenate(done, axis=0)


def factor_kernel(gram_ref, other_ref, inverse_ref, next_ref, sound_ref):
    gram, raw, line = load_grams(gram_ref, other_ref)
    inverse = inverse_factor(gram)
    inverse_ref[...] = inverse
    gram = exact(exact(inverse, raw), inverse, ((1,), (1,)))
    next_ref[...] = gram
    at_row, at_col = square(gram.shape[0])
    terms = jnp.sum(inverse * inverse * line, axis=1, keepdims=True)
    result = jnp.sum(jnp.where(at_row == at_col, gram, 0.0), axis=1, keepdims=True)
    worst = jnp.max(jnp.where(terms <= 64.0 * result, 0, 1))
    sound_ref[0] = 1 - worst


def rows_kernel(turned_ref, inverse_ref, gram_ref):
    turned = exact(inverse_ref[...], turned_ref[...])
    gram_ref[...] = exact(turned, turned, ((1,), (1,)))


def both_kernel(gram_ref, inverse_ref, both_ref):
    both_ref[...] = exact(inverse_factor(gram_ref[...]), inverse_ref[...])


def moved_columns(order, cols):
    devices = len(order[0])
    at_row, at_col = square(devices * cols)
    turn = at_col % cols * devices + at_col // cols
    me = lax.axis_index("rows") * lax.axis_size("coil") + lax.axis_index("coil")
    slot = at_col % devices
    mask = jnp.zeros_like(slot)
    bit = 1
    while bit < devices:
        step = jnp.where(2 * at_col < at_col.shape[1], order[0][bit], order[1][bit])
        mask = mask | jnp.where(slot & bit != 0, step, 0)
        bit *= 2
    source = at_col - slot + lax.bitwise_xor(mask, jnp.full_like(mask, me))
    return [(at_row == place).astype(jnp.float32) for place in (turn, source)]


def stacked_dot(a, b):
    a_high, a_low = split(a)
    b_high, b_low = split(b)
    left = jnp.concatenate(
        [
            jnp.concatenate([a_high, a_high], axis=1),
            jnp.concatenate([a_low, jnp.zeros_like(a_low)], axis=1),
        ],
        axis=0,
    )
    both = dot(left, jnp.concatenate([b_high, b_low], axis=0))
    return both[: a.shape[0]] + both[a.shape[0] :]


def last_kernel(
    cols,
    order,
    images_ref,
    both_ref,
    kspace_ref,
    mask_ref,
    top_near_ref,
    top_far_ref,
    low_near_ref,
    low_far_ref,
    recovered_ref,
    basis_ref,
    vectors_ref,
):
    both = both_ref[...]
    reach = images_ref.shape[1]
    factors = [exact(both, moved) for moved in moved_columns(order, cols)]
    chg, tile = kspace_ref.shape
    lanes = top_near_ref.shape[1]
    fold = lanes // chg
    deep = KER // fold
    step = cols // 2 * deep
    lead = reach - tile - KER - 2 * SUB
    images = stacked_dot(factors[0], images_ref[...]).T[lead:]
    rim = reach - tile - SUB - lead
    even, odd = None, None
    for a in range(0, deep, 2):
        turned = [
            jnp.concatenate(
                [
                    ref[pl.ds(k * deep + a + i, ref.shape[0] // step, stride=step), :]
                    for refs in ((top_near_ref, top_far_ref), (low_near_ref, low_far_ref))
                    for k in range(cols // 2)
                    for ref in refs
                ],
                axis=0,
            )
            for i in range(2)
        ]
        vectors = stacked_dot(factors[1], jnp.concatenate(turned, axis=1))
        vectors_ref[:, a * lanes : (a + 2) * lanes] = vectors
        projected = stacked_dot(images, vectors)
        shift = a * fold
        part = projected[rim - shift : rim - shift + tile + SUB, :lanes]
        even = part if even is None else even + part
        part = projected[rim - SUB - shift : rim - shift + tile + SUB, lanes:]
        odd = part if odd is None else odd + part
    total = even + odd[SUB - fold : SUB - fold + tile + SUB]
    estimate = total[SUB : SUB + tile]
    for f in range(1, fold):
        moved = pltpu.roll(total, lanes - f * chg, 1)
        estimate = estimate + moved[SUB - f : SUB - f + tile]
    estimate = estimate.T[:chg]
    owned = basis_ref.shape[0]
    start = pl.multiple_of(lax.axis_index("rows") * owned, owned)
    basis_ref[...] = vectors_ref[:, pl.ds(start, owned)].T
    estimate = estimate / KER
    residual = mask_ref[...].astype(jnp.float32) * (kspace_ref[...] - estimate)
    recovered_ref[...] = estimate + residual - jnp.clip(residual, -threshold, threshold)


def call(kernel, outs, *args, scratch=(), limit=12, scalars=0, micros=1):
    return pl.pallas_call(
        kernel,
        out_shape=[jax.ShapeDtypeStruct(shape, kind) for shape, kind in outs],
        in_specs=[pl.BlockSpec(memory_space=pltpu.VMEM)] * len(args),
        out_specs=[pl.BlockSpec(memory_space=pltpu.VMEM)] * (len(outs) - scalars)
        + [pl.BlockSpec(memory_space=pltpu.SMEM)] * scalars,
        scratch_shapes=list(scratch),
        compiler_params=pltpu.CompilerParams(vmem_limit_bytes=limit * 2**20),
        cost_estimate=pl.CostEstimate(
            flops=micros * 10**9, bytes_accessed=0, transcendentals=0
        ),
    )(*args)


def exchange(block, devices, mask, axes):
    return lax.ppermute(block, axes, [(i, i ^ mask) for i in range(devices)])


def with_masks(masks, mask):
    return masks + [m ^ mask for m in masks]


def after(value, *others):
    return lax.optimization_barrier((value,) + others)[0]


def rounds_of(low, high):
    masks = []
    while low < high:
        if 2 * low < high:
            masks.append([low, 2 * low, 3 * low])
        else:
            masks.append([low])
        low *= 4
    return masks


def gather_round(part, order, masks, devices, axes):
    part = jnp.concatenate(
        [part] + [exchange(part, devices, mask, axes) for mask in masks], axis=0
    )
    return part, order + [m ^ mask for mask in masks for m in order]


def gather_samples(sampled, basis, tiles, groups):
    devices = tiles * groups
    near, masks = sampled[None], [0]
    mask = devices // 2
    while mask > groups:
        near, masks = gather_round(near, masks, [mask], devices, AXES)
        if len(masks) == 2:
            basis = to_all(after(basis, near))
        mask //= 2
    half = near.shape[1] // 2
    halves = []
    for part, ways in (
        (near[:, :half], (groups, groups // 2)),
        (near[:, half:], (groups // 2, groups)),
    ):
        part, order = gather_round(part, masks, [ways[0]], devices, AXES)
        if halves:
            part = after(part, basis)
        pieces = [(part, order)]
        mask = ways[1]
        rest = groups // 4
        while mask > 1:
            pieces = pieces + [
                (exchange(part, devices, mask, AXES), [m ^ mask for m in order])
                for part, order in pieces
            ]
            mask, rest = rest, rest // 2
        halves.append(
            pieces
            + [(exchange(part, devices, 1, AXES), [m ^ 1 for m in order]) for part, order in pieces]
        )
    return halves, basis


def to_all(pieces, axes=AXES):
    return lax.all_to_all(pieces, axes, 0, 0, tiled=True)


def gather_group(group, devices):
    groups = group.shape[0]
    parts = [group[:1]]
    parts += [exchange(group[s : s + 1], devices, s, AXES) for s in range(1, groups)]
    return jnp.concatenate(parts, axis=0), list(range(groups))


def total_beside(kept, given, near, order, images, groups, devices):
    ways = []
    mask = devices // 2
    while mask >= groups:
        ways.append(mask)
        mask //= 2
    half = near.shape[1] // 2
    parts = [near[:, :half], near[:, half:]]
    orders = [order, order]
    ways = [ways, ways[-1:] + ways[:-1]]
    step = 0

    def advance():
        for i in range(2):
            parts[i], orders[i] = gather_round(
                parts[i], orders[i], [ways[i][step]], devices, AXES
            )

    total = kept + exchange(given, devices, 1, AXES)
    for partners in rounds_of(2, devices):
        terms = [exchange(total, devices, way, AXES) for way in partners]
        total = total + terms[0]
        if len(terms) == 3:
            total = total + (terms[1] + terms[2])
        images = after(images, terms[0])
        if step < len(ways[0]) - 1:
            advance()
            step += 1
    while step < len(ways[0]) - 1:
        advance()
        step += 1
    other = exchange(total, devices, 1, AXES)
    *parts, total, other = lax.optimization_barrier((*parts, total, other))
    pieces = []
    for i in range(2):
        mask = ways[i][-1]
        pieces += [parts[i], exchange(parts[i], devices, mask, AXES)]
        orders[i] = orders[i] + [m ^ mask for m in orders[i]]
    return (total, other), pieces, orders, to_all(images)


def column_shards(kspace, sample_mask, start_basis):
    f32, bf16 = jnp.float32, jnp.bfloat16
    tiles, groups = lax.axis_size("rows"), lax.axis_size("coil")
    devices = tiles * groups
    chg, tile = kspace.shape
    channels = chg * groups
    positions = tile * tiles
    owned, rank = start_basis.shape[1:]
    per_tile = owned // chg
    cols = rank // devices
    rows = cols * KER
    lanes = cols * chg

    sampled = kspace * sample_mask.astype(f32)
    (basis_send,) = call(
        functools.partial(prepare_kernel, cols, chg, per_tile),
        [((devices * per_tile, lanes), f32)],
        start_basis.reshape(owned, rank),
    )
    halves, basis_parts = gather_samples(
        sampled, basis_send.reshape(devices, per_tile, lanes), tiles, groups
    )
    starts = (0, chg // len(halves))
    orders = [(start, order) for start, half in zip(starts, halves) for _, order in half]
    wide = pltpu.VMEM((rows, positions), f32)
    moved = pltpu.VMEM((2 * rows, positions), bf16)
    samples, normal, send, group = call(
        functools.partial(passes_kernel, orders),
        [
            ((tiles, 2, groups, chg, tile), bf16),
            ((rows, channels), f32),
            ((tiles, groups, per_tile, lanes), f32),
            ((groups, rows * chg // lanes, lanes), f32),
        ],
        basis_parts.reshape(tiles, groups, per_tile, lanes),
        *[piece for half in halves for piece, _ in half],
        scratch=[wide, moved],
        limit=24,
        micros=12,
    )
    received = to_all(send.reshape(devices, per_tile, lanes))
    reach = tile + LANES
    (images,) = call(
        images_kernel,
        [((tiles, groups, cols, reach), f32)],
        samples,
        normal,
        scratch=[wide],
        limit=16,
        micros=2,
    )
    near, order = gather_group(group, devices)
    received, near = lax.optimization_barrier((received, images, near))[::2]
    half = ((rank // 2 + SUB, rank), f32)
    kept, given, turned = call(
        functools.partial(gram_kernel, cols, per_tile),
        [half, half, ((rank, owned), f32)],
        received.reshape(devices * per_tile, lanes),
        start_basis.reshape(owned, rank),
    )
    gram, pieces, order, images = total_beside(
        kept, given, near, order, images.reshape(devices, cols, reach), groups, devices
    )
    whole = ((rank, rank), f32)
    first, second, sound = call(
        factor_kernel, [whole, whole, ((1,), jnp.int32)], *gram, scalars=1, micros=12
    )

    def again():
        (gram,) = call(rows_kernel, [whole], turned, first)
        mask = 1
        while mask < devices:
            gram = gram + exchange(gram, devices, mask, AXES)
            mask *= 2
        return gram

    second = lax.cond(sound[0] == 1, lambda: second, again)
    (both,) = call(both_kernel, [whole], second, first, micros=0)
    recovered, basis = call(
        functools.partial(last_kernel, cols, order),
        [((chg, tile), f32), ((owned, rank), f32)],
        images.reshape(rank, reach),
        both,
        kspace,
        sample_mask,
        *[piece.reshape(-1, lanes) for piece in pieces],
        scratch=[pltpu.VMEM((rank, KER * chg), f32)],
        limit=16,
        micros=5,
    )
    return (recovered, basis.reshape(1, owned, rank))


def divides_columns(kspace, start_basis):
    tiles, groups = lax.axis_size("rows"), lax.axis_size("coil")
    devices = tiles * groups
    chg, tile = kspace.shape
    owned, rank = start_basis.shape[1:]
    return (
        devices & (devices - 1) == 0
        and tiles > 2
        and groups > 2
        and rank % (2 * SUB) == 0
        and rank % devices == 0
        and rank % LANES == 0
        and tile % LANES == 0
        and owned == SUB * chg
        and chg * (rank // devices) == LANES
        and 2 * (LANES // chg) == SUB
        and KER + 2 * SUB <= LANES
        and chg % (4 * SUB) == 0
        and (chg * groups) % LANES == 0
        and KER <= LANES
        and rank // devices <= SUB
        and rank // devices % 2 == 0
    )


def shards(kspace, sample_mask, start_basis):
    if divides_columns(kspace, start_basis):
        return column_shards(kspace, sample_mask, start_basis)
    return general_shards(kspace, sample_mask, start_basis)


def solution(mesh):
    return jax.shard_map(
        shards,
        mesh=mesh,
        in_specs=(P("coil", "rows"), P("coil", "rows"), P("coil", "rows", None)),
        out_specs=(P("coil", "rows"), P("coil", "rows", None)),
        check_vma=False,
    )
```

```python
import functools

import jax
import jax.numpy as jnp
from jax import lax
from jax.experimental import pallas as pl
from jax.experimental.pallas import tpu as pltpu
from jax.sharding import PartitionSpec as P

KER = 64
ITERS = 2
LANES = 128
SUB = 8
AXES = ("rows", "coil")


threshold = 0.05


def shifted(block, axis, distance):
    devices = range(lax.axis_size(axis))
    route = [((i - distance) % len(devices), i) for i in devices]
    return lax.ppermute(block, axis, route)


def orthonormal(normal_rows, gram_matrix):
    factor = jnp.linalg.cholesky(gram_matrix)
    return lax.linalg.triangular_solve(
        factor, normal_rows, left_side=False, lower=True, transpose_a=True
    )


def coil_total(partial_value):
    return lax.psum(partial_value, "coil")


def general_shards(kspace, sample_mask, start_basis):
    highest = lax.Precision.HIGHEST
    channels = kspace.shape[0]
    tile_rows = kspace.shape[1]
    mask_float = sample_mask.astype(jnp.float32)
    sampled = kspace * mask_float
    next_rim = shifted(sampled[:, : KER - 1], "rows", -1)
    extended = jnp.concatenate([sampled, next_rim], axis=1)
    hankel_cols = jnp.stack(
        [extended[:, offset : offset + tile_rows] for offset in range(KER)], axis=0
    )
    hankel_cols = hankel_cols.reshape(KER * channels, tile_rows)
    owned_basis = start_basis.reshape(start_basis.shape[1], start_basis.shape[2])
    whole_basis = lax.all_gather(owned_basis, "rows", axis=0, tiled=True)
    for iteration in range(ITERS):
        images = coil_total(
            lax.dot_general(
                whole_basis,
                hankel_cols,
                (((0,), (0,)), ((), ())),
                precision=highest,
                preferred_element_type=jnp.float32,
            )
        )
        local_normal = lax.dot_general(
            hankel_cols,
            images,
            (((1,), (1,)), ((), ())),
            precision=highest,
            preferred_element_type=jnp.float32,
        )
        normal_whole = lax.psum(local_normal, "rows")
        local_gram = jnp.dot(
            normal_whole.T, normal_whole, precision=highest, preferred_element_type=jnp.float32
        )
        gram_matrix = lax.psum(local_gram, "coil")
        whole_basis = orthonormal(normal_whole, gram_matrix)
    images = coil_total(
        lax.dot_general(
            whole_basis,
            hankel_cols,
            (((0,), (0,)), ((), ())),
            precision=highest,
            preferred_element_type=jnp.float32,
        )
    )
    projected = jnp.dot(whole_basis, images, precision=highest, preferred_element_type=jnp.float32)
    owned_count = whole_basis.shape[0] // lax.axis_size("rows")
    owned_basis = lax.dynamic_slice_in_dim(
        whole_basis, lax.axis_index("rows") * owned_count, owned_count, 0
    )
    stacked = projected.reshape(KER, channels, tile_rows)
    spread = jnp.zeros((channels, tile_rows + KER - 1), jnp.float32)
    for offset in range(KER):
        spread = spread.at[:, offset : offset + tile_rows].add(stacked[offset])
    carried = shifted(spread[:, tile_rows:], "rows", 1)
    estimate = spread[:, :tile_rows].at[:, : KER - 1].add(carried) / KER
    residual = mask_float * (kspace - estimate)
    recovered = estimate + residual - jnp.clip(residual, -threshold, threshold)
    return (recovered, owned_basis.reshape(1, owned_basis.shape[0], owned_basis.shape[1]))


def split(value):
    high = value.astype(jnp.bfloat16)
    low = (value - high.astype(jnp.float32)).astype(jnp.bfloat16)
    return high, low


def dot(a, b, dims=((1,), (0,))):
    return lax.dot_general(a, b, (dims, ((), ())), preferred_element_type=jnp.float32)


def dot3(a, b, dims=((1,), (0,))):
    a_high, a_low = split(a)
    b_high, b_low = split(b)
    return dot(a_high, b_high, dims) + (dot(a_high, b_low, dims) + dot(a_low, b_high, dims))


def square(size):
    at_row = lax.broadcasted_iota(jnp.int32, (size, size), 0)
    at_col = lax.broadcasted_iota(jnp.int32, (size, size), 1)
    return at_row, at_col


def prepare_kernel(cols, chg, per_tile, basis_ref, send_ref):
    turned = basis_ref[...].T
    devices = turned.shape[0] // cols
    for j in range(per_tile):
        part = turned[:, j * chg : (j + 1) * chg]
        row = jnp.concatenate([part[k * devices : (k + 1) * devices] for k in range(cols)], axis=1)
        send_ref[pl.ds(j, devices, stride=per_tile), :] = row


def images_of(vectors, samples_ref, wide_ref):
    rows, channels = vectors.shape
    cols = rows // KER
    high, low = split(vectors)
    at_row = lax.broadcasted_iota(jnp.int32, (rows, rows), 0)
    at_col = lax.broadcasted_iota(jnp.int32, (rows, rows), 1)
    flip = ((at_row // KER == at_col // KER) & (at_row % KER + at_col % KER == KER - 1)).astype(
        jnp.float32
    ).astype(jnp.bfloat16)
    both = dot(flip, jnp.concatenate([high, low], axis=1)).astype(jnp.bfloat16)
    high, low = both[:, :channels], both[:, channels:]
    parts = jnp.concatenate([high, high, low], axis=1)
    tiles = samples_ref.shape[0]
    tile = samples_ref.shape[-1]
    for t in range(tiles):
        block = samples_ref[t].reshape(2 * channels, tile)
        block = jnp.concatenate([block, block[:channels]], axis=0)
        wide_ref[:, t * tile : (t + 1) * tile] = dot(parts, block)
    images = []
    for k in range(cols):
        total = None
        for i in reversed(range(0, KER, SUB)):
            part = wide_ref[k * KER + i : k * KER + i + SUB, :]
            total = part if total is None else pltpu.roll(total, SUB, 1) + part
        total = pltpu.roll(total, 0, 1, stride=1, stride_axis=0)
        images.append(jnp.sum(total, axis=0, keepdims=True))
    return images


def normal_of(images, samples_ref, moved_ref):
    cols = len(images)
    positions = images[0].shape[1]
    tiles = samples_ref.shape[0]
    tile = samples_ref.shape[-1]
    channels = samples_ref.shape[2] * samples_ref.shape[3]
    rows = cols * KER
    for k in range(cols):
        base = jnp.broadcast_to(images[k], (SUB, positions))
        base = pltpu.roll(base, positions - (KER - 1), 1, stride=1, stride_axis=0)
        for j in range(0, KER, 2 * SUB):
            first = base if j == 0 else pltpu.roll(base, j, 1)
            second = pltpu.roll(base, j + SUB, 1)
            high, low = split(jnp.concatenate([first, second], axis=0))
            moved_ref[k * KER + j : k * KER + j + 2 * SUB, :] = high
            moved_ref[rows + k * KER + j : rows + k * KER + j + 2 * SUB, :] = low
    total = jnp.zeros((rows, channels), jnp.float32)
    for t in range(tiles):
        block = samples_ref[t].reshape(2 * channels, tile)
        block = jnp.concatenate([block[:channels], block[channels:], block[:channels]], axis=1)
        lanes = slice(t * tile, (t + 1) * tile)
        high, low = moved_ref[:rows, lanes], moved_ref[rows:, lanes]
        total = total + dot(jnp.concatenate([high, high, low], axis=1), block, ((1,), (1,)))
    return total


def store_by_rows(normal, send_ref):
    tiles, groups, per_tile, lanes = send_ref.shape
    cols = normal.shape[0] // KER
    chg = normal.shape[1] // groups
    for g in range(groups):
        joined = jnp.concatenate(
            [normal[k * KER : (k + 1) * KER, g * chg : (g + 1) * chg] for k in range(cols)], axis=1
        )
        send_ref[:, g] = joined.reshape(tiles, per_tile, lanes)


def store_by_groups(normal_ref, group_ref):
    groups, count, lanes = group_ref.shape
    rows, channels = normal_ref.shape
    chg = channels // groups
    fold = lanes // chg
    cols = rows // KER
    deep = KER // fold
    me = lax.axis_index("coil")
    parts = [
        [normal_ref[pl.ds(k * KER + f, deep, stride=fold), :] for f in range(fold)]
        for k in range(cols)
    ]
    for g in range(groups):
        joined = [
            jnp.concatenate([part[:, g * chg : (g + 1) * chg] for part in parts[k]], axis=1)
            for k in range(cols)
        ]
        group_ref[lax.bitwise_xor(me, g)] = jnp.concatenate(joined, axis=0)


def passes_kernel(orders, basis_ref, *refs):
    *pieces, samples_ref, normal_ref, send_ref, group_ref, wide_ref, moved_ref = refs
    tiles, _, groups, chg, tile = samples_ref.shape
    me = lax.axis_index("rows") * groups + lax.axis_index("coil")
    for (start, order), piece_ref in zip(orders, pieces):
        count = piece_ref.shape[1]
        for slot, mask in enumerate(order):
            high, low = split(piece_ref[slot])
            source = lax.bitwise_xor(me, mask)
            t, g = source // groups, source % groups
            samples_ref[t, 0, g, start : start + count] = high
            samples_ref[t, 1, g, start : start + count] = low
    cols = basis_ref.shape[-1] // chg
    rows = []
    for k in range(cols):
        rows.append(
            jnp.concatenate(
                [
                    basis_ref[:, g].reshape(KER, cols * chg)[:, k * chg : (k + 1) * chg]
                    for g in range(groups)
                ],
                axis=1,
            )
        )
    vectors = jnp.concatenate(rows, axis=0)
    normal = normal_of(images_of(vectors, samples_ref, wide_ref), samples_ref, moved_ref)
    power = jnp.zeros((1, tile), jnp.float32)
    for t in range(samples_ref.shape[0]):
        value = samples_ref[t, 0].reshape(groups * chg, tile).astype(jnp.float32)
        power = power + jnp.sum(value * value, axis=0, keepdims=True)
    normal = normal * (groups * chg / jnp.sum(power))
    normal = normal_of(images_of(normal, samples_ref, wide_ref), samples_ref, moved_ref)
    normal_ref[...] = normal
    store_by_rows(normal, send_ref)
    store_by_groups(normal_ref, group_ref)


def images_kernel(samples_ref, vectors_ref, send_ref, wide_ref):
    tiles, groups, cols, reach = send_ref.shape
    tile = samples_ref.shape[-1]
    images = jnp.concatenate(images_of(vectors_ref[...], samples_ref, wide_ref), axis=0)
    positions = images.shape[1]
    images = pltpu.roll(images, positions - (KER - 1), 1)
    rim = reach - tile
    for t in range(tiles):
        if t == 0:
            part = jnp.concatenate([images[:, positions - rim :], images[:, :tile]], axis=1)
        else:
            part = images[:, t * tile - rim : (t + 1) * tile]
        for g in range(groups):
            send_ref[t, g] = part


def gather_turned(received_ref, cols, per_tile):
    count, lanes = received_ref.shape
    devices = count // per_tile
    chg = lanes // cols
    loaded = [received_ref[pl.ds(j, devices, stride=per_tile), :] for j in range(per_tile)]
    return jnp.concatenate(
        [
            jnp.concatenate(
                [loaded[j][:, k * chg : (k + 1) * chg] for j in range(per_tile)], axis=1
            )
            for k in range(cols)
        ],
        axis=0,
    )


def exact(a, b, dims=((1,), (0,))):
    return lax.dot_general(
        a, b, (dims, ((), ())), precision=lax.Precision.HIGHEST, preferred_element_type=jnp.float32
    )


def gram_kernel(cols, per_tile, received_ref, basis_ref, kept_ref, given_ref, turned_ref):
    turned = gather_turned(received_ref, cols, per_tile)
    first = exact(basis_ref[...], turned, ((0,), (1,)))
    second = exact(turned, turned, ((1,), (1,)))
    turned_ref[...] = turned
    at_row, at_col = square(first.shape[0])
    packed = jnp.where(at_row >= at_col, first, second)
    line = jnp.sum(jnp.where(at_row == at_col, second, 0.0), axis=0, keepdims=True)
    line = jnp.broadcast_to(line, (SUB, line.shape[1]))
    half = packed.shape[0] // 2
    odd = lax.axis_index("coil") % 2 == 1
    kept_ref[:half] = jnp.where(odd, packed[half:], packed[:half])
    given_ref[:half] = jnp.where(odd, packed[:half], packed[half:])
    kept_ref[half:] = line
    given_ref[half:] = line


def load_grams(kept_ref, other_ref):
    odd = lax.axis_index("coil") % 2 == 1
    kept, other = kept_ref[...], other_ref[...]
    low, high = jnp.where(odd, other, kept), jnp.where(odd, kept, other)
    half = low.shape[0] - SUB
    packed = jnp.concatenate([low[:half], high[:half]], axis=0)
    line = low[half : half + 1]
    at_row, at_col = square(packed.shape[0])
    turned = packed.T
    first = jnp.where(at_row >= at_col, packed, turned)
    second = jnp.where(at_row > at_col, turned, packed)
    return first, jnp.where(at_row == at_col, line, second), line


def inverse_factor(gram):
    size = gram.shape[0]
    shape = (SUB, size)
    at_row = lax.broadcasted_iota(jnp.int32, (size, size), 0)
    at_col = lax.broadcasted_iota(jnp.int32, (size, size), 1)
    unit = (at_row == at_col).astype(jnp.float32)
    left = [gram[b : b + SUB] for b in range(0, size, SUB)]
    right = [unit[b : b + SUB] for b in range(0, size, SUB)]
    sub = lax.broadcasted_iota(jnp.int32, shape, 0)
    done = []
    for b in range(len(left)):
        spread = {
            c: [
                jnp.broadcast_to(left[c][:, b * SUB + k : b * SUB + k + 1], shape)
                for k in range(SUB)
            ]
            for c in range(b, len(left))
        }
        entry = {
            (i, k): jnp.broadcast_to(spread[b][k][i : i + 1], shape)
            for k in range(SUB)
            for i in range(k, SUB)
        }
        inverse = {}
        for k in range(SUB):
            root = lax.rsqrt(entry[k, k])
            inverse[k, k] = root
            for i in range(k + 1, SUB):
                entry[i, k] = entry[i, k] * root
            for i in range(k + 1, SUB):
                for m in range(k + 1, i + 1):
                    entry[i, m] = entry[i, m] - entry[i, k] * entry[m, k]
        for i in range(1, SUB):
            for k in range(i):
                total = entry[i, k] * inverse[k, k]
                for m in range(k + 1, i):
                    total = total + entry[i, m] * inverse[m, k]
                inverse[i, k] = -(total * inverse[i, i])

        def solved(rows):
            whole = [jnp.broadcast_to(rows[k : k + 1], shape) for k in range(SUB)]
            first = []
            for i in range(SUB):
                total = inverse[i, 0] * whole[0]
                for k in range(1, i + 1):
                    total = total + inverse[i, k] * whole[k]
                first.append(total)
            second = []
            for k in range(SUB):
                total = inverse[k, k] * first[k]
                for i in range(k + 1, SUB):
                    total = total + inverse[i, k] * first[i]
                second.append(total)
            return first, second

        lower, lower_again = solved(right[b])
        row = lower[0]
        for i in range(1, SUB):
            row = jnp.where(sub == i, lower[i], row)
        done.append(row)
        if b + 1 < len(left):
            _, upper_again = solved(left[b])
            for c in range(b + 1, len(left)):
                for k in range(SUB):
                    left[c] = left[c] - spread[c][k] * upper_again[k]
                    right[c] = right[c] - spread[c][k] * lower_again[k]
    return jnp.concatenate(done, axis=0)


def factor_kernel(gram_ref, other_ref, inverse_ref, next_ref, sound_ref):
    gram, raw, line = load_grams(gram_ref, other_ref)
    inverse = inverse_factor(gram)
    inverse_ref[...] = inverse
    gram = exact(exact(inverse, raw), inverse, ((1,), (1,)))
    next_ref[...] = gram
    at_row, at_col = square(gram.shape[0])
    terms = jnp.sum(inverse * inverse * line, axis=1, keepdims=True)
    result = jnp.sum(jnp.where(at_row == at_col, gram, 0.0), axis=1, keepdims=True)
    worst = jnp.max(jnp.where(terms <= 64.0 * result, 0, 1))
    sound_ref[0] = 1 - worst


def rows_kernel(turned_ref, inverse_ref, gram_ref):
    turned = exact(inverse_ref[...], turned_ref[...])
    gram_ref[...] = exact(turned, turned, ((1,), (1,)))


def both_kernel(gram_ref, inverse_ref, both_ref):
    both_ref[...] = exact(inverse_factor(gram_ref[...]), inverse_ref[...])


def moved_columns(order, cols):
    devices = len(order[0])
    at_row, at_col = square(devices * cols)
    turn = at_col % cols * devices + at_col // cols
    me = lax.axis_index("rows") * lax.axis_size("coil") + lax.axis_index("coil")
    slot = at_col % devices
    mask = jnp.zeros_like(slot)
    bit = 1
    while bit < devices:
        step = jnp.where(2 * at_col < at_col.shape[1], order[0][bit], order[1][bit])
        mask = mask | jnp.where(slot & bit != 0, step, 0)
        bit *= 2
    source = at_col - slot + lax.bitwise_xor(mask, jnp.full_like(mask, me))
    return [(at_row == place).astype(jnp.float32) for place in (turn, source)]


def stacked_dot(a, b):
    a_high, a_low = split(a)
    b_high, b_low = split(b)
    left = jnp.concatenate(
        [
            jnp.concatenate([a_high, a_high], axis=1),
            jnp.concatenate([a_low, jnp.zeros_like(a_low)], axis=1),
        ],
        axis=0,
    )
    both = dot(left, jnp.concatenate([b_high, b_low], axis=0))
    return both[: a.shape[0]] + both[a.shape[0] :]


def last_kernel(
    cols,
    order,
    images_ref,
    both_ref,
    kspace_ref,
    mask_ref,
    top_near_ref,
    top_far_ref,
    low_near_ref,
    low_far_ref,
    recovered_ref,
    basis_ref,
    vectors_ref,
):
    both = both_ref[...]
    reach = images_ref.shape[1]
    factors = [exact(both, moved) for moved in moved_columns(order, cols)]
    chg, tile = kspace_ref.shape
    lanes = top_near_ref.shape[1]
    fold = lanes // chg
    deep = KER // fold
    step = cols // 2 * deep
    lead = reach - tile - KER - 2 * SUB
    images = stacked_dot(factors[0], images_ref[...]).T[lead:]
    rim = reach - tile - SUB - lead
    even, odd = None, None
    for a in range(0, deep, 2):
        turned = [
            jnp.concatenate(
                [
                    ref[pl.ds(k * deep + a + i, ref.shape[0] // step, stride=step), :]
                    for refs in ((top_near_ref, top_far_ref), (low_near_ref, low_far_ref))
                    for k in range(cols // 2)
                    for ref in refs
                ],
                axis=0,
            )
            for i in range(2)
        ]
        vectors = stacked_dot(factors[1], jnp.concatenate(turned, axis=1))
        vectors_ref[:, a * lanes : (a + 2) * lanes] = vectors
        projected = stacked_dot(images, vectors)
        shift = a * fold
        part = projected[rim - shift : rim - shift + tile + SUB, :lanes]
        even = part if even is None else even + part
        part = projected[rim - SUB - shift : rim - shift + tile + SUB, lanes:]
        odd = part if odd is None else odd + part
    total = even + odd[SUB - fold : SUB - fold + tile + SUB]
    estimate = total[SUB : SUB + tile]
    for f in range(1, fold):
        moved = pltpu.roll(total, lanes - f * chg, 1)
        estimate = estimate + moved[SUB - f : SUB - f + tile]
    estimate = estimate.T[:chg]
    owned = basis_ref.shape[0]
    start = pl.multiple_of(lax.axis_index("rows") * owned, owned)
    basis_ref[...] = vectors_ref[:, pl.ds(start, owned)].T
    estimate = estimate / KER
    residual = mask_ref[...].astype(jnp.float32) * (kspace_ref[...] - estimate)
    recovered_ref[...] = estimate + residual - jnp.clip(residual, -threshold, threshold)


def call(kernel, outs, *args, scratch=(), limit=12, scalars=0, micros=1):
    return pl.pallas_call(
        kernel,
        out_shape=[jax.ShapeDtypeStruct(shape, kind) for shape, kind in outs],
        in_specs=[pl.BlockSpec(memory_space=pltpu.VMEM)] * len(args),
        out_specs=[pl.BlockSpec(memory_space=pltpu.VMEM)] * (len(outs) - scalars)
        + [pl.BlockSpec(memory_space=pltpu.SMEM)] * scalars,
        scratch_shapes=list(scratch),
        compiler_params=pltpu.CompilerParams(vmem_limit_bytes=limit * 2**20),
        cost_estimate=pl.CostEstimate(
            flops=micros * 10**9, bytes_accessed=0, transcendentals=0
        ),
    )(*args)


def exchange(block, devices, mask, axes):
    return lax.ppermute(block, axes, [(i, i ^ mask) for i in range(devices)])


def with_masks(masks, mask):
    return masks + [m ^ mask for m in masks]


def after(value, *others):
    return lax.optimization_barrier((value,) + others)[0]


def rounds_of(low, high):
    masks = []
    while low < high:
        if 2 * low < high:
            masks.append([low, 2 * low, 3 * low])
        else:
            masks.append([low])
        low *= 4
    return masks


def gather_round(part, order, masks, devices, axes):
    part = jnp.concatenate(
        [part] + [exchange(part, devices, mask, axes) for mask in masks], axis=0
    )
    return part, order + [m ^ mask for mask in masks for m in order]


def gather_samples(sampled, basis, tiles, groups):
    devices = tiles * groups
    near, masks = sampled[None], [0]
    mask = devices // 2
    while mask > groups:
        near, masks = gather_round(near, masks, [mask], devices, AXES)
        mask //= 2
    basis = to_all(basis)
    near = after(near, basis)
    half = near.shape[1] // 2
    halves = []
    for part, ways in (
        (near[:, :half], (groups, groups // 2)),
        (near[:, half:], (groups // 2, groups)),
    ):
        part, order = gather_round(part, masks, [ways[0]], devices, AXES)
        pieces = [(part, order)]
        mask = ways[1]
        rest = groups // 4
        while mask > 1:
            pieces = pieces + [
                (exchange(part, devices, mask, AXES), [m ^ mask for m in order])
                for part, order in pieces
            ]
            mask, rest = rest, rest // 2
        halves.append(
            pieces
            + [(exchange(part, devices, 1, AXES), [m ^ 1 for m in order]) for part, order in pieces]
        )
    return halves, basis


def to_all(pieces, axes=AXES):
    return lax.all_to_all(pieces, axes, 0, 0, tiled=True)


def gather_group(group, devices):
    groups = group.shape[0]
    parts = [group[:1]]
    parts += [exchange(group[s : s + 1], devices, s, AXES) for s in range(1, groups)]
    return jnp.concatenate(parts, axis=0), list(range(groups))


def total_beside(kept, given, near, order, images, groups, devices):
    ways = []
    mask = devices // 2
    while mask >= groups:
        ways.append(mask)
        mask //= 2
    half = near.shape[1] // 2
    parts = [near[:, :half], near[:, half:]]
    orders = [order, order]
    ways = [ways, ways[-1:] + ways[:-1]]
    step = 0

    def advance():
        for i in range(2):
            parts[i], orders[i] = gather_round(
                parts[i], orders[i], [ways[i][step]], devices, AXES
            )

    total = kept + exchange(given, devices, 1, AXES)
    for partners in rounds_of(2, devices):
        terms = [exchange(total, devices, way, AXES) for way in partners]
        total = total + terms[0]
        if len(terms) == 3:
            total = total + (terms[1] + terms[2])
        if step < len(ways[0]) - 1:
            advance()
            step += 1
    while step < len(ways[0]) - 1:
        advance()
        step += 1
    other = exchange(total, devices, 1, AXES)
    *parts, total, other, images = lax.optimization_barrier((*parts, total, other, images))
    pieces = []
    for i in range(2):
        mask = ways[i][-1]
        pieces += [parts[i], exchange(parts[i], devices, mask, AXES)]
        orders[i] = orders[i] + [m ^ mask for m in orders[i]]
    return (total, other), pieces, orders, to_all(images)


def column_shards(kspace, sample_mask, start_basis):
    f32, bf16 = jnp.float32, jnp.bfloat16
    tiles, groups = lax.axis_size("rows"), lax.axis_size("coil")
    devices = tiles * groups
    chg, tile = kspace.shape
    channels = chg * groups
    positions = tile * tiles
    owned, rank = start_basis.shape[1:]
    per_tile = owned // chg
    cols = rank // devices
    rows = cols * KER
    lanes = cols * chg

    sampled = kspace * sample_mask.astype(f32)
    (basis_send,) = call(
        functools.partial(prepare_kernel, cols, chg, per_tile),
        [((devices * per_tile, lanes), f32)],
        start_basis.reshape(owned, rank),
    )
    halves, basis_parts = gather_samples(
        sampled, basis_send.reshape(devices, per_tile, lanes), tiles, groups
    )
    starts = (0, chg // len(halves))
    orders = [(start, order) for start, half in zip(starts, halves) for _, order in half]
    wide = pltpu.VMEM((rows, positions), f32)
    moved = pltpu.VMEM((2 * rows, positions), bf16)
    samples, normal, send, group = call(
        functools.partial(passes_kernel, orders),
        [
            ((tiles, 2, groups, chg, tile), bf16),
            ((rows, channels), f32),
            ((tiles, groups, per_tile, lanes), f32),
            ((groups, rows * chg // lanes, lanes), f32),
        ],
        basis_parts.reshape(tiles, groups, per_tile, lanes),
        *[piece for half in halves for piece, _ in half],
        scratch=[wide, moved],
        limit=24,
        micros=12,
    )
    received = to_all(send.reshape(devices, per_tile, lanes))
    reach = tile + LANES
    (images,) = call(
        images_kernel,
        [((tiles, groups, cols, reach), f32)],
        samples,
        normal,
        scratch=[wide],
        limit=16,
        micros=2,
    )
    near, order = gather_group(group, devices)
    received = after(received, images, near)
    half = ((rank // 2 + SUB, rank), f32)
    kept, given, turned = call(
        functools.partial(gram_kernel, cols, per_tile),
        [half, half, ((rank, owned), f32)],
        received.reshape(devices * per_tile, lanes),
        start_basis.reshape(owned, rank),
    )
    gram, pieces, order, images = total_beside(
        kept, given, near, order, images.reshape(devices, cols, reach), groups, devices
    )
    whole = ((rank, rank), f32)
    first, second, sound = call(
        factor_kernel, [whole, whole, ((1,), jnp.int32)], *gram, scalars=1, micros=12
    )

    def again():
        (gram,) = call(rows_kernel, [whole], turned, first)
        mask = 1
        while mask < devices:
            gram = gram + exchange(gram, devices, mask, AXES)
            mask *= 2
        return gram

    second = lax.cond(sound[0] == 1, lambda: second, again)
    (both,) = call(both_kernel, [whole], second, first, micros=0)
    recovered, basis = call(
        functools.partial(last_kernel, cols, order),
        [((chg, tile), f32), ((owned, rank), f32)],
        images.reshape(rank, reach),
        both,
        kspace,
        sample_mask,
        *[piece.reshape(-1, lanes) for piece in pieces],
        scratch=[pltpu.VMEM((rank, KER * chg), f32)],
        limit=16,
        micros=5,
    )
    return (recovered, basis.reshape(1, owned, rank))


def divides_columns(kspace, start_basis):
    tiles, groups = lax.axis_size("rows"), lax.axis_size("coil")
    devices = tiles * groups
    chg, tile = kspace.shape
    owned, rank = start_basis.shape[1:]
    return (
        devices & (devices - 1) == 0
        and tiles > 2
        and groups > 2
        and rank % (2 * SUB) == 0
        and rank % devices == 0
        and rank % LANES == 0
        and tile % LANES == 0
        and owned == SUB * chg
        and chg * (rank // devices) == LANES
        and 2 * (LANES // chg) == SUB
        and KER + 2 * SUB <= LANES
        and chg % (4 * SUB) == 0
        and (chg * groups) % LANES == 0
        and KER <= LANES
        and rank // devices <= SUB
        and rank // devices % 2 == 0
    )


def shards(kspace, sample_mask, start_basis):
    if divides_columns(kspace, start_basis):
        return column_shards(kspace, sample_mask, start_basis)
    return general_shards(kspace, sample_mask, start_basis)


def solution(mesh):
    return jax.shard_map(
        shards,
        mesh=mesh,
        in_specs=(P("coil", "rows"), P("coil", "rows"), P("coil", "rows", None)),
        out_specs=(P("coil", "rows"), P("coil", "rows", None)),
        check_vma=False,
    )
```

```python
import functools

import jax
import jax.numpy as jnp
from jax import lax
from jax.experimental import pallas as pl
from jax.experimental.pallas import tpu as pltpu
from jax.sharding import PartitionSpec as P

KER = 64
ITERS = 2
LANES = 128
SUB = 8
AXES = ("rows", "coil")


threshold = 0.05


def shifted(block, axis, distance):
    devices = range(lax.axis_size(axis))
    route = [((i - distance) % len(devices), i) for i in devices]
    return lax.ppermute(block, axis, route)


def orthonormal(normal_rows, gram_matrix):
    factor = jnp.linalg.cholesky(gram_matrix)
    return lax.linalg.triangular_solve(
        factor, normal_rows, left_side=False, lower=True, transpose_a=True
    )


def coil_total(partial_value):
    return lax.psum(partial_value, "coil")


def general_shards(kspace, sample_mask, start_basis):
    highest = lax.Precision.HIGHEST
    channels = kspace.shape[0]
    tile_rows = kspace.shape[1]
    mask_float = sample_mask.astype(jnp.float32)
    sampled = kspace * mask_float
    next_rim = shifted(sampled[:, : KER - 1], "rows", -1)
    extended = jnp.concatenate([sampled, next_rim], axis=1)
    hankel_cols = jnp.stack(
        [extended[:, offset : offset + tile_rows] for offset in range(KER)], axis=0
    )
    hankel_cols = hankel_cols.reshape(KER * channels, tile_rows)
    owned_basis = start_basis.reshape(start_basis.shape[1], start_basis.shape[2])
    whole_basis = lax.all_gather(owned_basis, "rows", axis=0, tiled=True)
    for iteration in range(ITERS):
        images = coil_total(
            lax.dot_general(
                whole_basis,
                hankel_cols,
                (((0,), (0,)), ((), ())),
                precision=highest,
                preferred_element_type=jnp.float32,
            )
        )
        local_normal = lax.dot_general(
            hankel_cols,
            images,
            (((1,), (1,)), ((), ())),
            precision=highest,
            preferred_element_type=jnp.float32,
        )
        normal_whole = lax.psum(local_normal, "rows")
        local_gram = jnp.dot(
            normal_whole.T, normal_whole, precision=highest, preferred_element_type=jnp.float32
        )
        gram_matrix = lax.psum(local_gram, "coil")
        whole_basis = orthonormal(normal_whole, gram_matrix)
    images = coil_total(
        lax.dot_general(
            whole_basis,
            hankel_cols,
            (((0,), (0,)), ((), ())),
            precision=highest,
            preferred_element_type=jnp.float32,
        )
    )
    projected = jnp.dot(whole_basis, images, precision=highest, preferred_element_type=jnp.float32)
    owned_count = whole_basis.shape[0] // lax.axis_size("rows")
    owned_basis = lax.dynamic_slice_in_dim(
        whole_basis, lax.axis_index("rows") * owned_count, owned_count, 0
    )
    stacked = projected.reshape(KER, channels, tile_rows)
    spread = jnp.zeros((channels, tile_rows + KER - 1), jnp.float32)
    for offset in range(KER):
        spread = spread.at[:, offset : offset + tile_rows].add(stacked[offset])
    carried = shifted(spread[:, tile_rows:], "rows", 1)
    estimate = spread[:, :tile_rows].at[:, : KER - 1].add(carried) / KER
    residual = mask_float * (kspace - estimate)
    recovered = estimate + residual - jnp.clip(residual, -threshold, threshold)
    return (recovered, owned_basis.reshape(1, owned_basis.shape[0], owned_basis.shape[1]))


def split(value):
    high = value.astype(jnp.bfloat16)
    low = (value - high.astype(jnp.float32)).astype(jnp.bfloat16)
    return high, low


def dot(a, b, dims=((1,), (0,))):
    return lax.dot_general(a, b, (dims, ((), ())), preferred_element_type=jnp.float32)


def dot3(a, b, dims=((1,), (0,))):
    a_high, a_low = split(a)
    b_high, b_low = split(b)
    return dot(a_high, b_high, dims) + (dot(a_high, b_low, dims) + dot(a_low, b_high, dims))


def square(size):
    at_row = lax.broadcasted_iota(jnp.int32, (size, size), 0)
    at_col = lax.broadcasted_iota(jnp.int32, (size, size), 1)
    return at_row, at_col


def prepare_kernel(cols, chg, per_tile, basis_ref, send_ref):
    turned = basis_ref[...].T
    devices = turned.shape[0] // cols
    for j in range(per_tile):
        part = turned[:, j * chg : (j + 1) * chg]
        row = jnp.concatenate([part[k * devices : (k + 1) * devices] for k in range(cols)], axis=1)
        send_ref[pl.ds(j, devices, stride=per_tile), :] = row


def images_of(vectors, samples_ref, wide_ref):
    rows, channels = vectors.shape
    cols = rows // KER
    high, low = split(vectors)
    at_row = lax.broadcasted_iota(jnp.int32, (rows, rows), 0)
    at_col = lax.broadcasted_iota(jnp.int32, (rows, rows), 1)
    flip = ((at_row // KER == at_col // KER) & (at_row % KER + at_col % KER == KER - 1)).astype(
        jnp.float32
    ).astype(jnp.bfloat16)
    both = dot(flip, jnp.concatenate([high, low], axis=1)).astype(jnp.bfloat16)
    high, low = both[:, :channels], both[:, channels:]
    parts = jnp.concatenate([high, high, low], axis=1)
    tiles = samples_ref.shape[0]
    tile = samples_ref.shape[-1]
    for t in range(tiles):
        block = samples_ref[t].reshape(2 * channels, tile)
        block = jnp.concatenate([block, block[:channels]], axis=0)
        wide_ref[:, t * tile : (t + 1) * tile] = dot(parts, block)
    images = []
    for k in range(cols):
        total = None
        for i in reversed(range(0, KER, SUB)):
            part = wide_ref[k * KER + i : k * KER + i + SUB, :]
            total = part if total is None else pltpu.roll(total, SUB, 1) + part
        total = pltpu.roll(total, 0, 1, stride=1, stride_axis=0)
        images.append(jnp.sum(total, axis=0, keepdims=True))
    return images


def normal_of(images, samples_ref, moved_ref):
    cols = len(images)
    positions = images[0].shape[1]
    tiles = samples_ref.shape[0]
    tile = samples_ref.shape[-1]
    channels = samples_ref.shape[2] * samples_ref.shape[3]
    rows = cols * KER
    for k in range(cols):
        base = jnp.broadcast_to(images[k], (SUB, positions))
        base = pltpu.roll(base, positions - (KER - 1), 1, stride=1, stride_axis=0)
        for j in range(0, KER, 2 * SUB):
            first = base if j == 0 else pltpu.roll(base, j, 1)
            second = pltpu.roll(base, j + SUB, 1)
            high, low = split(jnp.concatenate([first, second], axis=0))
            moved_ref[k * KER + j : k * KER + j + 2 * SUB, :] = high
            moved_ref[rows + k * KER + j : rows + k * KER + j + 2 * SUB, :] = low
    high = jnp.zeros((rows, 2 * channels), jnp.float32)
    for t in range(tiles):
        block = samples_ref[t].reshape(2 * channels, tile)
        high = high + dot(moved_ref[:rows, t * tile : (t + 1) * tile], block, ((1,), (1,)))
    low = jnp.zeros((rows, channels), jnp.float32)
    for t in range(tiles):
        block = samples_ref[t, 0].reshape(channels, tile)
        low = low + dot(moved_ref[rows:, t * tile : (t + 1) * tile], block, ((1,), (1,)))
    return high[:, :channels] + (high[:, channels:] + low)


def store_by_rows(normal, send_ref):
    tiles, groups, per_tile, lanes = send_ref.shape
    cols = normal.shape[0] // KER
    chg = normal.shape[1] // groups
    for g in range(groups):
        joined = jnp.concatenate(
            [normal[k * KER : (k + 1) * KER, g * chg : (g + 1) * chg] for k in range(cols)], axis=1
        )
        send_ref[:, g] = joined.reshape(tiles, per_tile, lanes)


def store_by_groups(normal_ref, group_ref):
    groups, count, lanes = group_ref.shape
    rows, channels = normal_ref.shape
    chg = channels // groups
    fold = lanes // chg
    cols = rows // KER
    deep = KER // fold
    me = lax.axis_index("coil")
    parts = [
        [normal_ref[pl.ds(k * KER + f, deep, stride=fold), :] for f in range(fold)]
        for k in range(cols)
    ]
    for g in range(groups):
        joined = [
            jnp.concatenate([part[:, g * chg : (g + 1) * chg] for part in parts[k]], axis=1)
            for k in range(cols)
        ]
        group_ref[lax.bitwise_xor(me, g)] = jnp.concatenate(joined, axis=0)


def passes_kernel(orders, basis_ref, *refs):
    *pieces, samples_ref, normal_ref, send_ref, group_ref, wide_ref, moved_ref = refs
    tiles, _, groups, chg, tile = samples_ref.shape
    me = lax.axis_index("rows") * groups + lax.axis_index("coil")
    for (start, order), piece_ref in zip(orders, pieces):
        count = piece_ref.shape[1]
        for slot, mask in enumerate(order):
            high, low = split(piece_ref[slot])
            source = lax.bitwise_xor(me, mask)
            t, g = source // groups, source % groups
            samples_ref[t, 0, g, start : start + count] = high
            samples_ref[t, 1, g, start : start + count] = low
    cols = basis_ref.shape[-1] // chg
    rows = []
    for k in range(cols):
        rows.append(
            jnp.concatenate(
                [
                    basis_ref[:, g].reshape(KER, cols * chg)[:, k * chg : (k + 1) * chg]
                    for g in range(groups)
                ],
                axis=1,
            )
        )
    vectors = jnp.concatenate(rows, axis=0)
    normal = normal_of(images_of(vectors, samples_ref, wide_ref), samples_ref, moved_ref)
    power = jnp.zeros((1, tile), jnp.float32)
    for t in range(samples_ref.shape[0]):
        value = samples_ref[t, 0].reshape(groups * chg, tile).astype(jnp.float32)
        power = power + jnp.sum(value * value, axis=0, keepdims=True)
    normal = normal * (groups * chg / jnp.sum(power))
    normal = normal_of(images_of(normal, samples_ref, wide_ref), samples_ref, moved_ref)
    normal_ref[...] = normal
    store_by_rows(normal, send_ref)
    store_by_groups(normal_ref, group_ref)


def images_kernel(samples_ref, vectors_ref, send_ref, wide_ref):
    tiles, groups, cols, reach = send_ref.shape
    tile = samples_ref.shape[-1]
    images = jnp.concatenate(images_of(vectors_ref[...], samples_ref, wide_ref), axis=0)
    positions = images.shape[1]
    images = pltpu.roll(images, positions - (KER - 1), 1)
    rim = reach - tile
    for t in range(tiles):
        if t == 0:
            part = jnp.concatenate([images[:, positions - rim :], images[:, :tile]], axis=1)
        else:
            part = images[:, t * tile - rim : (t + 1) * tile]
        for g in range(groups):
            send_ref[t, g] = part


def gather_turned(received_ref, cols, per_tile):
    count, lanes = received_ref.shape
    devices = count // per_tile
    chg = lanes // cols
    loaded = [received_ref[pl.ds(j, devices, stride=per_tile), :] for j in range(per_tile)]
    return jnp.concatenate(
        [
            jnp.concatenate(
                [loaded[j][:, k * chg : (k + 1) * chg] for j in range(per_tile)], axis=1
            )
            for k in range(cols)
        ],
        axis=0,
    )


def exact(a, b, dims=((1,), (0,))):
    return lax.dot_general(
        a, b, (dims, ((), ())), precision=lax.Precision.HIGHEST, preferred_element_type=jnp.float32
    )


def gram_kernel(cols, per_tile, received_ref, basis_ref, kept_ref, given_ref, turned_ref):
    turned = gather_turned(received_ref, cols, per_tile)
    first = exact(basis_ref[...], turned, ((0,), (1,)))
    second = exact(turned, turned, ((1,), (1,)))
    turned_ref[...] = turned
    at_row, at_col = square(first.shape[0])
    packed = jnp.where(at_row >= at_col, first, second)
    line = jnp.sum(jnp.where(at_row == at_col, second, 0.0), axis=0, keepdims=True)
    line = jnp.broadcast_to(line, (SUB, line.shape[1]))
    half = packed.shape[0] // 2
    odd = lax.axis_index("coil") % 2 == 1
    kept_ref[:half] = jnp.where(odd, packed[half:], packed[:half])
    given_ref[:half] = jnp.where(odd, packed[:half], packed[half:])
    kept_ref[half:] = line
    given_ref[half:] = line


def load_grams(kept_ref, other_ref):
    odd = lax.axis_index("coil") % 2 == 1
    kept, other = kept_ref[...], other_ref[...]
    low, high = jnp.where(odd, other, kept), jnp.where(odd, kept, other)
    half = low.shape[0] - SUB
    packed = jnp.concatenate([low[:half], high[:half]], axis=0)
    line = low[half : half + 1]
    at_row, at_col = square(packed.shape[0])
    turned = packed.T
    first = jnp.where(at_row >= at_col, packed, turned)
    second = jnp.where(at_row > at_col, turned, packed)
    return first, jnp.where(at_row == at_col, line, second), line


def inverse_factor(gram):
    size = gram.shape[0]
    shape = (SUB, size)
    at_row = lax.broadcasted_iota(jnp.int32, (size, size), 0)
    at_col = lax.broadcasted_iota(jnp.int32, (size, size), 1)
    unit = (at_row == at_col).astype(jnp.float32)
    left = [gram[b : b + SUB] for b in range(0, size, SUB)]
    right = [unit[b : b + SUB] for b in range(0, size, SUB)]
    sub = lax.broadcasted_iota(jnp.int32, shape, 0)
    done = []
    for b in range(len(left)):
        spread = {
            c: [
                jnp.broadcast_to(left[c][:, b * SUB + k : b * SUB + k + 1], shape)
                for k in range(SUB)
            ]
            for c in range(b, len(left))
        }
        entry = {
            (i, k): jnp.broadcast_to(spread[b][k][i : i + 1], shape)
            for k in range(SUB)
            for i in range(k, SUB)
        }
        inverse = {}
        for k in range(SUB):
            root = lax.rsqrt(entry[k, k])
            inverse[k, k] = root
            for i in range(k + 1, SUB):
                entry[i, k] = entry[i, k] * root
            for i in range(k + 1, SUB):
                for m in range(k + 1, i + 1):
                    entry[i, m] = entry[i, m] - entry[i, k] * entry[m, k]
        for i in range(1, SUB):
            for k in range(i):
                total = entry[i, k] * inverse[k, k]
                for m in range(k + 1, i):
                    total = total + entry[i, m] * inverse[m, k]
                inverse[i, k] = -(total * inverse[i, i])

        def solved(rows):
            whole = [jnp.broadcast_to(rows[k : k + 1], shape) for k in range(SUB)]
            first = []
            for i in range(SUB):
                total = inverse[i, 0] * whole[0]
                for k in range(1, i + 1):
                    total = total + inverse[i, k] * whole[k]
                first.append(total)
            second = []
            for k in range(SUB):
                total = inverse[k, k] * first[k]
                for i in range(k + 1, SUB):
                    total = total + inverse[i, k] * first[i]
                second.append(total)
            return first, second

        lower, lower_again = solved(right[b])
        row = lower[0]
        for i in range(1, SUB):
            row = jnp.where(sub == i, lower[i], row)
        done.append(row)
        if b + 1 < len(left):
            _, upper_again = solved(left[b])
            for c in range(b + 1, len(left)):
                for k in range(SUB):
                    left[c] = left[c] - spread[c][k] * upper_again[k]
                    right[c] = right[c] - spread[c][k] * lower_again[k]
    return jnp.concatenate(done, axis=0)


def factor_kernel(gram_ref, other_ref, inverse_ref, next_ref, sound_ref):
    gram, raw, line = load_grams(gram_ref, other_ref)
    inverse = inverse_factor(gram)
    inverse_ref[...] = inverse
    gram = exact(exact(inverse, raw), inverse, ((1,), (1,)))
    next_ref[...] = gram
    at_row, at_col = square(gram.shape[0])
    terms = jnp.sum(inverse * inverse * line, axis=1, keepdims=True)
    result = jnp.sum(jnp.where(at_row == at_col, gram, 0.0), axis=1, keepdims=True)
    worst = jnp.max(jnp.where(terms <= 64.0 * result, 0, 1))
    sound_ref[0] = 1 - worst


def rows_kernel(turned_ref, inverse_ref, gram_ref):
    turned = exact(inverse_ref[...], turned_ref[...])
    gram_ref[...] = exact(turned, turned, ((1,), (1,)))


def both_kernel(gram_ref, inverse_ref, both_ref):
    both_ref[...] = exact(inverse_factor(gram_ref[...]), inverse_ref[...])


def moved_columns(order, cols):
    devices = len(order[0])
    at_row, at_col = square(devices * cols)
    turn = at_col % cols * devices + at_col // cols
    me = lax.axis_index("rows") * lax.axis_size("coil") + lax.axis_index("coil")
    slot = at_col % devices
    mask = jnp.zeros_like(slot)
    bit = 1
    while bit < devices:
        step = jnp.where(2 * at_col < at_col.shape[1], order[0][bit], order[1][bit])
        mask = mask | jnp.where(slot & bit != 0, step, 0)
        bit *= 2
    source = at_col - slot + lax.bitwise_xor(mask, jnp.full_like(mask, me))
    return [(at_row == place).astype(jnp.float32) for place in (turn, source)]


def stacked_dot(a, b):
    a_high, a_low = split(a)
    b_high, b_low = split(b)
    left = jnp.concatenate(
        [
            jnp.concatenate([a_high, a_high], axis=1),
            jnp.concatenate([a_low, jnp.zeros_like(a_low)], axis=1),
        ],
        axis=0,
    )
    both = dot(left, jnp.concatenate([b_high, b_low], axis=0))
    return both[: a.shape[0]] + both[a.shape[0] :]


def last_kernel(
    cols,
    order,
    images_ref,
    both_ref,
    kspace_ref,
    mask_ref,
    top_near_ref,
    top_far_ref,
    low_near_ref,
    low_far_ref,
    recovered_ref,
    basis_ref,
    vectors_ref,
):
    both = both_ref[...]
    reach = images_ref.shape[1]
    factors = [exact(both, moved) for moved in moved_columns(order, cols)]
    chg, tile = kspace_ref.shape
    lanes = top_near_ref.shape[1]
    fold = lanes // chg
    deep = KER // fold
    step = cols // 2 * deep
    lead = reach - tile - KER - 2 * SUB
    images = stacked_dot(factors[0], images_ref[...]).T[lead:]
    rim = reach - tile - SUB - lead
    even, odd = None, None
    for a in range(0, deep, 2):
        turned = [
            jnp.concatenate(
                [
                    ref[pl.ds(k * deep + a + i, ref.shape[0] // step, stride=step), :]
                    for refs in ((top_near_ref, top_far_ref), (low_near_ref, low_far_ref))
                    for k in range(cols // 2)
                    for ref in refs
                ],
                axis=0,
            )
            for i in range(2)
        ]
        vectors = stacked_dot(factors[1], jnp.concatenate(turned, axis=1))
        vectors_ref[:, a * lanes : (a + 2) * lanes] = vectors
        projected = stacked_dot(images, vectors)
        shift = a * fold
        part = projected[rim - shift : rim - shift + tile + SUB, :lanes]
        even = part if even is None else even + part
        part = projected[rim - SUB - shift : rim - shift + tile + SUB, lanes:]
        odd = part if odd is None else odd + part
    total = even + odd[SUB - fold : SUB - fold + tile + SUB]
    estimate = total[SUB : SUB + tile]
    for f in range(1, fold):
        moved = pltpu.roll(total, lanes - f * chg, 1)
        estimate = estimate + moved[SUB - f : SUB - f + tile]
    estimate = estimate.T[:chg]
    owned = basis_ref.shape[0]
    start = pl.multiple_of(lax.axis_index("rows") * owned, owned)
    basis_ref[...] = vectors_ref[:, pl.ds(start, owned)].T
    estimate = estimate / KER
    residual = mask_ref[...].astype(jnp.float32) * (kspace_ref[...] - estimate)
    recovered_ref[...] = estimate + residual - jnp.clip(residual, -threshold, threshold)


def call(kernel, outs, *args, scratch=(), limit=12, scalars=0, micros=1):
    return pl.pallas_call(
        kernel,
        out_shape=[jax.ShapeDtypeStruct(shape, kind) for shape, kind in outs],
        in_specs=[pl.BlockSpec(memory_space=pltpu.VMEM)] * len(args),
        out_specs=[pl.BlockSpec(memory_space=pltpu.VMEM)] * (len(outs) - scalars)
        + [pl.BlockSpec(memory_space=pltpu.SMEM)] * scalars,
        scratch_shapes=list(scratch),
        compiler_params=pltpu.CompilerParams(vmem_limit_bytes=limit * 2**20),
        cost_estimate=pl.CostEstimate(
            flops=micros * 10**9, bytes_accessed=0, transcendentals=0
        ),
    )(*args)


def exchange(block, devices, mask, axes):
    return lax.ppermute(block, axes, [(i, i ^ mask) for i in range(devices)])


def with_masks(masks, mask):
    return masks + [m ^ mask for m in masks]


def after(value, *others):
    return lax.optimization_barrier((value,) + others)[0]


def rounds_of(low, high):
    masks = []
    while low < high:
        if 2 * low < high:
            masks.append([low, 2 * low, 3 * low])
        else:
            masks.append([low])
        low *= 4
    return masks


def gather_round(part, order, masks, devices, axes):
    part = jnp.concatenate(
        [part] + [exchange(part, devices, mask, axes) for mask in masks], axis=0
    )
    return part, order + [m ^ mask for mask in masks for m in order]


def gather_samples(sampled, basis, tiles, groups):
    devices = tiles * groups
    near, masks = sampled[None], [0]
    mask = devices // 2
    while mask > groups:
        near, masks = gather_round(near, masks, [mask], devices, AXES)
        mask //= 2
    basis = to_all(basis)
    near = after(near, basis)
    half = near.shape[1] // 2
    halves = []
    for part, ways in (
        (near[:, :half], (groups, groups // 2)),
        (near[:, half:], (groups // 2, groups)),
    ):
        part, order = gather_round(part, masks, [ways[0]], devices, AXES)
        pieces = [(part, order)]
        mask = ways[1]
        rest = groups // 4
        while mask > 1:
            pieces = pieces + [
                (exchange(part, devices, mask, AXES), [m ^ mask for m in order])
                for part, order in pieces
            ]
            mask, rest = rest, rest // 2
        halves.append(
            pieces
            + [(exchange(part, devices, 1, AXES), [m ^ 1 for m in order]) for part, order in pieces]
        )
    return halves, basis


def to_all(pieces, axes=AXES):
    return lax.all_to_all(pieces, axes, 0, 0, tiled=True)


def gather_group(group, devices):
    groups = group.shape[0]
    parts = [group[:1]]
    parts += [exchange(group[s : s + 1], devices, s, AXES) for s in range(1, groups)]
    return jnp.concatenate(parts, axis=0), list(range(groups))


def total_beside(kept, given, near, order, images, groups, devices):
    ways = []
    mask = devices // 2
    while mask >= groups:
        ways.append(mask)
        mask //= 2
    half = near.shape[1] // 2
    parts = [near[:, :half], near[:, half:]]
    orders = [order, order]
    ways = [ways, ways[-1:] + ways[:-1]]
    step = 0

    def advance():
        for i in range(2):
            parts[i], orders[i] = gather_round(
                parts[i], orders[i], [ways[i][step]], devices, AXES
            )

    total = kept + exchange(given, devices, 1, AXES)
    for partners in reversed(rounds_of(2, devices)):
        terms = [exchange(total, devices, way, AXES) for way in partners]
        total = total + terms[0]
        if len(terms) == 3:
            total = total + (terms[1] + terms[2])
        if step < len(ways[0]) - 1:
            advance()
            step += 1
    while step < len(ways[0]) - 1:
        advance()
        step += 1
    other = exchange(total, devices, 1, AXES)
    *parts, total, other, images = lax.optimization_barrier((*parts, total, other, images))
    pieces = []
    for i in range(2):
        mask = ways[i][-1]
        pieces += [parts[i], exchange(parts[i], devices, mask, AXES)]
        orders[i] = orders[i] + [m ^ mask for m in orders[i]]
    return (total, other), pieces, orders, to_all(images)


def column_shards(kspace, sample_mask, start_basis):
    f32, bf16 = jnp.float32, jnp.bfloat16
    tiles, groups = lax.axis_size("rows"), lax.axis_size("coil")
    devices = tiles * groups
    chg, tile = kspace.shape
    channels = chg * groups
    positions = tile * tiles
    owned, rank = start_basis.shape[1:]
    per_tile = owned // chg
    cols = rank // devices
    rows = cols * KER
    lanes = cols * chg

    sampled = kspace * sample_mask.astype(f32)
    (basis_send,) = call(
        functools.partial(prepare_kernel, cols, chg, per_tile),
        [((devices * per_tile, lanes), f32)],
        start_basis.reshape(owned, rank),
    )
    halves, basis_parts = gather_samples(
        sampled, basis_send.reshape(devices, per_tile, lanes), tiles, groups
    )
    starts = (0, chg // len(halves))
    orders = [(start, order) for start, half in zip(starts, halves) for _, order in half]
    wide = pltpu.VMEM((rows, positions), f32)
    moved = pltpu.VMEM((2 * rows, positions), bf16)
    samples, normal, send, group = call(
        functools.partial(passes_kernel, orders),
        [
            ((tiles, 2, groups, chg, tile), bf16),
            ((rows, channels), f32),
            ((tiles, groups, per_tile, lanes), f32),
            ((groups, rows * chg // lanes, lanes), f32),
        ],
        basis_parts.reshape(tiles, groups, per_tile, lanes),
        *[piece for half in halves for piece, _ in half],
        scratch=[wide, moved],
        limit=24,
        micros=12,
    )
    received = to_all(send.reshape(devices, per_tile, lanes))
    reach = tile + LANES
    (images,) = call(
        images_kernel,
        [((tiles, groups, cols, reach), f32)],
        samples,
        normal,
        scratch=[wide],
        limit=16,
        micros=2,
    )
    near, order = gather_group(group, devices)
    received = after(received, images, near)
    half = ((rank // 2 + SUB, rank), f32)
    kept, given, turned = call(
        functools.partial(gram_kernel, cols, per_tile),
        [half, half, ((rank, owned), f32)],
        received.reshape(devices * per_tile, lanes),
        start_basis.reshape(owned, rank),
    )
    gram, pieces, order, images = total_beside(
        kept, given, near, order, images.reshape(devices, cols, reach), groups, devices
    )
    whole = ((rank, rank), f32)
    first, second, sound = call(
        factor_kernel, [whole, whole, ((1,), jnp.int32)], *gram, scalars=1, micros=12
    )

    def again():
        (gram,) = call(rows_kernel, [whole], turned, first)
        mask = 1
        while mask < devices:
            gram = gram + exchange(gram, devices, mask, AXES)
            mask *= 2
        return gram

    second = lax.cond(sound[0] == 1, lambda: second, again)
    (both,) = call(both_kernel, [whole], second, first, micros=0)
    recovered, basis = call(
        functools.partial(last_kernel, cols, order),
        [((chg, tile), f32), ((owned, rank), f32)],
        images.reshape(rank, reach),
        both,
        kspace,
        sample_mask,
        *[piece.reshape(-1, lanes) for piece in pieces],
        scratch=[pltpu.VMEM((rank, KER * chg), f32)],
        limit=16,
        micros=5,
    )
    return (recovered, basis.reshape(1, owned, rank))


def divides_columns(kspace, start_basis):
    tiles, groups = lax.axis_size("rows"), lax.axis_size("coil")
    devices = tiles * groups
    chg, tile = kspace.shape
    owned, rank = start_basis.shape[1:]
    return (
        devices & (devices - 1) == 0
        and tiles > 2
        and groups > 2
        and rank % (2 * SUB) == 0
        and rank % devices == 0
        and rank % LANES == 0
        and tile % LANES == 0
        and owned == SUB * chg
        and chg * (rank // devices) == LANES
        and 2 * (LANES // chg) == SUB
        and KER + 2 * SUB <= LANES
        and chg % (4 * SUB) == 0
        and (chg * groups) % LANES == 0
        and KER <= LANES
        and rank // devices <= SUB
        and rank // devices % 2 == 0
    )


def shards(kspace, sample_mask, start_basis):
    if divides_columns(kspace, start_basis):
        return column_shards(kspace, sample_mask, start_basis)
    return general_shards(kspace, sample_mask, start_basis)


def solution(mesh):
    return jax.shard_map(
        shards,
        mesh=mesh,
        in_specs=(P("coil", "rows"), P("coil", "rows"), P("coil", "rows", None)),
        out_specs=(P("coil", "rows"), P("coil", "rows", None)),
        check_vma=False,
    )
```

```python
import functools

import jax
import jax.numpy as jnp
from jax import lax
from jax.experimental import pallas as pl
from jax.experimental.pallas import tpu as pltpu
from jax.sharding import PartitionSpec as P

KER = 64
ITERS = 2
LANES = 128
SUB = 8
AXES = ("rows", "coil")


threshold = 0.05


def shifted(block, axis, distance):
    devices = range(lax.axis_size(axis))
    route = [((i - distance) % len(devices), i) for i in devices]
    return lax.ppermute(block, axis, route)


def orthonormal(normal_rows, gram_matrix):
    factor = jnp.linalg.cholesky(gram_matrix)
    return lax.linalg.triangular_solve(
        factor, normal_rows, left_side=False, lower=True, transpose_a=True
    )


def coil_total(partial_value):
    return lax.psum(partial_value, "coil")


def general_shards(kspace, sample_mask, start_basis):
    highest = lax.Precision.HIGHEST
    channels = kspace.shape[0]
    tile_rows = kspace.shape[1]
    mask_float = sample_mask.astype(jnp.float32)
    sampled = kspace * mask_float
    next_rim = shifted(sampled[:, : KER - 1], "rows", -1)
    extended = jnp.concatenate([sampled, next_rim], axis=1)
    hankel_cols = jnp.stack(
        [extended[:, offset : offset + tile_rows] for offset in range(KER)], axis=0
    )
    hankel_cols = hankel_cols.reshape(KER * channels, tile_rows)
    owned_basis = start_basis.reshape(start_basis.shape[1], start_basis.shape[2])
    whole_basis = lax.all_gather(owned_basis, "rows", axis=0, tiled=True)
    for iteration in range(ITERS):
        images = coil_total(
            lax.dot_general(
                whole_basis,
                hankel_cols,
                (((0,), (0,)), ((), ())),
                precision=highest,
                preferred_element_type=jnp.float32,
            )
        )
        local_normal = lax.dot_general(
            hankel_cols,
            images,
            (((1,), (1,)), ((), ())),
            precision=highest,
            preferred_element_type=jnp.float32,
        )
        normal_whole = lax.psum(local_normal, "rows")
        local_gram = jnp.dot(
            normal_whole.T, normal_whole, precision=highest, preferred_element_type=jnp.float32
        )
        gram_matrix = lax.psum(local_gram, "coil")
        whole_basis = orthonormal(normal_whole, gram_matrix)
    images = coil_total(
        lax.dot_general(
            whole_basis,
            hankel_cols,
            (((0,), (0,)), ((), ())),
            precision=highest,
            preferred_element_type=jnp.float32,
        )
    )
    projected = jnp.dot(whole_basis, images, precision=highest, preferred_element_type=jnp.float32)
    owned_count = whole_basis.shape[0] // lax.axis_size("rows")
    owned_basis = lax.dynamic_slice_in_dim(
        whole_basis, lax.axis_index("rows") * owned_count, owned_count, 0
    )
    stacked = projected.reshape(KER, channels, tile_rows)
    spread = jnp.zeros((channels, tile_rows + KER - 1), jnp.float32)
    for offset in range(KER):
        spread = spread.at[:, offset : offset + tile_rows].add(stacked[offset])
    carried = shifted(spread[:, tile_rows:], "rows", 1)
    estimate = spread[:, :tile_rows].at[:, : KER - 1].add(carried) / KER
    residual = mask_float * (kspace - estimate)
    recovered = estimate + residual - jnp.clip(residual, -threshold, threshold)
    return (recovered, owned_basis.reshape(1, owned_basis.shape[0], owned_basis.shape[1]))


def split(value):
    high = value.astype(jnp.bfloat16)
    low = (value - high.astype(jnp.float32)).astype(jnp.bfloat16)
    return high, low


def dot(a, b, dims=((1,), (0,))):
    return lax.dot_general(a, b, (dims, ((), ())), preferred_element_type=jnp.float32)


def dot3(a, b, dims=((1,), (0,))):
    a_high, a_low = split(a)
    b_high, b_low = split(b)
    return dot(a_high, b_high, dims) + (dot(a_high, b_low, dims) + dot(a_low, b_high, dims))


def square(size):
    at_row = lax.broadcasted_iota(jnp.int32, (size, size), 0)
    at_col = lax.broadcasted_iota(jnp.int32, (size, size), 1)
    return at_row, at_col


def prepare_kernel(cols, chg, per_tile, basis_ref, send_ref):
    turned = basis_ref[...].T
    devices = turned.shape[0] // cols
    for j in range(per_tile):
        part = turned[:, j * chg : (j + 1) * chg]
        row = jnp.concatenate([part[k * devices : (k + 1) * devices] for k in range(cols)], axis=1)
        send_ref[pl.ds(j, devices, stride=per_tile), :] = row


def images_of(vectors, samples_ref, wide_ref):
    rows, channels = vectors.shape
    cols = rows // KER
    high, low = split(vectors)
    at_row = lax.broadcasted_iota(jnp.int32, (rows, rows), 0)
    at_col = lax.broadcasted_iota(jnp.int32, (rows, rows), 1)
    flip = ((at_row // KER == at_col // KER) & (at_row % KER + at_col % KER == KER - 1)).astype(
        jnp.float32
    ).astype(jnp.bfloat16)
    both = dot(flip, jnp.concatenate([high, low], axis=1)).astype(jnp.bfloat16)
    high, low = both[:, :channels], both[:, channels:]
    parts = jnp.concatenate([high, high, low], axis=1)
    tiles = samples_ref.shape[0]
    tile = samples_ref.shape[-1]
    for t in range(tiles):
        block = samples_ref[t].reshape(2 * channels, tile)
        block = jnp.concatenate([block, block[:channels]], axis=0)
        wide_ref[:, t * tile : (t + 1) * tile] = dot(parts, block)
    images = []
    for k in range(cols):
        total = None
        for i in reversed(range(0, KER, SUB)):
            part = wide_ref[k * KER + i : k * KER + i + SUB, :]
            total = part if total is None else pltpu.roll(total, SUB, 1) + part
        total = pltpu.roll(total, 0, 1, stride=1, stride_axis=0)
        images.append(jnp.sum(total, axis=0, keepdims=True))
    return images


def normal_of(images, samples_ref, moved_ref):
    cols = len(images)
    positions = images[0].shape[1]
    tiles = samples_ref.shape[0]
    tile = samples_ref.shape[-1]
    channels = samples_ref.shape[2] * samples_ref.shape[3]
    rows = cols * KER
    for k in range(cols):
        base = jnp.broadcast_to(images[k], (SUB, positions))
        base = pltpu.roll(base, positions - (KER - 1), 1, stride=1, stride_axis=0)
        for j in range(0, KER, 2 * SUB):
            first = base if j == 0 else pltpu.roll(base, j, 1)
            second = pltpu.roll(base, j + SUB, 1)
            high, low = split(jnp.concatenate([first, second], axis=0))
            moved_ref[k * KER + j : k * KER + j + 2 * SUB, :] = high
            moved_ref[rows + k * KER + j : rows + k * KER + j + 2 * SUB, :] = low
    high = jnp.zeros((rows, 2 * channels), jnp.float32)
    low = jnp.zeros((rows, channels), jnp.float32)
    for t in range(tiles):
        block = samples_ref[t].reshape(2 * channels, tile)
        lanes = slice(t * tile, (t + 1) * tile)
        high = high + dot(moved_ref[:rows, lanes], block, ((1,), (1,)))
        low = low + dot(moved_ref[rows:, lanes], block[:channels], ((1,), (1,)))
    return high[:, :channels] + (high[:, channels:] + low)


def store_by_rows(normal, send_ref):
    tiles, groups, per_tile, lanes = send_ref.shape
    cols = normal.shape[0] // KER
    chg = normal.shape[1] // groups
    for g in range(groups):
        joined = jnp.concatenate(
            [normal[k * KER : (k + 1) * KER, g * chg : (g + 1) * chg] for k in range(cols)], axis=1
        )
        send_ref[:, g] = joined.reshape(tiles, per_tile, lanes)


def store_by_groups(normal_ref, group_ref):
    groups, count, lanes = group_ref.shape
    rows, channels = normal_ref.shape
    chg = channels // groups
    fold = lanes // chg
    cols = rows // KER
    deep = KER // fold
    me = lax.axis_index("coil")
    parts = [
        [normal_ref[pl.ds(k * KER + f, deep, stride=fold), :] for f in range(fold)]
        for k in range(cols)
    ]
    for g in range(groups):
        joined = [
            jnp.concatenate([part[:, g * chg : (g + 1) * chg] for part in parts[k]], axis=1)
            for k in range(cols)
        ]
        group_ref[lax.bitwise_xor(me, g)] = jnp.concatenate(joined, axis=0)


def passes_kernel(orders, basis_ref, *refs):
    *pieces, samples_ref, normal_ref, send_ref, group_ref, wide_ref, moved_ref = refs
    tiles, _, groups, chg, tile = samples_ref.shape
    me = lax.axis_index("rows") * groups + lax.axis_index("coil")
    for (start, order), piece_ref in zip(orders, pieces):
        count = piece_ref.shape[1]
        for slot, mask in enumerate(order):
            high, low = split(piece_ref[slot])
            source = lax.bitwise_xor(me, mask)
            t, g = source // groups, source % groups
            samples_ref[t, 0, g, start : start + count] = high
            samples_ref[t, 1, g, start : start + count] = low
    cols = basis_ref.shape[-1] // chg
    rows = []
    for k in range(cols):
        rows.append(
            jnp.concatenate(
                [
                    basis_ref[:, g].reshape(KER, cols * chg)[:, k * chg : (k + 1) * chg]
                    for g in range(groups)
                ],
                axis=1,
            )
        )
    vectors = jnp.concatenate(rows, axis=0)
    normal = normal_of(images_of(vectors, samples_ref, wide_ref), samples_ref, moved_ref)
    power = jnp.zeros((1, tile), jnp.float32)
    for t in range(samples_ref.shape[0]):
        value = samples_ref[t, 0].reshape(groups * chg, tile).astype(jnp.float32)
        power = power + jnp.sum(value * value, axis=0, keepdims=True)
    normal = normal * (groups * chg / jnp.sum(power))
    normal = normal_of(images_of(normal, samples_ref, wide_ref), samples_ref, moved_ref)
    normal_ref[...] = normal
    store_by_rows(normal, send_ref)
    store_by_groups(normal_ref, group_ref)


def images_kernel(samples_ref, vectors_ref, send_ref, wide_ref):
    tiles, groups, cols, reach = send_ref.shape
    tile = samples_ref.shape[-1]
    images = jnp.concatenate(images_of(vectors_ref[...], samples_ref, wide_ref), axis=0)
    positions = images.shape[1]
    images = pltpu.roll(images, positions - (KER - 1), 1)
    rim = reach - tile
    for t in range(tiles):
        if t == 0:
            part = jnp.concatenate([images[:, positions - rim :], images[:, :tile]], axis=1)
        else:
            part = images[:, t * tile - rim : (t + 1) * tile]
        for g in range(groups):
            send_ref[t, g] = part


def gather_turned(received_ref, cols, per_tile):
    count, lanes = received_ref.shape
    devices = count // per_tile
    chg = lanes // cols
    loaded = [received_ref[pl.ds(j, devices, stride=per_tile), :] for j in range(per_tile)]
    return jnp.concatenate(
        [
            jnp.concatenate(
                [loaded[j][:, k * chg : (k + 1) * chg] for j in range(per_tile)], axis=1
            )
            for k in range(cols)
        ],
        axis=0,
    )


def exact(a, b, dims=((1,), (0,))):
    return lax.dot_general(
        a, b, (dims, ((), ())), precision=lax.Precision.HIGHEST, preferred_element_type=jnp.float32
    )


def gram_kernel(cols, per_tile, received_ref, basis_ref, kept_ref, given_ref, turned_ref):
    turned = gather_turned(received_ref, cols, per_tile)
    first = exact(basis_ref[...], turned, ((0,), (1,)))
    second = exact(turned, turned, ((1,), (1,)))
    turned_ref[...] = turned
    at_row, at_col = square(first.shape[0])
    packed = jnp.where(at_row >= at_col, first, second)
    line = jnp.sum(jnp.where(at_row == at_col, second, 0.0), axis=0, keepdims=True)
    line = jnp.broadcast_to(line, (SUB, line.shape[1]))
    half = packed.shape[0] // 2
    odd = lax.axis_index("coil") % 2 == 1
    kept_ref[:half] = jnp.where(odd, packed[half:], packed[:half])
    given_ref[:half] = jnp.where(odd, packed[:half], packed[half:])
    kept_ref[half:] = line
    given_ref[half:] = line


def load_grams(kept_ref, other_ref):
    odd = lax.axis_index("coil") % 2 == 1
    kept, other = kept_ref[...], other_ref[...]
    low, high = jnp.where(odd, other, kept), jnp.where(odd, kept, other)
    half = low.shape[0] - SUB
    packed = jnp.concatenate([low[:half], high[:half]], axis=0)
    line = low[half : half + 1]
    at_row, at_col = square(packed.shape[0])
    turned = packed.T
    first = jnp.where(at_row >= at_col, packed, turned)
    second = jnp.where(at_row > at_col, turned, packed)
    return first, jnp.where(at_row == at_col, line, second), line


def inverse_factor(gram):
    size = gram.shape[0]
    shape = (SUB, size)
    at_row = lax.broadcasted_iota(jnp.int32, (size, size), 0)
    at_col = lax.broadcasted_iota(jnp.int32, (size, size), 1)
    unit = (at_row == at_col).astype(jnp.float32)
    left = [gram[b : b + SUB] for b in range(0, size, SUB)]
    right = [unit[b : b + SUB] for b in range(0, size, SUB)]
    sub = lax.broadcasted_iota(jnp.int32, shape, 0)
    done = []
    for b in range(len(left)):
        spread = {
            c: [
                jnp.broadcast_to(left[c][:, b * SUB + k : b * SUB + k + 1], shape)
                for k in range(SUB)
            ]
            for c in range(b, len(left))
        }
        entry = {
            (i, k): jnp.broadcast_to(spread[b][k][i : i + 1], shape)
            for k in range(SUB)
            for i in range(k, SUB)
        }
        inverse = {}
        for k in range(SUB):
            root = lax.rsqrt(entry[k, k])
            inverse[k, k] = root
            for i in range(k + 1, SUB):
                entry[i, k] = entry[i, k] * root
            for i in range(k + 1, SUB):
                for m in range(k + 1, i + 1):
                    entry[i, m] = entry[i, m] - entry[i, k] * entry[m, k]
        for i in range(1, SUB):
            for k in range(i):
                total = entry[i, k] * inverse[k, k]
                for m in range(k + 1, i):
                    total = total + entry[i, m] * inverse[m, k]
                inverse[i, k] = -(total * inverse[i, i])

        def solved(rows):
            whole = [jnp.broadcast_to(rows[k : k + 1], shape) for k in range(SUB)]
            first = []
            for i in range(SUB):
                total = inverse[i, 0] * whole[0]
                for k in range(1, i + 1):
                    total = total + inverse[i, k] * whole[k]
                first.append(total)
            second = []
            for k in range(SUB):
                total = inverse[k, k] * first[k]
                for i in range(k + 1, SUB):
                    total = total + inverse[i, k] * first[i]
                second.append(total)
            return first, second

        lower, lower_again = solved(right[b])
        row = lower[0]
        for i in range(1, SUB):
            row = jnp.where(sub == i, lower[i], row)
        done.append(row)
        if b + 1 < len(left):
            _, upper_again = solved(left[b])
            for c in range(b + 1, len(left)):
                for k in range(SUB):
                    left[c] = left[c] - spread[c][k] * upper_again[k]
                    right[c] = right[c] - spread[c][k] * lower_again[k]
    return jnp.concatenate(done, axis=0)


def factor_kernel(gram_ref, other_ref, inverse_ref, next_ref, sound_ref):
    gram, raw, line = load_grams(gram_ref, other_ref)
    inverse = inverse_factor(gram)
    inverse_ref[...] = inverse
    gram = exact(exact(inverse, raw), inverse, ((1,), (1,)))
    next_ref[...] = gram
    at_row, at_col = square(gram.shape[0])
    terms = jnp.sum(inverse * inverse * line, axis=1, keepdims=True)
    result = jnp.sum(jnp.where(at_row == at_col, gram, 0.0), axis=1, keepdims=True)
    worst = jnp.max(jnp.where(terms <= 64.0 * result, 0, 1))
    sound_ref[0] = 1 - worst


def rows_kernel(turned_ref, inverse_ref, gram_ref):
    turned = exact(inverse_ref[...], turned_ref[...])
    gram_ref[...] = exact(turned, turned, ((1,), (1,)))


def both_kernel(gram_ref, inverse_ref, both_ref):
    both_ref[...] = exact(inverse_factor(gram_ref[...]), inverse_ref[...])


def moved_columns(order, cols):
    devices = len(order[0])
    at_row, at_col = square(devices * cols)
    turn = at_col % cols * devices + at_col // cols
    me = lax.axis_index("rows") * lax.axis_size("coil") + lax.axis_index("coil")
    slot = at_col % devices
    mask = jnp.zeros_like(slot)
    bit = 1
    while bit < devices:
        step = jnp.where(2 * at_col < at_col.shape[1], order[0][bit], order[1][bit])
        mask = mask | jnp.where(slot & bit != 0, step, 0)
        bit *= 2
    source = at_col - slot + lax.bitwise_xor(mask, jnp.full_like(mask, me))
    return [(at_row == place).astype(jnp.float32) for place in (turn, source)]


def stacked_dot(a, b):
    a_high, a_low = split(a)
    b_high, b_low = split(b)
    left = jnp.concatenate(
        [
            jnp.concatenate([a_high, a_high], axis=1),
            jnp.concatenate([a_low, jnp.zeros_like(a_low)], axis=1),
        ],
        axis=0,
    )
    both = dot(left, jnp.concatenate([b_high, b_low], axis=0))
    return both[: a.shape[0]] + both[a.shape[0] :]


def last_kernel(
    cols,
    order,
    images_ref,
    both_ref,
    kspace_ref,
    mask_ref,
    top_near_ref,
    top_far_ref,
    low_near_ref,
    low_far_ref,
    recovered_ref,
    basis_ref,
    vectors_ref,
):
    both = both_ref[...]
    reach = images_ref.shape[1]
    factors = [exact(both, moved) for moved in moved_columns(order, cols)]
    chg, tile = kspace_ref.shape
    lanes = top_near_ref.shape[1]
    fold = lanes // chg
    deep = KER // fold
    step = cols // 2 * deep
    lead = reach - tile - KER - 2 * SUB
    images = stacked_dot(factors[0], images_ref[...]).T[lead:]
    rim = reach - tile - SUB - lead
    even, odd = None, None
    for a in range(0, deep, 2):
        turned = [
            jnp.concatenate(
                [
                    ref[pl.ds(k * deep + a + i, ref.shape[0] // step, stride=step), :]
                    for refs in ((top_near_ref, top_far_ref), (low_near_ref, low_far_ref))
                    for k in range(cols // 2)
                    for ref in refs
                ],
                axis=0,
            )
            for i in range(2)
        ]
        vectors = stacked_dot(factors[1], jnp.concatenate(turned, axis=1))
        vectors_ref[:, a * lanes : (a + 2) * lanes] = vectors
        projected = stacked_dot(images, vectors)
        shift = a * fold
        part = projected[rim - shift : rim - shift + tile + SUB, :lanes]
        even = part if even is None else even + part
        part = projected[rim - SUB - shift : rim - shift + tile + SUB, lanes:]
        odd = part if odd is None else odd + part
    total = even + odd[SUB - fold : SUB - fold + tile + SUB]
    estimate = total[SUB : SUB + tile]
    for f in range(1, fold):
        moved = pltpu.roll(total, lanes - f * chg, 1)
        estimate = estimate + moved[SUB - f : SUB - f + tile]
    estimate = estimate.T[:chg]
    owned = basis_ref.shape[0]
    start = pl.multiple_of(lax.axis_index("rows") * owned, owned)
    basis_ref[...] = vectors_ref[:, pl.ds(start, owned)].T
    estimate = estimate / KER
    residual = mask_ref[...].astype(jnp.float32) * (kspace_ref[...] - estimate)
    recovered_ref[...] = estimate + residual - jnp.clip(residual, -threshold, threshold)


def call(kernel, outs, *args, scratch=(), limit=12, scalars=0, micros=1):
    return pl.pallas_call(
        kernel,
        out_shape=[jax.ShapeDtypeStruct(shape, kind) for shape, kind in outs],
        in_specs=[pl.BlockSpec(memory_space=pltpu.VMEM)] * len(args),
        out_specs=[pl.BlockSpec(memory_space=pltpu.VMEM)] * (len(outs) - scalars)
        + [pl.BlockSpec(memory_space=pltpu.SMEM)] * scalars,
        scratch_shapes=list(scratch),
        compiler_params=pltpu.CompilerParams(vmem_limit_bytes=limit * 2**20),
        cost_estimate=pl.CostEstimate(
            flops=micros * 10**9, bytes_accessed=0, transcendentals=0
        ),
    )(*args)


def exchange(block, devices, mask, axes):
    return lax.ppermute(block, axes, [(i, i ^ mask) for i in range(devices)])


def with_masks(masks, mask):
    return masks + [m ^ mask for m in masks]


def after(value, *others):
    return lax.optimization_barrier((value,) + others)[0]


def rounds_of(low, high):
    masks = []
    while low < high:
        if 2 * low < high:
            masks.append([low, 2 * low, 3 * low])
        else:
            masks.append([low])
        low *= 4
    return masks


def gather_round(part, order, masks, devices, axes):
    part = jnp.concatenate(
        [part] + [exchange(part, devices, mask, axes) for mask in masks], axis=0
    )
    return part, order + [m ^ mask for mask in masks for m in order]


def gather_samples(sampled, basis, tiles, groups):
    devices = tiles * groups
    near, masks = sampled[None], [0]
    mask = devices // 2
    while mask > groups:
        near, masks = gather_round(near, masks, [mask], devices, AXES)
        mask //= 2
    basis = to_all(basis)
    near = after(near, basis)
    half = near.shape[1] // 2
    halves = []
    for part, ways in (
        (near[:, :half], (groups, groups // 2)),
        (near[:, half:], (groups // 2, groups)),
    ):
        part, order = gather_round(part, masks, [ways[0]], devices, AXES)
        pieces = [(part, order)]
        mask = ways[1]
        rest = groups // 4
        while mask > 1:
            pieces = pieces + [
                (exchange(part, devices, mask, AXES), [m ^ mask for m in order])
                for part, order in pieces
            ]
            mask, rest = rest, rest // 2
        halves.append(
            pieces
            + [(exchange(part, devices, 1, AXES), [m ^ 1 for m in order]) for part, order in pieces]
        )
    return halves, basis


def to_all(pieces, axes=AXES):
    return lax.all_to_all(pieces, axes, 0, 0, tiled=True)


def gather_group(group, devices):
    groups = group.shape[0]
    parts = [group[:1]]
    parts += [exchange(group[s : s + 1], devices, s, AXES) for s in range(1, groups)]
    return jnp.concatenate(parts, axis=0), list(range(groups))


def total_beside(kept, given, near, order, images, groups, devices):
    ways = []
    mask = devices // 2
    while mask >= groups:
        ways.append(mask)
        mask //= 2
    half = near.shape[1] // 2
    parts = [near[:, :half], near[:, half:]]
    orders = [order, order]
    ways = [ways, ways[-1:] + ways[:-1]]
    step = 0

    def advance():
        for i in range(2):
            parts[i], orders[i] = gather_round(
                parts[i], orders[i], [ways[i][step]], devices, AXES
            )

    total = kept + exchange(given, devices, 1, AXES)
    for partners in rounds_of(2, devices):
        terms = [exchange(total, devices, way, AXES) for way in partners]
        total = total + terms[0]
        if len(terms) == 3:
            total = total + (terms[1] + terms[2])
        images = after(images, terms[0])
        if step < len(ways[0]) - 1:
            advance()
            step += 1
    while step < len(ways[0]) - 1:
        advance()
        step += 1
    other = exchange(total, devices, 1, AXES)
    *parts, total, other = lax.optimization_barrier((*parts, total, other))
    pieces = []
    for i in range(2):
        mask = ways[i][-1]
        pieces += [parts[i], exchange(parts[i], devices, mask, AXES)]
        orders[i] = orders[i] + [m ^ mask for m in orders[i]]
    return (total, other), pieces, orders, to_all(images)


def column_shards(kspace, sample_mask, start_basis):
    f32, bf16 = jnp.float32, jnp.bfloat16
    tiles, groups = lax.axis_size("rows"), lax.axis_size("coil")
    devices = tiles * groups
    chg, tile = kspace.shape
    channels = chg * groups
    positions = tile * tiles
    owned, rank = start_basis.shape[1:]
    per_tile = owned // chg
    cols = rank // devices
    rows = cols * KER
    lanes = cols * chg

    sampled = kspace * sample_mask.astype(f32)
    (basis_send,) = call(
        functools.partial(prepare_kernel, cols, chg, per_tile),
        [((devices * per_tile, lanes), f32)],
        start_basis.reshape(owned, rank),
    )
    halves, basis_parts = gather_samples(
        sampled, basis_send.reshape(devices, per_tile, lanes), tiles, groups
    )
    starts = (0, chg // len(halves))
    orders = [(start, order) for start, half in zip(starts, halves) for _, order in half]
    wide = pltpu.VMEM((rows, positions), f32)
    moved = pltpu.VMEM((2 * rows, positions), bf16)
    samples, normal, send, group = call(
        functools.partial(passes_kernel, orders),
        [
            ((tiles, 2, groups, chg, tile), bf16),
            ((rows, channels), f32),
            ((tiles, groups, per_tile, lanes), f32),
            ((groups, rows * chg // lanes, lanes), f32),
        ],
        basis_parts.reshape(tiles, groups, per_tile, lanes),
        *[piece for half in halves for piece, _ in half],
        scratch=[wide, moved],
        limit=24,
        micros=12,
    )
    received = to_all(send.reshape(devices, per_tile, lanes))
    reach = tile + LANES
    (images,) = call(
        images_kernel,
        [((tiles, groups, cols, reach), f32)],
        samples,
        normal,
        scratch=[wide],
        limit=16,
        micros=2,
    )
    near, order = gather_group(group, devices)
    received, near = lax.optimization_barrier((received, images, near))[::2]
    half = ((rank // 2 + SUB, rank), f32)
    kept, given, turned = call(
        functools.partial(gram_kernel, cols, per_tile),
        [half, half, ((rank, owned), f32)],
        received.reshape(devices * per_tile, lanes),
        start_basis.reshape(owned, rank),
    )
    gram, pieces, order, images = total_beside(
        kept, given, near, order, images.reshape(devices, cols, reach), groups, devices
    )
    whole = ((rank, rank), f32)
    first, second, sound = call(
        factor_kernel, [whole, whole, ((1,), jnp.int32)], *gram, scalars=1, micros=12
    )

    def again():
        (gram,) = call(rows_kernel, [whole], turned, first)
        mask = 1
        while mask < devices:
            gram = gram + exchange(gram, devices, mask, AXES)
            mask *= 2
        return gram

    second = lax.cond(sound[0] == 1, lambda: second, again)
    (both,) = call(both_kernel, [whole], second, first, micros=0)
    recovered, basis = call(
        functools.partial(last_kernel, cols, order),
        [((chg, tile), f32), ((owned, rank), f32)],
        images.reshape(rank, reach),
        both,
        kspace,
        sample_mask,
        *[piece.reshape(-1, lanes) for piece in pieces],
        scratch=[pltpu.VMEM((rank, KER * chg), f32)],
        limit=16,
        micros=5,
    )
    return (recovered, basis.reshape(1, owned, rank))


def divides_columns(kspace, start_basis):
    tiles, groups = lax.axis_size("rows"), lax.axis_size("coil")
    devices = tiles * groups
    chg, tile = kspace.shape
    owned, rank = start_basis.shape[1:]
    return (
        devices & (devices - 1) == 0
        and tiles > 2
        and groups > 2
        and rank % (2 * SUB) == 0
        and rank % devices == 0
        and rank % LANES == 0
        and tile % LANES == 0
        and owned == SUB * chg
        and chg * (rank // devices) == LANES
        and 2 * (LANES // chg) == SUB
        and KER + 2 * SUB <= LANES
        and chg % (4 * SUB) == 0
        and (chg * groups) % LANES == 0
        and KER <= LANES
        and rank // devices <= SUB
        and rank // devices % 2 == 0
    )


def shards(kspace, sample_mask, start_basis):
    if divides_columns(kspace, start_basis):
        return column_shards(kspace, sample_mask, start_basis)
    return general_shards(kspace, sample_mask, start_basis)


def solution(mesh):
    return jax.shard_map(
        shards,
        mesh=mesh,
        in_specs=(P("coil", "rows"), P("coil", "rows"), P("coil", "rows", None)),
        out_specs=(P("coil", "rows"), P("coil", "rows", None)),
        check_vma=False,
    )
```
